32 devices in a mesh: head: 4 (over y, x), seq: 8 (over z, core).
Axes of the slice: x: 2, y: 2, z: 4, core: 2. Of those that a mesh axis runs over, the one named last changes fastest.
Arguments:
- post_stream: bfloat16 [16, 2048, 512], P('seq', 'head'), may hold values from -6 to 6
- accum_stream: bfloat16 [16, 2048, 512], P('seq', 'head'), may hold values from -6 to 6
- seq_lengths: int32 [16], P('seq'), may hold values from 1024 to 2048, as said below
- qkv_weight: bfloat16 [512, 1536], replicated, may hold values from -0.25 to 0.25
- out_weight: bfloat16 [512, 512], replicated, may hold values from -6 to 6
- norm1_gain: float32 [512], replicated, may hold values from 0.5 to 1.5
- norm1_bias: float32 [512], replicated, may hold values from -3 to 3
- up_weight: bfloat16 [512, 2048], replicated, may hold values from -0.25 to 0.25
- up_bias: float32 [2048], replicated, may hold values from -3 to 3
- down_weight: bfloat16 [2048, 512], replicated, may hold values from -0.125 to 0.125
- down_bias: float32 [512], replicated, may hold values from -3 to 3
- norm2_gain: float32 [512], replicated, may hold values from 0.5 to 1.5
- norm2_bias: float32 [512], replicated, may hold values from -3 to 3
- post_cotan: bfloat16 [16, 2048, 512], P('seq', 'head'), may hold values from -6 to 6
- accum_cotan: bfloat16 [16, 2048, 512], P('seq', 'head'), may hold values from -6 to 6
Outputs:
- post_result: float32 [16, 2048, 512], P('seq', 'head')
- accum_result: float32 [16, 2048, 512], P('seq', 'head')
- post_grad: float32 [16, 2048, 512], P('seq', 'head')
- accum_grad: float32 [16, 2048, 512], P('seq', 'head')
- qkv_weight_grad: float32 [512, 1536], P('seq')
- out_weight_grad: float32 [512, 512], P('seq')
- norm1_gain_grad: float32 [512], P('seq')
- norm1_bias_grad: float32 [512], P('seq')
- up_weight_grad: float32 [512, 2048], P('seq')
- up_bias_grad: float32 [2048], P('seq')
- down_weight_grad: float32 [2048, 512], P('seq')
- down_bias_grad: float32 [512], P('seq')
- norm2_gain_grad: float32 [512], P('seq')
- norm2_bias_grad: float32 [512], P('seq')
The draws below stay inside these ranges and needn't reach their ends.
Inputs may be any that keep to these rules, and one draw needn't show every extreme that they name: `seq_lengths`: positions from a sequence's length up to 2048 are padding. Some sequence has exactly 2048 tokens and some other exactly 1024.
All inputs are finite; a program needn't handle non-finite values.
Results may differ from the reference program's by a relative error of at most 0.013.
Values may be sent and summed in bfloat16 or wider, within the bound.
A program may use at most 128 MiB of HBM per device.

```python
import jax
import jax.numpy as jnp
from jax import lax

D = 512
H = 8
DH = 64
FF = 2048
SLOT = 2048
MIN_LEN = 1024
SEQS = 16


def draw_seq_lengths(key, part):
    drawn = jax.random.randint(key, (SEQS,), MIN_LEN, SLOT + 1)
    first = jax.random.randint(jax.random.fold_in(key, 1), (), 0, SEQS)
    offset = jax.random.randint(jax.random.fold_in(key, 2), (), 1, SEQS)
    second = (first + offset) % SEQS
    drawn = drawn.at[first].set(SLOT)
    drawn = drawn.at[second].set(MIN_LEN)
    return drawn.astype(jnp.int32)


def strengthened(result, own_key, source, target, blocks, factor):
    owner, partner = [(jnp.arange(result.shape[position]) // (result.shape[position] // blocks)).reshape([-1 if axis == position else 1 for axis in range(result.ndim)]) for position in (source, target)]
    chosen = jax.random.permutation(own_key, blocks)[partner]
    strong = (owner == chosen) | (owner == (partner + blocks // 2) % blocks)
    return jnp.where(strong, factor * result, result)


def shard_levels(own_key, dims, pieces, least, high):
    def one(axis_at, shards_of):
        steps = jax.random.uniform(jax.random.fold_in(jax.random.fold_in(own_key, 6), axis_at), (shards_of,), jnp.float32, least / len(pieces), high / len(pieces))
        return jnp.repeat(jnp.exp(steps), dims[axis_at] // shards_of).reshape((-1,) + (1,) * (len(dims) - axis_at - 1))

    level = one(*pieces[0])
    for cut in pieces[1:]:
        level = level * one(*cut)
    return level


def noise(own_key, dims, width, limit, split=(), kind=jnp.bfloat16):
    factor_of = shard_levels(own_key, dims, split, -0.22, 0.18) if split else 1.0
    array = jax.random.normal(own_key, dims, jnp.float32) * width * factor_of
    return jnp.minimum(jnp.maximum(array, -limit), limit).astype(kind)


def noise_with(own_key, dims, width, reach, pieces, heavy, held_as=jnp.bfloat16):
    values = width * jax.random.normal(own_key, dims, jnp.float32)
    if pieces:
        values = values * shard_levels(own_key, dims, pieces, -0.22, 0.18)
    return jnp.clip(strengthened(values, jax.random.fold_in(own_key, 3), *heavy), -reach, reach).astype(held_as)


def setup_inputs(seed: int = 0) -> dict:
    key_of = jax.random.split(jax.random.key(seed), 16)
    post_stream = noise(key_of[0], (SEQS, SLOT, D), 1.0, 6.0, ((0, 8), (1, 4)))
    accum_stream = noise(key_of[1], (SEQS, SLOT, D), 1.0, 6.0, ((0, 8), (1, 4)))
    seq_lengths = draw_seq_lengths(jax.random.fold_in(key_of[15], 71), 0)
    qkv_weight = noise(key_of[3], (D, 3 * D), D ** -0.5, 0.25)
    out_weight = noise(key_of[4], (D, D), ((SLOT // 3) ** 0.5 * D ** -0.5), 6.0)
    norm1_gain = jnp.clip(1.0 + 0.1 * jax.random.normal(key_of[5], (D,), jnp.float32), 0.5, 1.5)
    norm1_bias = noise(key_of[6], (D,), 0.5, 3.0, (), jnp.float32)
    up_weight = noise(key_of[7], (D, FF), D ** -0.5, 0.25)
    up_bias = noise(key_of[8], (FF,), 0.5, 3.0, (), jnp.float32)
    down_weight = noise(key_of[9], (FF, D), FF ** -0.5, 0.125)
    down_bias = noise(key_of[10], (D,), 0.5, 3.0, (), jnp.float32)
    norm2_gain = jnp.clip(1.0 + 0.1 * jax.random.normal(key_of[11], (D,), jnp.float32), 0.5, 1.5)
    norm2_bias = noise(key_of[12], (D,), 0.5, 3.0, (), jnp.float32)
    post_cotan = noise_with(key_of[13], (SEQS, SLOT, D), 1.0, 6.0, ((0, 8), (1, 4)), (0, 2, 8, 2.0))
    accum_cotan = noise(key_of[14], (SEQS, SLOT, D), 1.0, 6.0, ((0, 8), (1, 4)))
    return {"post_stream": post_stream, "accum_stream": accum_stream, "seq_lengths": seq_lengths, "qkv_weight": qkv_weight, "out_weight": out_weight, "norm1_gain": norm1_gain, "norm1_bias": norm1_bias, "up_weight": up_weight, "up_bias": up_bias, "down_weight": down_weight, "down_bias": down_bias, "norm2_gain": norm2_gain, "norm2_bias": norm2_bias, "post_cotan": post_cotan, "accum_cotan": accum_cotan}


EPS = 1e-05
NEG = -1e+30
HIGHEST = lax.Precision.HIGHEST

@jax.custom_vjp
def low(v):
    return lax.optimization_barrier(v.astype(jnp.bfloat16)).astype(jnp.float32)

@jax.custom_vjp
def low_back(v):
    return v

def low_keep(v):
    return (low(v), None)

def low_pass(kept, grad):
    return (grad,)

def back_keep(v):
    return (v, None)

def back_low(kept, grad):
    return (low(grad),)
low.defvjp(low_keep, low_pass)
low_back.defvjp(back_keep, back_low)

def product(left, right):
    return jnp.dot(left, right, precision=HIGHEST, preferred_element_type=jnp.float32)

def layer_norm(value, gain, bias):
    centre = value - lax.optimization_barrier(jnp.mean(value, axis=-1, keepdims=True))
    spread = lax.optimization_barrier(jnp.mean(centre * centre, axis=-1, keepdims=True))
    return centre * lax.rsqrt(spread + EPS) * gain + bias

def layer(params, post, accum, length):
    qkv_w, out_w, gain_one, bias_one, up_w, up_b, down_w, down_b, gain_two, bias_two = params
    key_valid = lax.iota(jnp.int32, SLOT) < length
    keep_mask = key_valid.astype(jnp.float32)[:, None]
    qkv = low(low_back(product(post, qkv_w)))
    heads = qkv.reshape(SLOT, 3, H, DH)
    query = heads[:, 0]
    key_heads = heads[:, 1]
    value_heads = heads[:, 2]
    block_rows = min(512, SLOT)
    score_scale = DH ** (-0.5)

    def one_block(piece):
        scores = jnp.einsum('qhd,khd->hqk', piece, key_heads, precision=HIGHEST) * score_scale
        scores = low_back(scores)
        scores = jnp.where(key_valid[None, None, :], scores, NEG)
        row_top = lax.optimization_barrier(jnp.max(scores, axis=-1, keepdims=True))
        exp_scores = jnp.exp(scores - row_top)
        probs = low(exp_scores / lax.optimization_barrier(jnp.sum(exp_scores, axis=-1, keepdims=True)))
        return jnp.einsum('hqk,khd->qhd', probs, value_heads, precision=HIGHEST)
    mixed = lax.map(jax.checkpoint(one_block), query.reshape(SLOT // block_rows, block_rows, H, DH))
    mixed = low(low_back(mixed.reshape(SLOT, H * DH)))
    attention = low_back(product(mixed, out_w))
    x_mid = layer_norm(post + attention, gain_one, bias_one)
    pre_act = low_back(product(low(x_mid), up_w) + up_b)
    hidden = low(low_back(jax.nn.gelu(pre_act, approximate=True)))
    feed_out = low_back(product(hidden, down_w) + down_b)
    post_out = keep_mask * layer_norm(x_mid + feed_out, gain_two, bias_two)
    accum_out = keep_mask * (accum + attention + feed_out)
    return (post_out, accum_out)

def reference(post_stream, accum_stream, seq_lengths, qkv_weight, out_weight, norm1_gain, norm1_bias, up_weight, up_bias, down_weight, down_bias, norm2_gain, norm2_bias, post_cotan, accum_cotan):
    params = tuple((item.astype(jnp.float32) for item in (qkv_weight, out_weight, norm1_gain, norm1_bias, up_weight, up_bias, down_weight, down_bias, norm2_gain, norm2_bias)))

    def step(totals, items):
        post, accum, length, post_c, accum_c = items

        def forward(param_set, post_in, accum_in):
            return layer(param_set, post_in, accum_in, length)
        outputs, backward = jax.vjp(forward, params, post.astype(jnp.float32), accum.astype(jnp.float32))
        param_grads, grad_post, grad_accum = backward((post_c.astype(jnp.float32), accum_c.astype(jnp.float32)))
        totals = jax.tree.map(lambda total, grad: total + grad, totals, param_grads)
        return (totals, (outputs[0], outputs[1], grad_post, grad_accum))
    zeros = jax.tree.map(jnp.zeros_like, params)
    totals, results = lax.scan(step, zeros, (post_stream, accum_stream, seq_lengths, post_cotan, accum_cotan))
    grad_norm = float(SEQS * SLOT) ** (-0.5)
    totals = tuple((entry * grad_norm for entry in totals))
    return (results[0], results[1], results[2], results[3], totals[0], totals[1], totals[2], totals[3], totals[4], totals[5], totals[6], totals[7], totals[8], totals[9])
```

```python
import functools

import jax
import jax.numpy as jnp
from jax import lax
from jax.experimental import pallas as pl
from jax.experimental.pallas import tpu as pltpu
from jax.sharding import PartitionSpec as P

H = 8
EPS = 1e-05
NEG = -1e30
LOG2E = 1.4426950408889634
BLOCK = 512
VMEM_LIMIT = 56 * 2**20
bf16 = jnp.bfloat16
f32 = jnp.float32


def dot(a, b):
    return jnp.dot(a, b, preferred_element_type=f32)


def dot_nt(a, b):
    return lax.dot_general(a, b, (((1,), (1,)), ((), ())), preferred_element_type=f32)


def dot_tn(a, b):
    return lax.dot_general(a, b, (((0,), (0,)), ((), ())), preferred_element_type=f32)


def split3(value):
    first = value.astype(bf16)
    rest = value - first.astype(f32)
    second = rest.astype(bf16)
    third = (rest - second.astype(f32)).astype(bf16)
    return first, second, third


def params(**more):
    return pltpu.CompilerParams(vmem_limit_bytes=VMEM_LIMIT, **more)


SMEM = pl.BlockSpec(memory_space=pltpu.SMEM)
VMEM = pl.BlockSpec(memory_space=pltpu.VMEM)
ANY = pl.BlockSpec(memory_space=pl.ANY)


def lane_sets():
    lane = lax.broadcasted_iota(jnp.int32, (1, 128), 1)
    return lane, (lane < 64, lane >= 64), (64, 0)


def position_bias(full, length):
    pos = lax.broadcasted_iota(jnp.int32, (full, 1), 0)
    return jnp.where(pos < length, 0.0, NEG).astype(bf16)


def attend_fwd_kernel(
    parts, seq, meta, x0, x1, x2, x3, w, q_out, k_out, v_out, lse_out, m0, m1, m2, m3, ka, qa, vt, mixed
):
    me = meta[0]
    length = meta[2 + seq]
    rows = x0.shape[0]
    full = rows * parts
    lane, mine, base = lane_sets()
    one = jnp.ones((), bf16)
    zero = jnp.zeros((), bf16)
    scale = LOG2E * 64 ** (-0.5)
    for k, x in enumerate((x0, x1, x2, x3)):
        at = pl.ds(pl.multiple_of((me ^ k) * rows, rows), rows)
        qkv = dot(x[...], w[...])
        q_out[at, :] = (qkv[:, :128] * scale).astype(bf16)
        k_out[at, :] = qkv[:, 128:256].astype(bf16)
        v_out[at, :] = qkv[:, 256:].astype(bf16)
    bias = position_bias(full, length)
    keys = k_out[...]
    query = q_out[...]
    for h in range(2):
        ka[h] = jnp.where(mine[h], keys, jnp.where(lane == base[h], bias, zero))
        qa[h] = jnp.where(mine[h], query, jnp.where(lane == base[h], one, zero))
    turned = v_out[...].T
    for h in range(2):
        vt[h, :64] = turned[h * 64 : h * 64 + 64]
        vt[h, 64:] = jnp.ones((8, full), bf16)
    used = lax.div(length + (BLOCK - 1), BLOCK)
    lse_out[...] = jnp.zeros_like(lse_out)
    for count in range(1, full // BLOCK + 1):

        @pl.when(used == count)
        def _():
            span = count * BLOCK

            def body(j, carry):
                at = pl.ds(pl.multiple_of(j * BLOCK, BLOCK), BLOCK)
                out = []
                for h in range(2):
                    top, acc = carry[h]
                    scores = dot_nt(ka[h, at, :], qa[h, :span, :])
                    new_top = jnp.maximum(top, jnp.max(scores, axis=0, keepdims=True))
                    probs = jnp.exp2(scores - new_top)
                    acc = acc * jnp.exp2(top - new_top) + dot(vt[h, :, at], probs.astype(bf16))
                    out.append((new_top, acc))
                return tuple(out)

            init = tuple((jnp.full((1, span), NEG, f32), jnp.zeros((72, span), f32)) for _ in range(2))
            both = lax.fori_loop(0, count, body, init)
            pieces = []
            for h in range(2):
                top, acc = both[h]
                total = acc[64:65]
                pieces.append(acc[:64] / total)
                lse_out[h : h + 1, :span] = top + jnp.log2(total)
            mixed[:span, :] = jnp.concatenate(pieces, 0).T.astype(bf16)
            if span < full:
                mixed[span:, :] = jnp.zeros((full - span, 128), bf16)

    for k, m in enumerate((m0, m1, m2, m3)):
        m[...] = mixed[pl.ds(pl.multiple_of((me ^ k) * rows, rows), rows), :]


def attend_fwd(parts, seq, meta, chunks, w):
    rows = chunks[0].shape[0]
    full = rows * parts
    heads = jax.ShapeDtypeStruct((full, 128), bf16)
    piece = jax.ShapeDtypeStruct((rows, 128), bf16)
    return pl.pallas_call(
        functools.partial(attend_fwd_kernel, parts, seq),
        in_specs=[SMEM] + [VMEM] * 5,
        out_specs=[VMEM] * 8,
        out_shape=[heads] * 3 + [jax.ShapeDtypeStruct((8, full), f32)] + [piece] * 4,
        scratch_shapes=[
            pltpu.VMEM((2, full, 128), bf16),
            pltpu.VMEM((2, full, 128), bf16),
            pltpu.VMEM((2, 72, full), bf16),
            pltpu.VMEM((full, 128), bf16),
        ],
        compiler_params=params(),
        cost_estimate=pl.CostEstimate(flops=40_000_000_000, bytes_accessed=8_000_000, transcendentals=0),
        name="attend_fwd",
    )(meta, *chunks, w)


def attend_bwd_kernel(
    parts,
    seq,
    meta,
    x0,
    x1,
    x2,
    x3,
    q_ref,
    k_ref,
    v_ref,
    lse,
    m0,
    m1,
    m2,
    m3,
    g0,
    g1,
    g2,
    g3,
    *rest,
):
    if seq:
        before, rest = rest[0], rest[1:]
    d0, d1, d2, d3, wgrad, ka, va, kt, qa, da, go, dqt, dqkv = rest
    me = meta[0]
    length = meta[2 + seq]
    rows = x0.shape[0]
    full = rows * parts
    lane, mine, base = lane_sets()
    one = jnp.ones((), bf16)
    zero = jnp.zeros((), bf16)
    bias = position_bias(full, length)
    keys = k_ref[...]
    values = v_ref[...]
    query = q_ref[...]
    kt[...] = keys.T
    for k, (m, g) in enumerate(((m0, g0), (m1, g1), (m2, g2), (m3, g3))):
        at = pl.ds(pl.multiple_of((me ^ k) * rows, rows), rows)
        grad = g[...]
        go[at, :] = grad
        prod = grad.astype(f32) * m[...].astype(f32)
        for h in range(2):
            a, b, c = split3(-jnp.sum(jnp.where(mine[h], prod, 0.0), axis=1, keepdims=True))
            extra = jnp.where(
                lane == base[h], a, jnp.where(lane == base[h] + 1, b, jnp.where(lane == base[h] + 2, c, zero))
            )
            da[h, at, :] = jnp.where(mine[h], grad, extra)
    turned = -lse[...].T
    for h in range(2):
        ka[h] = jnp.where(mine[h], keys, jnp.where(lane == base[h], bias, one))
        va[h] = jnp.where(mine[h], values, one)
        a, b, c = split3(turned[:, h : h + 1])
        extra = jnp.where(
            lane == base[h],
            one,
            jnp.where(
                lane == base[h] + 1,
                a,
                jnp.where(lane == base[h] + 2, b, jnp.where(lane == base[h] + 3, c, zero)),
            ),
        )
        qa[h] = jnp.where(mine[h], query, extra)
    used = lax.div(length + (BLOCK - 1), BLOCK)
    for count in range(1, full // BLOCK + 1):

        @pl.when(used == count)
        def _():
            span = count * BLOCK
            dqt[...] = jnp.zeros_like(dqt)
            if span < full:
                dqkv[span:, :] = jnp.zeros((full - span, 384), bf16)

            def body(j, carry):
                at = pl.ds(pl.multiple_of(j * BLOCK, BLOCK), BLOCK)
                out = []
                for h in range(2):
                    probs = jnp.exp2(dot_nt(ka[h, at, :], qa[h, :span, :]))
                    inner = dot_nt(va[h, at, :], da[h, :span, :])
                    low = probs.astype(bf16)
                    grad = (probs * inner).astype(bf16)
                    dv = dot(low, go[:span, :])
                    dk = dot(grad, q_ref[:span, :])
                    part = slice(h * 64, h * 64 + 64)
                    dqt[part, :span] += dot(kt[part, at], grad)
                    out.append((dv, dk))
                dv = jnp.where(mine[0], out[0][0], out[1][0])
                dk = jnp.where(mine[0], out[0][1], out[1][1]) * (1.0 / LOG2E)
                dqkv[at, 128:256] = dk.astype(bf16)
                dqkv[at, 256:] = dv.astype(bf16)
                return carry

            lax.fori_loop(0, count, body, 0)

    dqkv[:, :128] = (dqt[...] * 64 ** (-0.5)).T.astype(bf16)
    total = before[...] if seq else None
    for k, (x, d) in enumerate(((x0, d0), (x1, d1), (x2, d2), (x3, d3))):
        piece = dqkv[pl.ds(pl.multiple_of((me ^ k) * rows, rows), rows), :]
        d[...] = piece
        term = dot_tn(x[...], piece)
        total = term if total is None else total + term
    wgrad[...] = total


def attend_bwd(parts, seq, meta, chunks, q, k, v, lse, mixed, grads, before):
    rows = chunks[0].shape[0]
    full = rows * parts
    width = chunks[0].shape[1]
    piece = jax.ShapeDtypeStruct((rows, 384), bf16)
    more = [before] if seq else []
    return pl.pallas_call(
        functools.partial(attend_bwd_kernel, parts, seq),
        in_specs=[SMEM] + [VMEM] * (16 + len(more)),
        out_specs=[VMEM] * 5,
        out_shape=[piece] * 4 + [jax.ShapeDtypeStruct((width, 384), f32)],
        scratch_shapes=[
            pltpu.VMEM((2, full, 128), bf16),
            pltpu.VMEM((2, full, 128), bf16),
            pltpu.VMEM((128, full), bf16),
            pltpu.VMEM((2, full, 128), bf16),
            pltpu.VMEM((2, full, 128), bf16),
            pltpu.VMEM((full, 128), bf16),
            pltpu.VMEM((128, full), f32),
            pltpu.VMEM((full, 384), bf16),
        ],
        compiler_params=params(),
        cost_estimate=pl.CostEstimate(flops=60_000_000_000, bytes_accessed=10_000_000, transcendentals=0),
        name="attend_bwd",
    )(meta, *chunks, q, k, v, lse, *mixed, *grads, *more)


def normed(value):
    centre = value - jnp.mean(value, axis=-1, keepdims=True)
    spread = jnp.mean(centre * centre, axis=-1, keepdims=True)
    inv = lax.rsqrt(spread + EPS)
    return centre * inv, inv


def norm_back(cot, unit, inv):
    return (
        cot - jnp.mean(cot, axis=-1, keepdims=True) - unit * jnp.mean(cot * unit, axis=-1, keepdims=True)
    ) * inv


def feed_kernel(parts, seq, meta, m0, m1, m2, m3, x, y, pc, ac, wo, g1, b1, wu, bu, wd, bd, g2, b2, *rest):
    if seq:
        rest = rest[4:]
    (post, accum, accum_grad, first_grad, s0, s1, s2, s3, hid, pre, fgrad, mid, agrad, mixed, small) = rest[:15]
    slope, back = rest[15:]
    me = meta[0]
    length = meta[2 + seq]
    rows, width = x.shape[-2:]
    tile = 512
    tiles = wu.shape[1] // tile
    for k, m in enumerate((m0, m1, m2, m3)):
        mixed[:, pl.ds(pl.multiple_of((me ^ k) * 128, 128), 128)] = m[...]
    pos = lax.broadcasted_iota(jnp.int32, (rows, 1), 0) + me * rows
    keep = pos < length
    attention = dot(mixed[...], wo[...])
    unit1, inv1 = normed(x[0].astype(f32) + attention)
    x_mid = unit1 * g1[...] + b1[...]
    mid[...] = x_mid.astype(bf16)
    feed = jnp.zeros((rows, width), f32)
    c0 = 0.7978845608028654
    c1 = 0.044715
    for t in range(tiles):
        cols = slice(t * tile, (t + 1) * tile)
        act = dot(mid[...], wu[:, cols]) + bu[:, cols]
        square = act * act
        th = jnp.tanh(act * (c0 + (c0 * c1) * square))
        half = 0.5 * (1.0 + th)
        low = (act * half).astype(bf16)
        hid[:, cols] = low
        slope[:, cols] = half + (0.5 * act) * (1.0 - th * th) * (c0 + (3.0 * c0 * c1) * square)
        feed = feed + dot(low, wd[cols, :])
    feed = feed + bd[...]
    unit2, inv2 = normed(x_mid + feed)
    post[0] = jnp.where(keep, unit2 * g2[...] + b2[...], 0.0)
    accum[0] = jnp.where(keep, y[0].astype(f32) + attention + feed, 0.0)
    post_c = jnp.where(keep, pc[0].astype(f32), 0.0)
    accum_c = jnp.where(keep, ac[0].astype(f32), 0.0)
    accum_grad[0] = accum_c
    mid_grad2 = norm_back(post_c * g2[...], unit2, inv2)
    small[...] = jnp.zeros_like(small)
    small[2:3, :width] = jnp.sum(post_c * unit2, axis=0, keepdims=True)
    small[3:4, :width] = jnp.sum(post_c, axis=0, keepdims=True)
    feed_grad = (mid_grad2 + accum_c).astype(bf16)
    fgrad[...] = feed_grad
    small[4:5, :width] = jnp.sum(feed_grad.astype(f32), axis=0, keepdims=True)
    back[...] = mid_grad2
    for t in range(tiles):
        cols = slice(t * tile, (t + 1) * tile)
        hidden_grad = dot_nt(fgrad[...], wd[cols, :]).astype(bf16)
        pre_grad = (hidden_grad.astype(f32) * slope[:, cols]).astype(bf16)
        pre[:, cols] = pre_grad
        small[5:6, cols] = jnp.sum(pre_grad.astype(f32), axis=0, keepdims=True)
        back[...] += dot_nt(pre_grad, wu[:, cols])
    mid_grad = back[...]
    small[0:1, :width] = jnp.sum(mid_grad * unit1, axis=0, keepdims=True)
    small[1:2, :width] = jnp.sum(mid_grad, axis=0, keepdims=True)
    first = norm_back(mid_grad * g1[...], unit1, inv1)
    first_grad[0] = first
    attn_grad = (first + accum_c).astype(bf16)
    agrad[...] = attn_grad
    back[...] = dot_nt(attn_grad, wo[...])
    for k, s in enumerate((s0, s1, s2, s3)):
        s[...] = back[:, pl.ds(pl.multiple_of((me ^ k) * 128, 128), 128)].astype(bf16)


def feed(parts, seq, meta, mixed, streams, weights, before):
    groups, rows, width = streams[0].shape
    hidden = weights[3].shape[1]
    block = pl.BlockSpec((1, rows, width), lambda i: (seq, 0, 0))
    whole = jax.ShapeDtypeStruct((groups, rows, width), f32)
    piece = jax.ShapeDtypeStruct((rows, 128), bf16)
    wide = jax.ShapeDtypeStruct((rows, hidden), bf16)
    narrow = jax.ShapeDtypeStruct((rows, width), bf16)

    def fixed(shape):
        return pl.BlockSpec(shape, lambda i: (0,) * len(shape))

    out_shape = [whole] * 4 + [piece] * 4 + [wide, wide, narrow, narrow, narrow, narrow]
    out_shape += [jax.ShapeDtypeStruct((8, hidden), f32)]
    out_specs = [block] * 4 + [fixed(o.shape) for o in out_shape[4:]]
    in_specs = [SMEM] + [fixed(m.shape) for m in mixed] + [block] * 4 + [fixed(w.shape) for w in weights]
    more = list(before) if seq else []
    aliases = {len(in_specs) + i: i for i in range(len(more))}
    return pl.pallas_call(
        functools.partial(feed_kernel, parts, seq),
        grid=(1,),
        in_specs=in_specs + [ANY] * len(more),
        out_specs=out_specs,
        out_shape=out_shape,
        scratch_shapes=[pltpu.VMEM((rows, hidden), f32), pltpu.VMEM((rows, width), f32)],
        input_output_aliases=aliases,
        compiler_params=params(),
        cost_estimate=pl.CostEstimate(flops=15_000_000_000, bytes_accessed=14_000_000, transcendentals=0),
        name="feed",
    )(meta, *mixed, *streams, *weights, *more)


def weight_kernel(*refs):
    ins, (up, down, out, small) = refs[:-4], refs[-4:]
    hid0, pre0, fg0, mid0, ag0, mix0, sm0, hid1, pre1, fg1, mid1, ag1, mix1, sm1 = ins
    hidden = hid0.shape[1]
    tile = 512
    for t in range(hidden // tile):
        cols = slice(t * tile, (t + 1) * tile)
        up[:, cols] = (dot_tn(mid0[...], pre0[:, cols]) + dot_tn(mid1[...], pre1[:, cols])).astype(bf16)
        down[cols, :] = (dot_tn(hid0[:, cols], fg0[...]) + dot_tn(hid1[:, cols], fg1[...])).astype(bf16)
    out[...] = (dot_tn(mix0[...], ag0[...]) + dot_tn(mix1[...], ag1[...])).astype(bf16)
    small[...] = sm0[...] + sm1[...]


def weight_grads(first, second):
    rows, hidden = first[0].shape
    width = first[2].shape[1]
    return pl.pallas_call(
        weight_kernel,
        in_specs=[VMEM] * 14,
        out_specs=[VMEM] * 4,
        out_shape=[
            jax.ShapeDtypeStruct((width, hidden), bf16),
            jax.ShapeDtypeStruct((hidden, width), bf16),
            jax.ShapeDtypeStruct((width, width), bf16),
            jax.ShapeDtypeStruct((8, hidden), f32),
        ],
        compiler_params=params(),
        cost_estimate=pl.CostEstimate(flops=10_000_000_000, bytes_accessed=14_000_000, transcendentals=0),
        name="weight_grads",
    )(*first, *second)


def post_kernel(parts, seq, meta, d0, d1, d2, d3, w, first_grad, *rest):
    out = rest[-1]
    me = meta[0]
    width = w.shape[0]
    total = first_grad[0]
    for k, d in enumerate((d0, d1, d2, d3)):
        for part in range(3):
            cols = pl.ds(pl.multiple_of(part * width + (me ^ k) * 128, 128), 128)
            total = total + dot_nt(d[:, part * 128 : part * 128 + 128], w[:, cols])
    out[0] = total


def post_grads(parts, seq, meta, pieces, w, first_grad, before):
    groups, rows, width = first_grad.shape
    block = pl.BlockSpec((1, rows, width), lambda i: (seq, 0, 0))
    in_specs = [SMEM] + [pl.BlockSpec(p.shape, lambda i: (0, 0)) for p in pieces]
    in_specs += [pl.BlockSpec(w.shape, lambda i: (0, 0)), block]
    more = [before] if seq else []
    return pl.pallas_call(
        functools.partial(post_kernel, parts, seq),
        grid=(1,),
        in_specs=in_specs + [ANY] * len(more),
        out_specs=block,
        out_shape=jax.ShapeDtypeStruct(first_grad.shape, f32),
        input_output_aliases={len(in_specs): 0} if seq else {},
        compiler_params=params(),
        cost_estimate=pl.CostEstimate(flops=3_000_000_000, bytes_accessed=5_000_000, transcendentals=0),
        name="post_grads",
    )(meta, *pieces, w, first_grad, *more)


def local(
    post_stream,
    accum_stream,
    seq_lengths,
    qkv_weight,
    out_weight,
    norm1_gain,
    norm1_bias,
    up_weight,
    up_bias,
    down_weight,
    down_bias,
    norm2_gain,
    norm2_bias,
    post_cotan,
    accum_cotan,
):
    groups, rows, width = post_stream.shape
    parts = lax.axis_size("head")
    shards = lax.axis_size("seq")
    full = rows * parts
    hidden = up_weight.shape[1]
    grad_norm = float(groups * shards * full) ** (-0.5)
    me = lax.axis_index("head")

    def swap(value, k):
        return lax.ppermute(value, "head", [(i, i ^ k) for i in range(parts)])

    meta = jnp.concatenate([jnp.stack([me, lax.axis_index("seq")]).astype(jnp.int32), seq_lengths])
    w_mine = lax.dynamic_slice_in_dim(qkv_weight.reshape(width, 3, width), me * 128, 128, 2).reshape(width, 384)
    row = lambda v: v.reshape(1, -1)
    weights = (
        out_weight,
        row(norm1_gain),
        row(norm1_bias),
        up_weight,
        row(up_bias),
        down_weight,
        row(down_bias),
        row(norm2_gain),
        row(norm2_bias),
    )
    streams = (post_stream, accum_stream, post_cotan, accum_cotan)
    half = rows // 2
    chunks = []
    for s in range(groups):
        x = post_stream[s]
        xa = swap(x, 1)
        xb = swap(x, 2)
        xc = jnp.concatenate([swap(xa[:half], 2), swap(xb[half:], 1)], 0)
        chunks.append((x, xa, xb, xc))
    fwd = [attend_fwd(parts, s, meta, chunks[s], w_mine) for s in range(groups)]
    fed = []
    for s in range(groups):
        pieces = fwd[s][4:]
        mixed = [pieces[0]] + [swap(pieces[k], k) for k in range(1, parts)]
        fed.append(feed(parts, s, meta, mixed, streams, weights, fed[-1][:4] if s else None))
    post_result, accum_result, accum_grad, first_grad = fed[-1][:4]
    up_grad, down_grad, out_grad, small = weight_grads(fed[0][8:], fed[1][8:])
    early = jnp.concatenate(
        [
            up_grad.reshape(shards, -1, hidden),
            down_grad.reshape(shards, -1, hidden),
            out_grad.reshape(shards, -1, hidden),
        ],
        1,
    )
    early = lax.psum_scatter(early, "seq", scatter_dimension=0, tiled=True)[0]
    for k in (1, 2):
        early = (early.astype(f32) + swap(early, k).astype(f32)).astype(bf16)
    early = early.astype(f32) * grad_norm
    small = lax.psum(small, ("head", "seq")) * grad_norm
    back = []
    for s in range(groups):
        pieces = fed[s][4:8]
        grads = [pieces[0]] + [swap(pieces[k], k) for k in range(1, parts)]
        back.append(
            attend_bwd(
                parts, s, meta, chunks[s], *fwd[s][:4], fwd[s][4:], grads, back[-1][4] if s else None
            )
        )
    post_grad = None
    for s in range(groups):
        pieces = back[s][:4]
        got = [pieces[0]] + [swap(pieces[k], k) for k in range(1, parts)]
        post_grad = post_grads(parts, s, meta, got, qkv_weight, first_grad, post_grad)
    late = back[-1][4].astype(bf16)
    late = lax.psum_scatter(late, "seq", scatter_dimension=0, tiled=True)
    got = jnp.stack([late] + [swap(late, k) for k in range(1, parts)])
    late_rows = late.shape[0]
    order = jnp.arange(parts, dtype=jnp.int32) ^ me
    late = jnp.take(got, order, axis=0).astype(f32) * grad_norm
    late = late.reshape(parts, late_rows, 3, 128).transpose(1, 2, 0, 3).reshape(late_rows, 3 * width)
    place = lax.axis_index("seq")

    def pick(vector, count):
        return lax.dynamic_slice_in_dim(vector[:count], place * (count // shards), count // shards, 0)

    n_up = width // shards
    n_down = hidden // shards * width // hidden
    return (
        post_result,
        accum_result,
        post_grad,
        accum_grad,
        late,
        early[n_up + n_down :].reshape(width // shards, width),
        pick(small[0], width),
        pick(small[1], width),
        early[:n_up],
        pick(small[5], hidden),
        early[n_up : n_up + n_down].reshape(hidden // shards, width),
        pick(small[4], width),
        pick(small[2], width),
        pick(small[3], width),
    )


def solution(mesh):
    tokens = P("seq", "head", None)
    in_specs = (tokens, tokens, P("seq")) + (P(),) * 10 + (tokens, tokens)
    out_specs = (
        tokens,
        tokens,
        tokens,
        tokens,
        P("seq", None),
        P("seq", None),
        P("seq"),
        P("seq"),
        P("seq", None),
        P("seq"),
        P("seq", None),
        P("seq"),
        P("seq"),
        P("seq"),
    )
    return jax.shard_map(local, mesh=mesh, in_specs=in_specs, out_specs=out_specs, check_vma=False)
```

```python
import functools

import jax
import jax.numpy as jnp
from jax import lax
from jax.experimental import pallas as pl
from jax.experimental.pallas import tpu as pltpu
from jax.sharding import PartitionSpec as P

H = 8
EPS = 1e-05
NEG = -1e30
LOG2E = 1.4426950408889634
BLOCK = 512
VMEM_LIMIT = 56 * 2**20
bf16 = jnp.bfloat16
f32 = jnp.float32


def dot(a, b):
    return jnp.dot(a, b, preferred_element_type=f32)


def dot_nt(a, b):
    return lax.dot_general(a, b, (((1,), (1,)), ((), ())), preferred_element_type=f32)


def dot_tn(a, b):
    return lax.dot_general(a, b, (((0,), (0,)), ((), ())), preferred_element_type=f32)


def split3(value):
    first = value.astype(bf16)
    rest = value - first.astype(f32)
    second = rest.astype(bf16)
    third = (rest - second.astype(f32)).astype(bf16)
    return first, second, third


def params(**more):
    return pltpu.CompilerParams(vmem_limit_bytes=VMEM_LIMIT, **more)


SMEM = pl.BlockSpec(memory_space=pltpu.SMEM)
VMEM = pl.BlockSpec(memory_space=pltpu.VMEM)
ANY = pl.BlockSpec(memory_space=pl.ANY)


def lane_sets():
    lane = lax.broadcasted_iota(jnp.int32, (1, 128), 1)
    return lane, (lane < 64, lane >= 64), (64, 0)


def position_bias(full, length):
    pos = lax.broadcasted_iota(jnp.int32, (full, 1), 0)
    return jnp.where(pos < length, 0.0, NEG).astype(bf16)


def attend_fwd_kernel(
    parts, seq, meta, x0, x1, x2, x3, w, q_out, k_out, v_out, lse_out, m0, m1, m2, m3, ka, qa, vt, mixed
):
    me = meta[0]
    length = meta[2 + seq]
    rows = x0.shape[0]
    full = rows * parts
    lane, mine, base = lane_sets()
    one = jnp.ones((), bf16)
    zero = jnp.zeros((), bf16)
    scale = LOG2E * 64 ** (-0.5)
    for k, x in enumerate((x0, x1, x2, x3)):
        at = pl.ds(pl.multiple_of((me ^ k) * rows, rows), rows)
        qkv = dot(x[...], w[...])
        q_out[at, :] = (qkv[:, :128] * scale).astype(bf16)
        k_out[at, :] = qkv[:, 128:256].astype(bf16)
        v_out[at, :] = qkv[:, 256:].astype(bf16)
    bias = position_bias(full, length)
    keys = k_out[...]
    query = q_out[...]
    for h in range(2):
        ka[h] = jnp.where(mine[h], keys, jnp.where(lane == base[h], bias, zero))
        qa[h] = jnp.where(mine[h], query, jnp.where(lane == base[h], one, zero))
    turned = v_out[...].T
    for h in range(2):
        vt[h, :64] = turned[h * 64 : h * 64 + 64]
        vt[h, 64:] = jnp.ones((8, full), bf16)
    used = lax.div(length + (BLOCK - 1), BLOCK)
    lse_out[...] = jnp.zeros_like(lse_out)
    for count in range(1, full // BLOCK + 1):

        @pl.when(used == count)
        def _():
            span = count * BLOCK

            def body(j, carry):
                at = pl.ds(pl.multiple_of(j * BLOCK, BLOCK), BLOCK)
                out = []
                for h in range(2):
                    top, acc = carry[h]
                    scores = dot_nt(ka[h, at, :], qa[h, :span, :])
                    new_top = jnp.maximum(top, jnp.max(scores, axis=0, keepdims=True))
                    probs = jnp.exp2(scores - new_top)
                    acc = acc * jnp.exp2(top - new_top) + dot(vt[h, :, at], probs.astype(bf16))
                    out.append((new_top, acc))
                return tuple(out)

            init = tuple((jnp.full((1, span), NEG, f32), jnp.zeros((72, span), f32)) for _ in range(2))
            both = lax.fori_loop(0, count, body, init)
            pieces = []
            for h in range(2):
                top, acc = both[h]
                total = acc[64:65]
                pieces.append(acc[:64] / total)
                lse_out[h : h + 1, :span] = top + jnp.log2(total)
            mixed[:span, :] = jnp.concatenate(pieces, 0).T.astype(bf16)
            if span < full:
                mixed[span:, :] = jnp.zeros((full - span, 128), bf16)

    for k, m in enumerate((m0, m1, m2, m3)):
        m[...] = mixed[pl.ds(pl.multiple_of((me ^ k) * rows, rows), rows), :]


def attend_fwd(parts, seq, meta, chunks, w):
    rows = chunks[0].shape[0]
    full = rows * parts
    heads = jax.ShapeDtypeStruct((full, 128), bf16)
    piece = jax.ShapeDtypeStruct((rows, 128), bf16)
    return pl.pallas_call(
        functools.partial(attend_fwd_kernel, parts, seq),
        in_specs=[SMEM] + [VMEM] * 5,
        out_specs=[VMEM] * 8,
        out_shape=[heads] * 3 + [jax.ShapeDtypeStruct((8, full), f32)] + [piece] * 4,
        scratch_shapes=[
            pltpu.VMEM((2, full, 128), bf16),
            pltpu.VMEM((2, full, 128), bf16),
            pltpu.VMEM((2, 72, full), bf16),
            pltpu.VMEM((full, 128), bf16),
        ],
        compiler_params=params(),
        cost_estimate=pl.CostEstimate(flops=40_000_000_000, bytes_accessed=8_000_000, transcendentals=0),
        name="attend_fwd",
    )(meta, *chunks, w)


def attend_bwd_kernel(
    parts,
    seq,
    meta,
    x0,
    x1,
    x2,
    x3,
    q_ref,
    k_ref,
    v_ref,
    lse,
    m0,
    m1,
    m2,
    m3,
    g0,
    g1,
    g2,
    g3,
    *rest,
):
    if seq:
        before, rest = rest[0], rest[1:]
    d0, d1, d2, d3, wgrad, ka, va, kt, qa, da, go, dqt, dqkv = rest
    me = meta[0]
    length = meta[2 + seq]
    rows = x0.shape[0]
    full = rows * parts
    lane, mine, base = lane_sets()
    one = jnp.ones((), bf16)
    zero = jnp.zeros((), bf16)
    bias = position_bias(full, length)
    keys = k_ref[...]
    values = v_ref[...]
    query = q_ref[...]
    kt[...] = keys.T
    for k, (m, g) in enumerate(((m0, g0), (m1, g1), (m2, g2), (m3, g3))):
        at = pl.ds(pl.multiple_of((me ^ k) * rows, rows), rows)
        grad = g[...]
        go[at, :] = grad
        prod = grad.astype(f32) * m[...].astype(f32)
        for h in range(2):
            a, b, c = split3(-jnp.sum(jnp.where(mine[h], prod, 0.0), axis=1, keepdims=True))
            extra = jnp.where(
                lane == base[h], a, jnp.where(lane == base[h] + 1, b, jnp.where(lane == base[h] + 2, c, zero))
            )
            da[h, at, :] = jnp.where(mine[h], grad, extra)
    turned = -lse[...].T
    for h in range(2):
        ka[h] = jnp.where(mine[h], keys, jnp.where(lane == base[h], bias, one))
        va[h] = jnp.where(mine[h], values, one)
        a, b, c = split3(turned[:, h : h + 1])
        extra = jnp.where(
            lane == base[h],
            one,
            jnp.where(
                lane == base[h] + 1,
                a,
                jnp.where(lane == base[h] + 2, b, jnp.where(lane == base[h] + 3, c, zero)),
            ),
        )
        qa[h] = jnp.where(mine[h], query, extra)
    used = lax.div(length + (BLOCK - 1), BLOCK)
    for count in range(1, full // BLOCK + 1):

        @pl.when(used == count)
        def _():
            span = count * BLOCK
            dqt[...] = jnp.zeros_like(dqt)
            if span < full:
                dqkv[span:, :] = jnp.zeros((full - span, 384), bf16)

            def body(j, carry):
                at = pl.ds(pl.multiple_of(j * BLOCK, BLOCK), BLOCK)
                out = []
                for h in range(2):
                    probs = jnp.exp2(dot_nt(ka[h, at, :], qa[h, :span, :]))
                    inner = dot_nt(va[h, at, :], da[h, :span, :])
                    low = probs.astype(bf16)
                    grad = (probs * inner).astype(bf16)
                    dv = dot(low, go[:span, :])
                    dk = dot(grad, q_ref[:span, :])
                    part = slice(h * 64, h * 64 + 64)
                    dqt[part, :span] += dot(kt[part, at], grad)
                    out.append((dv, dk))
                dv = jnp.where(mine[0], out[0][0], out[1][0])
                dk = jnp.where(mine[0], out[0][1], out[1][1]) * (1.0 / LOG2E)
                dqkv[at, 128:256] = dk.astype(bf16)
                dqkv[at, 256:] = dv.astype(bf16)
                return carry

            lax.fori_loop(0, count, body, 0)

    dqkv[:, :128] = (dqt[...] * 64 ** (-0.5)).T.astype(bf16)
    total = before[...] if seq else None
    for k, (x, d) in enumerate(((x0, d0), (x1, d1), (x2, d2), (x3, d3))):
        piece = dqkv[pl.ds(pl.multiple_of((me ^ k) * rows, rows), rows), :]
        d[...] = piece
        term = dot_tn(x[...], piece)
        total = term if total is None else total + term
    wgrad[...] = total


def attend_bwd(parts, seq, meta, chunks, q, k, v, lse, mixed, grads, before):
    rows = chunks[0].shape[0]
    full = rows * parts
    width = chunks[0].shape[1]
    piece = jax.ShapeDtypeStruct((rows, 384), bf16)
    more = [before] if seq else []
    return pl.pallas_call(
        functools.partial(attend_bwd_kernel, parts, seq),
        in_specs=[SMEM] + [VMEM] * (16 + len(more)),
        out_specs=[VMEM] * 5,
        out_shape=[piece] * 4 + [jax.ShapeDtypeStruct((width, 384), f32)],
        scratch_shapes=[
            pltpu.VMEM((2, full, 128), bf16),
            pltpu.VMEM((2, full, 128), bf16),
            pltpu.VMEM((128, full), bf16),
            pltpu.VMEM((2, full, 128), bf16),
            pltpu.VMEM((2, full, 128), bf16),
            pltpu.VMEM((full, 128), bf16),
            pltpu.VMEM((128, full), f32),
            pltpu.VMEM((full, 384), bf16),
        ],
        compiler_params=params(),
        cost_estimate=pl.CostEstimate(flops=60_000_000_000, bytes_accessed=10_000_000, transcendentals=0),
        name="attend_bwd",
    )(meta, *chunks, q, k, v, lse, *mixed, *grads, *more)


def normed(value):
    centre = value - jnp.mean(value, axis=-1, keepdims=True)
    spread = jnp.mean(centre * centre, axis=-1, keepdims=True)
    inv = lax.rsqrt(spread + EPS)
    return centre * inv, inv


def norm_back(cot, unit, inv):
    return (
        cot - jnp.mean(cot, axis=-1, keepdims=True) - unit * jnp.mean(cot * unit, axis=-1, keepdims=True)
    ) * inv


def feed_kernel(parts, seq, meta, m0, m1, m2, m3, x, y, pc, ac, wo, g1, b1, wu, bu, wd, bd, g2, b2, *rest):
    if seq:
        rest = rest[4:]
    (post, accum, accum_grad, first_grad, s0, s1, s2, s3, hid, pre, fgrad, mid, agrad, mixed, small) = rest[:15]
    slope, back = rest[15:]
    me = meta[0]
    length = meta[2 + seq]
    rows, width = x.shape[-2:]
    tile = 512
    tiles = wu.shape[1] // tile
    for k, m in enumerate((m0, m1, m2, m3)):
        mixed[:, pl.ds(pl.multiple_of((me ^ k) * 128, 128), 128)] = m[...]
    pos = lax.broadcasted_iota(jnp.int32, (rows, 1), 0) + me * rows
    keep = pos < length
    attention = dot(mixed[...], wo[...])
    unit1, inv1 = normed(x[0].astype(f32) + attention)
    x_mid = unit1 * g1[...] + b1[...]
    mid[...] = x_mid.astype(bf16)
    feed = jnp.zeros((rows, width), f32)
    c0 = 0.7978845608028654
    c1 = 0.044715
    for t in range(tiles):
        cols = slice(t * tile, (t + 1) * tile)
        act = dot(mid[...], wu[:, cols]) + bu[:, cols]
        square = act * act
        th = jnp.tanh(act * (c0 + (c0 * c1) * square))
        half = 0.5 * (1.0 + th)
        low = (act * half).astype(bf16)
        hid[:, cols] = low
        slope[:, cols] = half + (0.5 * act) * (1.0 - th * th) * (c0 + (3.0 * c0 * c1) * square)
        feed = feed + dot(low, wd[cols, :])
    feed = feed + bd[...]
    unit2, inv2 = normed(x_mid + feed)
    post[0] = jnp.where(keep, unit2 * g2[...] + b2[...], 0.0)
    accum[0] = jnp.where(keep, y[0].astype(f32) + attention + feed, 0.0)
    post_c = jnp.where(keep, pc[0].astype(f32), 0.0)
    accum_c = jnp.where(keep, ac[0].astype(f32), 0.0)
    accum_grad[0] = accum_c
    mid_grad2 = norm_back(post_c * g2[...], unit2, inv2)
    small[...] = jnp.zeros_like(small)
    small[2:3, :width] = jnp.sum(post_c * unit2, axis=0, keepdims=True)
    small[3:4, :width] = jnp.sum(post_c, axis=0, keepdims=True)
    feed_grad = (mid_grad2 + accum_c).astype(bf16)
    fgrad[...] = feed_grad
    small[4:5, :width] = jnp.sum(feed_grad.astype(f32), axis=0, keepdims=True)
    back[...] = mid_grad2
    for t in range(tiles):
        cols = slice(t * tile, (t + 1) * tile)
        hidden_grad = dot_nt(fgrad[...], wd[cols, :]).astype(bf16)
        pre_grad = (hidden_grad.astype(f32) * slope[:, cols]).astype(bf16)
        pre[:, cols] = pre_grad
        small[5:6, cols] = jnp.sum(pre_grad.astype(f32), axis=0, keepdims=True)
        back[...] += dot_nt(pre_grad, wu[:, cols])
    mid_grad = back[...]
    small[0:1, :width] = jnp.sum(mid_grad * unit1, axis=0, keepdims=True)
    small[1:2, :width] = jnp.sum(mid_grad, axis=0, keepdims=True)
    first = norm_back(mid_grad * g1[...], unit1, inv1)
    first_grad[0] = first
    attn_grad = (first + accum_c).astype(bf16)
    agrad[...] = attn_grad
    back[...] = dot_nt(attn_grad, wo[...])
    for k, s in enumerate((s0, s1, s2, s3)):
        s[...] = back[:, pl.ds(pl.multiple_of((me ^ k) * 128, 128), 128)].astype(bf16)


def feed(parts, seq, meta, mixed, streams, weights, before):
    groups, rows, width = streams[0].shape
    hidden = weights[3].shape[1]
    block = pl.BlockSpec((1, rows, width), lambda i: (seq, 0, 0))
    whole = jax.ShapeDtypeStruct((groups, rows, width), f32)
    piece = jax.ShapeDtypeStruct((rows, 128), bf16)
    wide = jax.ShapeDtypeStruct((rows, hidden), bf16)
    narrow = jax.ShapeDtypeStruct((rows, width), bf16)

    def fixed(shape):
        return pl.BlockSpec(shape, lambda i: (0,) * len(shape))

    out_shape = [whole] * 4 + [piece] * 4 + [wide, wide, narrow, narrow, narrow, narrow]
    out_shape += [jax.ShapeDtypeStruct((8, hidden), f32)]
    out_specs = [block] * 4 + [fixed(o.shape) for o in out_shape[4:]]
    in_specs = [SMEM] + [fixed(m.shape) for m in mixed] + [block] * 4 + [fixed(w.shape) for w in weights]
    more = list(before) if seq else []
    aliases = {len(in_specs) + i: i for i in range(len(more))}
    return pl.pallas_call(
        functools.partial(feed_kernel, parts, seq),
        grid=(1,),
        in_specs=in_specs + [ANY] * len(more),
        out_specs=out_specs,
        out_shape=out_shape,
        scratch_shapes=[pltpu.VMEM((rows, hidden), f32), pltpu.VMEM((rows, width), f32)],
        input_output_aliases=aliases,
        compiler_params=params(),
        cost_estimate=pl.CostEstimate(flops=15_000_000_000, bytes_accessed=14_000_000, transcendentals=0),
        name="feed",
    )(meta, *mixed, *streams, *weights, *more)


def weight_kernel(*refs):
    ins, (up, down, out, small) = refs[:-4], refs[-4:]
    hid0, pre0, fg0, mid0, ag0, mix0, sm0, hid1, pre1, fg1, mid1, ag1, mix1, sm1 = ins
    hidden = hid0.shape[1]
    tile = 512
    for t in range(hidden // tile):
        cols = slice(t * tile, (t + 1) * tile)
        up[:, cols] = (dot_tn(mid0[...], pre0[:, cols]) + dot_tn(mid1[...], pre1[:, cols])).astype(bf16)
        down[cols, :] = (dot_tn(hid0[:, cols], fg0[...]) + dot_tn(hid1[:, cols], fg1[...])).astype(bf16)
    out[...] = (dot_tn(mix0[...], ag0[...]) + dot_tn(mix1[...], ag1[...])).astype(bf16)
    small[...] = sm0[...] + sm1[...]


def weight_grads(first, second):
    rows, hidden = first[0].shape
    width = first[2].shape[1]
    return pl.pallas_call(
        weight_kernel,
        in_specs=[VMEM] * 14,
        out_specs=[VMEM] * 4,
        out_shape=[
            jax.ShapeDtypeStruct((width, hidden), bf16),
            jax.ShapeDtypeStruct((hidden, width), bf16),
            jax.ShapeDtypeStruct((width, width), bf16),
            jax.ShapeDtypeStruct((8, hidden), f32),
        ],
        compiler_params=params(),
        cost_estimate=pl.CostEstimate(flops=10_000_000_000, bytes_accessed=14_000_000, transcendentals=0),
        name="weight_grads",
    )(*first, *second)


def post_kernel(parts, seq, meta, d0, d1, d2, d3, w, first_grad, *rest):
    out = rest[-1]
    me = meta[0]
    width = w.shape[0]
    total = first_grad[0]
    for k, d in enumerate((d0, d1, d2, d3)):
        for part in range(3):
            cols = pl.ds(pl.multiple_of(part * width + (me ^ k) * 128, 128), 128)
            total = total + dot_nt(d[:, part * 128 : part * 128 + 128], w[:, cols])
    out[0] = total


def post_grads(parts, seq, meta, pieces, w, first_grad, before):
    groups, rows, width = first_grad.shape
    block = pl.BlockSpec((1, rows, width), lambda i: (seq, 0, 0))
    in_specs = [SMEM] + [pl.BlockSpec(p.shape, lambda i: (0, 0)) for p in pieces]
    in_specs += [pl.BlockSpec(w.shape, lambda i: (0, 0)), block]
    more = [before] if seq else []
    return pl.pallas_call(
        functools.partial(post_kernel, parts, seq),
        grid=(1,),
        in_specs=in_specs + [ANY] * len(more),
        out_specs=block,
        out_shape=jax.ShapeDtypeStruct(first_grad.shape, f32),
        input_output_aliases={len(in_specs): 0} if seq else {},
        compiler_params=params(),
        cost_estimate=pl.CostEstimate(flops=3_000_000_000, bytes_accessed=5_000_000, transcendentals=0),
        name="post_grads",
    )(meta, *pieces, w, first_grad, *more)


def local(
    post_stream,
    accum_stream,
    seq_lengths,
    qkv_weight,
    out_weight,
    norm1_gain,
    norm1_bias,
    up_weight,
    up_bias,
    down_weight,
    down_bias,
    norm2_gain,
    norm2_bias,
    post_cotan,
    accum_cotan,
):
    groups, rows, width = post_stream.shape
    parts = lax.axis_size("head")
    shards = lax.axis_size("seq")
    full = rows * parts
    hidden = up_weight.shape[1]
    grad_norm = float(groups * shards * full) ** (-0.5)
    me = lax.axis_index("head")

    def swap(value, k):
        return lax.ppermute(value, "head", [(i, i ^ k) for i in range(parts)])

    meta = jnp.concatenate([jnp.stack([me, lax.axis_index("seq")]).astype(jnp.int32), seq_lengths])
    w_mine = lax.dynamic_slice_in_dim(qkv_weight.reshape(width, 3, width), me * 128, 128, 2).reshape(width, 384)
    row = lambda v: v.reshape(1, -1)
    weights = (
        out_weight,
        row(norm1_gain),
        row(norm1_bias),
        up_weight,
        row(up_bias),
        down_weight,
        row(down_bias),
        row(norm2_gain),
        row(norm2_bias),
    )
    streams = (post_stream, accum_stream, post_cotan, accum_cotan)
    half = rows // 2
    chunks = []
    for s in range(groups):
        x = post_stream[s]
        xa = swap(x, 1)
        xb = swap(x, 2)
        xc = jnp.concatenate([swap(xa[:half], 2), swap(xb[half:], 1)], 0)
        chunks.append((x, xa, xb, xc))
    fwd = [attend_fwd(parts, s, meta, chunks[s], w_mine) for s in range(groups)]
    fed = []
    for s in range(groups):
        pieces = fwd[s][4:]
        mixed = [pieces[0]] + [swap(pieces[k], k) for k in range(1, parts)]
        fed.append(feed(parts, s, meta, mixed, streams, weights, fed[-1][:4] if s else None))
    post_result, accum_result, accum_grad, first_grad = fed[-1][:4]
    up_grad, down_grad, out_grad, small = weight_grads(fed[0][8:], fed[1][8:])
    vectors = jnp.concatenate(
        [v.reshape(shards, -1) for v in [small[i, :width] for i in range(5)] + [small[5]]], 1
    ).astype(bf16)
    vectors = jnp.pad(vectors, ((0, 0), (0, hidden - vectors.shape[1])))
    early = jnp.concatenate(
        [
            up_grad.reshape(shards, -1, hidden),
            down_grad.reshape(shards, -1, hidden),
            out_grad.reshape(shards, -1, hidden),
            jnp.broadcast_to(vectors[:, None], (shards, 16, hidden)),
        ],
        1,
    )
    early = lax.psum_scatter(early, "seq", scatter_dimension=0, tiled=True)[0]
    for k in (1, 2):
        early = (early.astype(f32) + swap(early, k).astype(f32)).astype(bf16)
    early = early.astype(f32) * grad_norm
    back = []
    for s in range(groups):
        pieces = fed[s][4:8]
        grads = [pieces[0]] + [swap(pieces[k], k) for k in range(1, parts)]
        back.append(
            attend_bwd(
                parts, s, meta, chunks[s], *fwd[s][:4], fwd[s][4:], grads, back[-1][4] if s else None
            )
        )
    post_grad = None
    for s in range(groups):
        pieces = back[s][:4]
        got = [pieces[0]] + [swap(pieces[k], k) for k in range(1, parts)]
        post_grad = post_grads(parts, s, meta, got, qkv_weight, first_grad, post_grad)
    late = back[-1][4].astype(bf16)
    late = lax.psum_scatter(late, "seq", scatter_dimension=0, tiled=True)
    got = jnp.stack([late] + [swap(late, k) for k in range(1, parts)])
    late_rows = late.shape[0]
    order = jnp.arange(parts, dtype=jnp.int32) ^ me
    late = jnp.take(got, order, axis=0).astype(f32) * grad_norm
    late = late.reshape(parts, late_rows, 3, 128).transpose(1, 2, 0, 3).reshape(late_rows, 3 * width)
    n_up = width // shards
    n_down = hidden // shards * width // hidden
    n_out = width // shards * width // hidden
    vectors = early[n_up + n_down + n_out]
    each = width // shards
    return (
        post_result,
        accum_result,
        post_grad,
        accum_grad,
        late,
        early[n_up + n_down : n_up + n_down + n_out].reshape(width // shards, width),
        vectors[0 * each : 1 * each],
        vectors[1 * each : 2 * each],
        early[:n_up],
        vectors[5 * each : 5 * each + hidden // shards],
        early[n_up : n_up + n_down].reshape(hidden // shards, width),
        vectors[4 * each : 5 * each],
        vectors[2 * each : 3 * each],
        vectors[3 * each : 4 * each],
    )


def solution(mesh):
    tokens = P("seq", "head", None)
    in_specs = (tokens, tokens, P("seq")) + (P(),) * 10 + (tokens, tokens)
    out_specs = (
        tokens,
        tokens,
        tokens,
        tokens,
        P("seq", None),
        P("seq", None),
        P("seq"),
        P("seq"),
        P("seq", None),
        P("seq"),
        P("seq", None),
        P("seq"),
        P("seq"),
        P("seq"),
    )
    return jax.shard_map(local, mesh=mesh, in_specs=in_specs, out_specs=out_specs, check_vma=False)
```

```python
import functools
import itertools

import jax
import jax.numpy as jnp
from jax import lax
from jax.experimental import pallas as pl
from jax.experimental.pallas import tpu as pltpu
from jax.sharding import PartitionSpec as P

H = 8
EPS = 1e-05
NEG = -1e30
LOG2E = 1.4426950408889634
VMEM_LIMIT = 62 * 2**20
bf16 = jnp.bfloat16
f32 = jnp.float32
SMEM = pl.BlockSpec(memory_space=pltpu.SMEM)
VMEM = pl.BlockSpec(memory_space=pltpu.VMEM)
ANY = pl.BlockSpec(memory_space=pl.ANY)
DMA = pltpu.SemaphoreType.DMA


def dot(a, b):
    return jnp.dot(a, b, preferred_element_type=f32)


def dot_nt(a, b):
    return lax.dot_general(a, b, (((1,), (1,)), ((), ())), preferred_element_type=f32)


def dot_tn(a, b):
    return lax.dot_general(a, b, (((0,), (0,)), ((), ())), preferred_element_type=f32)


def split3(value):
    first = value.astype(bf16)
    rest = value - first.astype(f32)
    second = rest.astype(bf16)
    third = (rest - second.astype(f32)).astype(bf16)
    return first, second, third


def lane_sets():
    lane = lax.broadcasted_iota(jnp.int32, (1, 128), 1)
    return lane, (lane < 64, lane >= 64), (64, 0)


def bits_of(count):
    return [1 << b for b in range(count.bit_length() - 1)]


def flip(index, k, count):
    out = 0
    for bit in bits_of(count):
        out = out + (lax.rem(lax.div(index, bit) + (k // bit), 2)) * bit
    return out


def flip_any(index, k, count):
    if isinstance(k, int):
        return flip(index, k, count)
    out = 0
    for bit in bits_of(count):
        out = out + lax.rem(lax.div(index, bit) + lax.div(k, bit), 2) * bit
    return out


def aligned(start, step):
    if isinstance(start, int):
        return start
    return pl.multiple_of(start, step)


def send(src, dst, pair, axis, to):
    return pltpu.make_async_remote_copy(
        src_ref=src,
        dst_ref=dst,
        send_sem=pair[0],
        recv_sem=pair[1],
        device_id={axis: to},
        device_id_type=pl.DeviceIdType.MESH,
    )


def enter(partners):
    barrier = pltpu.get_barrier_semaphore()
    for axis, to in partners:
        pl.semaphore_signal(barrier, inc=1, device_id={axis: to}, device_id_type=pl.DeviceIdType.MESH)
    pl.semaphore_wait(barrier, len(partners))


def grad_rows(width, hidden, shards):
    n = width // shards
    up = n * (hidden // width)
    vectors = 16 - n % 16
    total = 2 * up + n + vectors
    return n, up, vectors, -(-total // 128) * 128


def normed(value):
    centre = value - jnp.mean(value, axis=-1, keepdims=True)
    spread = jnp.mean(centre * centre, axis=-1, keepdims=True)
    inv = lax.rsqrt(spread + EPS)
    return centre * inv, inv


def norm_back(cot, unit, inv):
    return (
        cot - jnp.mean(cot, axis=-1, keepdims=True) - unit * jnp.mean(cot * unit, axis=-1, keepdims=True)
    ) * inv


def first_kernel(
    parts,
    shards,
    lengths,
    x,
    y,
    pc,
    ac,
    wqkv,
    wo_h,
    g1,
    b1,
    wu_h,
    bu,
    wd_h,
    bd,
    g2,
    b2,
    post_o,
    accum_o,
    accg_o,
    first_o,
    qkv_o,
    lse_o,
    mixed_o,
    go_o,
    xs_o,
    grads_o,
    xs,
    w,
    qkv,
    ka,
    qa,
    vt,
    mixed,
    lse,
    wo,
    wu,
    wd,
    stream,
    mix,
    hid,
    pre,
    slope,
    back,
    fgrad,
    mid,
    agrad,
    mgrad,
    stage,
    small,
    grads,
    load_sem,
    store_sem,
    xsem,
    msem,
    gsem,
):
    groups, rows, width = x.shape
    hidden = wu.shape[1]
    full = rows * parts
    me = lax.axis_index("head")
    core = lax.rem(lax.axis_index("seq"), 2)
    lane, mine, base = lane_sets()
    one = jnp.ones((), bf16)
    zero = jnp.zeros((), bf16)
    half = rows // 2
    near, far = slice(0, half), slice(half, rows)

    loads = []

    def load(src, dst):
        copy = pltpu.make_async_copy(src, dst, load_sem.at[len(loads)])
        copy.start()
        loads.append(copy)
        return copy

    stores = []
    store_count = itertools.count()

    def store(src, dst):
        copy = pltpu.make_async_copy(src, dst, store_sem.at[next(store_count)])
        copy.start()
        stores.append(copy)
        return copy

    x_in = [load(x.at[0], xs.at[0, 0])]
    w_in = [
        load(
            wqkv.at[:, pl.ds(aligned(part * width + me * 128, 128), 128)],
            w.at[:, part * 128 : part * 128 + 128],
        )
        for part in range(3)
    ]
    x_in.append(load(x.at[1], xs.at[1, 0]))
    wo_in = load(wo_h, wo)
    wu_in = load(wu_h, wu)
    wd_in = load(wd_h, wd)

    def stream_load(s):
        return [load(a.at[s], stream.at[i]) for i, a in enumerate((y, pc, ac))]

    stream_in = stream_load(0)

    enter([("head", flip(me, k, parts)) for k in range(1, parts)])

    def x_copy(s, i):
        src, dst, k = (
            (x.at[s, near], xs.at[s, 1, near], 1),
            (x.at[s, far], xs.at[s, 1, far], 1),
            (x.at[s, far], xs.at[s, 2, far], 2),
            (x.at[s, near], xs.at[s, 2, near], 2),
            (xs.at[s, 1, near], xs.at[s, 3, near], 2),
            (xs.at[s, 2, far], xs.at[s, 3, far], 1),
        )[i]
        return send(src, dst, (xsem.at[0, s, i], xsem.at[1, s, i]), "head", flip(me, k, parts))

    def x_start(s):
        for i in (0, 2, 1, 3):
            x_copy(s, i).start()

    def x_forward(s):
        x_copy(s, 0).wait_recv()
        x_copy(s, 4).start()
        x_copy(s, 2).wait_recv()
        x_copy(s, 5).start()

    def x_wait(s, k):
        for i in ((), (1,), (3,), (4, 5))[k]:
            x_copy(s, i).wait_recv()

    def m_copy(s, k):
        return send(
            mixed.at[s, pl.ds(k * rows, rows)],
            mix.at[s, :, pl.ds(aligned(me * 128, 128), 128)],
            (msem.at[0, s, k], msem.at[1, s, k]),
            "head",
            flip(me, k, parts),
        )

    def g_copy(s, k):
        return send(
            mgrad.at[s, :, pl.ds(aligned(flip(me, k, parts) * 128, 128), 128)],
            go_o.at[s, k],
            (gsem.at[0, s, k], gsem.at[1, s, k]),
            "head",
            flip(me, k, parts),
        )

    def project(s, k):
        length = lengths[s]
        at = slice(k * rows, (k + 1) * rows)
        three = dot(xs[s, k], w[...])
        query = (three[:, :128] * (LOG2E * 64 ** (-0.5))).astype(bf16)
        keys = three[:, 128:256].astype(bf16)
        values = three[:, 256:].astype(bf16)
        qkv[s, 0, at] = query
        qkv[s, 1, at] = keys
        qkv[s, 2, at] = values
        pos = lax.broadcasted_iota(jnp.int32, (rows, 1), 0) + flip(me, k, parts) * rows
        bias = jnp.where(pos < length, 0.0, NEG).astype(bf16)
        turned = values.T
        for h in range(2):
            ka[h, at] = jnp.where(mine[h], keys, jnp.where(lane == base[h], bias, zero))
            qa[h, at] = jnp.where(mine[h], query, jnp.where(lane == base[h], one, zero))
            vt[h, :64, at] = turned[h * 64 : h * 64 + 64]
            vt[h, 64:, at] = jnp.ones((8, rows), bf16)

    def attend(s, between):
        def body(j, carry):
            between(j)
            at = pl.ds(aligned(j * rows, rows), rows)
            out = []
            for h in range(2):
                top, acc = carry[h]
                scores = dot_nt(ka[h, at, :], qa[h])
                new_top = jnp.maximum(top, jnp.max(scores, axis=0, keepdims=True))
                probs = jnp.exp2(scores - new_top)
                acc = acc * jnp.exp2(top - new_top) + dot(vt[h, :, at], probs.astype(bf16))
                out.append((new_top, acc))
            return tuple(out)

        init = tuple((jnp.full((1, full), NEG, f32), jnp.zeros((72, full), f32)) for _ in range(2))
        both = lax.fori_loop(0, parts, body, init)
        lse[s] = jnp.zeros((8, full), f32)
        pieces = []
        for h in range(2):
            top, acc = both[h]
            total = acc[64:65]
            pieces.append(acc[:64] / total)
            lse[s, h : h + 1, :] = top + jnp.log2(total)
        mixed[s] = jnp.concatenate(pieces, 0).T.astype(bf16)
        for k in range(parts - 1, 0, -1):
            m_copy(s, k).start()
        mix[s, :, pl.ds(aligned(me * 128, 128), 128)] = mixed[s, :rows]

    x_start(0)
    x_in[0].wait()
    for copy in w_in:
        copy.wait()
    project(0, 0)
    x_forward(0)
    for k in (1, 2):
        x_wait(0, k)
        project(0, k)
    x_wait(0, 3)
    x_start(1)
    project(0, 3)

    def forward_next(j):
        @pl.when(j == 2)
        def _():
            x_forward(1)

    attend(0, forward_next)
    x_in[1].wait()
    project(1, 0)
    for k in range(1, parts):
        x_wait(1, k)
        project(1, k)
    for s in range(groups):
        store(qkv.at[s], qkv_o.at[s])
        store(xs.at[s], xs_o.at[s])
    attend(1, lambda j: None)
    for s in range(groups):
        store(mixed.at[s], mixed_o.at[s])
        store(lse.at[s], lse_o.at[s])

    tile = 512
    tiles = hidden // tile
    small[...] = jnp.zeros_like(small)
    staged = []

    def feed(s):
        length = lengths[s]
        pos = lax.broadcasted_iota(jnp.int32, (rows, 1), 0) + me * rows
        keep = pos < length
        for k in range(1, parts):
            m_copy(s, k).wait_recv()
        attention = dot(mix[s], wo[...])
        unit1, inv1 = normed(xs[s, 0].astype(f32) + attention)
        x_mid = unit1 * g1[...] + b1[...]
        mid[s] = x_mid.astype(bf16)
        total = jnp.zeros((rows, width), f32)
        c0 = 0.7978845608028654
        c1 = 0.044715
        for t in range(tiles):
            cols = slice(t * tile, (t + 1) * tile)
            act = dot(mid[s], wu[:, cols]) + bu[:, cols]
            square = act * act
            th = jnp.tanh(act * (c0 + (c0 * c1) * square))
            part = 0.5 * (1.0 + th)
            low = (act * part).astype(bf16)
            hid[s, :, cols] = low
            slope[:rows, cols] = part + (0.5 * act) * (1.0 - th * th) * (c0 + (3.0 * c0 * c1) * square)
            total = total + dot(low, wd[cols, :])
        total = total + bd[...]
        unit2, inv2 = normed(x_mid + total)
        for copy in staged:
            copy.wait()
        stores[:] = [copy for copy in stores if not any(copy is done for done in staged)]
        staged.clear()
        stage[0] = jnp.where(keep, unit2 * g2[...] + b2[...], 0.0)
        stage[1] = jnp.where(keep, stream[0].astype(f32) + attention + total, 0.0)
        post_c = jnp.where(keep, stream[1].astype(f32), 0.0)
        accum_c = jnp.where(keep, stream[2].astype(f32), 0.0)
        stage[2] = accum_c
        for i, out in enumerate((post_o, accum_o, accg_o)):
            staged.append(store(stage.at[i], out.at[s]))
        mid_grad2 = norm_back(post_c * g2[...], unit2, inv2)
        small[2:3, :width] += jnp.sum(post_c * unit2, axis=0, keepdims=True)
        small[3:4, :width] += jnp.sum(post_c, axis=0, keepdims=True)
        feed_grad = (mid_grad2 + accum_c).astype(bf16)
        fgrad[s] = feed_grad
        small[4:5, :width] += jnp.sum(feed_grad.astype(f32), axis=0, keepdims=True)
        back[...] = mid_grad2
        for t in range(tiles):
            cols = slice(t * tile, (t + 1) * tile)
            hidden_grad = dot_nt(fgrad[s], wd[cols, :]).astype(bf16)
            pre_grad = (hidden_grad.astype(f32) * slope[:rows, cols]).astype(bf16)
            pre[s, :, cols] = pre_grad
            small[5:6, cols] += jnp.sum(pre_grad.astype(f32), axis=0, keepdims=True)
            back[...] += dot_nt(pre_grad, wu[:, cols])
        mid_grad = back[...]
        small[0:1, :width] += jnp.sum(mid_grad * unit1, axis=0, keepdims=True)
        small[1:2, :width] += jnp.sum(mid_grad, axis=0, keepdims=True)
        first = norm_back(mid_grad * g1[...], unit1, inv1)
        stage[3] = first
        staged.append(store(stage.at[3], first_o.at[s]))
        attn_grad = (first + accum_c).astype(bf16)
        agrad[s] = attn_grad
        mgrad[s] = dot_nt(attn_grad, wo[...]).astype(bf16)
        for k in range(parts - 1, 0, -1):
            g_copy(s, k).start()
        store(mgrad.at[s, :, pl.ds(aligned(me * 128, 128), 128)], go_o.at[s, 0])

    wo_in.wait()
    wu_in.wait()
    wd_in.wait()
    for s in range(groups):
        for copy in stream_in:
            copy.wait()
        feed(s)
        if s + 1 < groups:
            stream_in = stream_load(s + 1)

    n, up_rows, vector_rows, total_rows = grad_rows(width, hidden, shards)

    def place(shard):
        return lax.rem(core + shard % 2, 2), shard // 2

    def over_seqs(left, right, cols=slice(None)):
        return sum(dot_tn(left[s, :, cols], right[s]) for s in range(groups))

    for t in range(tiles):
        cols = slice(t * tile, (t + 1) * tile)
        slope[:, cols] = sum(dot_tn(mid[s], pre[s, :, cols]) for s in range(groups))
    for shard in range(shards):
        own = slice(shard * n, (shard + 1) * n)
        block = jnp.concatenate([slope[own, t * tile : (t + 1) * tile] for t in range(tiles)], 0)
        side, spot = place(shard)
        grads[side, spot, :up_rows] = block.astype(bf16)
    per = tile // up_rows
    for t in range(tiles):
        block = over_seqs(hid, fgrad, slice(t * tile, (t + 1) * tile)).astype(bf16)
        for i in range(per):
            side, spot = place(t * per + i)
            grads[side, spot, up_rows : 2 * up_rows] = block[i * up_rows : (i + 1) * up_rows]
    back_all = over_seqs(mix, agrad)
    which = lax.broadcasted_iota(jnp.int32, (8, width), 0)
    short = small[:, :width]
    long = small[...]
    for shard in range(shards):
        a = pltpu.roll(short, (width - shard * n) % width, 1)
        b = pltpu.roll(long, (hidden - shard * up_rows) % hidden, 1)[:, :width]
        extra = jnp.where(which == 5, b, a)
        rest = total_rows - 2 * up_rows - n - 8
        block = jnp.concatenate(
            [back_all[shard * n : (shard + 1) * n], extra, jnp.zeros((rest, width), f32)], 0
        )
        side, spot = place(shard)
        grads[side, spot, 2 * up_rows :] = block.astype(bf16)
    store(grads, grads_o)

    for s in range(groups):
        for k in range(1, parts):
            g_copy(s, k).wait()
            m_copy(s, k).wait_send()
        for i in range(6):
            x_copy(s, i).wait_send()
    for copy in stores:
        copy.wait()


def first_call(parts, shards, lengths, streams, weights):
    groups, rows, width = streams[0].shape
    hidden = weights[4].shape[1]
    full = rows * parts
    total_rows = grad_rows(width, hidden, shards)[3]
    whole = jax.ShapeDtypeStruct((groups, rows, width), f32)
    heads = jax.ShapeDtypeStruct((groups, full, 128), bf16)
    return pl.pallas_call(
        functools.partial(first_kernel, parts, shards),
        in_specs=[SMEM] + [ANY] * 6 + [VMEM, VMEM, ANY, VMEM, ANY, VMEM, VMEM, VMEM],
        out_specs=[ANY] * 10,
        out_shape=[whole] * 4
        + [
            jax.ShapeDtypeStruct((groups, 3, full, 128), bf16),
            jax.ShapeDtypeStruct((groups, 8, full), f32),
            heads,
            jax.ShapeDtypeStruct((groups, parts, rows, 128), bf16),
            jax.ShapeDtypeStruct((groups, parts, rows, width), bf16),
            jax.ShapeDtypeStruct((2, shards // 2, total_rows, width), bf16),
        ],
        scratch_shapes=[
            pltpu.VMEM((groups, parts, rows, width), bf16),
            pltpu.VMEM((width, 384), bf16),
            pltpu.VMEM((groups, 3, full, 128), bf16),
            pltpu.VMEM((2, full, 128), bf16),
            pltpu.VMEM((2, full, 128), bf16),
            pltpu.VMEM((2, 72, full), bf16),
            pltpu.VMEM((groups, full, 128), bf16),
            pltpu.VMEM((groups, 8, full), f32),
            pltpu.VMEM((width, width), bf16),
            pltpu.VMEM((width, hidden), bf16),
            pltpu.VMEM((hidden, width), bf16),
            pltpu.VMEM((3, rows, width), bf16),
            pltpu.VMEM((groups, rows, width), bf16),
            pltpu.VMEM((groups, rows, hidden), bf16),
            pltpu.VMEM((groups, rows, hidden), bf16),
            pltpu.VMEM((max(rows, width), hidden), f32),
            pltpu.VMEM((rows, width), f32),
            pltpu.VMEM((groups, rows, width), bf16),
            pltpu.VMEM((groups, rows, width), bf16),
            pltpu.VMEM((groups, rows, width), bf16),
            pltpu.VMEM((groups, rows, width), bf16),
            pltpu.VMEM((4, rows, width), f32),
            pltpu.VMEM((8, hidden), f32),
            pltpu.VMEM((2, shards // 2, total_rows, width), bf16),
            DMA((16,)),
            DMA((24,)),
            DMA((2, groups, 6)),
            DMA((2, groups, parts)),
            DMA((2, groups, parts)),
        ],
        compiler_params=pltpu.CompilerParams(
            vmem_limit_bytes=VMEM_LIMIT, collective_id=0, has_side_effects=True
        ),
        name="forward_and_feed",
    )(lengths, *streams, *weights)


def second_kernel(
    parts,
    shards,
    grad_norm,
    lengths,
    qkv_h,
    lse_h,
    mixed_h,
    go_h,
    xs_h,
    grads_h,
    first_h,
    wqkv_h,
    post_o,
    wqkv_o,
    up_o,
    down_o,
    out_o,
    vec_o,
    xs,
    qkv,
    lse,
    mixed,
    go,
    wqkv,
    first,
    grads,
    core_in,
    a1_in,
    b1_in,
    a2_in,
    b2_in,
    z_in,
    all_out,
    all_in,
    final,
    ka,
    va,
    qa,
    da,
    kt,
    dqt,
    dsend,
    dfull,
    late,
    late_out,
    late_in,
    late_all,
    load_sem,
    store_sem,
    dsem,
    rsem,
    lsem,
):
    groups, parts, rows, width = xs.shape
    full = rows * parts
    hidden = up_o.shape[1]
    me = lax.axis_index("head")
    place = lax.axis_index("seq")
    lane, mine, base = lane_sets()
    one = jnp.ones((), bf16)
    zero = jnp.zeros((), bf16)
    n, up_rows, vector_rows, total_rows = grad_rows(width, hidden, shards)
    seq_bits = bits_of(shards)
    load_count = itertools.count()

    def load(src, dst):
        copy = pltpu.make_async_copy(src, dst, load_sem.at[next(load_count)])
        copy.start()
        return copy

    stores = []
    store_count = itertools.count()

    def store(src, dst):
        copy = pltpu.make_async_copy(src, dst, store_sem.at[next(store_count)])
        copy.start()
        stores.append(copy)

    def seq_load(s):
        return [
            load(qkv_h.at[s], qkv.at[s]),
            load(go_h.at[s], go.at[s]),
            load(mixed_h.at[s], mixed.at[s]),
            load(lse_h.at[s], lse.at[s]),
            load(xs_h.at[s], xs.at[s]),
        ]

    seq_in = [seq_load(0)]
    grads_in = load(grads_h.at[0], grads)
    seq_in.append(seq_load(1))
    wqkv_in = load(wqkv_h, wqkv)
    first_in = load(first_h, first)

    enter(
        [("head", flip(me, k, parts)) for k in range(1, parts)]
        + [("seq", flip(place, bit, shards)) for bit in seq_bits]
    )

    sends = []

    def launch(make, *which):
        make(*which).start()
        sends.append(functools.partial(make, *which))

    spots = shards // 2
    half, quarter = total_rows // 2, total_rows // 4
    eighth = total_rows // 8
    x_bit = lax.rem(me, 2)
    y_bit = lax.div(me, 2)

    def to_head(src, dst, i, k):
        return send(src, dst, (rsem.at[0, i], rsem.at[1, i]), "head", flip(me, k, parts))

    def to_seq(src, dst, i, bit):
        return send(src, dst, (rsem.at[0, i], rsem.at[1, i]), "seq", flip(place, bit, shards))

    core_copy = lambda: to_seq(grads_h.at[1], core_in, 0, 1)
    a_keep = x_bit * quarter
    a_give = (1 - x_bit) * quarter
    b_keep = half + y_bit * quarter
    b_give = half + (1 - y_bit) * quarter
    a1_copy = lambda: to_head(grads.at[:, pl.ds(aligned(a_give, 16), quarter)], a1_in, 1, 1)
    b1_copy = lambda: to_head(grads.at[:, pl.ds(aligned(b_give, 16), quarter)], b1_in, 2, 2)
    a_own = a_keep + y_bit * eighth
    a_pass = a_keep + (1 - y_bit) * eighth
    b_own = b_keep + x_bit * eighth
    b_pass = b_keep + (1 - x_bit) * eighth
    a2_copy = lambda: to_head(grads.at[:, pl.ds(aligned(a_pass, 16), eighth)], a2_in, 3, 2)
    b2_copy = lambda: to_head(grads.at[:, pl.ds(aligned(b_pass, 16), eighth)], b2_in, 4, 1)

    def add_rows(into, spot, start, count, other):
        at = pl.ds(aligned(start, 16), count)
        into[spot, at] = (into[spot, at].astype(f32) + other.astype(f32)).astype(bf16)

    def early_core():
        grads_in.wait()
        core_copy().wait_recv()

        def body(i, carry):
            grads[i] = (grads[i].astype(f32) + core_in[i].astype(f32)).astype(bf16)
            return carry

        lax.fori_loop(0, spots, body, None)
        launch(a1_copy)
        launch(b1_copy)

    def early_first():
        a1_copy().wait_recv()
        b1_copy().wait_recv()

        def body(i, carry):
            add_rows(grads, i, a_keep, quarter, a1_in[i])
            add_rows(grads, i, b_keep, quarter, b1_in[i])
            return carry

        lax.fori_loop(0, spots, body, None)
        launch(a2_copy)
        launch(b2_copy)

    def early_second():
        a2_copy().wait_recv()
        b2_copy().wait_recv()

        def body(i, carry):
            add_rows(grads, i, a_own, eighth, a2_in[i])
            add_rows(grads, i, b_own, eighth, b2_in[i])
            return carry

        lax.fori_loop(0, spots, body, None)

        def gather(i, carry):
            all_out[i, :eighth] = grads[i, pl.ds(aligned(a_own, 16), eighth)]
            all_out[i, eighth:] = grads[i, pl.ds(aligned(b_own, 16), eighth)]
            return carry

        lax.fori_loop(0, spots, gather, None)

    offsets = []
    at = 0
    size = spots
    for bit in seq_bits[1:]:
        offsets.append((at, size))
        at += size
        size //= 2
    offsets.append((at, 1))
    z_offsets = []
    at = 0
    for _, size in offsets[:-1]:
        z_offsets.append(at)
        at += size // 2

    def z_copy(i):
        at, size = offsets[i]
        bit = seq_bits[1 + i]
        return to_seq(
            all_in.at[pl.ds(z_offsets[i], size // 2)], z_in.at[pl.ds(z_offsets[i], size // 2)], 5 + i, bit
        )

    def z_send(i):
        at, size = offsets[i]
        own = lax.rem(lax.div(place, seq_bits[1 + i]), 2)
        for j in range(size // 2):
            all_in[z_offsets[i] + j] = all_out[at + 2 * j + (1 - own)]
        launch(z_copy, i)

    def z_add(i):
        at, size = offsets[i]
        after = offsets[i + 1][0]
        own = lax.rem(lax.div(place, seq_bits[1 + i]), 2)
        z_copy(i).wait_recv()
        for j in range(size // 2):
            all_out[after + j] = (
                all_out[at + 2 * j + own].astype(f32) + z_in[z_offsets[i] + j].astype(f32)
            ).astype(bf16)

    steps = len(offsets) - 1
    ag_from = 5 + steps
    last = offsets[-1][0]
    ag = sum(size // 2 for _, size in offsets[:-1])

    def ag_copy(k):
        return to_head(all_out.at[last], all_in.at[ag + k], ag_from + k, k)

    def ag_send():
        for k in range(parts - 1, 0, -1):
            launch(ag_copy, k)

    def ag_finish():
        for k in range(parts):
            if k:
                ag_copy(k).wait_recv()
                block = all_in[ag + k]
            else:
                block = all_out[last]
            block = block.astype(f32) * grad_norm
            who = flip(me, k, parts)
            x_of, y_of = lax.rem(who, 2), lax.div(who, 2)
            a_at = x_of * quarter + y_of * eighth
            b_at = half + y_of * quarter + x_of * eighth
            final[pl.ds(aligned(a_at, 16), eighth)] = block[:eighth]
            final[pl.ds(aligned(b_at, 16), eighth)] = block[eighth:]
        for t in range(hidden // width):
            store(final.at[pl.ds(t * n, n)], up_o.at[:, pl.ds(t * width, width)])
        store(final.at[pl.ds(up_rows, up_rows)], down_o)
        store(final.at[pl.ds(2 * up_rows, n)], out_o)
        vec_o[...] = final[2 * up_rows + n : 2 * up_rows + n + 8]

    def d_copy(s, part, k):
        return send(
            dsend.at[s, part, pl.ds(aligned(k * rows, rows), rows)],
            dfull.at[s, :, pl.ds(aligned(part * width + me * 128, 128), 128)],
            (dsem.at[0, s, part, k], dsem.at[1, s, part, k]),
            "head",
            flip_any(me, k, parts),
        )

    def prepare(s):
        length = lengths[s]
        for copy in seq_in[s]:
            copy.wait()
        turned = -lse[s].T
        kt[...] = qkv[s, 1].T
        for k in range(parts):
            at = slice(k * rows, (k + 1) * rows)
            query, keys, values = qkv[s, 0, at], qkv[s, 1, at], qkv[s, 2, at]
            pos = lax.broadcasted_iota(jnp.int32, (rows, 1), 0) + flip(me, k, parts) * rows
            bias = jnp.where(pos < length, 0.0, NEG).astype(bf16)
            grad = go[s, k]
            prod = grad.astype(f32) * mixed[s, at].astype(f32)
            for h in range(2):
                ka[h, at] = jnp.where(mine[h], keys, jnp.where(lane == base[h], bias, one))
                va[h, at] = jnp.where(mine[h], values, one)
                a, b, c = split3(-jnp.sum(jnp.where(mine[h], prod, 0.0), axis=1, keepdims=True))
                extra = jnp.where(
                    lane == base[h],
                    a,
                    jnp.where(lane == base[h] + 1, b, jnp.where(lane == base[h] + 2, c, zero)),
                )
                da[h, at] = jnp.where(mine[h], grad, extra)
                a, b, c = split3(turned[at, h : h + 1])
                extra = jnp.where(
                    lane == base[h],
                    one,
                    jnp.where(
                        lane == base[h] + 1,
                        a,
                        jnp.where(lane == base[h] + 2, b, jnp.where(lane == base[h] + 3, c, zero)),
                    ),
                )
                qa[h, at] = jnp.where(mine[h], query, extra)
        dqt[...] = jnp.zeros_like(dqt)

    block = rows // 2
    steps_each = 2 * parts

    def attend_back(s, events):
        def body(i, carry):
            for when, event in events.items():
                pl.when(i == when)(event)
            chunk = parts - 1 - lax.div(i, 2)
            at = pl.ds(aligned(chunk * rows + lax.rem(i, 2) * block, block), block)
            out = []
            for h in range(2):
                probs = jnp.exp2(dot_nt(ka[h, at, :], qa[h]))
                inner = dot_nt(va[h, at, :], da[h])
                low = probs.astype(bf16)
                grad = (probs * inner).astype(bf16)
                dv = dot(low, go[s].reshape(full, 128))
                dk = dot(grad, qkv[s, 0])
                part = slice(h * 64, h * 64 + 64)
                dqt[part, :] += dot(kt[part, at], grad)
                out.append((dv, dk))
            dsend[s, 1, at] = (jnp.where(mine[0], out[0][1], out[1][1]) * (1.0 / LOG2E)).astype(bf16)
            dsend[s, 2, at] = jnp.where(mine[0], out[0][0], out[1][0]).astype(bf16)

            @pl.when((lax.rem(i, 2) == 1) & (chunk > 0))
            def _():
                for part in (1, 2):
                    d_copy(s, part, chunk).start()

            return carry

        lax.fori_loop(0, steps_each, body, None)
        dsend[s, 0] = (dqt[...] * 64 ** (-0.5)).T.astype(bf16)
        for k in range(parts - 1, 0, -1):
            d_copy(s, 0, k).start()
        for part in range(3):
            dfull[s, :, pl.ds(aligned(part * width + me * 128, 128), 128)] = dsend[s, part, :rows]

    def late_term(s):
        for part in range(3):
            cols = slice(part * 128, part * 128 + 128)
            term = sum(
                dot_tn(xs[s, k], dsend[s, part, k * rows : (k + 1) * rows]) for k in range(parts)
            )
            late[:, cols] = term if s == 0 else late[:, cols] + term

    launch(core_copy)
    prepare(0)
    attend_back(0, {1: early_core, 6: early_first})
    late_term(0)
    prepare(1)
    events = {1: early_second}
    events_z = [functools.partial(z_send, 0)] if steps else []
    for i in range(1, steps):

        def both(i=i):
            z_add(i - 1)
            z_send(i)

        events_z.append(both)
    if steps:

        def ending():
            z_add(steps - 1)
            ag_send()

        events_z.append(ending)
    else:
        events_z.append(ag_send)
    if len(events_z) <= 3:
        slots = (2, 4, 7)[: len(events_z)]
    else:
        slots = tuple(range(2, 2 + len(events_z)))
    later = []
    for slot, event in zip(slots, events_z):
        if slot < steps_each:
            events[slot] = event
        else:
            later.append(event)
    attend_back(1, events)
    for event in later:
        event()
    late_term(1)

    l_offsets = []
    at = 0
    size = shards
    for bit in seq_bits:
        l_offsets.append((at, size))
        at += size // 2
        size //= 2

    def l_copy(i):
        at, size = l_offsets[i]
        return send(
            late_out.at[pl.ds(at, size // 2)],
            late_in.at[pl.ds(at, size // 2)],
            (lsem.at[0, i], lsem.at[1, i]),
            "seq",
            flip(place, seq_bits[i], shards),
        )

    def l_rows(shard):
        return pl.ds(aligned(shard * n, 8), n)

    def l_send(i):
        at, size = l_offsets[i]
        own = lax.rem(lax.div(place, seq_bits[i]), 2)
        for j in range(size // 2):
            late_out[at + j] = late[l_rows(2 * j + 1 - own)].astype(bf16)
        launch(l_copy, i)

    def l_add(i):
        at, size = l_offsets[i]
        own = lax.rem(lax.div(place, seq_bits[i]), 2)
        l_copy(i).wait_recv()
        for j in range(size // 2):
            late[l_rows(j)] = late[l_rows(2 * j + own)] + late_in[at + j].astype(f32)

    l_steps = len(seq_bits)

    def lg_copy(k):
        return send(
            late_all.at[0],
            late_all.at[k],
            (lsem.at[0, l_steps + k], lsem.at[1, l_steps + k]),
            "head",
            flip(me, k, parts),
        )

    def post_part(s, low, high):
        first[s] += dot_nt(dfull[s, :, low:high], wqkv[:, low:high])

    l_send(0)
    ag_finish()
    wqkv_in.wait()
    first_in.wait()
    for part in range(3):
        for k in range(1, parts):
            d_copy(0, part, k).wait_recv()
    l_add(0)
    for i in range(1, l_steps):
        l_send(i)
        if i == 1:
            post_part(0, 0, 3 * width)
            store(first.at[0], post_o.at[0])
        if i == 2:
            for part in (1, 2):
                for k in range(1, parts):
                    d_copy(1, part, k).wait_recv()
            post_part(1, width, 3 * width)
        l_add(i)
    late_all[0] = late[:n].astype(bf16)
    for k in range(parts - 1, 0, -1):
        launch(lg_copy, k)
    if l_steps < 2:
        post_part(0, 0, 3 * width)
        store(first.at[0], post_o.at[0])
    if l_steps < 3:
        for part in (1, 2):
            for k in range(1, parts):
                d_copy(1, part, k).wait_recv()
        post_part(1, width, 3 * width)
    for k in range(1, parts):
        d_copy(1, 0, k).wait_recv()
    post_part(1, 0, width)
    store(first.at[1], post_o.at[1])
    for k in range(parts):
        if k:
            lg_copy(k).wait_recv()
        block_of = late_all[k].astype(f32) * grad_norm
        for part in range(3):
            cols = pl.ds(aligned(part * width + flip(me, k, parts) * 128, 128), 128)
            wqkv_o[:, cols] = block_of[:, part * 128 : part * 128 + 128]
    for make in sends:
        make().wait_send()
    for s in range(groups):
        for part in range(3):
            for k in range(1, parts):
                d_copy(s, part, k).wait_send()
    for copy in stores:
        copy.wait()


def second_call(parts, shards, grad_norm, lengths, saved, grads, first, wqkv, hidden):
    xs_shape = saved[4].shape
    groups, _, rows, width = xs_shape
    full = rows * parts
    n, up_rows, vector_rows, total_rows = grad_rows(width, hidden, shards)
    spots = shards // 2
    quarter, eighth = total_rows // 4, total_rows // 8
    two = total_rows // 4
    heads = (2, full, 128)
    all_spots = 2 * spots
    in_spots = spots + parts
    return pl.pallas_call(
        functools.partial(second_kernel, parts, shards, grad_norm),
        in_specs=[SMEM] + [ANY] * 8,
        out_specs=[ANY, VMEM, ANY, ANY, ANY, VMEM],
        out_shape=[
            jax.ShapeDtypeStruct((groups, rows, width), f32),
            jax.ShapeDtypeStruct((n, 3 * width), f32),
            jax.ShapeDtypeStruct((n, hidden), f32),
            jax.ShapeDtypeStruct((up_rows, width), f32),
            jax.ShapeDtypeStruct((n, width), f32),
            jax.ShapeDtypeStruct((8, width), f32),
        ],
        scratch_shapes=[
            pltpu.VMEM(xs_shape, bf16),
            pltpu.VMEM((groups, 3, full, 128), bf16),
            pltpu.VMEM((groups, 8, full), f32),
            pltpu.VMEM((groups, full, 128), bf16),
            pltpu.VMEM((groups, parts, rows, 128), bf16),
            pltpu.VMEM((width, 3 * width), bf16),
            pltpu.VMEM((groups, rows, width), f32),
            pltpu.VMEM((spots, total_rows, width), bf16),
            pltpu.VMEM((spots, total_rows, width), bf16),
            pltpu.VMEM((spots, quarter, width), bf16),
            pltpu.VMEM((spots, quarter, width), bf16),
            pltpu.VMEM((spots, eighth, width), bf16),
            pltpu.VMEM((spots, eighth, width), bf16),
            pltpu.VMEM((spots, two, width), bf16),
            pltpu.VMEM((all_spots, two, width), bf16),
            pltpu.VMEM((in_spots, two, width), bf16),
            pltpu.VMEM((total_rows, width), f32),
            pltpu.VMEM(heads, bf16),
            pltpu.VMEM(heads, bf16),
            pltpu.VMEM(heads, bf16),
            pltpu.VMEM(heads, bf16),
            pltpu.VMEM((128, full), bf16),
            pltpu.VMEM((128, full), f32),
            pltpu.VMEM((groups, 3, full, 128), bf16),
            pltpu.VMEM((groups, rows, 3 * width), bf16),
            pltpu.VMEM((width, 384), f32),
            pltpu.VMEM((shards, n, 384), bf16),
            pltpu.VMEM((shards, n, 384), bf16),
            pltpu.VMEM((parts, n, 384), bf16),
            DMA((16,)),
            DMA((16,)),
            DMA((2, groups, 3, parts)),
            DMA((2, 24)),
            DMA((2, 16)),
        ],
        compiler_params=pltpu.CompilerParams(
            vmem_limit_bytes=VMEM_LIMIT, collective_id=1, has_side_effects=True
        ),
        name="backward_and_sums",
    )(lengths, *saved, grads, first, wqkv)


def local(
    post_stream,
    accum_stream,
    seq_lengths,
    qkv_weight,
    out_weight,
    norm1_gain,
    norm1_bias,
    up_weight,
    up_bias,
    down_weight,
    down_bias,
    norm2_gain,
    norm2_bias,
    post_cotan,
    accum_cotan,
):
    groups, rows, width = post_stream.shape
    parts = lax.axis_size("head")
    shards = lax.axis_size("seq")
    hidden = up_weight.shape[1]
    grad_norm = float(groups * shards * rows * parts) ** (-0.5)

    def row(vector):
        return vector.reshape(1, -1)

    streams = (post_stream, accum_stream, post_cotan, accum_cotan)
    weights = (
        qkv_weight,
        out_weight,
        row(norm1_gain),
        row(norm1_bias),
        up_weight,
        row(up_bias),
        down_weight,
        row(down_bias),
        row(norm2_gain),
        row(norm2_bias),
    )
    post, accum, accum_grad, first, qkv, lse, mixed, go, xs, grads = first_call(
        parts, shards, seq_lengths, streams, weights
    )
    post_grad, qkv_grad, up_grad, down_grad, out_grad, vectors = second_call(
        parts, shards, grad_norm, seq_lengths, (qkv, lse, mixed, go, xs), grads, first, qkv_weight, hidden
    )
    n = width // shards
    return (
        post,
        accum,
        post_grad,
        accum_grad,
        qkv_grad,
        out_grad,
        vectors[0, :n],
        vectors[1, :n],
        up_grad,
        vectors[5, : hidden // shards],
        down_grad,
        vectors[4, :n],
        vectors[2, :n],
        vectors[3, :n],
    )


def solution(mesh):
    tokens = P("seq", "head", None)
    in_specs = (tokens, tokens, P("seq")) + (P(),) * 10 + (tokens, tokens)
    rows = P("seq", None)
    vector = P("seq")
    out_specs = (tokens,) * 4 + (rows, rows, vector, vector, rows, vector, rows, vector, vector, vector)
    return jax.shard_map(local, mesh=mesh, in_specs=in_specs, out_specs=out_specs, check_vma=False)
```

```python
import functools
import itertools

import jax
import jax.numpy as jnp
from jax import lax
from jax.experimental import pallas as pl
from jax.experimental.pallas import tpu as pltpu
from jax.sharding import PartitionSpec as P

H = 8
EPS = 1e-05
NEG = -1e30
LOG2E = 1.4426950408889634
VMEM_LIMIT = 62 * 2**20
bf16 = jnp.bfloat16
f32 = jnp.float32
SMEM = pl.BlockSpec(memory_space=pltpu.SMEM)
VMEM = pl.BlockSpec(memory_space=pltpu.VMEM)
ANY = pl.BlockSpec(memory_space=pl.ANY)
DMA = pltpu.SemaphoreType.DMA


def dot(a, b):
    return jnp.dot(a, b, preferred_element_type=f32)


def dot_nt(a, b):
    return lax.dot_general(a, b, (((1,), (1,)), ((), ())), preferred_element_type=f32)


def dot_tn(a, b):
    return lax.dot_general(a, b, (((0,), (0,)), ((), ())), preferred_element_type=f32)


def split3(value):
    first = value.astype(bf16)
    rest = value - first.astype(f32)
    second = rest.astype(bf16)
    third = (rest - second.astype(f32)).astype(bf16)
    return first, second, third


def lane_sets():
    lane = lax.broadcasted_iota(jnp.int32, (1, 128), 1)
    return lane, (lane < 64, lane >= 64), (64, 0)


def bits_of(count):
    return [1 << b for b in range(count.bit_length() - 1)]


def flip(index, k, count):
    out = 0
    for bit in bits_of(count):
        out = out + (lax.rem(lax.div(index, bit) + (k // bit), 2)) * bit
    return out


def aligned(start, step):
    if isinstance(start, int):
        return start
    return pl.multiple_of(start, step)


def send(src, dst, pair, to):
    return pltpu.make_async_remote_copy(
        src_ref=src,
        dst_ref=dst,
        send_sem=pair[0],
        recv_sem=pair[1],
        device_id=to,
        device_id_type=pl.DeviceIdType.MESH,
    )


def enter(partners):
    barrier = pltpu.get_barrier_semaphore()
    for to in partners:
        pl.semaphore_signal(barrier, inc=1, device_id=to, device_id_type=pl.DeviceIdType.MESH)
    pl.semaphore_wait(barrier, len(partners))


def plane(me, place, parts):
    core = lax.rem(place, 2)
    others = []
    for k in range(parts):
        for other in range(2):
            if k or other:
                seat = place if not other else place + 1 - 2 * core
                others.append((flip(me, k, parts), seat))
    return others


def grad_rows(width, hidden, shards):
    n = width // shards
    up = n * (hidden // width)
    vectors = 16 - n % 16
    total = 2 * up + n + vectors
    return n, up, vectors, -(-total // 128) * 128


def normed(value):
    centre = value - jnp.mean(value, axis=-1, keepdims=True)
    spread = jnp.mean(centre * centre, axis=-1, keepdims=True)
    inv = lax.rsqrt(spread + EPS)
    return centre * inv, inv


def norm_back(cot, unit, inv):
    return (
        cot - jnp.mean(cot, axis=-1, keepdims=True) - unit * jnp.mean(cot * unit, axis=-1, keepdims=True)
    ) * inv


def first_kernel(
    parts,
    shards,
    lengths,
    x,
    pc,
    ac,
    wqkv,
    wo_h,
    g1,
    b1,
    wu_h,
    bu,
    wd_h,
    bd,
    g2,
    b2,
    post_o,
    added_o,
    first_o,
    qkv_o,
    lse_o,
    mixed_o,
    go_o,
    xs_o,
    grads_o,
    length_o,
    xs,
    pcs,
    acs,
    w,
    qkv,
    ka,
    qa,
    vt,
    mixed,
    lse,
    wo,
    wu,
    wd,
    mix,
    hid,
    pre,
    slope,
    back,
    fgrad,
    mid,
    agrad,
    mgrad,
    post_v,
    added_v,
    first_v,
    small,
    grads,
    sizes,
    load_sem,
    store_sem,
    self_sem,
    insem,
    fsem,
    msem,
    gsem,
    osem,
    nsem,
):
    groups, rows, width = x.shape
    hidden = wu.shape[1]
    full = rows * parts
    half = rows // 2
    me = lax.axis_index("head")
    place = lax.axis_index("seq")
    core = lax.rem(place, 2)
    other = place + 1 - 2 * core
    from_core = lax.div(me, 2)
    from_group = lax.rem(me, 2)
    lane, mine, base = lane_sets()
    one = jnp.ones((), bf16)
    zero = jnp.zeros((), bf16)
    here = pl.ds(aligned(core * half, half), half)
    there = pl.ds(aligned((1 - core) * half, half), half)

    load_count = itertools.count()

    def load(src, dst):
        copy = pltpu.make_async_copy(src, dst, load_sem.at[next(load_count)])
        copy.start()
        return copy

    stores = []
    store_count = itertools.count()

    def store(src, dst):
        copy = pltpu.make_async_copy(src, dst, store_sem.at[next(store_count)])
        copy.start()
        stores.append(copy)

    w_in = [
        load(
            wqkv.at[:, pl.ds(aligned(part * width + core * 256, 128), 256)],
            w.at[:, part * 256 : part * 256 + 256],
        )
        for part in range(3)
    ]
    wo_in = load(wo_h, wo)
    wu_in = load(wu_h, wu)
    wd_in = load(wd_h, wd)

    enter(plane(me, place, parts))

    def in_copies(a, s, r):
        src = (x, pc, ac)[a].at[s, r * half : (r + 1) * half]
        dst = xs.at[me, r * half : (r + 1) * half] if a == 0 else (pcs, acs)[a - 1].at[me]
        chip = 2 * core + s
        remote = send(src, dst, (insem.at[0, a, 2 * s + r], insem.at[1, a, me]), (chip, place - core + r))
        local = pltpu.make_async_copy(src, dst, self_sem.at[a])
        return remote, local, (chip == me) & (core == r)

    def in_start(a):
        for s in (0, 1):
            for r in (0, 1):
                remote, local, own = in_copies(a, s, r)
                pl.when(own)(local.start)
                pl.when(jnp.logical_not(own))(remote.start)

    def in_sent(a):
        for s in (0, 1):
            for r in (0, 1):
                remote, local, own = in_copies(a, s, r)
                pl.when(jnp.logical_not(own))(remote.wait_send)

    def in_wait(a, k):
        chunk = flip(me, k, parts)
        dst = xs.at[chunk, here] if a == 0 else (pcs, acs)[a - 1].at[chunk]
        src = (x, pc, ac)[a].at[0, :half]
        remote = send(src, dst, (insem.at[0, a, 0], insem.at[1, a, chunk]), (chunk, place))
        if k:
            remote.wait_recv()
        else:
            local = pltpu.make_async_copy(src, dst, self_sem.at[a])
            pl.when(from_core == core)(local.wait)
            pl.when(from_core != core)(remote.wait_recv)

    def across(src, dst, pair):
        return send(src, dst, pair, (me, other))

    def pass_on(k):
        part = xs.at[flip(me, k, parts), here]
        return across(part, part, (fsem.at[0, k], fsem.at[1, k]))

    size_copy = across(sizes.at[0], sizes.at[1], (nsem.at[0], nsem.at[1]))

    def m_copy(p):
        return across(
            mixed.at[p, :, there],
            mix.at[:, :, pl.ds(aligned((2 * core + p) * 128, 128), 128)],
            (msem.at[0, p], msem.at[1, p]),
        )

    def g_copy(p, u):
        chunks = slice(2 * u, 2 * u + 2)
        return across(
            mgrad.at[chunks, :, pl.ds(aligned((2 * (1 - core) + p) * 128, 128), 128)],
            go_o.at[p, chunks, here],
            (gsem.at[0, p, u], gsem.at[1, p, u]),
        )

    def out_copies(a, h):
        src = (post_v, added_v)[a].at[h]
        dst = (post_o, added_o)[a].at[from_group, here]
        remote = send(
            src,
            dst,
            (osem.at[0, a, h], osem.at[1, a, 2 * from_group + core]),
            (h, place - core + from_core),
        )
        local = pltpu.make_async_copy(src, dst, self_sem.at[3 + a])
        return remote, local, (h == me) & (from_core == core)

    def out_start(a, h):
        remote, local, own = out_copies(a, h)
        pl.when(own)(local.start)
        pl.when(jnp.logical_not(own))(remote.start)

    def out_wait(a):
        for h in range(parts):
            remote, local, own = out_copies(a, h)
            pl.when(own)(local.wait)
            pl.when(jnp.logical_not(own))(remote.wait_send)
        for s in (0, 1):
            for r in (0, 1):
                chip = 2 * core + s
                dst = (post_o, added_o)[a].at[s, r * half : (r + 1) * half]
                remote = send(
                    (post_v, added_v)[a].at[0],
                    dst,
                    (osem.at[0, a, 0], osem.at[1, a, 2 * s + r]),
                    (chip, place - core + r),
                )
                pl.when(jnp.logical_not((chip == me) & (core == r)))(remote.wait_recv)

    in_start(0)
    which = lax.broadcasted_iota(jnp.int32, (8, 128), 0)
    sizes[0] = jnp.where(which == 0, lengths[0], lengths[1]).astype(f32)
    size_copy.start()
    for copy in w_in:
        copy.wait()
    size_copy.wait_recv()
    held = jnp.where(from_core == core, sizes[0], sizes[1])
    length = jnp.sum(jnp.where(which == from_group, held, 0.0), axis=0, keepdims=True)
    length_o[...] = jnp.broadcast_to(length, (8, 128))
    length = length[:, :1]

    def below(count, start):
        pos = lax.broadcasted_iota(jnp.int32, (count, 1), 0) + start
        return pos.astype(f32) < length

    for k in range(parts):
        in_wait(0, k)
        pass_on(k).start()
    in_start(1)
    in_start(2)
    for k in range(parts):
        chunk = flip(me, k, parts)
        pass_on(k).wait_recv()
        at = pl.ds(aligned(chunk * rows, rows), rows)
        three = dot(xs[chunk], w[...])
        bias = jnp.where(below(rows, chunk * rows), 0.0, NEG).astype(bf16)
        for p in (0, 1):
            cut = slice(p * 128, p * 128 + 128)
            query = (three[:, :256][:, cut] * (LOG2E * 64 ** (-0.5))).astype(bf16)
            keys = three[:, 256:512][:, cut].astype(bf16)
            values = three[:, 512:][:, cut].astype(bf16)
            qkv[p, 0, at] = query
            qkv[p, 1, at] = keys
            qkv[p, 2, at] = values
            turned = values.T
            for h in range(2):
                ka[2 * p + h, at] = jnp.where(mine[h], keys, jnp.where(lane == base[h], bias, zero))
                qa[2 * p + h, at] = jnp.where(mine[h], query, jnp.where(lane == base[h], one, zero))
                vt[2 * p + h, :64, at] = turned[h * 64 : h * 64 + 64]
                vt[2 * p + h, 64:, at] = jnp.ones((8, rows), bf16)
    store(qkv, qkv_o)
    store(xs, xs_o)

    def attend(p):
        def body(j, carry):
            at = pl.ds(aligned(j * rows, rows), rows)
            out = []
            for h in range(2):
                top, acc = carry[h]
                scores = dot_nt(ka[2 * p + h, at, :], qa[2 * p + h])
                new_top = jnp.maximum(top, jnp.max(scores, axis=0, keepdims=True))
                probs = jnp.exp2(scores - new_top)
                acc = acc * jnp.exp2(top - new_top) + dot(vt[2 * p + h, :, at], probs.astype(bf16))
                out.append((new_top, acc))
            return tuple(out)

        init = tuple((jnp.full((1, full), NEG, f32), jnp.zeros((72, full), f32)) for _ in range(2))
        both = lax.fori_loop(0, parts, body, init)
        lse[p] = jnp.zeros((8, full), f32)
        pieces = []
        for h in range(2):
            top, acc = both[h]
            total = acc[64:65]
            pieces.append(acc[:64] / total)
            lse[p, h : h + 1, :] = top + jnp.log2(total)
        mixed[p] = jnp.concatenate(pieces, 0).T.astype(bf16).reshape(parts, rows, 128)
        m_copy(p).start()
        mix[:, :, pl.ds(aligned((2 * core + p) * 128, 128), 128)] = mixed[p, :, here]

    attend(0)
    attend(1)
    store(mixed, mixed_o)
    store(lse, lse_o)

    tile = 512
    tiles = hidden // tile
    small[...] = jnp.zeros_like(small)

    def feed(u):
        chunks = (2 * u, 2 * u + 1)
        keep = jnp.concatenate([below(half, h * rows + core * half) for h in chunks], 0)
        mix_u = mix[2 * u : 2 * u + 2].reshape(rows, width)
        x_u = jnp.concatenate([xs[h, here] for h in chunks], 0)
        attention = dot(mix_u, wo[...])
        unit1, inv1 = normed(x_u.astype(f32) + attention)
        x_mid = unit1 * g1[...] + b1[...]
        mid[u] = x_mid.astype(bf16)
        total = jnp.zeros((rows, width), f32)
        c0 = 0.7978845608028654
        c1 = 0.044715
        for t in range(tiles):
            cols = slice(t * tile, (t + 1) * tile)
            act = dot(mid[u], wu[:, cols]) + bu[:, cols]
            square = act * act
            th = jnp.tanh(act * (c0 + (c0 * c1) * square))
            part = 0.5 * (1.0 + th)
            low = (act * part).astype(bf16)
            hid[u, :, cols] = low
            slope[:rows, cols] = part + (0.5 * act) * (1.0 - th * th) * (c0 + (3.0 * c0 * c1) * square)
            total = total + dot(low, wd[cols, :])
        total = total + bd[...]
        unit2, inv2 = normed(x_mid + total)
        post = jnp.where(keep, unit2 * g2[...] + b2[...], 0.0).astype(bf16)
        added = jnp.where(keep, attention + total, 0.0).astype(bf16)
        post_v[2 * u : 2 * u + 2] = post.reshape(2, half, width)
        added_v[2 * u : 2 * u + 2] = added.reshape(2, half, width)
        for h in chunks:
            out_start(0, h)
            out_start(1, h)
        post_c = jnp.where(keep, pcs[2 * u : 2 * u + 2].reshape(rows, width).astype(f32), 0.0)
        accum_c = jnp.where(keep, acs[2 * u : 2 * u + 2].reshape(rows, width).astype(f32), 0.0)
        mid_grad2 = norm_back(post_c * g2[...], unit2, inv2)
        small[2:3, :width] += jnp.sum(post_c * unit2, axis=0, keepdims=True)
        small[3:4, :width] += jnp.sum(post_c, axis=0, keepdims=True)
        feed_grad = (mid_grad2 + accum_c).astype(bf16)
        fgrad[u] = feed_grad
        small[4:5, :width] += jnp.sum(feed_grad.astype(f32), axis=0, keepdims=True)
        back[...] = mid_grad2
        for t in range(tiles):
            cols = slice(t * tile, (t + 1) * tile)
            hidden_grad = dot_nt(fgrad[u], wd[cols, :]).astype(bf16)
            pre_grad = (hidden_grad.astype(f32) * slope[:rows, cols]).astype(bf16)
            pre[u, :, cols] = pre_grad
            small[5:6, cols] += jnp.sum(pre_grad.astype(f32), axis=0, keepdims=True)
            back[...] += dot_nt(pre_grad, wu[:, cols])
        mid_grad = back[...]
        small[0:1, :width] += jnp.sum(mid_grad * unit1, axis=0, keepdims=True)
        small[1:2, :width] += jnp.sum(mid_grad, axis=0, keepdims=True)
        first = norm_back(mid_grad * g1[...], unit1, inv1)
        first_v[2 * u : 2 * u + 2] = first.reshape(2, half, width)
        store(first_v.at[2 * u : 2 * u + 2], first_o.at[2 * u : 2 * u + 2])
        attn_grad = (first + accum_c).astype(bf16)
        agrad[u] = attn_grad
        mgrad[2 * u : 2 * u + 2] = dot_nt(attn_grad, wo[...]).astype(bf16).reshape(2, half, width)
        for p in (0, 1):
            g_copy(p, u).start()
            own = mgrad.at[2 * u : 2 * u + 2, :, pl.ds(aligned((2 * core + p) * 128, 128), 128)]
            store(own, go_o.at[p, 2 * u : 2 * u + 2, here])

    wo_in.wait()
    wu_in.wait()
    wd_in.wait()
    for a in (1, 2):
        for k in range(parts):
            in_wait(a, k)
    for p in (0, 1):
        m_copy(p).wait_recv()
    for u in (0, 1):
        feed(u)

    n, up_rows, vector_rows, total_rows = grad_rows(width, hidden, shards)
    halves = (0, 1)

    def spot_of(shard):
        return lax.rem(core + shard % 2, 2), shard // 2

    for t in range(tiles):
        cols = slice(t * tile, (t + 1) * tile)
        slope[:width, cols] = sum(dot_tn(mid[u], pre[u, :, cols]) for u in halves)
    for shard in range(shards):
        own = slice(shard * n, (shard + 1) * n)
        block = jnp.concatenate([slope[own, t * tile : (t + 1) * tile] for t in range(tiles)], 0)
        side, spot = spot_of(shard)
        grads[side, spot, :up_rows] = block.astype(bf16)
    per = tile // up_rows
    for t in range(tiles):
        cols = slice(t * tile, (t + 1) * tile)
        block = sum(dot_tn(hid[u, :, cols], fgrad[u]) for u in halves).astype(bf16)
        for i in range(per):
            side, spot = spot_of(t * per + i)
            grads[side, spot, up_rows : 2 * up_rows] = block[i * up_rows : (i + 1) * up_rows]
    out_all = sum(dot_tn(mix[2 * u : 2 * u + 2].reshape(rows, width), agrad[u]) for u in halves)
    line = lax.broadcasted_iota(jnp.int32, (8, width), 0)
    short = small[:, :width]
    long = small[...]
    for shard in range(shards):
        a = pltpu.roll(short, (width - shard * n) % width, 1)
        b = pltpu.roll(long, (hidden - shard * up_rows) % hidden, 1)[:, :width]
        extra = jnp.where(line == 5, b, a)
        rest = total_rows - 2 * up_rows - n - 8
        block = jnp.concatenate(
            [out_all[shard * n : (shard + 1) * n], extra, jnp.zeros((rest, width), f32)], 0
        )
        side, spot = spot_of(shard)
        grads[side, spot, 2 * up_rows :] = block.astype(bf16)
    store(grads, grads_o)

    for a in range(3):
        in_sent(a)
    for k in range(parts):
        pass_on(k).wait_send()
    size_copy.wait_send()
    for p in (0, 1):
        m_copy(p).wait_send()
        for u in (0, 1):
            g_copy(p, u).wait()
    for a in (0, 1):
        out_wait(a)
    for copy in stores:
        copy.wait()


def first_call(parts, shards, lengths, streams, weights):
    groups, rows, width = streams[0].shape
    hidden = weights[4].shape[1]
    full = rows * parts
    half = rows // 2
    total_rows = grad_rows(width, hidden, shards)[3]
    held = jax.ShapeDtypeStruct((groups, rows, width), bf16)
    return pl.pallas_call(
        functools.partial(first_kernel, parts, shards),
        in_specs=[SMEM] + [ANY] * 5 + [VMEM, VMEM, ANY, VMEM, ANY, VMEM, VMEM, VMEM],
        out_specs=[ANY] * 9 + [VMEM],
        out_shape=[
            held,
            held,
            jax.ShapeDtypeStruct((parts, half, width), f32),
            jax.ShapeDtypeStruct((2, 3, full, 128), bf16),
            jax.ShapeDtypeStruct((2, 8, full), f32),
            jax.ShapeDtypeStruct((2, parts, rows, 128), bf16),
            jax.ShapeDtypeStruct((2, parts, rows, 128), bf16),
            jax.ShapeDtypeStruct((parts, rows, width), bf16),
            jax.ShapeDtypeStruct((2, shards // 2, total_rows, width), bf16),
            jax.ShapeDtypeStruct((8, 128), f32),
        ],
        scratch_shapes=[
            pltpu.VMEM((parts, rows, width), bf16),
            pltpu.VMEM((parts, half, width), bf16),
            pltpu.VMEM((parts, half, width), bf16),
            pltpu.VMEM((width, 768), bf16),
            pltpu.VMEM((2, 3, full, 128), bf16),
            pltpu.VMEM((4, full, 128), bf16),
            pltpu.VMEM((4, full, 128), bf16),
            pltpu.VMEM((4, 72, full), bf16),
            pltpu.VMEM((2, parts, rows, 128), bf16),
            pltpu.VMEM((2, 8, full), f32),
            pltpu.VMEM((width, width), bf16),
            pltpu.VMEM((width, hidden), bf16),
            pltpu.VMEM((hidden, width), bf16),
            pltpu.VMEM((parts, half, width), bf16),
            pltpu.VMEM((2, rows, hidden), bf16),
            pltpu.VMEM((2, rows, hidden), bf16),
            pltpu.VMEM((max(rows, width), hidden), f32),
            pltpu.VMEM((rows, width), f32),
            pltpu.VMEM((2, rows, width), bf16),
            pltpu.VMEM((2, rows, width), bf16),
            pltpu.VMEM((2, rows, width), bf16),
            pltpu.VMEM((parts, half, width), bf16),
            pltpu.VMEM((parts, half, width), bf16),
            pltpu.VMEM((parts, half, width), bf16),
            pltpu.VMEM((parts, half, width), f32),
            pltpu.VMEM((8, hidden), f32),
            pltpu.VMEM((2, shards // 2, total_rows, width), bf16),
            pltpu.VMEM((2, 8, 128), f32),
            DMA((8,)),
            DMA((16,)),
            DMA((5,)),
            DMA((2, 3, 4)),
            DMA((2, parts)),
            DMA((2, 2)),
            DMA((2, 2, 2)),
            DMA((2, 2, 4)),
            DMA((2,)),
        ],
        compiler_params=pltpu.CompilerParams(
            vmem_limit_bytes=VMEM_LIMIT, collective_id=0, has_side_effects=True
        ),
        name="forward_and_feed",
    )(lengths, *streams, *weights)


def second_kernel(
    parts,
    shards,
    grad_norm,
    length_v,
    qkv_h,
    lse_h,
    mixed_h,
    go_h,
    xs_h,
    grads_h,
    first_h,
    wqkv_h,
    dx_o,
    wqkv_o,
    up_o,
    down_o,
    out_o,
    vec_o,
    xs,
    qkv,
    lse,
    mixed,
    go,
    wqkv,
    first,
    grads,
    core_in,
    a1_in,
    b1_in,
    a2_in,
    b2_in,
    z_in,
    all_out,
    all_in,
    final,
    ka,
    va,
    qa,
    da,
    kt,
    dqt,
    dsend,
    dfull,
    dx_v,
    late,
    late_out,
    late_in,
    late_sum,
    late_step,
    late_got,
    late_all,
    load_sem,
    store_sem,
    self_sem,
    dsem,
    rsem,
    lsem,
    osem,
):
    parts, rows, width = xs.shape
    half_rows = rows // 2
    full = rows * parts
    hidden = up_o.shape[1]
    me = lax.axis_index("head")
    place = lax.axis_index("seq")
    core = lax.rem(place, 2)
    other = place + 1 - 2 * core
    from_core = lax.div(me, 2)
    from_group = lax.rem(me, 2)
    here = pl.ds(aligned(core * half_rows, half_rows), half_rows)
    there = pl.ds(aligned((1 - core) * half_rows, half_rows), half_rows)
    length = length_v[0:1, 0:1]
    lane, mine, base = lane_sets()
    one = jnp.ones((), bf16)
    zero = jnp.zeros((), bf16)
    n, up_rows, vector_rows, total_rows = grad_rows(width, hidden, shards)
    seq_bits = bits_of(shards)
    load_count = itertools.count()

    def load(src, dst):
        copy = pltpu.make_async_copy(src, dst, load_sem.at[next(load_count)])
        copy.start()
        return copy

    stores = []
    store_count = itertools.count()

    def store(src, dst):
        copy = pltpu.make_async_copy(src, dst, store_sem.at[next(store_count)])
        copy.start()
        stores.append(copy)

    def pair_load(p):
        return [
            load(qkv_h.at[p], qkv.at[p]),
            load(go_h.at[p], go.at[p]),
            load(mixed_h.at[p], mixed.at[p]),
            load(lse_h.at[p], lse.at[p]),
        ]

    pair_in = [pair_load(0)]
    grads_in = load(grads_h.at[0], grads)
    xs_in = load(xs_h, xs)
    pair_in.append(pair_load(1))
    wqkv_in = load(wqkv_h, wqkv)
    first_in = load(first_h, first)

    enter(plane(me, place, parts) + [(me, flip(place, bit, shards)) for bit in seq_bits[1:]])

    sends = []

    def launch(make, *which):
        make(*which).start()
        sends.append(functools.partial(make, *which))

    spots = shards // 2
    half, quarter = total_rows // 2, total_rows // 4
    eighth = total_rows // 8
    x_bit = lax.rem(me, 2)
    y_bit = lax.div(me, 2)

    def to_head(src, dst, i, k):
        return send(src, dst, (rsem.at[0, i], rsem.at[1, i]), (flip(me, k, parts), place))

    def to_seq(src, dst, i, bit):
        return send(src, dst, (rsem.at[0, i], rsem.at[1, i]), (me, flip(place, bit, shards)))

    core_copy = lambda: to_seq(grads_h.at[1], core_in, 0, 1)
    a_keep = x_bit * quarter
    a_give = (1 - x_bit) * quarter
    b_keep = half + y_bit * quarter
    b_give = half + (1 - y_bit) * quarter
    a1_copy = lambda: to_head(grads.at[:, pl.ds(aligned(a_give, 16), quarter)], a1_in, 1, 1)
    b1_copy = lambda: to_head(grads.at[:, pl.ds(aligned(b_give, 16), quarter)], b1_in, 2, 2)
    a_own = a_keep + y_bit * eighth
    a_pass = a_keep + (1 - y_bit) * eighth
    b_own = b_keep + x_bit * eighth
    b_pass = b_keep + (1 - x_bit) * eighth
    a2_copy = lambda: to_head(grads.at[:, pl.ds(aligned(a_pass, 16), eighth)], a2_in, 3, 2)
    b2_copy = lambda: to_head(grads.at[:, pl.ds(aligned(b_pass, 16), eighth)], b2_in, 4, 1)

    def add_rows(into, spot, start, count, other):
        at = pl.ds(aligned(start, 16), count)
        into[spot, at] = (into[spot, at].astype(f32) + other.astype(f32)).astype(bf16)

    def early_core():
        grads_in.wait()
        core_copy().wait_recv()

        def body(i, carry):
            grads[i] = (grads[i].astype(f32) + core_in[i].astype(f32)).astype(bf16)
            return carry

        lax.fori_loop(0, spots, body, None)
        launch(a1_copy)
        launch(b1_copy)

    def early_first():
        a1_copy().wait_recv()
        b1_copy().wait_recv()

        def body(i, carry):
            add_rows(grads, i, a_keep, quarter, a1_in[i])
            add_rows(grads, i, b_keep, quarter, b1_in[i])
            return carry

        lax.fori_loop(0, spots, body, None)
        launch(a2_copy)
        launch(b2_copy)

    def early_second_and_on():
        a2_copy().wait_recv()
        b2_copy().wait_recv()

        def body(i, carry):
            add_rows(grads, i, a_own, eighth, a2_in[i])
            add_rows(grads, i, b_own, eighth, b2_in[i])
            return carry

        lax.fori_loop(0, spots, body, None)

        def gather(i, carry):
            all_out[i, :eighth] = grads[i, pl.ds(aligned(a_own, 16), eighth)]
            all_out[i, eighth:] = grads[i, pl.ds(aligned(b_own, 16), eighth)]
            return carry

        lax.fori_loop(0, spots, gather, None)
        if steps:
            z_send(0)

    offsets = []
    at = 0
    size = spots
    for bit in seq_bits[1:]:
        offsets.append((at, size))
        at += size
        size //= 2
    offsets.append((at, 1))
    steps = len(offsets) - 1
    z_offsets = []
    at = 0
    for _, size in offsets[:-1]:
        z_offsets.append(at)
        at += size // 2

    def z_copy(i):
        at, size = offsets[i]
        bit = seq_bits[1 + i]
        return to_seq(
            all_in.at[pl.ds(z_offsets[i], size // 2)], z_in.at[pl.ds(z_offsets[i], size // 2)], 5 + i, bit
        )

    def z_send(i):
        at, size = offsets[i]
        own = lax.rem(lax.div(place, seq_bits[1 + i]), 2)
        for j in range(size // 2):
            all_in[z_offsets[i] + j] = all_out[at + 2 * j + (1 - own)]
        launch(z_copy, i)

    def z_add(i):
        at, size = offsets[i]
        after = offsets[i + 1][0]
        own = lax.rem(lax.div(place, seq_bits[1 + i]), 2)
        z_copy(i).wait_recv()
        for j in range(size // 2):
            all_out[after + j] = (
                all_out[at + 2 * j + own].astype(f32) + z_in[z_offsets[i] + j].astype(f32)
            ).astype(bf16)

    ag_from = 5 + steps
    last = offsets[-1][0]
    ag = sum(size // 2 for _, size in offsets[:-1])

    def ag_copy(k):
        return to_head(all_out.at[last], all_in.at[ag + k], ag_from + k, k)

    def ag_send():
        for k in range(parts - 1, 0, -1):
            launch(ag_copy, k)

    def ag_finish():
        for k in range(parts):
            if k:
                ag_copy(k).wait_recv()
                block = all_in[ag + k]
            else:
                block = all_out[last]
            block = block.astype(f32) * grad_norm
            who = flip(me, k, parts)
            x_of, y_of = lax.rem(who, 2), lax.div(who, 2)
            a_at = x_of * quarter + y_of * eighth
            b_at = half + y_of * quarter + x_of * eighth
            final[pl.ds(aligned(a_at, 16), eighth)] = block[:eighth]
            final[pl.ds(aligned(b_at, 16), eighth)] = block[eighth:]
        for t in range(hidden // width):
            store(final.at[pl.ds(t * n, n)], up_o.at[:, pl.ds(t * width, width)])
        store(final.at[pl.ds(up_rows, up_rows)], down_o)
        store(final.at[pl.ds(2 * up_rows, n)], out_o)
        vec_o[...] = final[2 * up_rows + n : 2 * up_rows + n + 8]

    def d_copy(p, part):
        return send(
            dsend.at[p, part, :, there],
            dfull.at[:, :, pl.ds(aligned(part * width + (2 * core + p) * 128, 128), 128)],
            (dsem.at[0, p, part], dsem.at[1, p, part]),
            (me, other),
        )

    def prepare(p):
        for copy in pair_in[p]:
            copy.wait()
        turned = -lse[p].T
        kt[...] = qkv[p, 1].T
        for k in range(parts):
            at = slice(k * rows, (k + 1) * rows)
            query, keys, values = qkv[p, 0, at], qkv[p, 1, at], qkv[p, 2, at]
            pos = lax.broadcasted_iota(jnp.int32, (rows, 1), 0) + k * rows
            bias = jnp.where(pos.astype(f32) < length, 0.0, NEG).astype(bf16)
            grad = go[p, k]
            prod = grad.astype(f32) * mixed[p, k].astype(f32)
            for h in range(2):
                ka[h, at] = jnp.where(mine[h], keys, jnp.where(lane == base[h], bias, one))
                va[h, at] = jnp.where(mine[h], values, one)
                a, b, c = split3(-jnp.sum(jnp.where(mine[h], prod, 0.0), axis=1, keepdims=True))
                extra = jnp.where(
                    lane == base[h],
                    a,
                    jnp.where(lane == base[h] + 1, b, jnp.where(lane == base[h] + 2, c, zero)),
                )
                da[h, at] = jnp.where(mine[h], grad, extra)
                a, b, c = split3(turned[at, h : h + 1])
                extra = jnp.where(
                    lane == base[h],
                    one,
                    jnp.where(
                        lane == base[h] + 1,
                        a,
                        jnp.where(lane == base[h] + 2, b, jnp.where(lane == base[h] + 3, c, zero)),
                    ),
                )
                qa[h, at] = jnp.where(mine[h], query, extra)
        dqt[...] = jnp.zeros_like(dqt)

    block = rows // 2
    steps_each = 2 * parts

    def attend_back(p, events):
        def body(i, carry):
            for when, event in events.items():
                pl.when(i == when)(event)
            at = pl.ds(aligned(i * block, block), block)
            out = []
            for h in range(2):
                probs = jnp.exp2(dot_nt(ka[h, at, :], qa[h]))
                inner = dot_nt(va[h, at, :], da[h])
                low = probs.astype(bf16)
                grad = (probs * inner).astype(bf16)
                dv = dot(low, go[p].reshape(full, 128))
                dk = dot(grad, qkv[p, 0])
                part = slice(h * 64, h * 64 + 64)
                dqt[part, :] += dot(kt[part, at], grad)
                out.append((dv, dk))
            chunk = lax.div(i, 2)
            at = pl.ds(aligned(lax.rem(i, 2) * block, block), block)
            dsend[p, 1, chunk, at] = (jnp.where(mine[0], out[0][1], out[1][1]) * (1.0 / LOG2E)).astype(bf16)
            dsend[p, 2, chunk, at] = jnp.where(mine[0], out[0][0], out[1][0]).astype(bf16)
            return carry

        lax.fori_loop(0, steps_each, body, None)
        dsend[p, 0] = (dqt[...] * 64 ** (-0.5)).T.astype(bf16).reshape(parts, rows, 128)
        for part in range(3):
            d_copy(p, part).start()
            dfull[:, :, pl.ds(aligned(part * width + (2 * core + p) * 128, 128), 128)] = dsend[p, part, :, here]

    def late_term(p):
        for part in range(3):
            late[p, :, part * 128 : part * 128 + 128] = sum(
                dot_tn(xs[k], dsend[p, part, k]) for k in range(parts)
            )

    l_sizes = [spots] + [spots >> i for i in range(len(seq_bits) - 1)]
    l_offsets = [0] + [sum(size // 2 for size in l_sizes[1:i]) for i in range(1, len(seq_bits))]

    def l_core(p):
        return send(late_out.at[p], late_in.at[p], (lsem.at[0, p, 0], lsem.at[1, p, 0]), (me, other))

    def l_copy(p, i):
        size = l_sizes[i] // 2
        at = l_offsets[i]
        return send(
            late_step.at[p, pl.ds(at, size)],
            late_got.at[p, pl.ds(at, size)],
            (lsem.at[0, p, i], lsem.at[1, p, i]),
            (me, flip(place, seq_bits[i], shards)),
        )

    l_steps = len(seq_bits)

    def lg_copy(p, k):
        return send(
            late_all.at[p, 0],
            late_all.at[p, k],
            (lsem.at[0, p, l_steps + k], lsem.at[1, p, l_steps + k]),
            (flip(me, k, parts), place),
        )

    def late_start(p):
        for z in range(spots):
            late_out[p, z] = late[p, pl.ds(aligned((2 * z + 1 - core) * n, 8), n)].astype(bf16)
        launch(l_core, p)

    def late_split(p, i):
        own = lax.rem(lax.div(place, seq_bits[i]), 2)
        size = l_sizes[i] // 2
        for j in range(size):
            late_step[p, l_offsets[i] + j] = late_sum[p, 2 * j + 1 - own].astype(bf16)
        launch(l_copy, p, i)

    def late_merge(p, i):
        own = lax.rem(lax.div(place, seq_bits[i]), 2)
        l_copy(p, i).wait_recv()
        for j in range(l_sizes[i] // 2):
            late_sum[p, j] = late_sum[p, 2 * j + own] + late_got[p, l_offsets[i] + j].astype(f32)

    def late_cores(p):
        l_core(p).wait_recv()
        for z in range(spots):
            own = late[p, pl.ds(aligned((2 * z + core) * n, 8), n)]
            late_sum[p, z, :, pl.ds(aligned(core * 384, 128), 384)] = own
            late_sum[p, z, :, pl.ds(aligned((1 - core) * 384, 128), 384)] = late_in[p, z].astype(f32)

    def late_share(p):
        late_all[p, 0] = late_sum[p, 0].astype(bf16)
        for k in range(parts - 1, 0, -1):
            launch(lg_copy, p, k)

    def late_finish(p):
        for k in range(1, parts):
            lg_copy(p, k).wait_recv()
        total = sum(late_all[p, k].astype(f32) for k in range(parts)) * grad_norm
        for owner in range(2):
            for part in range(3):
                to = part * width + (2 * owner + p) * 128
                at = owner * 384 + part * 128
                wqkv_o[:, to : to + 128] = total[:, at : at + 128]

    def late_events(p):
        steps_of = []

        def first_step():
            late_cores(p)
            if l_steps > 1:
                late_split(p, 1)
            else:
                late_share(p)

        steps_of.append(first_step)
        for i in range(1, l_steps):

            def step(i=i):
                late_merge(p, i)
                if i + 1 < l_steps:
                    late_split(p, i + 1)
                else:
                    late_share(p)

            steps_of.append(step)
        return steps_of

    def both_events(one_event, two_event):
        def run():
            one_event()
            two_event()

        return run

    def out_copies(h):
        dst = dx_o.at[from_group, here]
        remote = send(
            dx_v.at[h],
            dst,
            (osem.at[0, h], osem.at[1, 2 * from_group + core]),
            (h, place - core + from_core),
        )
        local = pltpu.make_async_copy(dx_v.at[h], dst, self_sem.at[0])
        return remote, local, (h == me) & (from_core == core)

    def out_start(h):
        remote, local, own = out_copies(h)
        pl.when(own)(local.start)
        pl.when(jnp.logical_not(own))(remote.start)

    def out_wait():
        for h in range(parts):
            remote, local, own = out_copies(h)
            pl.when(own)(local.wait)
            pl.when(jnp.logical_not(own))(remote.wait_send)
        for s in (0, 1):
            for r in (0, 1):
                chip = 2 * core + s
                dst = dx_o.at[s, r * half_rows : (r + 1) * half_rows]
                remote = send(dx_v.at[0], dst, (osem.at[0, 0], osem.at[1, 2 * s + r]), (chip, place - core + r))
                pl.when(jnp.logical_not((chip == me) & (core == r)))(remote.wait_recv)

    launch(core_copy)
    prepare(0)
    attend_back(0, {1: early_core, 5: early_first})
    xs_in.wait()
    late_term(0)
    late_start(0)
    prepare(1)
    early_steps = [early_second_and_on]
    for i in range(1, steps):

        def early_step(i=i):
            z_add(i - 1)
            z_send(i)

        early_steps.append(early_step)

    def early_last():
        if steps:
            z_add(steps - 1)
        ag_send()

    early_steps.append(early_last)
    events = {}
    later = []

    def schedule(steps_list, slots):
        for index, event in enumerate(steps_list):
            slot = slots[index] if index < len(slots) else steps_each
            if slot >= steps_each:
                later.append(event)
            elif slot in events:
                events[slot] = both_events(events[slot], event)
            else:
                events[slot] = event

    schedule(early_steps, (0, 3, 6))
    schedule(late_events(0), (1, 4, 7))
    attend_back(1, events)
    for event in later:
        event()
    late_term(1)
    late_start(1)
    tail = late_events(1)
    wqkv_in.wait()
    first_in.wait()
    for p in range(2):
        for part in range(3):
            d_copy(p, part).wait_recv()
    tail.pop(0)()
    for h in range(parts):
        dx_v[h] = (first[h] + dot_nt(dfull[h], wqkv[...])).astype(bf16)
        out_start(h)
    for event in tail:
        event()
    ag_finish()
    late_finish(0)
    late_finish(1)
    for make in sends:
        make().wait_send()
    for p in range(2):
        for part in range(3):
            d_copy(p, part).wait_send()
    out_wait()
    for copy in stores:
        copy.wait()


def second_call(parts, shards, grad_norm, length, saved, grads, first, wqkv, hidden):
    xs_shape = saved[4].shape
    _, rows, width = xs_shape
    full = rows * parts
    half_rows = rows // 2
    n, up_rows, vector_rows, total_rows = grad_rows(width, hidden, shards)
    spots = shards // 2
    quarter, eighth = total_rows // 4, total_rows // 8
    heads = (2, full, 128)
    return pl.pallas_call(
        functools.partial(second_kernel, parts, shards, grad_norm),
        in_specs=[VMEM] + [ANY] * 8,
        out_specs=[ANY, VMEM, ANY, ANY, ANY, VMEM],
        out_shape=[
            jax.ShapeDtypeStruct((2, rows, width), bf16),
            jax.ShapeDtypeStruct((n, 3 * width), f32),
            jax.ShapeDtypeStruct((n, hidden), f32),
            jax.ShapeDtypeStruct((up_rows, width), f32),
            jax.ShapeDtypeStruct((n, width), f32),
            jax.ShapeDtypeStruct((8, width), f32),
        ],
        scratch_shapes=[
            pltpu.VMEM(xs_shape, bf16),
            pltpu.VMEM((2, 3, full, 128), bf16),
            pltpu.VMEM((2, 8, full), f32),
            pltpu.VMEM((2, parts, rows, 128), bf16),
            pltpu.VMEM((2, parts, rows, 128), bf16),
            pltpu.VMEM((width, 3 * width), bf16),
            pltpu.VMEM((parts, half_rows, width), f32),
            pltpu.VMEM((spots, total_rows, width), bf16),
            pltpu.VMEM((spots, total_rows, width), bf16),
            pltpu.VMEM((spots, quarter, width), bf16),
            pltpu.VMEM((spots, quarter, width), bf16),
            pltpu.VMEM((spots, eighth, width), bf16),
            pltpu.VMEM((spots, eighth, width), bf16),
            pltpu.VMEM((spots, quarter, width), bf16),
            pltpu.VMEM((2 * spots, quarter, width), bf16),
            pltpu.VMEM((spots + parts, quarter, width), bf16),
            pltpu.VMEM((total_rows, width), f32),
            pltpu.VMEM(heads, bf16),
            pltpu.VMEM(heads, bf16),
            pltpu.VMEM(heads, bf16),
            pltpu.VMEM(heads, bf16),
            pltpu.VMEM((128, full), bf16),
            pltpu.VMEM((128, full), f32),
            pltpu.VMEM((2, 3, parts, rows, 128), bf16),
            pltpu.VMEM((parts, half_rows, 3 * width), bf16),
            pltpu.VMEM((parts, half_rows, width), bf16),
            pltpu.VMEM((2, width, 384), f32),
            pltpu.VMEM((2, spots, n, 384), bf16),
            pltpu.VMEM((2, spots, n, 384), bf16),
            pltpu.VMEM((2, spots, n, 768), f32),
            pltpu.VMEM((2, spots, n, 768), bf16),
            pltpu.VMEM((2, spots, n, 768), bf16),
            pltpu.VMEM((2, parts, n, 768), bf16),
            DMA((16,)),
            DMA((16,)),
            DMA((1,)),
            DMA((2, 2, 3)),
            DMA((2, 24)),
            DMA((2, 2, 16)),
            DMA((2, 4)),
        ],
        compiler_params=pltpu.CompilerParams(
            vmem_limit_bytes=VMEM_LIMIT, collective_id=1, has_side_effects=True
        ),
        name="backward_and_sums",
    )(length, *saved, grads, first, wqkv)


def last_kernel(rows_here, lengths, post_h, added_h, dx_h, y, ac, vec, *rest):
    ins, (post_o, accum_o, dx_o, accg_o), outs, vectors, (sem,) = (
        rest[:4],
        rest[4:8],
        rest[8:12],
        rest[12:18],
        rest[18:],
    )
    step = pl.program_id(0)
    copies = [pltpu.make_async_copy(src, dst, sem.at[i]) for i, (src, dst) in enumerate(zip(ins, outs))]

    @pl.when(step == 0)
    def _():
        for copy in copies:
            copy.start()
        for i, out in enumerate(vectors):
            out[...] = vec[i : i + 1, : out.shape[1]]

    _, rows, _ = y.shape
    steps = pl.num_programs(0)
    length = lengths[lax.div(step * 2, steps)]
    start = lax.axis_index("head") * rows_here + lax.rem(step, lax.div(steps, 2)) * rows
    keep = lax.broadcasted_iota(jnp.int32, (1, rows, 1), 1) + start < length
    post_o[...] = post_h[...].astype(f32)
    accum_o[...] = jnp.where(keep, y[...].astype(f32) + added_h[...].astype(f32), 0.0)
    dx_o[...] = dx_h[...].astype(f32)
    accg_o[...] = jnp.where(keep, ac[...].astype(f32), 0.0)

    @pl.when(step == steps - 1)
    def _():
        for copy in copies:
            copy.wait()


def last_call(lengths, tokens, streams, vectors, grads, shards):
    groups, rows, width = tokens[0].shape
    cut = 2
    block = pl.BlockSpec((1, rows // cut, width), lambda i: (i // cut, i % cut, 0))
    whole = jax.ShapeDtypeStruct((groups, rows, width), f32)
    n = width // shards
    hidden = grads[1].shape[1]
    short = [jax.ShapeDtypeStruct((1, n), f32)] * 5 + [jax.ShapeDtypeStruct((1, hidden // shards), f32)]
    return pl.pallas_call(
        functools.partial(last_kernel, rows),
        grid=(groups * cut,),
        in_specs=[SMEM] + [block] * 5 + [pl.BlockSpec(vectors.shape, lambda i: (0, 0))] + [ANY] * len(grads),
        out_specs=[block] * 4 + [ANY] * len(grads) + [pl.BlockSpec(o.shape, lambda i: (0, 0)) for o in short],
        out_shape=[whole] * 4 + [jax.ShapeDtypeStruct(g.shape, f32) for g in grads] + short,
        scratch_shapes=[DMA((len(grads),))],
        compiler_params=pltpu.CompilerParams(vmem_limit_bytes=VMEM_LIMIT),
        name="outputs",
    )(lengths, *tokens, *streams, vectors, *grads)


def local(
    post_stream,
    accum_stream,
    seq_lengths,
    qkv_weight,
    out_weight,
    norm1_gain,
    norm1_bias,
    up_weight,
    up_bias,
    down_weight,
    down_bias,
    norm2_gain,
    norm2_bias,
    post_cotan,
    accum_cotan,
):
    groups, rows, width = post_stream.shape
    parts = lax.axis_size("head")
    shards = lax.axis_size("seq")
    hidden = up_weight.shape[1]
    grad_norm = float(groups * shards * rows * parts) ** (-0.5)

    def row(vector):
        return vector.reshape(1, -1)

    weights = (
        qkv_weight,
        out_weight,
        row(norm1_gain),
        row(norm1_bias),
        up_weight,
        row(up_bias),
        down_weight,
        row(down_bias),
        row(norm2_gain),
        row(norm2_bias),
    )
    post, added, first, qkv, lse, mixed, go, xs, grads, length = first_call(
        parts, shards, seq_lengths, (post_stream, post_cotan, accum_cotan), weights
    )
    dx, qkv_grad, up_grad, down_grad, out_grad, vectors = second_call(
        parts, shards, grad_norm, length, (qkv, lse, mixed, go, xs), grads, first, qkv_weight, hidden
    )
    post, accum, post_grad, accum_grad, qkv_grad, up_grad, down_grad, out_grad, *short = last_call(
        seq_lengths,
        (post, added, dx),
        (accum_stream, accum_cotan),
        vectors,
        (qkv_grad, up_grad, down_grad, out_grad),
        shards,
    )
    gain1, bias1, gain2, bias2, down_bias_grad, up_bias_grad = [v.reshape(-1) for v in short]
    return (
        post,
        accum,
        post_grad,
        accum_grad,
        qkv_grad,
        out_grad,
        gain1,
        bias1,
        up_grad,
        up_bias_grad,
        down_grad,
        down_bias_grad,
        gain2,
        bias2,
    )


def solution(mesh):
    tokens = P("seq", "head", None)
    in_specs = (tokens, tokens, P("seq")) + (P(),) * 10 + (tokens, tokens)
    rows = P("seq", None)
    vector = P("seq")
    out_specs = (tokens,) * 4 + (rows, rows, vector, vector, rows, vector, rows, vector, vector, vector)
    return jax.shard_map(local, mesh=mesh, in_specs=in_specs, out_specs=out_specs, check_vma=False)
```

```python
import functools
import itertools

import jax
import jax.numpy as jnp
from jax import lax
from jax.experimental import pallas as pl
from jax.experimental.pallas import tpu as pltpu
from jax.sharding import PartitionSpec as P

H = 8
EPS = 1e-05
NEG = -1e30
LOG2E = 1.4426950408889634
VMEM_LIMIT = 62 * 2**20
bf16 = jnp.bfloat16
f32 = jnp.float32
SMEM = pl.BlockSpec(memory_space=pltpu.SMEM)
VMEM = pl.BlockSpec(memory_space=pltpu.VMEM)
ANY = pl.BlockSpec(memory_space=pl.ANY)
DMA = pltpu.SemaphoreType.DMA


def dot(a, b):
    return jnp.dot(a, b, preferred_element_type=f32)


def dot_nt(a, b):
    return lax.dot_general(a, b, (((1,), (1,)), ((), ())), preferred_element_type=f32)


def dot_tn(a, b):
    return lax.dot_general(a, b, (((0,), (0,)), ((), ())), preferred_element_type=f32)


def split3(value):
    first = value.astype(bf16)
    rest = value - first.astype(f32)
    second = rest.astype(bf16)
    third = (rest - second.astype(f32)).astype(bf16)
    return first, second, third


def lane_sets():
    lane = lax.broadcasted_iota(jnp.int32, (1, 128), 1)
    return lane, (lane < 64, lane >= 64), (64, 0)


def bits_of(count):
    return [1 << b for b in range(count.bit_length() - 1)]


def flip(index, k, count):
    out = 0
    for bit in bits_of(count):
        out = out + (lax.rem(lax.div(index, bit) + (k // bit), 2)) * bit
    return out


def aligned(start, step):
    if isinstance(start, int):
        return start
    return pl.multiple_of(start, step)


def send(src, dst, pair, to):
    return pltpu.make_async_remote_copy(
        src_ref=src,
        dst_ref=dst,
        send_sem=pair[0],
        recv_sem=pair[1],
        device_id=to,
        device_id_type=pl.DeviceIdType.MESH,
    )


def enter(partners):
    barrier = pltpu.get_barrier_semaphore()
    for to in partners:
        pl.semaphore_signal(barrier, inc=1, device_id=to, device_id_type=pl.DeviceIdType.MESH)
    pl.semaphore_wait(barrier, len(partners))


def plane(me, place, parts):
    core = lax.rem(place, 2)
    others = []
    for k in range(parts):
        for other in range(2):
            if k or other:
                seat = place if not other else place + 1 - 2 * core
                others.append((flip(me, k, parts), seat))
    return others


def grad_rows(width, hidden, shards):
    n = width // shards
    up = n * (hidden // width)
    vectors = 16 - n % 16
    total = 2 * up + n + vectors
    return n, up, vectors, -(-total // 128) * 128


def normed(value):
    centre = value - jnp.mean(value, axis=-1, keepdims=True)
    spread = jnp.mean(centre * centre, axis=-1, keepdims=True)
    inv = lax.rsqrt(spread + EPS)
    return centre * inv, inv


def norm_back(cot, unit, inv):
    return (
        cot - jnp.mean(cot, axis=-1, keepdims=True) - unit * jnp.mean(cot * unit, axis=-1, keepdims=True)
    ) * inv


def first_kernel(
    parts,
    shards,
    lengths,
    x,
    pc,
    ac,
    wqkv,
    wo_h,
    g1,
    b1,
    wu_h,
    bu,
    wd_h,
    bd,
    g2,
    b2,
    post_o,
    added_o,
    first_o,
    qkv_o,
    lse_o,
    mixed_o,
    go_o,
    xs_o,
    grads_o,
    length_o,
    xs,
    pcs,
    acs,
    w,
    qkv,
    ka,
    qa,
    vt,
    mixed,
    lse,
    wo,
    wu,
    wd,
    mix,
    hid,
    pre,
    slope,
    back,
    fgrad,
    mid,
    agrad,
    mgrad,
    post_v,
    added_v,
    first_v,
    small,
    grads,
    sizes,
    load_sem,
    store_sem,
    self_sem,
    insem,
    fsem,
    msem,
    gsem,
    osem,
    nsem,
):
    groups, rows, width = x.shape
    hidden = wu.shape[1]
    full = rows * parts
    half = rows // 2
    me = lax.axis_index("head")
    place = lax.axis_index("seq")
    core = lax.rem(place, 2)
    other = place + 1 - 2 * core
    from_core = lax.div(me, 2)
    from_group = lax.rem(me, 2)
    lane, mine, base = lane_sets()
    one = jnp.ones((), bf16)
    zero = jnp.zeros((), bf16)
    here = pl.ds(aligned(core * half, half), half)
    there = pl.ds(aligned((1 - core) * half, half), half)

    load_count = itertools.count()

    def load(src, dst):
        copy = pltpu.make_async_copy(src, dst, load_sem.at[next(load_count)])
        copy.start()
        return copy

    stores = []
    store_count = itertools.count()

    def store(src, dst):
        copy = pltpu.make_async_copy(src, dst, store_sem.at[next(store_count)])
        copy.start()
        stores.append(copy)

    w_in = [
        load(
            wqkv.at[:, pl.ds(aligned(part * width + core * 256, 128), 256)],
            w.at[:, part * 256 : part * 256 + 256],
        )
        for part in range(3)
    ]
    wo_in = load(wo_h, wo)
    wu_in = load(wu_h, wu)
    wd_in = load(wd_h, wd)

    enter(plane(me, place, parts))

    def in_copies(a, s, r):
        src = (x, pc, ac)[a].at[s, r * half : (r + 1) * half]
        dst = xs.at[me, r * half : (r + 1) * half] if a == 0 else (pcs, acs)[a - 1].at[me]
        chip = 2 * core + s
        remote = send(src, dst, (insem.at[0, a, 2 * s + r], insem.at[1, a, me]), (chip, place - core + r))
        local = pltpu.make_async_copy(src, dst, self_sem.at[a])
        return remote, local, (chip == me) & (core == r)

    def in_start(a):
        for s in (0, 1):
            for r in (0, 1):
                remote, local, own = in_copies(a, s, r)
                pl.when(own)(local.start)
                pl.when(jnp.logical_not(own))(remote.start)

    def in_sent(a):
        for s in (0, 1):
            for r in (0, 1):
                remote, local, own = in_copies(a, s, r)
                pl.when(jnp.logical_not(own))(remote.wait_send)

    def in_wait(a, k):
        chunk = flip(me, k, parts)
        dst = xs.at[chunk, here] if a == 0 else (pcs, acs)[a - 1].at[chunk]
        src = (x, pc, ac)[a].at[0, :half]
        remote = send(src, dst, (insem.at[0, a, 0], insem.at[1, a, chunk]), (chunk, place))
        if k:
            remote.wait_recv()
        else:
            local = pltpu.make_async_copy(src, dst, self_sem.at[a])
            pl.when(from_core == core)(local.wait)
            pl.when(from_core != core)(remote.wait_recv)

    def across(src, dst, pair):
        return send(src, dst, pair, (me, other))

    def pass_on(k):
        part = xs.at[flip(me, k, parts), here]
        return across(part, part, (fsem.at[0, k], fsem.at[1, k]))

    size_copy = across(sizes.at[0], sizes.at[1], (nsem.at[0], nsem.at[1]))

    def m_copy(p):
        return across(
            mixed.at[p, :, there],
            mix.at[:, :, pl.ds(aligned((2 * core + p) * 128, 128), 128)],
            (msem.at[0, p], msem.at[1, p]),
        )

    def g_copy(p, u):
        chunks = slice(2 * u, 2 * u + 2)
        return across(
            mgrad.at[chunks, :, pl.ds(aligned((2 * (1 - core) + p) * 128, 128), 128)],
            go_o.at[p, chunks, here],
            (gsem.at[0, p, u], gsem.at[1, p, u]),
        )

    def out_copies(h):
        dst = post_o.at[from_group, here]
        remote = send(
            post_v.at[h],
            dst,
            (osem.at[0, h], osem.at[1, 2 * from_group + core]),
            (h, place - core + from_core),
        )
        local = pltpu.make_async_copy(post_v.at[h], dst, self_sem.at[3])
        return remote, local, (h == me) & (from_core == core)

    def out_start(h):
        remote, local, own = out_copies(h)
        pl.when(own)(local.start)
        pl.when(jnp.logical_not(own))(remote.start)

    def out_wait():
        for h in range(parts):
            remote, local, own = out_copies(h)
            pl.when(own)(local.wait)
            pl.when(jnp.logical_not(own))(remote.wait_send)
        for s in (0, 1):
            for r in (0, 1):
                chip = 2 * core + s
                dst = post_o.at[s, r * half : (r + 1) * half]
                remote = send(
                    post_v.at[0], dst, (osem.at[0, 0], osem.at[1, 2 * s + r]), (chip, place - core + r)
                )
                pl.when(jnp.logical_not((chip == me) & (core == r)))(remote.wait_recv)

    in_start(0)
    which = lax.broadcasted_iota(jnp.int32, (8, 128), 0)
    sizes[0] = jnp.where(which == 0, lengths[0], lengths[1]).astype(f32)
    size_copy.start()
    for copy in w_in:
        copy.wait()
    size_copy.wait_recv()
    held = jnp.where(from_core == core, sizes[0], sizes[1])
    length = jnp.sum(jnp.where(which == from_group, held, 0.0), axis=0, keepdims=True)
    length_o[...] = jnp.broadcast_to(length, (8, 128))
    length = length[:, :1]

    def below(count, start):
        pos = lax.broadcasted_iota(jnp.int32, (count, 1), 0) + start
        return pos.astype(f32) < length

    for k in range(parts):
        in_wait(0, k)
        pass_on(k).start()
    in_start(1)
    in_start(2)
    for k in range(parts):
        chunk = flip(me, k, parts)
        pass_on(k).wait_recv()
        at = pl.ds(aligned(chunk * rows, rows), rows)
        three = dot(xs[chunk], w[...])
        bias = jnp.where(below(rows, chunk * rows), 0.0, NEG).astype(bf16)
        for p in (0, 1):
            cut = slice(p * 128, p * 128 + 128)
            query = (three[:, :256][:, cut] * (LOG2E * 64 ** (-0.5))).astype(bf16)
            keys = three[:, 256:512][:, cut].astype(bf16)
            values = three[:, 512:][:, cut].astype(bf16)
            qkv[p, 0, at] = query
            qkv[p, 1, at] = keys
            qkv[p, 2, at] = values
            turned = values.T
            for h in range(2):
                ka[2 * p + h, at] = jnp.where(mine[h], keys, jnp.where(lane == base[h], bias, zero))
                qa[2 * p + h, at] = jnp.where(mine[h], query, jnp.where(lane == base[h], one, zero))
                vt[2 * p + h, :64, at] = turned[h * 64 : h * 64 + 64]
                vt[2 * p + h, 64:, at] = jnp.ones((8, rows), bf16)
    store(qkv, qkv_o)
    store(xs, xs_o)

    def attend(p):
        def body(j, carry):
            at = pl.ds(aligned(j * rows, rows), rows)
            out = []
            for h in range(2):
                top, acc = carry[h]
                scores = dot_nt(ka[2 * p + h, at, :], qa[2 * p + h])
                new_top = jnp.maximum(top, jnp.max(scores, axis=0, keepdims=True))
                probs = jnp.exp2(scores - new_top)
                acc = acc * jnp.exp2(top - new_top) + dot(vt[2 * p + h, :, at], probs.astype(bf16))
                out.append((new_top, acc))
            return tuple(out)

        init = tuple((jnp.full((1, full), NEG, f32), jnp.zeros((72, full), f32)) for _ in range(2))
        both = lax.fori_loop(0, parts, body, init)
        lse[p] = jnp.zeros((8, full), f32)
        pieces = []
        for h in range(2):
            top, acc = both[h]
            total = acc[64:65]
            pieces.append(acc[:64] / total)
            lse[p, h : h + 1, :] = top + jnp.log2(total)
        mixed[p] = jnp.concatenate(pieces, 0).T.astype(bf16).reshape(parts, rows, 128)
        m_copy(p).start()
        mix[:, :, pl.ds(aligned((2 * core + p) * 128, 128), 128)] = mixed[p, :, here]

    attend(0)
    attend(1)
    store(mixed, mixed_o)
    store(lse, lse_o)

    tile = 512
    tiles = hidden // tile
    small[...] = jnp.zeros_like(small)

    def feed(u):
        chunks = (2 * u, 2 * u + 1)
        keep = jnp.concatenate([below(half, h * rows + core * half) for h in chunks], 0)
        mix_u = mix[2 * u : 2 * u + 2].reshape(rows, width)
        x_u = jnp.concatenate([xs[h, here] for h in chunks], 0)
        attention = dot(mix_u, wo[...])
        unit1, inv1 = normed(x_u.astype(f32) + attention)
        x_mid = unit1 * g1[...] + b1[...]
        mid[u] = x_mid.astype(bf16)
        total = jnp.zeros((rows, width), f32)
        c0 = 0.7978845608028654
        c1 = 0.044715
        for t in range(tiles):
            cols = slice(t * tile, (t + 1) * tile)
            act = dot(mid[u], wu[:, cols]) + bu[:, cols]
            square = act * act
            th = jnp.tanh(act * (c0 + (c0 * c1) * square))
            part = 0.5 * (1.0 + th)
            low = (act * part).astype(bf16)
            hid[u, :, cols] = low
            slope[:rows, cols] = part + (0.5 * act) * (1.0 - th * th) * (c0 + (3.0 * c0 * c1) * square)
            total = total + dot(low, wd[cols, :])
        total = total + bd[...]
        unit2, inv2 = normed(x_mid + total)
        post = jnp.where(keep, unit2 * g2[...] + b2[...], 0.0).astype(bf16)
        added = jnp.where(keep, attention + total, 0.0).astype(bf16)
        post_v[2 * u : 2 * u + 2] = post.reshape(2, half, width)
        added_v[2 * u : 2 * u + 2] = added.reshape(2, half, width)
        for h in chunks:
            out_start(h)
        store(added_v.at[2 * u : 2 * u + 2], added_o.at[2 * u : 2 * u + 2])
        post_c = jnp.where(keep, pcs[2 * u : 2 * u + 2].reshape(rows, width).astype(f32), 0.0)
        accum_c = jnp.where(keep, acs[2 * u : 2 * u + 2].reshape(rows, width).astype(f32), 0.0)
        mid_grad2 = norm_back(post_c * g2[...], unit2, inv2)
        small[2:3, :width] += jnp.sum(post_c * unit2, axis=0, keepdims=True)
        small[3:4, :width] += jnp.sum(post_c, axis=0, keepdims=True)
        feed_grad = (mid_grad2 + accum_c).astype(bf16)
        fgrad[u] = feed_grad
        small[4:5, :width] += jnp.sum(feed_grad.astype(f32), axis=0, keepdims=True)
        back[...] = mid_grad2
        for t in range(tiles):
            cols = slice(t * tile, (t + 1) * tile)
            hidden_grad = dot_nt(fgrad[u], wd[cols, :]).astype(bf16)
            pre_grad = (hidden_grad.astype(f32) * slope[:rows, cols]).astype(bf16)
            pre[u, :, cols] = pre_grad
            small[5:6, cols] += jnp.sum(pre_grad.astype(f32), axis=0, keepdims=True)
            back[...] += dot_nt(pre_grad, wu[:, cols])
        mid_grad = back[...]
        small[0:1, :width] += jnp.sum(mid_grad * unit1, axis=0, keepdims=True)
        small[1:2, :width] += jnp.sum(mid_grad, axis=0, keepdims=True)
        first = norm_back(mid_grad * g1[...], unit1, inv1)
        first_v[2 * u : 2 * u + 2] = first.reshape(2, half, width)
        store(first_v.at[2 * u : 2 * u + 2], first_o.at[2 * u : 2 * u + 2])
        attn_grad = (first + accum_c).astype(bf16)
        agrad[u] = attn_grad
        mgrad[2 * u : 2 * u + 2] = dot_nt(attn_grad, wo[...]).astype(bf16).reshape(2, half, width)
        for p in (0, 1):
            g_copy(p, u).start()
            own = mgrad.at[2 * u : 2 * u + 2, :, pl.ds(aligned((2 * core + p) * 128, 128), 128)]
            store(own, go_o.at[p, 2 * u : 2 * u + 2, here])

    wo_in.wait()
    wu_in.wait()
    wd_in.wait()
    for a in (1, 2):
        for k in range(parts):
            in_wait(a, k)
    for p in (0, 1):
        m_copy(p).wait_recv()
    for u in (0, 1):
        feed(u)

    n, up_rows, vector_rows, total_rows = grad_rows(width, hidden, shards)
    halves = (0, 1)

    def spot_of(shard):
        return lax.rem(core + shard % 2, 2), shard // 2

    for t in range(tiles):
        cols = slice(t * tile, (t + 1) * tile)
        slope[:width, cols] = sum(dot_tn(mid[u], pre[u, :, cols]) for u in halves)
    for shard in range(shards):
        own = slice(shard * n, (shard + 1) * n)
        block = jnp.concatenate([slope[own, t * tile : (t + 1) * tile] for t in range(tiles)], 0)
        side, spot = spot_of(shard)
        grads[side, spot, :up_rows] = block.astype(bf16)
    per = tile // up_rows
    for t in range(tiles):
        cols = slice(t * tile, (t + 1) * tile)
        block = sum(dot_tn(hid[u, :, cols], fgrad[u]) for u in halves).astype(bf16)
        for i in range(per):
            side, spot = spot_of(t * per + i)
            grads[side, spot, up_rows : 2 * up_rows] = block[i * up_rows : (i + 1) * up_rows]
    out_all = sum(dot_tn(mix[2 * u : 2 * u + 2].reshape(rows, width), agrad[u]) for u in halves)
    line = lax.broadcasted_iota(jnp.int32, (8, width), 0)
    short = small[:, :width]
    long = small[...]
    for shard in range(shards):
        a = pltpu.roll(short, (width - shard * n) % width, 1)
        b = pltpu.roll(long, (hidden - shard * up_rows) % hidden, 1)[:, :width]
        extra = jnp.where(line == 5, b, a)
        rest = total_rows - 2 * up_rows - n - 8
        block = jnp.concatenate(
            [out_all[shard * n : (shard + 1) * n], extra, jnp.zeros((rest, width), f32)], 0
        )
        side, spot = spot_of(shard)
        grads[side, spot, 2 * up_rows :] = block.astype(bf16)
    store(grads, grads_o)

    for a in range(3):
        in_sent(a)
    for k in range(parts):
        pass_on(k).wait_send()
    size_copy.wait_send()
    for p in (0, 1):
        m_copy(p).wait_send()
        for u in (0, 1):
            g_copy(p, u).wait()
    out_wait()
    for copy in stores:
        copy.wait()


def first_call(parts, shards, lengths, streams, weights):
    groups, rows, width = streams[0].shape
    hidden = weights[4].shape[1]
    full = rows * parts
    half = rows // 2
    total_rows = grad_rows(width, hidden, shards)[3]
    held = jax.ShapeDtypeStruct((groups, rows, width), bf16)
    return pl.pallas_call(
        functools.partial(first_kernel, parts, shards),
        in_specs=[SMEM] + [ANY] * 5 + [VMEM, VMEM, ANY, VMEM, ANY, VMEM, VMEM, VMEM],
        out_specs=[ANY] * 9 + [VMEM],
        out_shape=[
            held,
            jax.ShapeDtypeStruct((parts, half, width), bf16),
            jax.ShapeDtypeStruct((parts, half, width), f32),
            jax.ShapeDtypeStruct((2, 3, full, 128), bf16),
            jax.ShapeDtypeStruct((2, 8, full), f32),
            jax.ShapeDtypeStruct((2, parts, rows, 128), bf16),
            jax.ShapeDtypeStruct((2, parts, rows, 128), bf16),
            jax.ShapeDtypeStruct((parts, rows, width), bf16),
            jax.ShapeDtypeStruct((2, shards // 2, total_rows, width), bf16),
            jax.ShapeDtypeStruct((8, 128), f32),
        ],
        scratch_shapes=[
            pltpu.VMEM((parts, rows, width), bf16),
            pltpu.VMEM((parts, half, width), bf16),
            pltpu.VMEM((parts, half, width), bf16),
            pltpu.VMEM((width, 768), bf16),
            pltpu.VMEM((2, 3, full, 128), bf16),
            pltpu.VMEM((4, full, 128), bf16),
            pltpu.VMEM((4, full, 128), bf16),
            pltpu.VMEM((4, 72, full), bf16),
            pltpu.VMEM((2, parts, rows, 128), bf16),
            pltpu.VMEM((2, 8, full), f32),
            pltpu.VMEM((width, width), bf16),
            pltpu.VMEM((width, hidden), bf16),
            pltpu.VMEM((hidden, width), bf16),
            pltpu.VMEM((parts, half, width), bf16),
            pltpu.VMEM((2, rows, hidden), bf16),
            pltpu.VMEM((2, rows, hidden), bf16),
            pltpu.VMEM((max(rows, width), hidden), f32),
            pltpu.VMEM((rows, width), f32),
            pltpu.VMEM((2, rows, width), bf16),
            pltpu.VMEM((2, rows, width), bf16),
            pltpu.VMEM((2, rows, width), bf16),
            pltpu.VMEM((parts, half, width), bf16),
            pltpu.VMEM((parts, half, width), bf16),
            pltpu.VMEM((parts, half, width), bf16),
            pltpu.VMEM((parts, half, width), f32),
            pltpu.VMEM((8, hidden), f32),
            pltpu.VMEM((2, shards // 2, total_rows, width), bf16),
            pltpu.VMEM((2, 8, 128), f32),
            DMA((8,)),
            DMA((16,)),
            DMA((5,)),
            DMA((2, 3, 4)),
            DMA((2, parts)),
            DMA((2, 2)),
            DMA((2, 2, 2)),
            DMA((2, 4)),
            DMA((2,)),
        ],
        compiler_params=pltpu.CompilerParams(
            vmem_limit_bytes=VMEM_LIMIT, collective_id=0, has_side_effects=True
        ),
        name="forward_and_feed",
    )(lengths, *streams, *weights)


def second_kernel(
    parts,
    shards,
    grad_norm,
    length_v,
    qkv_h,
    lse_h,
    mixed_h,
    go_h,
    xs_h,
    grads_h,
    first_h,
    added_h,
    wqkv_h,
    dx_o,
    added_o,
    wqkv_o,
    up_o,
    down_o,
    out_o,
    vec_o,
    xs,
    qkv,
    lse,
    mixed,
    go,
    wqkv,
    first,
    grads,
    core_in,
    a1_in,
    b1_in,
    a2_in,
    b2_in,
    z_in,
    all_out,
    all_in,
    final,
    ka,
    va,
    qa,
    da,
    kt,
    dqt,
    dsend,
    dfull,
    dx_v,
    late,
    late_out,
    late_in,
    late_sum,
    late_step,
    late_got,
    late_all,
    load_sem,
    store_sem,
    self_sem,
    dsem,
    rsem,
    lsem,
    osem,
):
    parts, rows, width = xs.shape
    half_rows = rows // 2
    full = rows * parts
    hidden = up_o.shape[1]
    me = lax.axis_index("head")
    place = lax.axis_index("seq")
    core = lax.rem(place, 2)
    other = place + 1 - 2 * core
    from_core = lax.div(me, 2)
    from_group = lax.rem(me, 2)
    here = pl.ds(aligned(core * half_rows, half_rows), half_rows)
    there = pl.ds(aligned((1 - core) * half_rows, half_rows), half_rows)
    length = length_v[0:1, 0:1]
    lane, mine, base = lane_sets()
    one = jnp.ones((), bf16)
    zero = jnp.zeros((), bf16)
    n, up_rows, vector_rows, total_rows = grad_rows(width, hidden, shards)
    seq_bits = bits_of(shards)
    load_count = itertools.count()

    def load(src, dst):
        copy = pltpu.make_async_copy(src, dst, load_sem.at[next(load_count)])
        copy.start()
        return copy

    stores = []
    store_count = itertools.count()

    def store(src, dst):
        copy = pltpu.make_async_copy(src, dst, store_sem.at[next(store_count)])
        copy.start()
        stores.append(copy)

    def pair_load(p):
        return [
            load(qkv_h.at[p], qkv.at[p]),
            load(go_h.at[p], go.at[p]),
            load(mixed_h.at[p], mixed.at[p]),
            load(lse_h.at[p], lse.at[p]),
        ]

    pair_in = [pair_load(0)]
    grads_in = load(grads_h.at[0], grads)
    xs_in = load(xs_h, xs)
    pair_in.append(pair_load(1))
    wqkv_in = load(wqkv_h, wqkv)
    first_in = load(first_h, first)

    enter(plane(me, place, parts) + [(me, flip(place, bit, shards)) for bit in seq_bits[1:]])

    sends = []

    def launch(make, *which):
        make(*which).start()
        sends.append(functools.partial(make, *which))

    spots = shards // 2
    half, quarter = total_rows // 2, total_rows // 4
    eighth = total_rows // 8
    x_bit = lax.rem(me, 2)
    y_bit = lax.div(me, 2)

    def to_head(src, dst, i, k):
        return send(src, dst, (rsem.at[0, i], rsem.at[1, i]), (flip(me, k, parts), place))

    def to_seq(src, dst, i, bit):
        return send(src, dst, (rsem.at[0, i], rsem.at[1, i]), (me, flip(place, bit, shards)))

    core_copy = lambda: to_seq(grads_h.at[1], core_in, 0, 1)
    a_keep = x_bit * quarter
    a_give = (1 - x_bit) * quarter
    b_keep = half + y_bit * quarter
    b_give = half + (1 - y_bit) * quarter
    a1_copy = lambda: to_head(grads.at[:, pl.ds(aligned(a_give, 16), quarter)], a1_in, 1, 1)
    b1_copy = lambda: to_head(grads.at[:, pl.ds(aligned(b_give, 16), quarter)], b1_in, 2, 2)
    a_own = a_keep + y_bit * eighth
    a_pass = a_keep + (1 - y_bit) * eighth
    b_own = b_keep + x_bit * eighth
    b_pass = b_keep + (1 - x_bit) * eighth
    a2_copy = lambda: to_head(grads.at[:, pl.ds(aligned(a_pass, 16), eighth)], a2_in, 3, 2)
    b2_copy = lambda: to_head(grads.at[:, pl.ds(aligned(b_pass, 16), eighth)], b2_in, 4, 1)

    def add_rows(into, spot, start, count, other):
        at = pl.ds(aligned(start, 16), count)
        into[spot, at] = (into[spot, at].astype(f32) + other.astype(f32)).astype(bf16)

    def early_core():
        grads_in.wait()
        core_copy().wait_recv()

        def body(i, carry):
            grads[i] = (grads[i].astype(f32) + core_in[i].astype(f32)).astype(bf16)
            return carry

        lax.fori_loop(0, spots, body, None)
        launch(a1_copy)
        launch(b1_copy)

    def early_first():
        a1_copy().wait_recv()
        b1_copy().wait_recv()

        def body(i, carry):
            add_rows(grads, i, a_keep, quarter, a1_in[i])
            add_rows(grads, i, b_keep, quarter, b1_in[i])
            return carry

        lax.fori_loop(0, spots, body, None)
        launch(a2_copy)
        launch(b2_copy)

    def early_second_and_on():
        a2_copy().wait_recv()
        b2_copy().wait_recv()

        def body(i, carry):
            add_rows(grads, i, a_own, eighth, a2_in[i])
            add_rows(grads, i, b_own, eighth, b2_in[i])
            return carry

        lax.fori_loop(0, spots, body, None)

        def gather(i, carry):
            all_out[i, :eighth] = grads[i, pl.ds(aligned(a_own, 16), eighth)]
            all_out[i, eighth:] = grads[i, pl.ds(aligned(b_own, 16), eighth)]
            return carry

        lax.fori_loop(0, spots, gather, None)
        if steps:
            z_send(0)

    offsets = []
    at = 0
    size = spots
    for bit in seq_bits[1:]:
        offsets.append((at, size))
        at += size
        size //= 2
    offsets.append((at, 1))
    steps = len(offsets) - 1
    z_offsets = []
    at = 0
    for _, size in offsets[:-1]:
        z_offsets.append(at)
        at += size // 2

    def z_copy(i):
        at, size = offsets[i]
        bit = seq_bits[1 + i]
        return to_seq(
            all_in.at[pl.ds(z_offsets[i], size // 2)], z_in.at[pl.ds(z_offsets[i], size // 2)], 5 + i, bit
        )

    def z_send(i):
        at, size = offsets[i]
        own = lax.rem(lax.div(place, seq_bits[1 + i]), 2)
        for j in range(size // 2):
            all_in[z_offsets[i] + j] = all_out[at + 2 * j + (1 - own)]
        launch(z_copy, i)

    def z_add(i):
        at, size = offsets[i]
        after = offsets[i + 1][0]
        own = lax.rem(lax.div(place, seq_bits[1 + i]), 2)
        z_copy(i).wait_recv()
        for j in range(size // 2):
            all_out[after + j] = (
                all_out[at + 2 * j + own].astype(f32) + z_in[z_offsets[i] + j].astype(f32)
            ).astype(bf16)

    ag_from = 5 + steps
    last = offsets[-1][0]
    ag = sum(size // 2 for _, size in offsets[:-1])

    def ag_copy(k):
        return to_head(all_out.at[last], all_in.at[ag + k], ag_from + k, k)

    def ag_send():
        for k in range(parts - 1, 0, -1):
            launch(ag_copy, k)

    def ag_finish():
        for k in range(parts):
            if k:
                ag_copy(k).wait_recv()
                block = all_in[ag + k]
            else:
                block = all_out[last]
            block = block.astype(f32) * grad_norm
            who = flip(me, k, parts)
            x_of, y_of = lax.rem(who, 2), lax.div(who, 2)
            a_at = x_of * quarter + y_of * eighth
            b_at = half + y_of * quarter + x_of * eighth
            final[pl.ds(aligned(a_at, 16), eighth)] = block[:eighth]
            final[pl.ds(aligned(b_at, 16), eighth)] = block[eighth:]
        for t in range(hidden // width):
            store(final.at[pl.ds(t * n, n)], up_o.at[:, pl.ds(t * width, width)])
        store(final.at[pl.ds(up_rows, up_rows)], down_o)
        store(final.at[pl.ds(2 * up_rows, n)], out_o)
        vec_o[...] = final[2 * up_rows + n : 2 * up_rows + n + 8]

    def d_copy(p, part):
        return send(
            dsend.at[p, part, :, there],
            dfull.at[:, :, pl.ds(aligned(part * width + (2 * core + p) * 128, 128), 128)],
            (dsem.at[0, p, part], dsem.at[1, p, part]),
            (me, other),
        )

    def prepare(p):
        for copy in pair_in[p]:
            copy.wait()
        turned = -lse[p].T
        kt[...] = qkv[p, 1].T
        for k in range(parts):
            at = slice(k * rows, (k + 1) * rows)
            query, keys, values = qkv[p, 0, at], qkv[p, 1, at], qkv[p, 2, at]
            pos = lax.broadcasted_iota(jnp.int32, (rows, 1), 0) + k * rows
            bias = jnp.where(pos.astype(f32) < length, 0.0, NEG).astype(bf16)
            grad = go[p, k]
            prod = grad.astype(f32) * mixed[p, k].astype(f32)
            for h in range(2):
                ka[h, at] = jnp.where(mine[h], keys, jnp.where(lane == base[h], bias, one))
                va[h, at] = jnp.where(mine[h], values, one)
                a, b, c = split3(-jnp.sum(jnp.where(mine[h], prod, 0.0), axis=1, keepdims=True))
                extra = jnp.where(
                    lane == base[h],
                    a,
                    jnp.where(lane == base[h] + 1, b, jnp.where(lane == base[h] + 2, c, zero)),
                )
                da[h, at] = jnp.where(mine[h], grad, extra)
                a, b, c = split3(turned[at, h : h + 1])
                extra = jnp.where(
                    lane == base[h],
                    one,
                    jnp.where(
                        lane == base[h] + 1,
                        a,
                        jnp.where(lane == base[h] + 2, b, jnp.where(lane == base[h] + 3, c, zero)),
                    ),
                )
                qa[h, at] = jnp.where(mine[h], query, extra)
        dqt[...] = jnp.zeros_like(dqt)

    block = rows // 2
    steps_each = 2 * parts

    def attend_back(p, events):
        def body(i, carry):
            for when, event in events.items():
                pl.when(i == when)(event)
            at = pl.ds(aligned(i * block, block), block)
            out = []
            for h in range(2):
                probs = jnp.exp2(dot_nt(ka[h, at, :], qa[h]))
                inner = dot_nt(va[h, at, :], da[h])
                low = probs.astype(bf16)
                grad = (probs * inner).astype(bf16)
                dv = dot(low, go[p].reshape(full, 128))
                dk = dot(grad, qkv[p, 0])
                part = slice(h * 64, h * 64 + 64)
                dqt[part, :] += dot(kt[part, at], grad)
                out.append((dv, dk))
            chunk = lax.div(i, 2)
            at = pl.ds(aligned(lax.rem(i, 2) * block, block), block)
            dsend[p, 1, chunk, at] = (jnp.where(mine[0], out[0][1], out[1][1]) * (1.0 / LOG2E)).astype(bf16)
            dsend[p, 2, chunk, at] = jnp.where(mine[0], out[0][0], out[1][0]).astype(bf16)
            return carry

        lax.fori_loop(0, steps_each, body, None)
        dsend[p, 0] = (dqt[...] * 64 ** (-0.5)).T.astype(bf16).reshape(parts, rows, 128)
        for part in range(3):
            d_copy(p, part).start()
            dfull[:, :, pl.ds(aligned(part * width + (2 * core + p) * 128, 128), 128)] = dsend[p, part, :, here]

    def late_term(p):
        for part in range(3):
            late[p, :, part * 128 : part * 128 + 128] = sum(
                dot_tn(xs[k], dsend[p, part, k]) for k in range(parts)
            )

    l_sizes = [spots] + [spots >> i for i in range(len(seq_bits) - 1)]
    l_offsets = [0] + [sum(size // 2 for size in l_sizes[1:i]) for i in range(1, len(seq_bits))]

    def l_core(p):
        return send(late_out.at[p], late_in.at[p], (lsem.at[0, p, 0], lsem.at[1, p, 0]), (me, other))

    def l_copy(p, i):
        size = l_sizes[i] // 2
        at = l_offsets[i]
        return send(
            late_step.at[p, pl.ds(at, size)],
            late_got.at[p, pl.ds(at, size)],
            (lsem.at[0, p, i], lsem.at[1, p, i]),
            (me, flip(place, seq_bits[i], shards)),
        )

    l_steps = len(seq_bits)

    def lg_copy(p, k):
        return send(
            late_all.at[p, 0],
            late_all.at[p, k],
            (lsem.at[0, p, l_steps + k], lsem.at[1, p, l_steps + k]),
            (flip(me, k, parts), place),
        )

    def late_start(p):
        for z in range(spots):
            late_out[p, z] = late[p, pl.ds(aligned((2 * z + 1 - core) * n, 8), n)].astype(bf16)
        launch(l_core, p)

    def late_split(p, i):
        own = lax.rem(lax.div(place, seq_bits[i]), 2)
        size = l_sizes[i] // 2
        for j in range(size):
            late_step[p, l_offsets[i] + j] = late_sum[p, 2 * j + 1 - own].astype(bf16)
        launch(l_copy, p, i)

    def late_merge(p, i):
        own = lax.rem(lax.div(place, seq_bits[i]), 2)
        l_copy(p, i).wait_recv()
        for j in range(l_sizes[i] // 2):
            late_sum[p, j] = late_sum[p, 2 * j + own] + late_got[p, l_offsets[i] + j].astype(f32)

    def late_cores(p):
        l_core(p).wait_recv()
        for z in range(spots):
            own = late[p, pl.ds(aligned((2 * z + core) * n, 8), n)]
            late_sum[p, z, :, pl.ds(aligned(core * 384, 128), 384)] = own
            late_sum[p, z, :, pl.ds(aligned((1 - core) * 384, 128), 384)] = late_in[p, z].astype(f32)

    def late_share(p):
        late_all[p, 0] = late_sum[p, 0].astype(bf16)
        for k in range(parts - 1, 0, -1):
            launch(lg_copy, p, k)

    def late_finish(p):
        for k in range(1, parts):
            lg_copy(p, k).wait_recv()
        total = sum(late_all[p, k].astype(f32) for k in range(parts)) * grad_norm
        for owner in range(2):
            for part in range(3):
                to = part * width + (2 * owner + p) * 128
                at = owner * 384 + part * 128
                wqkv_o[:, to : to + 128] = total[:, at : at + 128]

    def late_events(p):
        steps_of = []

        def first_step():
            late_cores(p)
            if l_steps > 1:
                late_split(p, 1)
            else:
                late_share(p)

        steps_of.append(first_step)
        for i in range(1, l_steps):

            def step(i=i):
                late_merge(p, i)
                if i + 1 < l_steps:
                    late_split(p, i + 1)
                else:
                    late_share(p)

            steps_of.append(step)
        return steps_of

    def both_events(one_event, two_event):
        def run():
            one_event()
            two_event()

        return run

    def out_copies(a, h):
        src = (added_h, dx_v)[a].at[h]
        dst = (added_o, dx_o)[a].at[from_group, here]
        remote = send(
            src,
            dst,
            (osem.at[0, a, h], osem.at[1, a, 2 * from_group + core]),
            (h, place - core + from_core),
        )
        local = pltpu.make_async_copy(src, dst, self_sem.at[a])
        return remote, local, (h == me) & (from_core == core)

    def out_start(a):
        for h in range(parts):
            remote, local, own = out_copies(a, h)
            pl.when(own)(local.start)
            pl.when(jnp.logical_not(own))(remote.start)

    def out_wait(a):
        for h in range(parts):
            remote, local, own = out_copies(a, h)
            pl.when(own)(local.wait)
            pl.when(jnp.logical_not(own))(remote.wait_send)
        for s in (0, 1):
            for r in (0, 1):
                chip = 2 * core + s
                dst = (added_o, dx_o)[a].at[s, r * half_rows : (r + 1) * half_rows]
                remote = send(
                    (added_h, dx_v)[a].at[0],
                    dst,
                    (osem.at[0, a, 0], osem.at[1, a, 2 * s + r]),
                    (chip, place - core + r),
                )
                pl.when(jnp.logical_not((chip == me) & (core == r)))(remote.wait_recv)

    launch(core_copy)
    out_start(0)
    prepare(0)
    attend_back(0, {2: early_core})
    xs_in.wait()
    late_term(0)
    late_start(0)
    prepare(1)
    early_first()
    early_steps = [early_second_and_on]
    for i in range(1, steps):

        def early_step(i=i):
            z_add(i - 1)
            z_send(i)

        early_steps.append(early_step)

    def early_last():
        if steps:
            z_add(steps - 1)
        ag_send()

    early_steps.append(early_last)
    events = {}
    later = []

    def schedule(steps_list, slots):
        for index, event in enumerate(steps_list):
            slot = slots[index] if index < len(slots) else steps_each
            if slot >= steps_each:
                later.append(event)
            elif slot in events:
                events[slot] = both_events(events[slot], event)
            else:
                events[slot] = event

    schedule(early_steps, (2, 4, 7))
    schedule(late_events(0), (0, 3, 6))
    attend_back(1, events)
    for event in later:
        event()
    late_term(1)
    late_start(1)
    tail = late_events(1)
    wqkv_in.wait()
    first_in.wait()
    for p in range(2):
        for part in range(3):
            d_copy(p, part).wait_recv()
    tail.pop(0)()
    for h in range(parts):
        dx_v[h] = (first[h] + dot_nt(dfull[h], wqkv[...])).astype(bf16)
    out_start(1)
    for event in tail:
        event()
    ag_finish()
    late_finish(0)
    late_finish(1)
    for make in sends:
        make().wait_send()
    for p in range(2):
        for part in range(3):
            d_copy(p, part).wait_send()
    out_wait(0)
    out_wait(1)
    for copy in stores:
        copy.wait()


def second_call(parts, shards, grad_norm, length, saved, grads, first, added, wqkv, hidden):
    xs_shape = saved[4].shape
    _, rows, width = xs_shape
    full = rows * parts
    half_rows = rows // 2
    n, up_rows, vector_rows, total_rows = grad_rows(width, hidden, shards)
    spots = shards // 2
    quarter, eighth = total_rows // 4, total_rows // 8
    heads = (2, full, 128)
    return pl.pallas_call(
        functools.partial(second_kernel, parts, shards, grad_norm),
        in_specs=[VMEM] + [ANY] * 9,
        out_specs=[ANY, ANY, VMEM, ANY, ANY, ANY, VMEM],
        out_shape=[
            jax.ShapeDtypeStruct((2, rows, width), bf16),
            jax.ShapeDtypeStruct((2, rows, width), bf16),
            jax.ShapeDtypeStruct((n, 3 * width), f32),
            jax.ShapeDtypeStruct((n, hidden), f32),
            jax.ShapeDtypeStruct((up_rows, width), f32),
            jax.ShapeDtypeStruct((n, width), f32),
            jax.ShapeDtypeStruct((8, width), f32),
        ],
        scratch_shapes=[
            pltpu.VMEM(xs_shape, bf16),
            pltpu.VMEM((2, 3, full, 128), bf16),
            pltpu.VMEM((2, 8, full), f32),
            pltpu.VMEM((2, parts, rows, 128), bf16),
            pltpu.VMEM((2, parts, rows, 128), bf16),
            pltpu.VMEM((width, 3 * width), bf16),
            pltpu.VMEM((parts, half_rows, width), f32),
            pltpu.VMEM((spots, total_rows, width), bf16),
            pltpu.VMEM((spots, total_rows, width), bf16),
            pltpu.VMEM((spots, quarter, width), bf16),
            pltpu.VMEM((spots, quarter, width), bf16),
            pltpu.VMEM((spots, eighth, width), bf16),
            pltpu.VMEM((spots, eighth, width), bf16),
            pltpu.VMEM((spots, quarter, width), bf16),
            pltpu.VMEM((2 * spots, quarter, width), bf16),
            pltpu.VMEM((spots + parts, quarter, width), bf16),
            pltpu.VMEM((total_rows, width), f32),
            pltpu.VMEM(heads, bf16),
            pltpu.VMEM(heads, bf16),
            pltpu.VMEM(heads, bf16),
            pltpu.VMEM(heads, bf16),
            pltpu.VMEM((128, full), bf16),
            pltpu.VMEM((128, full), f32),
            pltpu.VMEM((2, 3, parts, rows, 128), bf16),
            pltpu.VMEM((parts, half_rows, 3 * width), bf16),
            pltpu.VMEM((parts, half_rows, width), bf16),
            pltpu.VMEM((2, width, 384), f32),
            pltpu.VMEM((2, spots, n, 384), bf16),
            pltpu.VMEM((2, spots, n, 384), bf16),
            pltpu.VMEM((2, spots, n, 768), f32),
            pltpu.VMEM((2, spots, n, 768), bf16),
            pltpu.VMEM((2, spots, n, 768), bf16),
            pltpu.VMEM((2, parts, n, 768), bf16),
            DMA((16,)),
            DMA((16,)),
            DMA((2,)),
            DMA((2, 2, 3)),
            DMA((2, 24)),
            DMA((2, 2, 16)),
            DMA((2, 2, 4)),
        ],
        compiler_params=pltpu.CompilerParams(
            vmem_limit_bytes=VMEM_LIMIT, collective_id=1, has_side_effects=True
        ),
        name="backward_and_sums",
    )(length, *saved, grads, first, added, wqkv)


def last_kernel(rows_here, lengths, post_h, added_h, dx_h, y, ac, vec, *rest):
    ins, (post_o, accum_o, dx_o, accg_o), outs, vectors = rest[:4], rest[4:8], rest[8:12], rest[12:]
    step = pl.program_id(0)
    for src, dst in zip(ins, outs):
        dst[...] = src[...]

    @pl.when(step == 0)
    def _():
        for i, out in enumerate(vectors):
            out[...] = vec[i : i + 1, : out.shape[1]]

    _, rows, _ = y.shape
    steps = pl.num_programs(0)
    length = lengths[lax.div(step * 2, steps)]
    start = lax.axis_index("head") * rows_here + lax.rem(step, lax.div(steps, 2)) * rows
    keep = lax.broadcasted_iota(jnp.int32, (1, rows, 1), 1) + start < length
    post_o[...] = post_h[...].astype(f32)
    accum_o[...] = jnp.where(keep, y[...].astype(f32) + added_h[...].astype(f32), 0.0)
    dx_o[...] = dx_h[...].astype(f32)
    accg_o[...] = jnp.where(keep, ac[...].astype(f32), 0.0)


def last_call(lengths, tokens, streams, vectors, grads, shards):
    groups, rows, width = tokens[0].shape
    cut = 2
    steps = groups * cut
    block = pl.BlockSpec((1, rows // cut, width), lambda i: (i // cut, i % cut, 0))
    whole = jax.ShapeDtypeStruct((groups, rows, width), f32)
    n = width // shards
    hidden = grads[1].shape[1]
    short = [jax.ShapeDtypeStruct((1, n), f32)] * 5 + [jax.ShapeDtypeStruct((1, hidden // shards), f32)]
    moved = [pl.BlockSpec((g.shape[0], g.shape[1] // steps), lambda i: (0, i)) for g in grads]
    return pl.pallas_call(
        functools.partial(last_kernel, rows),
        grid=(steps,),
        in_specs=[SMEM] + [block] * 5 + [pl.BlockSpec(vectors.shape, lambda i: (0, 0))] + moved,
        out_specs=[block] * 4 + moved + [pl.BlockSpec(o.shape, lambda i: (0, 0)) for o in short],
        out_shape=[whole] * 4 + [jax.ShapeDtypeStruct(g.shape, f32) for g in grads] + short,
        compiler_params=pltpu.CompilerParams(vmem_limit_bytes=VMEM_LIMIT),
        name="outputs",
    )(lengths, *tokens, *streams, vectors, *grads)


def local(
    post_stream,
    accum_stream,
    seq_lengths,
    qkv_weight,
    out_weight,
    norm1_gain,
    norm1_bias,
    up_weight,
    up_bias,
    down_weight,
    down_bias,
    norm2_gain,
    norm2_bias,
    post_cotan,
    accum_cotan,
):
    groups, rows, width = post_stream.shape
    parts = lax.axis_size("head")
    shards = lax.axis_size("seq")
    hidden = up_weight.shape[1]
    grad_norm = float(groups * shards * rows * parts) ** (-0.5)

    def row(vector):
        return vector.reshape(1, -1)

    weights = (
        qkv_weight,
        out_weight,
        row(norm1_gain),
        row(norm1_bias),
        up_weight,
        row(up_bias),
        down_weight,
        row(down_bias),
        row(norm2_gain),
        row(norm2_bias),
    )
    post, added, first, qkv, lse, mixed, go, xs, grads, length = first_call(
        parts, shards, seq_lengths, (post_stream, post_cotan, accum_cotan), weights
    )
    dx, added, qkv_grad, up_grad, down_grad, out_grad, vectors = second_call(
        parts, shards, grad_norm, length, (qkv, lse, mixed, go, xs), grads, first, added, qkv_weight, hidden
    )
    post, accum, post_grad, accum_grad, qkv_grad, up_grad, down_grad, out_grad, *short = last_call(
        seq_lengths,
        (post, added, dx),
        (accum_stream, accum_cotan),
        vectors,
        (qkv_grad, up_grad, down_grad, out_grad),
        shards,
    )
    gain1, bias1, gain2, bias2, down_bias_grad, up_bias_grad = [v.reshape(-1) for v in short]
    return (
        post,
        accum,
        post_grad,
        accum_grad,
        qkv_grad,
        out_grad,
        gain1,
        bias1,
        up_grad,
        up_bias_grad,
        down_grad,
        down_bias_grad,
        gain2,
        bias2,
    )


def solution(mesh):
    tokens = P("seq", "head", None)
    in_specs = (tokens, tokens, P("seq")) + (P(),) * 10 + (tokens, tokens)
    rows = P("seq", None)
    vector = P("seq")
    out_specs = (tokens,) * 4 + (rows, rows, vector, vector, rows, vector, rows, vector, vector, vector)
    return jax.shard_map(local, mesh=mesh, in_specs=in_specs, out_specs=out_specs, check_vma=False)
```

```python
import functools
import itertools

import jax
import jax.numpy as jnp
from jax import lax
from jax.experimental import pallas as pl
from jax.experimental.pallas import tpu as pltpu
from jax.sharding import PartitionSpec as P

H = 8
EPS = 1e-05
NEG = -1e30
LOG2E = 1.4426950408889634
VMEM_LIMIT = 62 * 2**20
bf16 = jnp.bfloat16
f32 = jnp.float32
SMEM = pl.BlockSpec(memory_space=pltpu.SMEM)
VMEM = pl.BlockSpec(memory_space=pltpu.VMEM)
ANY = pl.BlockSpec(memory_space=pl.ANY)
DMA = pltpu.SemaphoreType.DMA


def dot(a, b):
    return jnp.dot(a, b, preferred_element_type=f32)


def dot_nt(a, b):
    return lax.dot_general(a, b, (((1,), (1,)), ((), ())), preferred_element_type=f32)


def dot_tn(a, b):
    return lax.dot_general(a, b, (((0,), (0,)), ((), ())), preferred_element_type=f32)


def split3(value):
    first = value.astype(bf16)
    rest = value - first.astype(f32)
    second = rest.astype(bf16)
    third = (rest - second.astype(f32)).astype(bf16)
    return first, second, third


def lane_sets():
    lane = lax.broadcasted_iota(jnp.int32, (1, 128), 1)
    return lane, (lane < 64, lane >= 64), (64, 0)


def bits_of(count):
    return [1 << b for b in range(count.bit_length() - 1)]


def flip(index, k, count):
    out = 0
    for bit in bits_of(count):
        out = out + (lax.rem(lax.div(index, bit) + (k // bit), 2)) * bit
    return out


def aligned(start, step):
    if isinstance(start, int):
        return start
    return pl.multiple_of(start, step)


def send(src, dst, pair, to):
    return pltpu.make_async_remote_copy(
        src_ref=src,
        dst_ref=dst,
        send_sem=pair[0],
        recv_sem=pair[1],
        device_id=to,
        device_id_type=pl.DeviceIdType.MESH,
    )


def enter(partners):
    barrier = pltpu.get_barrier_semaphore()
    for to in partners:
        pl.semaphore_signal(barrier, inc=1, device_id=to, device_id_type=pl.DeviceIdType.MESH)
    pl.semaphore_wait(barrier, len(partners))


def plane(me, place, parts):
    core = lax.rem(place, 2)
    others = []
    for k in range(parts):
        for other in range(2):
            if k or other:
                seat = place if not other else place + 1 - 2 * core
                others.append((flip(me, k, parts), seat))
    return others


def grad_rows(width, hidden, shards):
    n = width // shards
    up = n * (hidden // width)
    vectors = 16 - n % 16
    total = 2 * up + n + vectors
    return n, up, vectors, -(-total // 128) * 128


def normed(value):
    centre = value - jnp.mean(value, axis=-1, keepdims=True)
    spread = jnp.mean(centre * centre, axis=-1, keepdims=True)
    inv = lax.rsqrt(spread + EPS)
    return centre * inv, inv


def norm_back(cot, unit, inv):
    return (
        cot - jnp.mean(cot, axis=-1, keepdims=True) - unit * jnp.mean(cot * unit, axis=-1, keepdims=True)
    ) * inv


def first_kernel(
    parts,
    shards,
    lengths,
    x,
    pc,
    ac,
    wqkv,
    wo_h,
    g1,
    b1,
    wu_h,
    bu,
    wd_h,
    bd,
    g2,
    b2,
    post_o,
    added_o,
    first_o,
    qkv_o,
    lse_o,
    mixed_o,
    go_o,
    xs_o,
    grads_o,
    length_o,
    xs,
    pcs,
    acs,
    w,
    qkv,
    ka,
    qa,
    vt,
    mixed,
    lse,
    wo,
    wu,
    wd,
    mix,
    hid,
    pre,
    slope,
    back,
    fgrad,
    mid,
    agrad,
    mgrad,
    post_v,
    added_v,
    first_v,
    small,
    grads,
    core_in,
    sizes,
    load_sem,
    store_sem,
    self_sem,
    insem,
    fsem,
    msem,
    gsem,
    osem,
    nsem,
    csem,
):
    groups, rows, width = x.shape
    hidden = wu.shape[1]
    full = rows * parts
    half = rows // 2
    me = lax.axis_index("head")
    place = lax.axis_index("seq")
    core = lax.rem(place, 2)
    other = place + 1 - 2 * core
    from_core = lax.div(me, 2)
    from_group = lax.rem(me, 2)
    lane, mine, base = lane_sets()
    one = jnp.ones((), bf16)
    zero = jnp.zeros((), bf16)
    here = pl.ds(aligned(core * half, half), half)
    there = pl.ds(aligned((1 - core) * half, half), half)

    load_count = itertools.count()

    def load(src, dst):
        copy = pltpu.make_async_copy(src, dst, load_sem.at[next(load_count)])
        copy.start()
        return copy

    stores = []
    store_count = itertools.count()

    def store(src, dst):
        copy = pltpu.make_async_copy(src, dst, store_sem.at[next(store_count)])
        copy.start()
        stores.append(copy)

    w_in = [
        load(
            wqkv.at[:, pl.ds(aligned(part * width + core * 256, 128), 256)],
            w.at[:, part * 256 : part * 256 + 256],
        )
        for part in range(3)
    ]
    wo_in = load(wo_h, wo)
    wu_in = load(wu_h, wu)
    wd_in = load(wd_h, wd)

    enter(plane(me, place, parts))

    def in_copies(a, s, r):
        src = (x, pc, ac)[a].at[s, r * half : (r + 1) * half]
        dst = xs.at[me, r * half : (r + 1) * half] if a == 0 else (pcs, acs)[a - 1].at[me]
        chip = 2 * core + s
        remote = send(src, dst, (insem.at[0, a, 2 * s + r], insem.at[1, a, me]), (chip, place - core + r))
        local = pltpu.make_async_copy(src, dst, self_sem.at[a])
        return remote, local, (chip == me) & (core == r)

    def in_start(a):
        for s in (0, 1):
            for r in (0, 1):
                remote, local, own = in_copies(a, s, r)
                pl.when(own)(local.start)
                pl.when(jnp.logical_not(own))(remote.start)

    def in_sent(a):
        for s in (0, 1):
            for r in (0, 1):
                remote, local, own = in_copies(a, s, r)
                pl.when(jnp.logical_not(own))(remote.wait_send)

    def in_wait(a, k):
        chunk = flip(me, k, parts)
        dst = xs.at[chunk, here] if a == 0 else (pcs, acs)[a - 1].at[chunk]
        src = (x, pc, ac)[a].at[0, :half]
        remote = send(src, dst, (insem.at[0, a, 0], insem.at[1, a, chunk]), (chunk, place))
        if k:
            remote.wait_recv()
        else:
            local = pltpu.make_async_copy(src, dst, self_sem.at[a])
            pl.when(from_core == core)(local.wait)
            pl.when(from_core != core)(remote.wait_recv)

    def across(src, dst, pair):
        return send(src, dst, pair, (me, other))

    def pass_on(k):
        part = xs.at[flip(me, k, parts), here]
        return across(part, part, (fsem.at[0, k], fsem.at[1, k]))

    size_copy = across(sizes.at[0], sizes.at[1], (nsem.at[0], nsem.at[1]))

    def m_copy(p):
        return across(
            mixed.at[p, :, there],
            mix.at[:, :, pl.ds(aligned((2 * core + p) * 128, 128), 128)],
            (msem.at[0, p], msem.at[1, p]),
        )

    def g_copy(p, u):
        chunks = slice(2 * u, 2 * u + 2)
        return across(
            mgrad.at[chunks, :, pl.ds(aligned((2 * (1 - core) + p) * 128, 128), 128)],
            go_o.at[p, chunks, here],
            (gsem.at[0, p, u], gsem.at[1, p, u]),
        )

    def out_copies(h):
        dst = post_o.at[from_group, here]
        remote = send(
            post_v.at[h],
            dst,
            (osem.at[0, h], osem.at[1, 2 * from_group + core]),
            (h, place - core + from_core),
        )
        local = pltpu.make_async_copy(post_v.at[h], dst, self_sem.at[3])
        return remote, local, (h == me) & (from_core == core)

    def out_start(h):
        remote, local, own = out_copies(h)
        pl.when(own)(local.start)
        pl.when(jnp.logical_not(own))(remote.start)

    def out_wait():
        for h in range(parts):
            remote, local, own = out_copies(h)
            pl.when(own)(local.wait)
            pl.when(jnp.logical_not(own))(remote.wait_send)
        for s in (0, 1):
            for r in (0, 1):
                chip = 2 * core + s
                dst = post_o.at[s, r * half : (r + 1) * half]
                remote = send(
                    post_v.at[0], dst, (osem.at[0, 0], osem.at[1, 2 * s + r]), (chip, place - core + r)
                )
                pl.when(jnp.logical_not((chip == me) & (core == r)))(remote.wait_recv)

    in_start(0)
    which = lax.broadcasted_iota(jnp.int32, (8, 128), 0)
    sizes[0] = jnp.where(which == 0, lengths[0], lengths[1]).astype(f32)
    size_copy.start()
    for copy in w_in:
        copy.wait()
    size_copy.wait_recv()
    held = jnp.where(from_core == core, sizes[0], sizes[1])
    length = jnp.sum(jnp.where(which == from_group, held, 0.0), axis=0, keepdims=True)
    length_o[...] = jnp.broadcast_to(length, (8, 128))
    length = length[:, :1]

    def below(count, start):
        pos = lax.broadcasted_iota(jnp.int32, (count, 1), 0) + start
        return pos.astype(f32) < length

    for k in range(parts):
        in_wait(0, k)
        pass_on(k).start()
    in_start(1)
    in_start(2)
    for k in range(parts):
        chunk = flip(me, k, parts)
        pass_on(k).wait_recv()
        at = pl.ds(aligned(chunk * rows, rows), rows)
        three = dot(xs[chunk], w[...])
        bias = jnp.where(below(rows, chunk * rows), 0.0, NEG).astype(bf16)
        for p in (0, 1):
            cut = slice(p * 128, p * 128 + 128)
            query = (three[:, :256][:, cut] * (LOG2E * 64 ** (-0.5))).astype(bf16)
            keys = three[:, 256:512][:, cut].astype(bf16)
            values = three[:, 512:][:, cut].astype(bf16)
            qkv[p, 0, at] = query
            qkv[p, 1, at] = keys
            qkv[p, 2, at] = values
            turned = values.T
            for h in range(2):
                ka[2 * p + h, at] = jnp.where(mine[h], keys, jnp.where(lane == base[h], bias, zero))
                qa[2 * p + h, at] = jnp.where(mine[h], query, jnp.where(lane == base[h], one, zero))
                vt[2 * p + h, :64, at] = turned[h * 64 : h * 64 + 64]
                vt[2 * p + h, 64:, at] = jnp.ones((8, rows), bf16)
    store(qkv, qkv_o)
    store(xs, xs_o)

    def attend(p):
        def body(j, carry):
            at = pl.ds(aligned(j * rows, rows), rows)
            out = []
            for h in range(2):
                top, acc = carry[h]
                scores = dot_nt(ka[2 * p + h, at, :], qa[2 * p + h])
                new_top = jnp.maximum(top, jnp.max(scores, axis=0, keepdims=True))
                probs = jnp.exp2(scores - new_top)
                acc = acc * jnp.exp2(top - new_top) + dot(vt[2 * p + h, :, at], probs.astype(bf16))
                out.append((new_top, acc))
            return tuple(out)

        init = tuple((jnp.full((1, full), NEG, f32), jnp.zeros((72, full), f32)) for _ in range(2))
        both = lax.fori_loop(0, parts, body, init)
        pieces = []
        terms = []
        for h in range(2):
            top, acc = both[h]
            total = acc[64:65]
            pieces.append(acc[:64] / total)
            a, b, c = split3(-(top + jnp.log2(total)))
            flat = [jnp.ones((1, full), f32)] + [v.astype(f32) for v in (a, b, c)]
            terms.append(jnp.concatenate(flat + [jnp.zeros((60, full), f32)], 0))
        lse[p] = jnp.concatenate([terms[1], terms[0]], 0).T.astype(bf16)
        mixed[p] = jnp.concatenate(pieces, 0).T.astype(bf16).reshape(parts, rows, 128)
        m_copy(p).start()
        mix[:, :, pl.ds(aligned((2 * core + p) * 128, 128), 128)] = mixed[p, :, here]

    attend(0)
    attend(1)
    store(mixed, mixed_o)
    store(lse, lse_o)

    tile = 512
    tiles = hidden // tile
    small[...] = jnp.zeros_like(small)

    def feed(u):
        chunks = (2 * u, 2 * u + 1)
        keep = jnp.concatenate([below(half, h * rows + core * half) for h in chunks], 0)
        mix_u = mix[2 * u : 2 * u + 2].reshape(rows, width)
        x_u = jnp.concatenate([xs[h, here] for h in chunks], 0)
        attention = dot(mix_u, wo[...])
        unit1, inv1 = normed(x_u.astype(f32) + attention)
        x_mid = unit1 * g1[...] + b1[...]
        mid[u] = x_mid.astype(bf16)
        total = jnp.zeros((rows, width), f32)
        c0 = 0.7978845608028654
        c1 = 0.044715
        for t in range(tiles):
            cols = slice(t * tile, (t + 1) * tile)
            act = dot(mid[u], wu[:, cols]) + bu[:, cols]
            square = act * act
            th = jnp.tanh(act * (c0 + (c0 * c1) * square))
            part = 0.5 * (1.0 + th)
            low = (act * part).astype(bf16)
            hid[u, :, cols] = low
            slope[:rows, cols] = part + (0.5 * act) * (1.0 - th * th) * (c0 + (3.0 * c0 * c1) * square)
            total = total + dot(low, wd[cols, :])
        total = total + bd[...]
        unit2, inv2 = normed(x_mid + total)
        post = jnp.where(keep, unit2 * g2[...] + b2[...], 0.0).astype(bf16)
        added = jnp.where(keep, attention + total, 0.0).astype(bf16)
        post_v[2 * u : 2 * u + 2] = post.reshape(2, half, width)
        added_v[2 * u : 2 * u + 2] = added.reshape(2, half, width)
        for h in chunks:
            out_start(h)
        store(added_v.at[2 * u : 2 * u + 2], added_o.at[2 * u : 2 * u + 2])
        post_c = jnp.where(keep, pcs[2 * u : 2 * u + 2].reshape(rows, width).astype(f32), 0.0)
        accum_c = jnp.where(keep, acs[2 * u : 2 * u + 2].reshape(rows, width).astype(f32), 0.0)
        mid_grad2 = norm_back(post_c * g2[...], unit2, inv2)
        small[2:3, :width] += jnp.sum(post_c * unit2, axis=0, keepdims=True)
        small[3:4, :width] += jnp.sum(post_c, axis=0, keepdims=True)
        feed_grad = (mid_grad2 + accum_c).astype(bf16)
        fgrad[u] = feed_grad
        small[4:5, :width] += jnp.sum(feed_grad.astype(f32), axis=0, keepdims=True)
        back[...] = mid_grad2
        for t in range(tiles):
            cols = slice(t * tile, (t + 1) * tile)
            hidden_grad = dot_nt(fgrad[u], wd[cols, :]).astype(bf16)
            pre_grad = (hidden_grad.astype(f32) * slope[:rows, cols]).astype(bf16)
            pre[u, :, cols] = pre_grad
            small[5:6, cols] += jnp.sum(pre_grad.astype(f32), axis=0, keepdims=True)
            back[...] += dot_nt(pre_grad, wu[:, cols])
        mid_grad = back[...]
        small[0:1, :width] += jnp.sum(mid_grad * unit1, axis=0, keepdims=True)
        small[1:2, :width] += jnp.sum(mid_grad, axis=0, keepdims=True)
        first = norm_back(mid_grad * g1[...], unit1, inv1)
        first_v[2 * u : 2 * u + 2] = first.reshape(2, half, width)
        store(first_v.at[2 * u : 2 * u + 2], first_o.at[2 * u : 2 * u + 2])
        attn_grad = (first + accum_c).astype(bf16)
        agrad[u] = attn_grad
        mgrad[2 * u : 2 * u + 2] = dot_nt(attn_grad, wo[...]).astype(bf16).reshape(2, half, width)
        for p in (0, 1):
            g_copy(p, u).start()
            own = mgrad.at[2 * u : 2 * u + 2, :, pl.ds(aligned((2 * core + p) * 128, 128), 128)]
            store(own, go_o.at[p, 2 * u : 2 * u + 2, here])

    wo_in.wait()
    wu_in.wait()
    wd_in.wait()
    for a in (1, 2):
        for k in range(parts):
            in_wait(a, k)
    for p in (0, 1):
        m_copy(p).wait_recv()
    for u in (0, 1):
        feed(u)

    n, up_rows, vector_rows, total_rows = grad_rows(width, hidden, shards)
    halves = (0, 1)

    def spot_of(shard):
        return lax.rem(core + shard % 2, 2), shard // 2

    edges = (0, up_rows, 2 * up_rows, total_rows)

    def c_copy(i):
        at = slice(edges[i], edges[i + 1])
        return across(grads.at[1, :, at], core_in.at[:, at], (csem.at[0, i], csem.at[1, i]))

    for t in range(tiles):
        cols = slice(t * tile, (t + 1) * tile)
        slope[:width, cols] = sum(dot_tn(mid[u], pre[u, :, cols]) for u in halves)
    for shard in range(shards):
        own = slice(shard * n, (shard + 1) * n)
        block = jnp.concatenate([slope[own, t * tile : (t + 1) * tile] for t in range(tiles)], 0)
        side, spot = spot_of(shard)
        grads[side, spot, :up_rows] = block.astype(bf16)
    c_copy(0).start()
    per = tile // up_rows
    for t in range(tiles):
        cols = slice(t * tile, (t + 1) * tile)
        block = sum(dot_tn(hid[u, :, cols], fgrad[u]) for u in halves).astype(bf16)
        for i in range(per):
            side, spot = spot_of(t * per + i)
            grads[side, spot, up_rows : 2 * up_rows] = block[i * up_rows : (i + 1) * up_rows]
    c_copy(1).start()
    out_all = sum(dot_tn(mix[2 * u : 2 * u + 2].reshape(rows, width), agrad[u]) for u in halves)
    line = lax.broadcasted_iota(jnp.int32, (8, width), 0)
    short = small[:, :width]
    long = small[...]
    for shard in range(shards):
        a = pltpu.roll(short, (width - shard * n) % width, 1)
        b = pltpu.roll(long, (hidden - shard * up_rows) % hidden, 1)[:, :width]
        extra = jnp.where(line == 5, b, a)
        rest = total_rows - 2 * up_rows - n - 8
        block = jnp.concatenate(
            [out_all[shard * n : (shard + 1) * n], extra, jnp.zeros((rest, width), f32)], 0
        )
        side, spot = spot_of(shard)
        grads[side, spot, 2 * up_rows :] = block.astype(bf16)
    c_copy(2).start()
    for i in range(3):
        c_copy(i).wait_recv()

        def add_cores(spot, carry, i=i):
            at = slice(edges[i], edges[i + 1])
            grads[0, spot, at] = (grads[0, spot, at].astype(f32) + core_in[spot, at].astype(f32)).astype(bf16)
            return carry

        lax.fori_loop(0, shards // 2, add_cores, None)
    store(grads.at[0], grads_o)
    for i in range(3):
        c_copy(i).wait_send()

    for a in range(3):
        in_sent(a)
    for k in range(parts):
        pass_on(k).wait_send()
    size_copy.wait_send()
    for p in (0, 1):
        m_copy(p).wait_send()
        for u in (0, 1):
            g_copy(p, u).wait()
    out_wait()
    for copy in stores:
        copy.wait()


def first_call(parts, shards, lengths, streams, weights):
    groups, rows, width = streams[0].shape
    hidden = weights[4].shape[1]
    full = rows * parts
    half = rows // 2
    total_rows = grad_rows(width, hidden, shards)[3]
    held = jax.ShapeDtypeStruct((groups, rows, width), bf16)
    return pl.pallas_call(
        functools.partial(first_kernel, parts, shards),
        in_specs=[SMEM] + [ANY] * 5 + [VMEM, VMEM, ANY, VMEM, ANY, VMEM, VMEM, VMEM],
        out_specs=[ANY] * 9 + [VMEM],
        out_shape=[
            held,
            jax.ShapeDtypeStruct((parts, half, width), bf16),
            jax.ShapeDtypeStruct((parts, half, width), f32),
            jax.ShapeDtypeStruct((2, 3, full, 128), bf16),
            jax.ShapeDtypeStruct((2, full, 128), bf16),
            jax.ShapeDtypeStruct((2, parts, rows, 128), bf16),
            jax.ShapeDtypeStruct((2, parts, rows, 128), bf16),
            jax.ShapeDtypeStruct((parts, rows, width), bf16),
            jax.ShapeDtypeStruct((shards // 2, total_rows, width), bf16),
            jax.ShapeDtypeStruct((8, 128), f32),
        ],
        scratch_shapes=[
            pltpu.VMEM((parts, rows, width), bf16),
            pltpu.VMEM((parts, half, width), bf16),
            pltpu.VMEM((parts, half, width), bf16),
            pltpu.VMEM((width, 768), bf16),
            pltpu.VMEM((2, 3, full, 128), bf16),
            pltpu.VMEM((4, full, 128), bf16),
            pltpu.VMEM((4, full, 128), bf16),
            pltpu.VMEM((4, 72, full), bf16),
            pltpu.VMEM((2, parts, rows, 128), bf16),
            pltpu.VMEM((2, full, 128), bf16),
            pltpu.VMEM((width, width), bf16),
            pltpu.VMEM((width, hidden), bf16),
            pltpu.VMEM((hidden, width), bf16),
            pltpu.VMEM((parts, half, width), bf16),
            pltpu.VMEM((2, rows, hidden), bf16),
            pltpu.VMEM((2, rows, hidden), bf16),
            pltpu.VMEM((max(rows, width), hidden), f32),
            pltpu.VMEM((rows, width), f32),
            pltpu.VMEM((2, rows, width), bf16),
            pltpu.VMEM((2, rows, width), bf16),
            pltpu.VMEM((2, rows, width), bf16),
            pltpu.VMEM((parts, half, width), bf16),
            pltpu.VMEM((parts, half, width), bf16),
            pltpu.VMEM((parts, half, width), bf16),
            pltpu.VMEM((parts, half, width), f32),
            pltpu.VMEM((8, hidden), f32),
            pltpu.VMEM((2, shards // 2, total_rows, width), bf16),
            pltpu.VMEM((shards // 2, total_rows, width), bf16),
            pltpu.VMEM((2, 8, 128), f32),
            DMA((8,)),
            DMA((16,)),
            DMA((5,)),
            DMA((2, 3, 4)),
            DMA((2, parts)),
            DMA((2, 2)),
            DMA((2, 2, 2)),
            DMA((2, 4)),
            DMA((2,)),
            DMA((2, 3)),
        ],
        compiler_params=pltpu.CompilerParams(
            vmem_limit_bytes=VMEM_LIMIT, collective_id=0, has_side_effects=True
        ),
        name="forward_and_feed",
    )(lengths, *streams, *weights)


def second_kernel(
    parts,
    shards,
    grad_norm,
    length_v,
    qkv_h,
    lse_h,
    mixed_h,
    go_h,
    xs_h,
    grads_h,
    first_h,
    added_h,
    wqkv_h,
    dx_o,
    added_o,
    wqkv_o,
    up_o,
    down_o,
    out_o,
    vec_o,
    xs,
    qkv,
    lse,
    mixed,
    go,
    wqkv,
    first,
    grads,
    a1_in,
    b1_in,
    a2_in,
    b2_in,
    z_in,
    all_out,
    all_in,
    final,
    ka,
    va,
    qa,
    da,
    kt,
    qt,
    gt,
    dqt,
    dsend,
    dfull,
    dx_v,
    late,
    late_out,
    late_in,
    late_sum,
    late_step,
    late_got,
    late_all,
    load_sem,
    store_sem,
    self_sem,
    dsem,
    rsem,
    lsem,
    osem,
):
    parts, rows, width = xs.shape
    half_rows = rows // 2
    full = rows * parts
    hidden = up_o.shape[1]
    me = lax.axis_index("head")
    place = lax.axis_index("seq")
    core = lax.rem(place, 2)
    other = place + 1 - 2 * core
    from_core = lax.div(me, 2)
    from_group = lax.rem(me, 2)
    here = pl.ds(aligned(core * half_rows, half_rows), half_rows)
    there = pl.ds(aligned((1 - core) * half_rows, half_rows), half_rows)
    length = length_v[0:1, 0:1]
    lane, mine, base = lane_sets()
    one = jnp.ones((), bf16)
    zero = jnp.zeros((), bf16)
    n, up_rows, vector_rows, total_rows = grad_rows(width, hidden, shards)
    seq_bits = bits_of(shards)
    load_count = itertools.count()

    def load(src, dst):
        copy = pltpu.make_async_copy(src, dst, load_sem.at[next(load_count)])
        copy.start()
        return copy

    def pair_load(p):
        return [
            load(qkv_h.at[p], qkv.at[p]),
            load(go_h.at[p], go.at[p]),
            load(mixed_h.at[p], mixed.at[p]),
            load(lse_h.at[p], lse.at[p]),
        ]

    pair_in = [pair_load(0)]
    grads_in = load(grads_h, grads)
    xs_in = load(xs_h, xs)
    pair_in.append(pair_load(1))
    wqkv_in = load(wqkv_h, wqkv)
    first_in = load(first_h, first)

    enter(plane(me, place, parts) + [(me, flip(place, bit, shards)) for bit in seq_bits[1:]])

    sends = []

    def launch(make, *which):
        make(*which).start()
        sends.append(functools.partial(make, *which))

    spots = shards // 2
    half, quarter = total_rows // 2, total_rows // 4
    eighth = total_rows // 8
    x_bit = lax.rem(me, 2)
    y_bit = lax.div(me, 2)

    def to_head(src, dst, i, k):
        return send(src, dst, (rsem.at[0, i], rsem.at[1, i]), (flip(me, k, parts), place))

    def to_seq(src, dst, i, bit):
        return send(src, dst, (rsem.at[0, i], rsem.at[1, i]), (me, flip(place, bit, shards)))

    a_keep = x_bit * quarter
    a_give = (1 - x_bit) * quarter
    b_keep = half + y_bit * quarter
    b_give = half + (1 - y_bit) * quarter
    a1_copy = lambda: to_head(grads_h.at[:, pl.ds(aligned(a_give, 16), quarter)], a1_in, 1, 1)
    b1_copy = lambda: to_head(grads_h.at[:, pl.ds(aligned(b_give, 16), quarter)], b1_in, 2, 2)
    a_own = a_keep + y_bit * eighth
    a_pass = a_keep + (1 - y_bit) * eighth
    b_own = b_keep + x_bit * eighth
    b_pass = b_keep + (1 - x_bit) * eighth
    a2_copy = lambda: to_head(grads.at[:, pl.ds(aligned(a_pass, 16), eighth)], a2_in, 3, 2)
    b2_copy = lambda: to_head(grads.at[:, pl.ds(aligned(b_pass, 16), eighth)], b2_in, 4, 1)

    def add_rows(into, spot, start, count, other):
        at = pl.ds(aligned(start, 16), count)
        into[spot, at] = (into[spot, at].astype(f32) + other.astype(f32)).astype(bf16)

    def early_first():
        grads_in.wait()
        a1_copy().wait_recv()
        b1_copy().wait_recv()

        def body(i, carry):
            add_rows(grads, i, a_keep, quarter, a1_in[i])
            add_rows(grads, i, b_keep, quarter, b1_in[i])
            return carry

        lax.fori_loop(0, spots, body, None)
        launch(a2_copy)
        launch(b2_copy)

    def early_second_and_on():
        a2_copy().wait_recv()
        b2_copy().wait_recv()

        def body(i, carry):
            add_rows(grads, i, a_own, eighth, a2_in[i])
            add_rows(grads, i, b_own, eighth, b2_in[i])
            return carry

        lax.fori_loop(0, spots, body, None)

        def gather(i, carry):
            all_out[i, :eighth] = grads[i, pl.ds(aligned(a_own, 16), eighth)]
            all_out[i, eighth:] = grads[i, pl.ds(aligned(b_own, 16), eighth)]
            return carry

        lax.fori_loop(0, spots, gather, None)
        if steps:
            z_send(0)

    offsets = []
    at = 0
    size = spots
    for bit in seq_bits[1:]:
        offsets.append((at, size))
        at += size
        size //= 2
    offsets.append((at, 1))
    steps = len(offsets) - 1
    z_offsets = []
    at = 0
    for _, size in offsets[:-1]:
        z_offsets.append(at)
        at += size // 2

    def z_copy(i):
        at, size = offsets[i]
        bit = seq_bits[1 + i]
        return to_seq(
            all_in.at[pl.ds(z_offsets[i], size // 2)], z_in.at[pl.ds(z_offsets[i], size // 2)], 5 + i, bit
        )

    def z_send(i):
        at, size = offsets[i]
        own = lax.rem(lax.div(place, seq_bits[1 + i]), 2)
        for j in range(size // 2):
            all_in[z_offsets[i] + j] = all_out[at + 2 * j + (1 - own)]
        launch(z_copy, i)

    def z_add(i):
        at, size = offsets[i]
        after = offsets[i + 1][0]
        own = lax.rem(lax.div(place, seq_bits[1 + i]), 2)
        z_copy(i).wait_recv()
        for j in range(size // 2):
            all_out[after + j] = (
                all_out[at + 2 * j + own].astype(f32) + z_in[z_offsets[i] + j].astype(f32)
            ).astype(bf16)

    ag_from = 5 + steps
    last = offsets[-1][0]
    ag = sum(size // 2 for _, size in offsets[:-1])

    def ag_copy(k):
        return to_head(all_out.at[last], all_in.at[ag + k], ag_from + k, k)

    def ag_send():
        for k in range(parts - 1, 0, -1):
            launch(ag_copy, k)

    def ag_out():
        moves = [
            (final.at[t * n : (t + 1) * n], up_o.at[:, t * width : (t + 1) * width])
            for t in range(hidden // width)
        ]
        moves.append((final.at[up_rows : 2 * up_rows], down_o))
        moves.append((final.at[2 * up_rows : 2 * up_rows + n], out_o))
        return [pltpu.make_async_copy(src, dst, store_sem.at[i]) for i, (src, dst) in enumerate(moves)]

    def ag_finish():
        for k in range(parts):
            if k:
                ag_copy(k).wait_recv()
                block = all_in[ag + k]
            else:
                block = all_out[last]
            block = block.astype(f32) * grad_norm
            who = flip(me, k, parts)
            x_of, y_of = lax.rem(who, 2), lax.div(who, 2)
            a_at = x_of * quarter + y_of * eighth
            b_at = half + y_of * quarter + x_of * eighth
            final[pl.ds(aligned(a_at, 16), eighth)] = block[:eighth]
            final[pl.ds(aligned(b_at, 16), eighth)] = block[eighth:]
        for copy in ag_out():
            copy.start()
        vec_o[...] = final[2 * up_rows + n : 2 * up_rows + n + 8]

    def d_copy(p, part):
        return send(
            dsend.at[p, part, :, there],
            dfull.at[:, :, pl.ds(aligned(part * width + (2 * core + p) * 128, 128), 128)],
            (dsem.at[0, p, part], dsem.at[1, p, part]),
            (me, other),
        )

    def prepare(p):
        for copy in pair_in[p]:
            copy.wait()
        low_half = lane < 64
        row_of = lax.broadcasted_iota(jnp.int32, (128, 128), 0)
        lane_of = lax.broadcasted_iota(jnp.int32, (128, 128), 1)
        picks = ((row_of < 64) & (lane_of >= 64) & (lane_of < 67)) | ((row_of >= 64) & (lane_of < 3))
        picks = jnp.where(picks, -1.0, 0.0).astype(bf16)
        step = lax.rem(lane, 64)
        kt[...] = qkv[p, 1].T
        qt[...] = qkv[p, 0].T
        gt[...] = go[p].reshape(full, 128).T
        for k in range(parts):
            at = slice(k * rows, (k + 1) * rows)
            query, keys, values = qkv[p, 0, at], qkv[p, 1, at], qkv[p, 2, at]
            pos = lax.broadcasted_iota(jnp.int32, (rows, 1), 0) + k * rows
            bias = jnp.where(pos.astype(f32) < length, 0.0, NEG)
            key_more = jnp.where(step == 0, bias, 1.0).astype(bf16)
            grad = go[p, k]
            prod = grad.astype(f32) * mixed[p, k].astype(f32)
            high = prod.astype(bf16)
            sums = dot(high, picks) + dot((prod - high.astype(f32)).astype(bf16), picks)
            second = sums - sums.astype(bf16).astype(f32)
            third = second - second.astype(bf16).astype(f32)
            grad_more = jnp.where(step == 0, sums, jnp.where(step == 1, second, third)).astype(bf16)
            query_more = lse[p, at]
            ka[0, at] = jnp.where(low_half, keys, key_more)
            ka[1, at] = jnp.where(low_half, key_more, keys)
            va[0, at] = jnp.where(low_half, values, one)
            va[1, at] = jnp.where(low_half, one, values)
            qa[0, at] = jnp.where(low_half, query, query_more)
            qa[1, at] = jnp.where(low_half, query_more, query)
            da[0, at] = jnp.where(low_half, grad, grad_more)
            da[1, at] = jnp.where(low_half, grad_more, grad)
        dqt[...] = jnp.zeros_like(dqt)

    steps_each = 2 * parts
    cols_each = full // 2

    def attend_back(p, events):
        def body(j, carry):
            at = pl.ds(aligned(j * rows, rows), rows)
            totals = [None, None]
            for i in range(2):
                for when, event in events.items():
                    if when % 2 == i:
                        pl.when(j == when // 2)(event)
                cols = slice(i * cols_each, (i + 1) * cols_each)
                for h in range(2):
                    part = slice(h * 64, h * 64 + 64)
                    probs = jnp.exp2(dot_nt(qa[h, cols], ka[h, at, :]))
                    inner = dot_nt(da[h, cols], va[h, at, :])
                    low = probs.astype(bf16)
                    grad = (probs * inner).astype(bf16)
                    dv = dot(gt[part, cols], low)
                    dk = dot(qt[part, cols], grad)
                    dqt[part, cols] += dot_nt(kt[part, at], grad)
                    totals[h] = (dv, dk) if i == 0 else (totals[h][0] + dv, totals[h][1] + dk)
            dv = jnp.concatenate([totals[0][0], totals[1][0]], 0).T
            dk = jnp.concatenate([totals[0][1], totals[1][1]], 0).T
            dsend[p, 1, j] = (dk * (1.0 / LOG2E)).astype(bf16)
            dsend[p, 2, j] = dv.astype(bf16)
            return carry

        lax.fori_loop(0, parts, body, None)
        dsend[p, 0] = (dqt[...] * 64 ** (-0.5)).T.astype(bf16).reshape(parts, rows, 128)
        for part in range(3):
            d_copy(p, part).start()
            dfull[:, :, pl.ds(aligned(part * width + (2 * core + p) * 128, 128), 128)] = dsend[p, part, :, here]

    def late_term(p):
        late[p] = sum(
            dot_tn(xs[k], jnp.concatenate([dsend[p, part, k] for part in range(3)], 1)) for k in range(parts)
        )

    l_sizes = [spots] + [spots >> i for i in range(len(seq_bits) - 1)]
    l_offsets = [0] + [sum(size // 2 for size in l_sizes[1:i]) for i in range(1, len(seq_bits))]

    def l_core(p):
        return send(late_out.at[p], late_in.at[p], (lsem.at[0, p, 0], lsem.at[1, p, 0]), (me, other))

    def l_copy(p, i):
        size = l_sizes[i] // 2
        at = l_offsets[i]
        return send(
            late_step.at[p, pl.ds(at, size)],
            late_got.at[p, pl.ds(at, size)],
            (lsem.at[0, p, i], lsem.at[1, p, i]),
            (me, flip(place, seq_bits[i], shards)),
        )

    l_steps = len(seq_bits)

    def lg_copy(p, k):
        return send(
            late_all.at[p, 0],
            late_all.at[p, k],
            (lsem.at[0, p, l_steps + k], lsem.at[1, p, l_steps + k]),
            (flip(me, k, parts), place),
        )

    def late_start(p):
        for z in range(spots):
            late_out[p, z] = late[p, pl.ds(aligned((2 * z + 1 - core) * n, 8), n)].astype(bf16)
        launch(l_core, p)

    def late_split(p, i):
        own = lax.rem(lax.div(place, seq_bits[i]), 2)
        size = l_sizes[i] // 2
        for j in range(size):
            late_step[p, l_offsets[i] + j] = late_sum[p, 2 * j + 1 - own].astype(bf16)
        launch(l_copy, p, i)

    def late_merge(p, i):
        own = lax.rem(lax.div(place, seq_bits[i]), 2)
        l_copy(p, i).wait_recv()
        for j in range(l_sizes[i] // 2):
            late_sum[p, j] = late_sum[p, 2 * j + own] + late_got[p, l_offsets[i] + j].astype(f32)

    def late_cores(p):
        l_core(p).wait_recv()
        for z in range(spots):
            own = late[p, pl.ds(aligned((2 * z + core) * n, 8), n)]
            late_sum[p, z, :, pl.ds(aligned(core * 384, 128), 384)] = own
            late_sum[p, z, :, pl.ds(aligned((1 - core) * 384, 128), 384)] = late_in[p, z].astype(f32)

    def late_share(p):
        late_all[p, 0] = late_sum[p, 0].astype(bf16)
        for k in range(parts - 1, 0, -1):
            launch(lg_copy, p, k)

    def late_finish(p):
        for k in range(1, parts):
            lg_copy(p, k).wait_recv()
        total = sum(late_all[p, k].astype(f32) for k in range(parts)) * grad_norm
        for owner in range(2):
            for part in range(3):
                to = part * width + (2 * owner + p) * 128
                at = owner * 384 + part * 128
                wqkv_o[:, to : to + 128] = total[:, at : at + 128]

    def late_events(p):
        steps_of = []

        def first_step():
            late_cores(p)
            if l_steps > 1:
                late_split(p, 1)
            else:
                late_share(p)

        steps_of.append(first_step)
        for i in range(1, l_steps):

            def step(i=i):
                late_merge(p, i)
                if i + 1 < l_steps:
                    late_split(p, i + 1)
                else:
                    late_share(p)

            steps_of.append(step)
        return steps_of

    def both_events(one_event, two_event):
        def run():
            one_event()
            two_event()

        return run

    def out_copies(a, h):
        src = (added_h, dx_v)[a].at[h]
        dst = (added_o, dx_o)[a].at[from_group, here]
        remote = send(
            src,
            dst,
            (osem.at[0, a, h], osem.at[1, a, 2 * from_group + core]),
            (h, place - core + from_core),
        )
        local = pltpu.make_async_copy(src, dst, self_sem.at[a])
        return remote, local, (h == me) & (from_core == core)

    def out_start(a):
        for h in range(parts):
            remote, local, own = out_copies(a, h)
            pl.when(own)(local.start)
            pl.when(jnp.logical_not(own))(remote.start)

    def out_wait(a):
        for h in range(parts):
            remote, local, own = out_copies(a, h)
            pl.when(own)(local.wait)
            pl.when(jnp.logical_not(own))(remote.wait_send)
        for s in (0, 1):
            for r in (0, 1):
                chip = 2 * core + s
                dst = (added_o, dx_o)[a].at[s, r * half_rows : (r + 1) * half_rows]
                remote = send(
                    (added_h, dx_v)[a].at[0],
                    dst,
                    (osem.at[0, a, 0], osem.at[1, a, 2 * s + r]),
                    (chip, place - core + r),
                )
                pl.when(jnp.logical_not((chip == me) & (core == r)))(remote.wait_recv)

    def early_second_and_added():
        early_second_and_on()
        out_start(0)

    launch(a1_copy)
    launch(b1_copy)
    prepare(0)
    attend_back(0, {4: early_first, 7: early_second_and_added})
    xs_in.wait()
    late_term(0)
    late_start(0)
    prepare(1)
    early_steps = []
    for i in range(1, steps):

        def early_step(i=i):
            z_add(i - 1)
            z_send(i)

        early_steps.append(early_step)

    def early_last():
        if steps:
            z_add(steps - 1)
        ag_send()

    early_steps.append(early_last)
    events = {}
    later = []

    def schedule(steps_list, slots):
        for index, event in enumerate(steps_list):
            slot = slots[index] if index < len(slots) else steps_each
            if slot >= steps_each:
                later.append(event)
            elif slot in events:
                events[slot] = both_events(events[slot], event)
            else:
                events[slot] = event

    early_steps.append(ag_finish)
    schedule(early_steps, (1, 4, 7))
    schedule(late_events(0), (0, 3, 6))
    attend_back(1, events)
    for event in later:
        event()
    late_term(1)
    late_start(1)
    tail = late_events(1)
    wqkv_in.wait()
    first_in.wait()
    for p in range(2):
        for part in range(3):
            d_copy(p, part).wait_recv()
    tail.pop(0)()
    for h in range(parts):
        dx_v[h] = (first[h] + dot_nt(dfull[h], wqkv[...])).astype(bf16)
    out_start(1)
    for event in tail:
        event()
    late_finish(0)
    late_finish(1)
    for make in sends:
        make().wait_send()
    for p in range(2):
        for part in range(3):
            d_copy(p, part).wait_send()
    out_wait(0)
    out_wait(1)
    for copy in ag_out():
        copy.wait()


def second_call(parts, shards, grad_norm, length, saved, grads, first, added, wqkv, hidden):
    xs_shape = saved[4].shape
    _, rows, width = xs_shape
    full = rows * parts
    half_rows = rows // 2
    n, up_rows, vector_rows, total_rows = grad_rows(width, hidden, shards)
    spots = shards // 2
    quarter, eighth = total_rows // 4, total_rows // 8
    heads = (2, full, 128)
    return pl.pallas_call(
        functools.partial(second_kernel, parts, shards, grad_norm),
        in_specs=[VMEM] + [ANY] * 9,
        out_specs=[ANY, ANY, VMEM, ANY, ANY, ANY, VMEM],
        out_shape=[
            jax.ShapeDtypeStruct((2, rows, width), bf16),
            jax.ShapeDtypeStruct((2, rows, width), bf16),
            jax.ShapeDtypeStruct((n, 3 * width), f32),
            jax.ShapeDtypeStruct((n, hidden), f32),
            jax.ShapeDtypeStruct((up_rows, width), f32),
            jax.ShapeDtypeStruct((n, width), f32),
            jax.ShapeDtypeStruct((8, width), f32),
        ],
        scratch_shapes=[
            pltpu.VMEM(xs_shape, bf16),
            pltpu.VMEM((2, 3, full, 128), bf16),
            pltpu.VMEM((2, full, 128), bf16),
            pltpu.VMEM((2, parts, rows, 128), bf16),
            pltpu.VMEM((2, parts, rows, 128), bf16),
            pltpu.VMEM((width, 3 * width), bf16),
            pltpu.VMEM((parts, half_rows, width), f32),
            pltpu.VMEM((spots, total_rows, width), bf16),
            pltpu.VMEM((spots, quarter, width), bf16),
            pltpu.VMEM((spots, quarter, width), bf16),
            pltpu.VMEM((spots, eighth, width), bf16),
            pltpu.VMEM((spots, eighth, width), bf16),
            pltpu.VMEM((spots, quarter, width), bf16),
            pltpu.VMEM((2 * spots, quarter, width), bf16),
            pltpu.VMEM((spots + parts, quarter, width), bf16),
            pltpu.VMEM((total_rows, width), f32),
            pltpu.VMEM(heads, bf16),
            pltpu.VMEM(heads, bf16),
            pltpu.VMEM(heads, bf16),
            pltpu.VMEM(heads, bf16),
            pltpu.VMEM((128, full), bf16),
            pltpu.VMEM((128, full), bf16),
            pltpu.VMEM((128, full), bf16),
            pltpu.VMEM((128, full), f32),
            pltpu.VMEM((2, 3, parts, rows, 128), bf16),
            pltpu.VMEM((parts, half_rows, 3 * width), bf16),
            pltpu.VMEM((parts, half_rows, width), bf16),
            pltpu.VMEM((2, width, 384), f32),
            pltpu.VMEM((2, spots, n, 384), bf16),
            pltpu.VMEM((2, spots, n, 384), bf16),
            pltpu.VMEM((2, spots, n, 768), f32),
            pltpu.VMEM((2, spots, n, 768), bf16),
            pltpu.VMEM((2, spots, n, 768), bf16),
            pltpu.VMEM((2, parts, n, 768), bf16),
            DMA((16,)),
            DMA((16,)),
            DMA((2,)),
            DMA((2, 2, 3)),
            DMA((2, 24)),
            DMA((2, 2, 16)),
            DMA((2, 2, 4)),
        ],
        compiler_params=pltpu.CompilerParams(
            vmem_limit_bytes=VMEM_LIMIT, collective_id=1, has_side_effects=True
        ),
        name="backward_and_sums",
    )(length, *saved, grads, first, added, wqkv)


def last_kernel(rows_here, lengths, post_h, added_h, dx_h, y, ac, vec, *rest):
    ins, (post_o, accum_o, dx_o, accg_o), outs, vectors = rest[:4], rest[4:8], rest[8:12], rest[12:]
    step = pl.program_id(0)
    for src, dst in zip(ins, outs):
        dst[...] = src[...]

    @pl.when(step == 0)
    def _():
        for i, out in enumerate(vectors):
            out[...] = vec[i : i + 1, : out.shape[1]]

    _, rows, _ = y.shape
    steps = pl.num_programs(0)
    length = lengths[lax.div(step * 2, steps)]
    start = lax.axis_index("head") * rows_here + lax.rem(step, lax.div(steps, 2)) * rows
    keep = lax.broadcasted_iota(jnp.int32, (1, rows, 1), 1) + start < length
    post_o[...] = post_h[...].astype(f32)
    accum_o[...] = jnp.where(keep, y[...].astype(f32) + added_h[...].astype(f32), 0.0)
    dx_o[...] = dx_h[...].astype(f32)
    accg_o[...] = jnp.where(keep, ac[...].astype(f32), 0.0)


def last_call(lengths, tokens, streams, vectors, grads, shards):
    groups, rows, width = tokens[0].shape
    cut = 2
    steps = groups * cut
    block = pl.BlockSpec((1, rows // cut, width), lambda i: (i // cut, i % cut, 0))
    whole = jax.ShapeDtypeStruct((groups, rows, width), f32)
    n = width // shards
    hidden = grads[1].shape[1]
    short = [jax.ShapeDtypeStruct((1, n), f32)] * 5 + [jax.ShapeDtypeStruct((1, hidden // shards), f32)]
    moved = [pl.BlockSpec((g.shape[0], g.shape[1] // steps), lambda i: (0, i)) for g in grads]
    return pl.pallas_call(
        functools.partial(last_kernel, rows),
        grid=(steps,),
        in_specs=[SMEM] + [block] * 5 + [pl.BlockSpec(vectors.shape, lambda i: (0, 0))] + moved,
        out_specs=[block] * 4 + moved + [pl.BlockSpec(o.shape, lambda i: (0, 0)) for o in short],
        out_shape=[whole] * 4 + [jax.ShapeDtypeStruct(g.shape, f32) for g in grads] + short,
        compiler_params=pltpu.CompilerParams(vmem_limit_bytes=VMEM_LIMIT),
        name="outputs",
    )(lengths, *tokens, *streams, vectors, *grads)


def local(
    post_stream,
    accum_stream,
    seq_lengths,
    qkv_weight,
    out_weight,
    norm1_gain,
    norm1_bias,
    up_weight,
    up_bias,
    down_weight,
    down_bias,
    norm2_gain,
    norm2_bias,
    post_cotan,
    accum_cotan,
):
    groups, rows, width = post_stream.shape
    parts = lax.axis_size("head")
    shards = lax.axis_size("seq")
    hidden = up_weight.shape[1]
    grad_norm = float(groups * shards * rows * parts) ** (-0.5)

    def row(vector):
        return vector.reshape(1, -1)

    weights = (
        qkv_weight,
        out_weight,
        row(norm1_gain),
        row(norm1_bias),
        up_weight,
        row(up_bias),
        down_weight,
        row(down_bias),
        row(norm2_gain),
        row(norm2_bias),
    )
    post, added, first, qkv, lse, mixed, go, xs, grads, length = first_call(
        parts, shards, seq_lengths, (post_stream, post_cotan, accum_cotan), weights
    )
    dx, added, qkv_grad, up_grad, down_grad, out_grad, vectors = second_call(
        parts, shards, grad_norm, length, (qkv, lse, mixed, go, xs), grads, first, added, qkv_weight, hidden
    )
    post, accum, post_grad, accum_grad, qkv_grad, up_grad, down_grad, out_grad, *short = last_call(
        seq_lengths,
        (post, added, dx),
        (accum_stream, accum_cotan),
        vectors,
        (qkv_grad, up_grad, down_grad, out_grad),
        shards,
    )
    gain1, bias1, gain2, bias2, down_bias_grad, up_bias_grad = [v.reshape(-1) for v in short]
    return (
        post,
        accum,
        post_grad,
        accum_grad,
        qkv_grad,
        out_grad,
        gain1,
        bias1,
        up_grad,
        up_bias_grad,
        down_grad,
        down_bias_grad,
        gain2,
        bias2,
    )


def solution(mesh):
    tokens = P("seq", "head", None)
    in_specs = (tokens, tokens, P("seq")) + (P(),) * 10 + (tokens, tokens)
    rows = P("seq", None)
    vector = P("seq")
    out_specs = (tokens,) * 4 + (rows, rows, vector, vector, rows, vector, rows, vector, vector, vector)
    return jax.shard_map(local, mesh=mesh, in_specs=in_specs, out_specs=out_specs, check_vma=False)
```

```python
import functools
import itertools

import jax
import jax.numpy as jnp
from jax import lax
from jax.experimental import pallas as pl
from jax.experimental.pallas import tpu as pltpu
from jax.sharding import PartitionSpec as P

H = 8
EPS = 1e-05
NEG = -1e30
LOG2E = 1.4426950408889634
VMEM_LIMIT = 62 * 2**20
bf16 = jnp.bfloat16
f32 = jnp.float32
SMEM = pl.BlockSpec(memory_space=pltpu.SMEM)
VMEM = pl.BlockSpec(memory_space=pltpu.VMEM)
ANY = pl.BlockSpec(memory_space=pl.ANY)
DMA = pltpu.SemaphoreType.DMA


def dot(a, b):
    return jnp.dot(a, b, preferred_element_type=f32)


def dot_nt(a, b):
    return lax.dot_general(a, b, (((1,), (1,)), ((), ())), preferred_element_type=f32)


def dot_tn(a, b):
    return lax.dot_general(a, b, (((0,), (0,)), ((), ())), preferred_element_type=f32)


def split3(value):
    first = value.astype(bf16)
    rest = value - first.astype(f32)
    second = rest.astype(bf16)
    third = (rest - second.astype(f32)).astype(bf16)
    return first, second, third


def lane_sets():
    lane = lax.broadcasted_iota(jnp.int32, (1, 128), 1)
    return lane, (lane < 64, lane >= 64), (64, 0)


def bits_of(count):
    return [1 << b for b in range(count.bit_length() - 1)]


def flip(index, k, count):
    out = 0
    for bit in bits_of(count):
        out = out + (lax.rem(lax.div(index, bit) + (k // bit), 2)) * bit
    return out


def aligned(start, step):
    if isinstance(start, int):
        return start
    return pl.multiple_of(start, step)


def send(src, dst, pair, to):
    return pltpu.make_async_remote_copy(
        src_ref=src,
        dst_ref=dst,
        send_sem=pair[0],
        recv_sem=pair[1],
        device_id=to,
        device_id_type=pl.DeviceIdType.MESH,
    )


def enter(partners):
    barrier = pltpu.get_barrier_semaphore()
    for to in partners:
        pl.semaphore_signal(barrier, inc=1, device_id=to, device_id_type=pl.DeviceIdType.MESH)
    pl.semaphore_wait(barrier, len(partners))


def plane(me, place, parts):
    core = lax.rem(place, 2)
    others = []
    for k in range(parts):
        for other in range(2):
            if k or other:
                seat = place if not other else place + 1 - 2 * core
                others.append((flip(me, k, parts), seat))
    return others


def grad_rows(width, hidden, shards):
    n = width // shards
    up = n * (hidden // width)
    vectors = 16 - n % 16
    total = 2 * up + n + vectors
    return n, up, vectors, -(-total // 128) * 128


def normed(value):
    centre = value - jnp.mean(value, axis=-1, keepdims=True)
    spread = jnp.mean(centre * centre, axis=-1, keepdims=True)
    inv = lax.rsqrt(spread + EPS)
    return centre * inv, inv


def norm_back(cot, unit, inv):
    return (
        cot - jnp.mean(cot, axis=-1, keepdims=True) - unit * jnp.mean(cot * unit, axis=-1, keepdims=True)
    ) * inv


def first_kernel(
    parts,
    shards,
    lengths,
    x,
    pc,
    ac,
    wqkv,
    wo_h,
    g1,
    b1,
    wu_h,
    bu,
    wd_h,
    bd,
    g2,
    b2,
    post_o,
    added_o,
    first_o,
    qkv_o,
    lse_o,
    mixed_o,
    go_o,
    xs_o,
    grads_o,
    length_o,
    xs,
    pcs,
    acs,
    w,
    qkv,
    ka,
    qa,
    vt,
    mixed,
    lse,
    tops,
    accs,
    wo,
    wu,
    wd,
    mix,
    hid,
    pre,
    slope,
    back,
    fgrad,
    mid,
    agrad,
    mgrad,
    post_v,
    added_v,
    first_v,
    small,
    grads,
    core_in,
    sizes,
    load_sem,
    store_sem,
    self_sem,
    insem,
    fsem,
    msem,
    gsem,
    osem,
    nsem,
    csem,
):
    groups, rows, width = x.shape
    hidden = wu.shape[1]
    full = rows * parts
    half = rows // 2
    me = lax.axis_index("head")
    place = lax.axis_index("seq")
    core = lax.rem(place, 2)
    other = place + 1 - 2 * core
    from_core = lax.div(me, 2)
    from_group = lax.rem(me, 2)
    lane, mine, base = lane_sets()
    one = jnp.ones((), bf16)
    zero = jnp.zeros((), bf16)
    here = pl.ds(aligned(core * half, half), half)
    there = pl.ds(aligned((1 - core) * half, half), half)

    load_count = itertools.count()

    def load(src, dst):
        copy = pltpu.make_async_copy(src, dst, load_sem.at[next(load_count)])
        copy.start()
        return copy

    stores = []
    store_count = itertools.count()

    def store(src, dst):
        copy = pltpu.make_async_copy(src, dst, store_sem.at[next(store_count)])
        copy.start()
        stores.append(copy)

    w_in = [
        load(
            wqkv.at[:, pl.ds(aligned(part * width + core * 256, 128), 256)],
            w.at[:, part * 256 : part * 256 + 256],
        )
        for part in range(3)
    ]
    wo_in = load(wo_h, wo)
    wu_in = load(wu_h, wu)
    wd_in = load(wd_h, wd)

    enter(plane(me, place, parts))

    def in_copies(a, twist, r):
        group = from_group if not twist else 1 - from_group
        src = (x, pc, ac)[a].at[group, r * half : (r + 1) * half]
        slot = twist + 2 * lax.rem(from_core + core, 2)
        dst = xs.at[slot, r * half : (r + 1) * half] if a == 0 else (pcs, acs)[a - 1].at[slot]
        sems = (insem.at[0, a, 2 * twist + r], insem.at[1, a, slot])
        remote = send(src, dst, sems, (2 * core + group, place - core + r))
        if twist:
            return remote, None, None
        return remote, pltpu.make_async_copy(src, dst, self_sem.at[a]), (from_core == core) & (core == r)

    def in_start(a, twist):
        for r in (0, 1):
            remote, local, own = in_copies(a, twist, r)
            if twist:
                remote.start()
            else:
                pl.when(own)(local.start)
                pl.when(jnp.logical_not(own))(remote.start)

    def in_sent(a, twist):
        for r in (0, 1):
            remote, local, own = in_copies(a, twist, r)
            if twist:
                remote.wait_send()
            else:
                pl.when(jnp.logical_not(own))(remote.wait_send)

    def in_wait(a, k):
        dst = xs.at[k, here] if a == 0 else (pcs, acs)[a - 1].at[k]
        src = (x, pc, ac)[a].at[0, :half]
        remote = send(src, dst, (insem.at[0, a, 0], insem.at[1, a, k]), (flip(me, k, parts), place))
        if k:
            remote.wait_recv()
        else:
            local = pltpu.make_async_copy(src, dst, self_sem.at[a])
            pl.when(from_core == core)(local.wait)
            pl.when(from_core != core)(remote.wait_recv)

    def across(src, dst, pair):
        return send(src, dst, pair, (me, other))

    def pass_on(k):
        part = xs.at[k, here]
        return across(part, part, (fsem.at[0, k], fsem.at[1, k]))

    size_copy = across(sizes.at[0], sizes.at[1], (nsem.at[0], nsem.at[1]))

    def m_copy(p):
        return across(
            mixed.at[p, :, there],
            mix.at[:, :, pl.ds(aligned((2 * core + p) * 128, 128), 128)],
            (msem.at[0, p], msem.at[1, p]),
        )

    def g_copy(p, u):
        chunks = slice(2 * u, 2 * u + 2)
        return across(
            mgrad.at[chunks, :, pl.ds(aligned((2 * (1 - core) + p) * 128, 128), 128)],
            go_o.at[p, chunks, here],
            (gsem.at[0, p, u], gsem.at[1, p, u]),
        )

    def out_copies(k):
        dst = post_o.at[from_group, here]
        to = (flip(me, k, parts), place - core + from_core)
        remote = send(post_v.at[k], dst, (osem.at[0, k], osem.at[1, 2 * from_group + core]), to)
        return remote, pltpu.make_async_copy(post_v.at[k], dst, self_sem.at[3])

    def out_start(k):
        remote, local = out_copies(k)
        if k:
            remote.start()
        else:
            pl.when(from_core == core)(local.start)
            pl.when(from_core != core)(remote.start)

    def out_wait():
        for k in range(parts):
            remote, local = out_copies(k)
            if k:
                remote.wait_send()
            else:
                pl.when(from_core == core)(local.wait)
                pl.when(from_core != core)(remote.wait_send)
        for s in (0, 1):
            for r in (0, 1):
                chip = 2 * core + s
                dst = post_o.at[s, r * half : (r + 1) * half]
                remote = send(
                    post_v.at[0], dst, (osem.at[0, 0], osem.at[1, 2 * s + r]), (chip, place - core + r)
                )
                pl.when(jnp.logical_not((chip == me) & (core == r)))(remote.wait_recv)

    in_start(0, 0)
    pl.when(from_core == core)(functools.partial(in_start, 0, 1))
    which = lax.broadcasted_iota(jnp.int32, (8, 128), 0)
    sizes[0] = jnp.where(which == 0, lengths[0], lengths[1]).astype(f32)
    size_copy.start()
    for copy in w_in:
        copy.wait()
    size_copy.wait_recv()
    held = jnp.where(from_core == core, sizes[0], sizes[1])
    length = jnp.sum(jnp.where(which == from_group, held, 0.0), axis=0, keepdims=True)
    length_o[...] = jnp.broadcast_to(length, (8, 128))
    length = length[:, :1]

    def below(count, start):
        pos = lax.broadcasted_iota(jnp.int32, (count, 1), 0) + start
        return pos.astype(f32) < length

    @pl.when(from_core != core)
    def _():
        in_sent(0, 0)
        in_start(0, 1)

    def project(k):
        pass_on(k).wait_recv()
        at = slice(k * rows, (k + 1) * rows)
        three = dot(xs[k], w[...])
        bias = jnp.where(below(rows, flip(me, k, parts) * rows), 0.0, NEG)
        step = lax.rem(lane, 64)
        key_more = jnp.where(step == 0, bias, 0.0).astype(bf16)
        query_more = jnp.where(step == 0, one, zero)
        for p in (0, 1):
            cut = slice(p * 128, p * 128 + 128)
            query = (three[:, :256][:, cut] * (LOG2E * 64 ** (-0.5))).astype(bf16)
            keys = three[:, 256:512][:, cut].astype(bf16)
            values = three[:, 512:][:, cut].astype(bf16)
            qkv[p, 0, at] = query
            qkv[p, 1, at] = keys
            qkv[p, 2, at] = values
            turned = values.T
            for h in range(2):
                ka[2 * p + h, at] = jnp.where(mine[h], keys, key_more)
                qa[2 * p + h, at] = jnp.where(mine[h], query, query_more)
                vt[2 * p + h, :64, at] = turned[h * 64 : h * 64 + 64]
                vt[2 * p + h, 64:, at] = jnp.ones((8, rows), bf16)

    def rectangle(p, keys, queries):
        for h in range(2):
            g = 2 * p + h
            scores = dot_nt(ka[g, keys, :], qa[g, queries, :])
            top = tops[g, 0:1, queries]
            new_top = jnp.maximum(top, jnp.max(scores, axis=0, keepdims=True))
            probs = jnp.exp2(scores - new_top)
            tops[g, 0:1, queries] = new_top
            accs[g, :, queries] = accs[g, :, queries] * jnp.exp2(top - new_top) + dot(
                vt[g, :, keys], probs.astype(bf16)
            )

    early = full - rows

    def attend_early(p):
        def body(j, carry):
            rectangle(p, pl.ds(aligned(j * rows, rows), rows), slice(0, early))
            return carry

        lax.fori_loop(0, parts - 1, body, None)

    tops[...] = jnp.full(tops.shape, NEG, f32)
    accs[...] = jnp.zeros_like(accs)
    for k in range(parts - 1):
        in_wait(0, k)
        pass_on(k).start()
    for k in range(parts - 1):
        project(k)
    for a in (1, 2):
        for twist in (0, 1):
            in_start(a, twist)
    attend_early(0)
    in_wait(0, parts - 1)
    pass_on(parts - 1).start()
    attend_early(1)
    project(parts - 1)
    store(qkv, qkv_o)
    store(xs, xs_o)

    def attend(p):
        rectangle(p, slice(early, full), slice(0, full))
        rectangle(p, slice(0, early), slice(early, full))
        pieces = []
        terms = []
        for h in range(2):
            top, acc = tops[2 * p + h, 0:1], accs[2 * p + h]
            total = acc[64:65]
            pieces.append(acc[:64] / total)
            a, b, c = split3(-(top + jnp.log2(total)))
            flat = [jnp.ones((1, full), f32)] + [v.astype(f32) for v in (a, b, c)]
            terms.append(jnp.concatenate(flat + [jnp.zeros((60, full), f32)], 0))
        lse[p] = jnp.concatenate([terms[1], terms[0]], 0).T.astype(bf16)
        mixed[p] = jnp.concatenate(pieces, 0).T.astype(bf16).reshape(parts, rows, 128)
        m_copy(p).start()
        mix[:, :, pl.ds(aligned((2 * core + p) * 128, 128), 128)] = mixed[p, :, here]

    attend(0)
    attend(1)
    store(mixed, mixed_o)
    store(lse, lse_o)

    tile = 512
    tiles = hidden // tile
    small[...] = jnp.zeros_like(small)

    def feed(u):
        chunks = (2 * u, 2 * u + 1)
        keep = jnp.concatenate([below(half, flip(me, k, parts) * rows + core * half) for k in chunks], 0)
        mix_u = mix[2 * u : 2 * u + 2].reshape(rows, width)
        x_u = jnp.concatenate([xs[k, here] for k in chunks], 0)
        attention = dot(mix_u, wo[...])
        unit1, inv1 = normed(x_u.astype(f32) + attention)
        x_mid = unit1 * g1[...] + b1[...]
        mid[u] = x_mid.astype(bf16)
        total = jnp.zeros((rows, width), f32)
        c0 = 0.7978845608028654
        c1 = 0.044715
        for t in range(tiles):
            cols = slice(t * tile, (t + 1) * tile)
            act = dot(mid[u], wu[:, cols]) + bu[:, cols]
            square = act * act
            th = jnp.tanh(act * (c0 + (c0 * c1) * square))
            part = 0.5 + 0.5 * th
            smooth = act * part
            low = smooth.astype(bf16)
            hid[u, :, cols] = low
            slope[:rows, cols] = part + smooth * (1.0 - part) * (2.0 * c0 + (6.0 * c0 * c1) * square)
            total = total + dot(low, wd[cols, :])
        total = total + bd[...]
        unit2, inv2 = normed(x_mid + total)
        post = jnp.where(keep, unit2 * g2[...] + b2[...], 0.0).astype(bf16)
        added = jnp.where(keep, attention + total, 0.0).astype(bf16)
        post_v[2 * u : 2 * u + 2] = post.reshape(2, half, width)
        added_v[2 * u : 2 * u + 2] = added.reshape(2, half, width)
        for k in chunks:
            out_start(k)
        store(added_v.at[2 * u : 2 * u + 2], added_o.at[2 * u : 2 * u + 2])
        post_c = jnp.where(keep, pcs[2 * u : 2 * u + 2].reshape(rows, width).astype(f32), 0.0)
        accum_c = jnp.where(keep, acs[2 * u : 2 * u + 2].reshape(rows, width).astype(f32), 0.0)
        mid_grad2 = norm_back(post_c * g2[...], unit2, inv2)
        small[2:3, :width] += jnp.sum(post_c * unit2, axis=0, keepdims=True)
        small[3:4, :width] += jnp.sum(post_c, axis=0, keepdims=True)
        feed_grad = (mid_grad2 + accum_c).astype(bf16)
        fgrad[u] = feed_grad
        small[4:5, :width] += jnp.sum(feed_grad.astype(f32), axis=0, keepdims=True)
        back[...] = mid_grad2
        for t in range(tiles):
            cols = slice(t * tile, (t + 1) * tile)
            hidden_grad = dot_nt(fgrad[u], wd[cols, :]).astype(bf16)
            pre_grad = (hidden_grad.astype(f32) * slope[:rows, cols]).astype(bf16)
            pre[u, :, cols] = pre_grad
            small[5:6, cols] += jnp.sum(pre_grad.astype(f32), axis=0, keepdims=True)
            back[...] += dot_nt(pre_grad, wu[:, cols])
        mid_grad = back[...]
        small[0:1, :width] += jnp.sum(mid_grad * unit1, axis=0, keepdims=True)
        small[1:2, :width] += jnp.sum(mid_grad, axis=0, keepdims=True)
        first = norm_back(mid_grad * g1[...], unit1, inv1)
        first_v[2 * u : 2 * u + 2] = first.reshape(2, half, width)
        store(first_v.at[2 * u : 2 * u + 2], first_o.at[2 * u : 2 * u + 2])
        attn_grad = (first + accum_c).astype(bf16)
        agrad[u] = attn_grad
        mgrad[2 * u : 2 * u + 2] = dot_nt(attn_grad, wo[...]).astype(bf16).reshape(2, half, width)
        for p in (0, 1):
            g_copy(p, u).start()
            own = mgrad.at[2 * u : 2 * u + 2, :, pl.ds(aligned((2 * core + p) * 128, 128), 128)]
            store(own, go_o.at[p, 2 * u : 2 * u + 2, here])

    wo_in.wait()
    wu_in.wait()
    wd_in.wait()
    for a in (1, 2):
        for k in range(parts):
            in_wait(a, k)
    for p in (0, 1):
        m_copy(p).wait_recv()
    for u in (0, 1):
        feed(u)

    n, up_rows, vector_rows, total_rows = grad_rows(width, hidden, shards)
    halves = (0, 1)

    def spot_of(shard):
        return lax.rem(core + shard % 2, 2), shard // 2

    edges = (0, up_rows, 2 * up_rows, total_rows)

    def c_copy(i):
        at = slice(edges[i], edges[i + 1])
        return across(grads.at[1, :, at], core_in.at[:, at], (csem.at[0, i], csem.at[1, i]))

    for t in range(tiles):
        cols = slice(t * tile, (t + 1) * tile)
        slope[:width, cols] = sum(dot_tn(mid[u], pre[u, :, cols]) for u in halves)
    for shard in range(shards):
        own = slice(shard * n, (shard + 1) * n)
        block = jnp.concatenate([slope[own, t * tile : (t + 1) * tile] for t in range(tiles)], 0)
        side, spot = spot_of(shard)
        grads[side, spot, :up_rows] = block.astype(bf16)
    c_copy(0).start()
    per = tile // up_rows
    for t in range(tiles):
        cols = slice(t * tile, (t + 1) * tile)
        block = sum(dot_tn(hid[u, :, cols], fgrad[u]) for u in halves).astype(bf16)
        for i in range(per):
            side, spot = spot_of(t * per + i)
            grads[side, spot, up_rows : 2 * up_rows] = block[i * up_rows : (i + 1) * up_rows]
    c_copy(1).start()
    out_all = sum(dot_tn(mix[2 * u : 2 * u + 2].reshape(rows, width), agrad[u]) for u in halves)
    line = lax.broadcasted_iota(jnp.int32, (8, width), 0)
    short = small[:, :width]
    long = small[...]
    for shard in range(shards):
        a = pltpu.roll(short, (width - shard * n) % width, 1)
        b = pltpu.roll(long, (hidden - shard * up_rows) % hidden, 1)[:, :width]
        extra = jnp.where(line == 5, b, a)
        rest = total_rows - 2 * up_rows - n - 8
        block = jnp.concatenate(
            [out_all[shard * n : (shard + 1) * n], extra, jnp.zeros((rest, width), f32)], 0
        )
        side, spot = spot_of(shard)
        grads[side, spot, 2 * up_rows :] = block.astype(bf16)
    c_copy(2).start()
    for i in range(3):
        c_copy(i).wait_recv()

        def add_cores(spot, carry, i=i):
            at = slice(edges[i], edges[i + 1])
            grads[0, spot, at] = (grads[0, spot, at].astype(f32) + core_in[spot, at].astype(f32)).astype(bf16)
            return carry

        lax.fori_loop(0, shards // 2, add_cores, None)
    store(grads.at[0], grads_o)
    for i in range(3):
        c_copy(i).wait_send()

    pl.when(from_core == core)(functools.partial(in_sent, 0, 0))
    in_sent(0, 1)
    for a in (1, 2):
        for twist in (0, 1):
            in_sent(a, twist)
    for k in range(parts):
        pass_on(k).wait_send()
    size_copy.wait_send()
    for p in (0, 1):
        m_copy(p).wait_send()
        for u in (0, 1):
            g_copy(p, u).wait()
    out_wait()
    for copy in stores:
        copy.wait()


def first_call(parts, shards, lengths, streams, weights):
    groups, rows, width = streams[0].shape
    hidden = weights[4].shape[1]
    full = rows * parts
    half = rows // 2
    total_rows = grad_rows(width, hidden, shards)[3]
    held = jax.ShapeDtypeStruct((groups, rows, width), bf16)
    return pl.pallas_call(
        functools.partial(first_kernel, parts, shards),
        in_specs=[SMEM] + [ANY] * 5 + [VMEM, VMEM, ANY, VMEM, ANY, VMEM, VMEM, VMEM],
        out_specs=[ANY] * 9 + [VMEM],
        out_shape=[
            held,
            jax.ShapeDtypeStruct((parts, half, width), bf16),
            jax.ShapeDtypeStruct((parts, half, width), f32),
            jax.ShapeDtypeStruct((2, 3, full, 128), bf16),
            jax.ShapeDtypeStruct((2, full, 128), bf16),
            jax.ShapeDtypeStruct((2, parts, rows, 128), bf16),
            jax.ShapeDtypeStruct((2, parts, rows, 128), bf16),
            jax.ShapeDtypeStruct((parts, rows, width), bf16),
            jax.ShapeDtypeStruct((shards // 2, total_rows, width), bf16),
            jax.ShapeDtypeStruct((8, 128), f32),
        ],
        scratch_shapes=[
            pltpu.VMEM((parts, rows, width), bf16),
            pltpu.VMEM((parts, half, width), bf16),
            pltpu.VMEM((parts, half, width), bf16),
            pltpu.VMEM((width, 768), bf16),
            pltpu.VMEM((2, 3, full, 128), bf16),
            pltpu.VMEM((4, full, 128), bf16),
            pltpu.VMEM((4, full, 128), bf16),
            pltpu.VMEM((4, 72, full), bf16),
            pltpu.VMEM((2, parts, rows, 128), bf16),
            pltpu.VMEM((2, full, 128), bf16),
            pltpu.VMEM((4, 8, full), f32),
            pltpu.VMEM((4, 72, full), f32),
            pltpu.VMEM((width, width), bf16),
            pltpu.VMEM((width, hidden), bf16),
            pltpu.VMEM((hidden, width), bf16),
            pltpu.VMEM((parts, half, width), bf16),
            pltpu.VMEM((2, rows, hidden), bf16),
            pltpu.VMEM((2, rows, hidden), bf16),
            pltpu.VMEM((max(rows, width), hidden), f32),
            pltpu.VMEM((rows, width), f32),
            pltpu.VMEM((2, rows, width), bf16),
            pltpu.VMEM((2, rows, width), bf16),
            pltpu.VMEM((2, rows, width), bf16),
            pltpu.VMEM((parts, half, width), bf16),
            pltpu.VMEM((parts, half, width), bf16),
            pltpu.VMEM((parts, half, width), bf16),
            pltpu.VMEM((parts, half, width), f32),
            pltpu.VMEM((8, hidden), f32),
            pltpu.VMEM((2, shards // 2, total_rows, width), bf16),
            pltpu.VMEM((shards // 2, total_rows, width), bf16),
            pltpu.VMEM((2, 8, 128), f32),
            DMA((8,)),
            DMA((16,)),
            DMA((5,)),
            DMA((2, 3, 4)),
            DMA((2, parts)),
            DMA((2, 2)),
            DMA((2, 2, 2)),
            DMA((2, 4)),
            DMA((2,)),
            DMA((2, 3)),
        ],
        compiler_params=pltpu.CompilerParams(
            vmem_limit_bytes=VMEM_LIMIT, collective_id=0, has_side_effects=True
        ),
        name="forward_and_feed",
    )(lengths, *streams, *weights)


def second_kernel(
    parts,
    shards,
    grad_norm,
    length_v,
    qkv_h,
    lse_h,
    mixed_h,
    go_h,
    xs_h,
    grads_h,
    first_h,
    added_h,
    wqkv_h,
    dx_o,
    added_o,
    wqkv_o,
    up_o,
    down_o,
    out_o,
    vec_o,
    xs,
    qkv,
    lse,
    mixed,
    go,
    wqkv,
    first,
    grads,
    a1_in,
    b1_in,
    a2_in,
    b2_in,
    z_in,
    all_out,
    all_in,
    final,
    ka,
    va,
    qa,
    da,
    kt,
    qt,
    gt,
    dqt,
    dsend,
    dfull,
    dx_v,
    late,
    late_out,
    late_in,
    late_sum,
    late_step,
    late_got,
    late_all,
    load_sem,
    store_sem,
    self_sem,
    dsem,
    rsem,
    lsem,
    osem,
):
    parts, rows, width = xs.shape
    half_rows = rows // 2
    full = rows * parts
    hidden = up_o.shape[1]
    me = lax.axis_index("head")
    place = lax.axis_index("seq")
    core = lax.rem(place, 2)
    other = place + 1 - 2 * core
    from_core = lax.div(me, 2)
    from_group = lax.rem(me, 2)
    here = pl.ds(aligned(core * half_rows, half_rows), half_rows)
    there = pl.ds(aligned((1 - core) * half_rows, half_rows), half_rows)
    length = length_v[0:1, 0:1]
    lane, mine, base = lane_sets()
    one = jnp.ones((), bf16)
    zero = jnp.zeros((), bf16)
    n, up_rows, vector_rows, total_rows = grad_rows(width, hidden, shards)
    seq_bits = bits_of(shards)
    load_count = itertools.count()

    def load(src, dst):
        copy = pltpu.make_async_copy(src, dst, load_sem.at[next(load_count)])
        copy.start()
        return copy

    def pair_load(p):
        return [
            load(qkv_h.at[p], qkv.at[p]),
            load(go_h.at[p], go.at[p]),
            load(mixed_h.at[p], mixed.at[p]),
            load(lse_h.at[p], lse.at[p]),
        ]

    pair_in = [pair_load(0)]
    grads_in = load(grads_h, grads)
    xs_in = load(xs_h, xs)
    pair_in.append(pair_load(1))
    wqkv_in = load(wqkv_h, wqkv)
    first_in = load(first_h, first)

    enter(plane(me, place, parts) + [(me, flip(place, bit, shards)) for bit in seq_bits[1:]])

    sends = []

    def launch(make, *which):
        make(*which).start()
        sends.append(functools.partial(make, *which))

    spots = shards // 2
    half, quarter = total_rows // 2, total_rows // 4
    eighth = total_rows // 8
    x_bit = lax.rem(me, 2)
    y_bit = lax.div(me, 2)

    def to_head(src, dst, i, k):
        return send(src, dst, (rsem.at[0, i], rsem.at[1, i]), (flip(me, k, parts), place))

    def to_seq(src, dst, i, bit):
        return send(src, dst, (rsem.at[0, i], rsem.at[1, i]), (me, flip(place, bit, shards)))

    a_keep = x_bit * quarter
    a_give = (1 - x_bit) * quarter
    b_keep = half + y_bit * quarter
    b_give = half + (1 - y_bit) * quarter
    a1_copy = lambda: to_head(grads_h.at[:, pl.ds(aligned(a_give, 16), quarter)], a1_in, 1, 1)
    b1_copy = lambda: to_head(grads_h.at[:, pl.ds(aligned(b_give, 16), quarter)], b1_in, 2, 2)
    a_own = a_keep + y_bit * eighth
    a_pass = a_keep + (1 - y_bit) * eighth
    b_own = b_keep + x_bit * eighth
    b_pass = b_keep + (1 - x_bit) * eighth
    a2_copy = lambda: to_head(grads.at[:, pl.ds(aligned(a_pass, 16), eighth)], a2_in, 3, 2)
    b2_copy = lambda: to_head(grads.at[:, pl.ds(aligned(b_pass, 16), eighth)], b2_in, 4, 1)

    def add_rows(into, spot, start, count, other):
        at = pl.ds(aligned(start, 16), count)
        into[spot, at] = (into[spot, at].astype(f32) + other.astype(f32)).astype(bf16)

    def early_first():
        grads_in.wait()
        a1_copy().wait_recv()
        b1_copy().wait_recv()

        def body(i, carry):
            add_rows(grads, i, a_keep, quarter, a1_in[i])
            add_rows(grads, i, b_keep, quarter, b1_in[i])
            return carry

        lax.fori_loop(0, spots, body, None)
        launch(a2_copy)
        launch(b2_copy)

    def early_second_and_on():
        a2_copy().wait_recv()
        b2_copy().wait_recv()

        def body(i, carry):
            add_rows(grads, i, a_own, eighth, a2_in[i])
            add_rows(grads, i, b_own, eighth, b2_in[i])
            return carry

        lax.fori_loop(0, spots, body, None)

        def gather(i, carry):
            all_out[i, :eighth] = grads[i, pl.ds(aligned(a_own, 16), eighth)]
            all_out[i, eighth:] = grads[i, pl.ds(aligned(b_own, 16), eighth)]
            return carry

        lax.fori_loop(0, spots, gather, None)
        if steps:
            z_send(0)

    offsets = []
    at = 0
    size = spots
    for bit in seq_bits[1:]:
        offsets.append((at, size))
        at += size
        size //= 2
    offsets.append((at, 1))
    steps = len(offsets) - 1
    z_offsets = []
    at = 0
    for _, size in offsets[:-1]:
        z_offsets.append(at)
        at += size // 2

    def z_copy(i):
        at, size = offsets[i]
        bit = seq_bits[1 + i]
        return to_seq(
            all_in.at[pl.ds(z_offsets[i], size // 2)], z_in.at[pl.ds(z_offsets[i], size // 2)], 5 + i, bit
        )

    def z_send(i):
        at, size = offsets[i]
        own = lax.rem(lax.div(place, seq_bits[1 + i]), 2)
        for j in range(size // 2):
            all_in[z_offsets[i] + j] = all_out[at + 2 * j + (1 - own)]
        launch(z_copy, i)

    def z_add(i):
        at, size = offsets[i]
        after = offsets[i + 1][0]
        own = lax.rem(lax.div(place, seq_bits[1 + i]), 2)
        z_copy(i).wait_recv()
        for j in range(size // 2):
            all_out[after + j] = (
                all_out[at + 2 * j + own].astype(f32) + z_in[z_offsets[i] + j].astype(f32)
            ).astype(bf16)

    ag_from = 5 + steps
    last = offsets[-1][0]
    ag = sum(size // 2 for _, size in offsets[:-1])

    def ag_copy(k):
        return to_head(all_out.at[last], all_in.at[ag + k], ag_from + k, k)

    def ag_send():
        for k in range(parts - 1, 0, -1):
            launch(ag_copy, k)

    def ag_out():
        moves = [
            (final.at[t * n : (t + 1) * n], up_o.at[:, t * width : (t + 1) * width])
            for t in range(hidden // width)
        ]
        moves.append((final.at[up_rows : 2 * up_rows], down_o))
        moves.append((final.at[2 * up_rows : 2 * up_rows + n], out_o))
        return [pltpu.make_async_copy(src, dst, store_sem.at[i]) for i, (src, dst) in enumerate(moves)]

    def ag_finish():
        for k in range(parts):
            if k:
                ag_copy(k).wait_recv()
                block = all_in[ag + k]
            else:
                block = all_out[last]
            block = block.astype(f32) * grad_norm
            who = flip(me, k, parts)
            x_of, y_of = lax.rem(who, 2), lax.div(who, 2)
            a_at = x_of * quarter + y_of * eighth
            b_at = half + y_of * quarter + x_of * eighth
            final[pl.ds(aligned(a_at, 16), eighth)] = block[:eighth]
            final[pl.ds(aligned(b_at, 16), eighth)] = block[eighth:]
        for copy in ag_out():
            copy.start()
        vec_o[...] = final[2 * up_rows + n : 2 * up_rows + n + 8]

    def d_copy(p, part):
        return send(
            dsend.at[p, part, :, there],
            dfull.at[:, :, pl.ds(aligned(part * width + (2 * core + p) * 128, 128), 128)],
            (dsem.at[0, p, part], dsem.at[1, p, part]),
            (me, other),
        )

    def prepare(p):
        for copy in pair_in[p]:
            copy.wait()
        low_half = lane < 64
        row_of = lax.broadcasted_iota(jnp.int32, (128, 128), 0)
        lane_of = lax.broadcasted_iota(jnp.int32, (128, 128), 1)
        picks = ((row_of < 64) & (lane_of >= 64) & (lane_of < 67)) | ((row_of >= 64) & (lane_of < 3))
        picks = jnp.where(picks, -1.0, 0.0).astype(bf16)
        step = lax.rem(lane, 64)
        kt[...] = qkv[p, 1].T
        qt[...] = qkv[p, 0].T
        gt[...] = go[p].reshape(full, 128).T
        for k in range(parts):
            at = slice(k * rows, (k + 1) * rows)
            query, keys, values = qkv[p, 0, at], qkv[p, 1, at], qkv[p, 2, at]
            pos = lax.broadcasted_iota(jnp.int32, (rows, 1), 0) + flip(me, k, parts) * rows
            bias = jnp.where(pos.astype(f32) < length, 0.0, NEG)
            key_more = jnp.where(step == 0, bias, 1.0).astype(bf16)
            grad = go[p, k]
            prod = grad.astype(f32) * mixed[p, k].astype(f32)
            high = prod.astype(bf16)
            sums = dot(high, picks) + dot((prod - high.astype(f32)).astype(bf16), picks)
            second = sums - sums.astype(bf16).astype(f32)
            third = second - second.astype(bf16).astype(f32)
            grad_more = jnp.where(step == 0, sums, jnp.where(step == 1, second, third)).astype(bf16)
            query_more = lse[p, at]
            ka[0, at] = jnp.where(low_half, keys, key_more)
            ka[1, at] = jnp.where(low_half, key_more, keys)
            va[0, at] = jnp.where(low_half, values, one)
            va[1, at] = jnp.where(low_half, one, values)
            qa[0, at] = jnp.where(low_half, query, query_more)
            qa[1, at] = jnp.where(low_half, query_more, query)
            da[0, at] = jnp.where(low_half, grad, grad_more)
            da[1, at] = jnp.where(low_half, grad_more, grad)
        dqt[...] = jnp.zeros_like(dqt)

    steps_each = 2 * parts
    cols_each = full // 2

    def attend_back(p, events):
        def body(j, carry):
            at = pl.ds(aligned(j * rows, rows), rows)
            totals = [None, None]
            for i in range(2):
                for when, event in events.items():
                    if when % 2 == i:
                        pl.when(j == when // 2)(event)
                cols = slice(i * cols_each, (i + 1) * cols_each)
                for h in range(2):
                    part = slice(h * 64, h * 64 + 64)
                    probs = jnp.exp2(dot_nt(qa[h, cols], ka[h, at, :]))
                    inner = dot_nt(da[h, cols], va[h, at, :])
                    low = probs.astype(bf16)
                    grad = (probs * inner).astype(bf16)
                    dv = dot(gt[part, cols], low)
                    dk = dot(qt[part, cols], grad)
                    dqt[part, cols] += dot_nt(kt[part, at], grad)
                    totals[h] = (dv, dk) if i == 0 else (totals[h][0] + dv, totals[h][1] + dk)
            dv = jnp.concatenate([totals[0][0], totals[1][0]], 0).T
            dk = jnp.concatenate([totals[0][1], totals[1][1]], 0).T
            dsend[p, 1, j] = (dk * (1.0 / LOG2E)).astype(bf16)
            dsend[p, 2, j] = dv.astype(bf16)
            return carry

        lax.fori_loop(0, parts, body, None)
        dsend[p, 0] = (dqt[...] * 64 ** (-0.5)).T.astype(bf16).reshape(parts, rows, 128)
        for part in range(3):
            d_copy(p, part).start()
            dfull[:, :, pl.ds(aligned(part * width + (2 * core + p) * 128, 128), 128)] = dsend[p, part, :, here]

    def late_term(p):
        late[p] = sum(
            dot_tn(xs[k], jnp.concatenate([dsend[p, part, k] for part in range(3)], 1)) for k in range(parts)
        )

    l_sizes = [spots] + [spots >> i for i in range(len(seq_bits) - 1)]
    l_offsets = [0] + [sum(size // 2 for size in l_sizes[1:i]) for i in range(1, len(seq_bits))]

    def l_core(p):
        return send(late_out.at[p], late_in.at[p], (lsem.at[0, p, 0], lsem.at[1, p, 0]), (me, other))

    def l_copy(p, i):
        size = l_sizes[i] // 2
        at = l_offsets[i]
        return send(
            late_step.at[p, pl.ds(at, size)],
            late_got.at[p, pl.ds(at, size)],
            (lsem.at[0, p, i], lsem.at[1, p, i]),
            (me, flip(place, seq_bits[i], shards)),
        )

    l_steps = len(seq_bits)

    def lg_copy(p, k):
        return send(
            late_all.at[p, 0],
            late_all.at[p, k],
            (lsem.at[0, p, l_steps + k], lsem.at[1, p, l_steps + k]),
            (flip(me, k, parts), place),
        )

    def late_start(p):
        for z in range(spots):
            late_out[p, z] = late[p, pl.ds(aligned((2 * z + 1 - core) * n, 8), n)].astype(bf16)
        launch(l_core, p)

    def late_split(p, i):
        own = lax.rem(lax.div(place, seq_bits[i]), 2)
        size = l_sizes[i] // 2
        for j in range(size):
            late_step[p, l_offsets[i] + j] = late_sum[p, 2 * j + 1 - own].astype(bf16)
        launch(l_copy, p, i)

    def late_merge(p, i):
        own = lax.rem(lax.div(place, seq_bits[i]), 2)
        l_copy(p, i).wait_recv()
        for j in range(l_sizes[i] // 2):
            late_sum[p, j] = late_sum[p, 2 * j + own] + late_got[p, l_offsets[i] + j].astype(f32)

    def late_cores(p):
        l_core(p).wait_recv()
        for z in range(spots):
            own = late[p, pl.ds(aligned((2 * z + core) * n, 8), n)]
            late_sum[p, z, :, pl.ds(aligned(core * 384, 128), 384)] = own
            late_sum[p, z, :, pl.ds(aligned((1 - core) * 384, 128), 384)] = late_in[p, z].astype(f32)

    def late_share(p):
        late_all[p, 0] = late_sum[p, 0].astype(bf16)
        for k in range(parts - 1, 0, -1):
            launch(lg_copy, p, k)

    def late_finish(p):
        for k in range(1, parts):
            lg_copy(p, k).wait_recv()
        total = sum(late_all[p, k].astype(f32) for k in range(parts)) * grad_norm
        for owner in range(2):
            for part in range(3):
                to = part * width + (2 * owner + p) * 128
                at = owner * 384 + part * 128
                wqkv_o[:, to : to + 128] = total[:, at : at + 128]

    def late_events(p):
        steps_of = []

        def first_step():
            late_cores(p)
            if l_steps > 1:
                late_split(p, 1)
            else:
                late_share(p)

        steps_of.append(first_step)
        for i in range(1, l_steps):

            def step(i=i):
                late_merge(p, i)
                if i + 1 < l_steps:
                    late_split(p, i + 1)
                else:
                    late_share(p)

            steps_of.append(step)
        return steps_of

    def both_events(one_event, two_event):
        def run():
            one_event()
            two_event()

        return run

    def out_copies(a, k):
        src = (added_h, dx_v)[a].at[k]
        dst = (added_o, dx_o)[a].at[from_group, here]
        to = (flip(me, k, parts), place - core + from_core)
        remote = send(src, dst, (osem.at[0, a, k], osem.at[1, a, 2 * from_group + core]), to)
        return remote, pltpu.make_async_copy(src, dst, self_sem.at[a])

    def out_start(a):
        for k in range(parts - 1, -1, -1):
            remote, local = out_copies(a, k)
            if k:
                remote.start()
            else:
                pl.when(from_core == core)(local.start)
                pl.when(from_core != core)(remote.start)

    def out_wait(a):
        for k in range(parts):
            remote, local = out_copies(a, k)
            if k:
                remote.wait_send()
            else:
                pl.when(from_core == core)(local.wait)
                pl.when(from_core != core)(remote.wait_send)
        for s in (0, 1):
            for r in (0, 1):
                chip = 2 * core + s
                dst = (added_o, dx_o)[a].at[s, r * half_rows : (r + 1) * half_rows]
                remote = send(
                    (added_h, dx_v)[a].at[0],
                    dst,
                    (osem.at[0, a, 0], osem.at[1, a, 2 * s + r]),
                    (chip, place - core + r),
                )
                pl.when(jnp.logical_not((chip == me) & (core == r)))(remote.wait_recv)

    def early_second_and_added():
        early_second_and_on()
        out_start(0)

    launch(a1_copy)
    launch(b1_copy)
    prepare(0)
    attend_back(0, {6: early_first})
    xs_in.wait()
    late_term(0)
    late_start(0)
    prepare(1)
    early_steps = [early_second_and_added]
    for i in range(1, steps):

        def early_step(i=i):
            z_add(i - 1)
            z_send(i)

        early_steps.append(early_step)

    def early_last():
        if steps:
            z_add(steps - 1)
        ag_send()

    early_steps.append(early_last)
    events = {}
    later = []

    def schedule(steps_list, slots):
        for index, event in enumerate(steps_list):
            slot = slots[index] if index < len(slots) else steps_each
            if slot >= steps_each:
                later.append(event)
            elif slot in events:
                events[slot] = both_events(events[slot], event)
            else:
                events[slot] = event

    schedule(early_steps, (0, 4, 7))
    schedule(late_events(0), (1, 3, 6))
    attend_back(1, events)
    for event in later:
        event()
    late_term(1)
    late_start(1)
    tail = late_events(1)
    wqkv_in.wait()
    first_in.wait()
    for p in range(2):
        for part in range(3):
            d_copy(p, part).wait_recv()
    for k in range(parts):
        dx_v[k] = (first[k] + dot_nt(dfull[k], wqkv[...])).astype(bf16)
    out_start(1)
    tail.pop(0)()
    ag_finish()
    for event in tail:
        event()
    late_finish(0)
    late_finish(1)
    for make in sends:
        make().wait_send()
    for p in range(2):
        for part in range(3):
            d_copy(p, part).wait_send()
    out_wait(0)
    out_wait(1)
    for copy in ag_out():
        copy.wait()


def second_call(parts, shards, grad_norm, length, saved, grads, first, added, wqkv, hidden):
    xs_shape = saved[4].shape
    _, rows, width = xs_shape
    full = rows * parts
    half_rows = rows // 2
    n, up_rows, vector_rows, total_rows = grad_rows(width, hidden, shards)
    spots = shards // 2
    quarter, eighth = total_rows // 4, total_rows // 8
    heads = (2, full, 128)
    return pl.pallas_call(
        functools.partial(second_kernel, parts, shards, grad_norm),
        in_specs=[VMEM] + [ANY] * 9,
        out_specs=[ANY, ANY, VMEM, ANY, ANY, ANY, VMEM],
        out_shape=[
            jax.ShapeDtypeStruct((2, rows, width), bf16),
            jax.ShapeDtypeStruct((2, rows, width), bf16),
            jax.ShapeDtypeStruct((n, 3 * width), f32),
            jax.ShapeDtypeStruct((n, hidden), f32),
            jax.ShapeDtypeStruct((up_rows, width), f32),
            jax.ShapeDtypeStruct((n, width), f32),
            jax.ShapeDtypeStruct((8, width), f32),
        ],
        scratch_shapes=[
            pltpu.VMEM(xs_shape, bf16),
            pltpu.VMEM((2, 3, full, 128), bf16),
            pltpu.VMEM((2, full, 128), bf16),
            pltpu.VMEM((2, parts, rows, 128), bf16),
            pltpu.VMEM((2, parts, rows, 128), bf16),
            pltpu.VMEM((width, 3 * width), bf16),
            pltpu.VMEM((parts, half_rows, width), f32),
            pltpu.VMEM((spots, total_rows, width), bf16),
            pltpu.VMEM((spots, quarter, width), bf16),
            pltpu.VMEM((spots, quarter, width), bf16),
            pltpu.VMEM((spots, eighth, width), bf16),
            pltpu.VMEM((spots, eighth, width), bf16),
            pltpu.VMEM((spots, quarter, width), bf16),
            pltpu.VMEM((2 * spots, quarter, width), bf16),
            pltpu.VMEM((spots + parts, quarter, width), bf16),
            pltpu.VMEM((total_rows, width), f32),
            pltpu.VMEM(heads, bf16),
            pltpu.VMEM(heads, bf16),
            pltpu.VMEM(heads, bf16),
            pltpu.VMEM(heads, bf16),
            pltpu.VMEM((128, full), bf16),
            pltpu.VMEM((128, full), bf16),
            pltpu.VMEM((128, full), bf16),
            pltpu.VMEM((128, full), f32),
            pltpu.VMEM((2, 3, parts, rows, 128), bf16),
            pltpu.VMEM((parts, half_rows, 3 * width), bf16),
            pltpu.VMEM((parts, half_rows, width), bf16),
            pltpu.VMEM((2, width, 384), f32),
            pltpu.VMEM((2, spots, n, 384), bf16),
            pltpu.VMEM((2, spots, n, 384), bf16),
            pltpu.VMEM((2, spots, n, 768), f32),
            pltpu.VMEM((2, spots, n, 768), bf16),
            pltpu.VMEM((2, spots, n, 768), bf16),
            pltpu.VMEM((2, parts, n, 768), bf16),
            DMA((16,)),
            DMA((16,)),
            DMA((2,)),
            DMA((2, 2, 3)),
            DMA((2, 24)),
            DMA((2, 2, 16)),
            DMA((2, 2, 4)),
        ],
        compiler_params=pltpu.CompilerParams(
            vmem_limit_bytes=VMEM_LIMIT, collective_id=1, has_side_effects=True
        ),
        name="backward_and_sums",
    )(length, *saved, grads, first, added, wqkv)


def last_kernel(rows_here, lengths, post_h, added_h, dx_h, y, ac, vec, *rest):
    ins, (post_o, accum_o, dx_o, accg_o), outs, vectors = rest[:4], rest[4:8], rest[8:12], rest[12:]
    step = pl.program_id(0)
    for src, dst in zip(ins, outs):
        dst[...] = src[...]

    @pl.when(step == 0)
    def _():
        for i, out in enumerate(vectors):
            out[...] = vec[i : i + 1, : out.shape[1]]

    _, rows, _ = y.shape
    steps = pl.num_programs(0)
    length = lengths[lax.div(step * 2, steps)]
    start = lax.axis_index("head") * rows_here + lax.rem(step, lax.div(steps, 2)) * rows
    keep = lax.broadcasted_iota(jnp.int32, (1, rows, 1), 1) + start < length
    post_o[...] = post_h[...].astype(f32)
    accum_o[...] = jnp.where(keep, y[...].astype(f32) + added_h[...].astype(f32), 0.0)
    dx_o[...] = dx_h[...].astype(f32)
    accg_o[...] = jnp.where(keep, ac[...].astype(f32), 0.0)


def last_call(lengths, tokens, streams, vectors, grads, shards):
    groups, rows, width = tokens[0].shape
    cut = 2
    steps = groups * cut
    block = pl.BlockSpec((1, rows // cut, width), lambda i: (i // cut, i % cut, 0))
    whole = jax.ShapeDtypeStruct((groups, rows, width), f32)
    n = width // shards
    hidden = grads[1].shape[1]
    short = [jax.ShapeDtypeStruct((1, n), f32)] * 5 + [jax.ShapeDtypeStruct((1, hidden // shards), f32)]
    moved = [pl.BlockSpec((g.shape[0], g.shape[1] // steps), lambda i: (0, i)) for g in grads]
    return pl.pallas_call(
        functools.partial(last_kernel, rows),
        grid=(steps,),
        in_specs=[SMEM] + [block] * 5 + [pl.BlockSpec(vectors.shape, lambda i: (0, 0))] + moved,
        out_specs=[block] * 4 + moved + [pl.BlockSpec(o.shape, lambda i: (0, 0)) for o in short],
        out_shape=[whole] * 4 + [jax.ShapeDtypeStruct(g.shape, f32) for g in grads] + short,
        compiler_params=pltpu.CompilerParams(vmem_limit_bytes=VMEM_LIMIT),
        name="outputs",
    )(lengths, *tokens, *streams, vectors, *grads)


def local(
    post_stream,
    accum_stream,
    seq_lengths,
    qkv_weight,
    out_weight,
    norm1_gain,
    norm1_bias,
    up_weight,
    up_bias,
    down_weight,
    down_bias,
    norm2_gain,
    norm2_bias,
    post_cotan,
    accum_cotan,
):
    groups, rows, width = post_stream.shape
    parts = lax.axis_size("head")
    shards = lax.axis_size("seq")
    hidden = up_weight.shape[1]
    grad_norm = float(groups * shards * rows * parts) ** (-0.5)

    def row(vector):
        return vector.reshape(1, -1)

    weights = (
        qkv_weight,
        out_weight,
        row(norm1_gain),
        row(norm1_bias),
        up_weight,
        row(up_bias),
        down_weight,
        row(down_bias),
        row(norm2_gain),
        row(norm2_bias),
    )
    post, added, first, qkv, lse, mixed, go, xs, grads, length = first_call(
        parts, shards, seq_lengths, (post_stream, post_cotan, accum_cotan), weights
    )
    dx, added, qkv_grad, up_grad, down_grad, out_grad, vectors = second_call(
        parts, shards, grad_norm, length, (qkv, lse, mixed, go, xs), grads, first, added, qkv_weight, hidden
    )
    post, accum, post_grad, accum_grad, qkv_grad, up_grad, down_grad, out_grad, *short = last_call(
        seq_lengths,
        (post, added, dx),
        (accum_stream, accum_cotan),
        vectors,
        (qkv_grad, up_grad, down_grad, out_grad),
        shards,
    )
    gain1, bias1, gain2, bias2, down_bias_grad, up_bias_grad = [v.reshape(-1) for v in short]
    return (
        post,
        accum,
        post_grad,
        accum_grad,
        qkv_grad,
        out_grad,
        gain1,
        bias1,
        up_grad,
        up_bias_grad,
        down_grad,
        down_bias_grad,
        gain2,
        bias2,
    )


def solution(mesh):
    tokens = P("seq", "head", None)
    in_specs = (tokens, tokens, P("seq")) + (P(),) * 10 + (tokens, tokens)
    rows = P("seq", None)
    vector = P("seq")
    out_specs = (tokens,) * 4 + (rows, rows, vector, vector, rows, vector, rows, vector, vector, vector)
    return jax.shard_map(local, mesh=mesh, in_specs=in_specs, out_specs=out_specs, check_vma=False)
```

```python
import functools
import itertools

import jax
import jax.numpy as jnp
from jax import lax
from jax.experimental import pallas as pl
from jax.experimental.pallas import tpu as pltpu
from jax.sharding import PartitionSpec as P

H = 8
EPS = 1e-05
NEG = -1e30
LOG2E = 1.4426950408889634
VMEM_LIMIT = 62 * 2**20
bf16 = jnp.bfloat16
f32 = jnp.float32
SMEM = pl.BlockSpec(memory_space=pltpu.SMEM)
VMEM = pl.BlockSpec(memory_space=pltpu.VMEM)
ANY = pl.BlockSpec(memory_space=pl.ANY)
DMA = pltpu.SemaphoreType.DMA


def dot(a, b):
    return jnp.dot(a, b, preferred_element_type=f32)


def dot_nt(a, b):
    return lax.dot_general(a, b, (((1,), (1,)), ((), ())), preferred_element_type=f32)


def dot_tn(a, b):
    return lax.dot_general(a, b, (((0,), (0,)), ((), ())), preferred_element_type=f32)


def split3(value):
    first = value.astype(bf16)
    rest = value - first.astype(f32)
    second = rest.astype(bf16)
    third = (rest - second.astype(f32)).astype(bf16)
    return first, second, third


def lane_sets():
    lane = lax.broadcasted_iota(jnp.int32, (1, 128), 1)
    return lane, (lane < 64, lane >= 64), (64, 0)


def bits_of(count):
    return [1 << b for b in range(count.bit_length() - 1)]


def flip(index, k, count):
    out = 0
    for bit in bits_of(count):
        out = out + (lax.rem(lax.div(index, bit) + (k // bit), 2)) * bit
    return out


def aligned(start, step):
    if isinstance(start, int):
        return start
    return pl.multiple_of(start, step)


def send(src, dst, pair, to):
    return pltpu.make_async_remote_copy(
        src_ref=src,
        dst_ref=dst,
        send_sem=pair[0],
        recv_sem=pair[1],
        device_id=to,
        device_id_type=pl.DeviceIdType.MESH,
    )


def enter(partners):
    barrier = pltpu.get_barrier_semaphore()
    for to in partners:
        pl.semaphore_signal(barrier, inc=1, device_id=to, device_id_type=pl.DeviceIdType.MESH)
    pl.semaphore_wait(barrier, len(partners))


def plane(me, place, parts):
    core = lax.rem(place, 2)
    others = []
    for k in range(parts):
        for other in range(2):
            if k or other:
                seat = place if not other else place + 1 - 2 * core
                others.append((flip(me, k, parts), seat))
    return others


def grad_rows(width, hidden, shards):
    n = width // shards
    up = n * (hidden // width)
    vectors = 16 - n % 16
    total = 2 * up + n + vectors
    return n, up, vectors, -(-total // 128) * 128


def normed(value):
    centre = value - jnp.mean(value, axis=-1, keepdims=True)
    spread = jnp.mean(centre * centre, axis=-1, keepdims=True)
    inv = lax.rsqrt(spread + EPS)
    return centre * inv, inv


def norm_back(cot, unit, inv):
    return (
        cot - jnp.mean(cot, axis=-1, keepdims=True) - unit * jnp.mean(cot * unit, axis=-1, keepdims=True)
    ) * inv


def first_kernel(
    parts,
    shards,
    lengths,
    x,
    pc,
    ac,
    wqkv,
    wo_h,
    g1,
    b1,
    wu_h,
    bu,
    wd_h,
    bd,
    g2,
    b2,
    post_o,
    added_o,
    first_o,
    qkv_o,
    lse_o,
    mixed_o,
    go_o,
    xs_o,
    grads_o,
    length_o,
    xs,
    pcs,
    acs,
    w,
    qkv,
    ka,
    qa,
    vt,
    mixed,
    lse,
    tops,
    accs,
    wo,
    wu,
    wd,
    mix,
    hid,
    pre,
    slope,
    back,
    fgrad,
    mid,
    agrad,
    mgrad,
    post_v,
    added_v,
    first_v,
    small,
    grads,
    core_in,
    sizes,
    load_sem,
    store_sem,
    self_sem,
    insem,
    fsem,
    msem,
    gsem,
    osem,
    nsem,
    csem,
):
    groups, rows, width = x.shape
    hidden = wu.shape[1]
    full = rows * parts
    half = rows // 2
    me = lax.axis_index("head")
    place = lax.axis_index("seq")
    core = lax.rem(place, 2)
    other = place + 1 - 2 * core
    from_core = lax.div(me, 2)
    from_group = lax.rem(me, 2)
    lane, mine, base = lane_sets()
    one = jnp.ones((), bf16)
    zero = jnp.zeros((), bf16)
    here = pl.ds(aligned(core * half, half), half)
    there = pl.ds(aligned((1 - core) * half, half), half)

    load_count = itertools.count()

    def load(src, dst):
        copy = pltpu.make_async_copy(src, dst, load_sem.at[next(load_count)])
        copy.start()
        return copy

    stores = []
    store_count = itertools.count()

    def store(src, dst):
        copy = pltpu.make_async_copy(src, dst, store_sem.at[next(store_count)])
        copy.start()
        stores.append(copy)

    w_in = [
        load(
            wqkv.at[:, pl.ds(aligned(part * width + core * 256, 128), 256)],
            w.at[:, part * 256 : part * 256 + 256],
        )
        for part in range(3)
    ]
    wo_in = load(wo_h, wo)
    wu_in = load(wu_h, wu)
    wd_in = load(wd_h, wd)

    enter(plane(me, place, parts))

    def in_copies(a, twist, r):
        group = from_group if not twist else 1 - from_group
        src = (x, pc, ac)[a].at[group, r * half : (r + 1) * half]
        slot = twist + 2 * lax.rem(from_core + core, 2)
        dst = xs.at[slot, r * half : (r + 1) * half] if a == 0 else (pcs, acs)[a - 1].at[slot]
        sems = (insem.at[0, a, 2 * twist + r], insem.at[1, a, slot])
        remote = send(src, dst, sems, (2 * core + group, place - core + r))
        if twist:
            return remote, None, None
        return remote, pltpu.make_async_copy(src, dst, self_sem.at[a]), (from_core == core) & (core == r)

    def in_start(a, twist):
        for r in (0, 1):
            remote, local, own = in_copies(a, twist, r)
            if twist:
                remote.start()
            else:
                pl.when(own)(local.start)
                pl.when(jnp.logical_not(own))(remote.start)

    def in_sent(a, twist):
        for r in (0, 1):
            remote, local, own = in_copies(a, twist, r)
            if twist:
                remote.wait_send()
            else:
                pl.when(jnp.logical_not(own))(remote.wait_send)

    def in_wait(a, k):
        dst = xs.at[k, here] if a == 0 else (pcs, acs)[a - 1].at[k]
        src = (x, pc, ac)[a].at[0, :half]
        remote = send(src, dst, (insem.at[0, a, 0], insem.at[1, a, k]), (flip(me, k, parts), place))
        if k:
            remote.wait_recv()
        else:
            local = pltpu.make_async_copy(src, dst, self_sem.at[a])
            pl.when(from_core == core)(local.wait)
            pl.when(from_core != core)(remote.wait_recv)

    def across(src, dst, pair):
        return send(src, dst, pair, (me, other))

    def pass_on(k):
        part = xs.at[k, here]
        return across(part, part, (fsem.at[0, k], fsem.at[1, k]))

    size_copy = across(sizes.at[0], sizes.at[1], (nsem.at[0], nsem.at[1]))

    def m_copy(p):
        return across(
            mixed.at[p, :, there],
            mix.at[:, :, pl.ds(aligned((2 * core + p) * 128, 128), 128)],
            (msem.at[0, p], msem.at[1, p]),
        )

    def g_copy(p, u):
        chunks = slice(2 * u, 2 * u + 2)
        return across(
            mgrad.at[chunks, :, pl.ds(aligned((2 * (1 - core) + p) * 128, 128), 128)],
            go_o.at[p, chunks, here],
            (gsem.at[0, p, u], gsem.at[1, p, u]),
        )

    def out_copies(k):
        dst = post_o.at[from_group, here]
        to = (flip(me, k, parts), place - core + from_core)
        remote = send(post_v.at[k], dst, (osem.at[0, k], osem.at[1, 2 * from_group + core]), to)
        return remote, pltpu.make_async_copy(post_v.at[k], dst, self_sem.at[3])

    def out_start(k):
        remote, local = out_copies(k)
        if k:
            remote.start()
        else:
            pl.when(from_core == core)(local.start)
            pl.when(from_core != core)(remote.start)

    def out_wait():
        for k in range(parts):
            remote, local = out_copies(k)
            if k:
                remote.wait_send()
            else:
                pl.when(from_core == core)(local.wait)
                pl.when(from_core != core)(remote.wait_send)
        for s in (0, 1):
            for r in (0, 1):
                chip = 2 * core + s
                dst = post_o.at[s, r * half : (r + 1) * half]
                remote = send(
                    post_v.at[0], dst, (osem.at[0, 0], osem.at[1, 2 * s + r]), (chip, place - core + r)
                )
                pl.when(jnp.logical_not((chip == me) & (core == r)))(remote.wait_recv)

    in_start(0, 0)
    pl.when(from_core == core)(functools.partial(in_start, 0, 1))
    which = lax.broadcasted_iota(jnp.int32, (8, 128), 0)
    sizes[0] = jnp.where(which == 0, lengths[0], lengths[1]).astype(f32)
    size_copy.start()
    for copy in w_in:
        copy.wait()
    size_copy.wait_recv()
    held = jnp.where(from_core == core, sizes[0], sizes[1])
    length = jnp.sum(jnp.where(which == from_group, held, 0.0), axis=0, keepdims=True)
    length_o[...] = jnp.broadcast_to(length, (8, 128))
    length = length[:, :1]

    def below(count, start):
        pos = lax.broadcasted_iota(jnp.int32, (count, 1), 0) + start
        return pos.astype(f32) < length

    def project(k):
        pass_on(k).wait_recv()
        at = slice(k * rows, (k + 1) * rows)
        three = dot(xs[k], w[...])
        bias = jnp.where(below(rows, flip(me, k, parts) * rows), 0.0, NEG)
        step = lax.rem(lane, 64)
        key_more = jnp.where(step == 0, bias, 0.0).astype(bf16)
        query_more = jnp.where(step == 0, one, zero)
        for p in (0, 1):
            cut = slice(p * 128, p * 128 + 128)
            query = (three[:, :256][:, cut] * (LOG2E * 64 ** (-0.5))).astype(bf16)
            keys = three[:, 256:512][:, cut].astype(bf16)
            values = three[:, 512:][:, cut].astype(bf16)
            qkv[p, 0, at] = query
            qkv[p, 1, at] = keys
            qkv[p, 2, at] = values
            turned = values.T
            for h in range(2):
                ka[2 * p + h, at] = jnp.where(mine[h], keys, key_more)
                qa[2 * p + h, at] = jnp.where(mine[h], query, query_more)
                vt[2 * p + h, :64, at] = turned[h * 64 : h * 64 + 64]
                vt[2 * p + h, 64:, at] = jnp.ones((8, rows), bf16)

    def rectangle(p, keys, queries):
        for h in range(2):
            g = 2 * p + h
            scores = dot_nt(ka[g, keys, :], qa[g, queries, :])
            top = tops[g, 0:1, queries]
            new_top = jnp.maximum(top, jnp.max(scores, axis=0, keepdims=True))
            probs = jnp.exp2(scores - new_top)
            tops[g, 0:1, queries] = new_top
            accs[g, :, queries] = accs[g, :, queries] * jnp.exp2(top - new_top) + dot(
                vt[g, :, keys], probs.astype(bf16)
            )

    early = full - rows

    def attend_early(p):
        def body(j, carry):
            rectangle(p, pl.ds(aligned(j * rows, rows), rows), slice(rows, early))
            return carry

        rectangle(p, slice(rows, early), slice(0, rows))
        lax.fori_loop(0, parts - 1, body, None)

    tops[...] = jnp.full(tops.shape, NEG, f32)
    accs[...] = jnp.zeros_like(accs)
    in_wait(0, 0)
    pass_on(0).start()
    project(0)

    @pl.when(from_core != core)
    def _():
        in_sent(0, 0)
        in_start(0, 1)

    for p in (0, 1):
        rectangle(p, slice(0, rows), slice(0, rows))
    for k in range(1, parts - 1):
        in_wait(0, k)
        pass_on(k).start()
    for k in range(1, parts - 1):
        project(k)
    for a in (1, 2):
        for twist in (0, 1):
            in_start(a, twist)
    attend_early(0)
    in_wait(0, parts - 1)
    pass_on(parts - 1).start()
    attend_early(1)
    project(parts - 1)
    store(qkv, qkv_o)
    store(xs, xs_o)

    def attend(p):
        rectangle(p, slice(early, full), slice(0, full))
        rectangle(p, slice(0, early), slice(early, full))
        pieces = []
        terms = []
        for h in range(2):
            top, acc = tops[2 * p + h, 0:1], accs[2 * p + h]
            total = acc[64:65]
            pieces.append(acc[:64] / total)
            a, b, c = split3(-(top + jnp.log2(total)))
            flat = [jnp.ones((1, full), f32)] + [v.astype(f32) for v in (a, b, c)]
            terms.append(jnp.concatenate(flat + [jnp.zeros((60, full), f32)], 0))
        lse[p] = jnp.concatenate([terms[1], terms[0]], 0).T.astype(bf16)
        mixed[p] = jnp.concatenate(pieces, 0).T.astype(bf16).reshape(parts, rows, 128)
        m_copy(p).start()
        mix[:, :, pl.ds(aligned((2 * core + p) * 128, 128), 128)] = mixed[p, :, here]

    attend(0)
    attend(1)
    store(mixed, mixed_o)
    store(lse, lse_o)

    tile = 512
    tiles = hidden // tile
    small[...] = jnp.zeros_like(small)

    def feed(u):
        chunks = (2 * u, 2 * u + 1)
        keep = jnp.concatenate([below(half, flip(me, k, parts) * rows + core * half) for k in chunks], 0)
        mix_u = mix[2 * u : 2 * u + 2].reshape(rows, width)
        x_u = jnp.concatenate([xs[k, here] for k in chunks], 0)
        attention = dot(mix_u, wo[...])
        unit1, inv1 = normed(x_u.astype(f32) + attention)
        x_mid = unit1 * g1[...] + b1[...]
        mid[u] = x_mid.astype(bf16)
        total = jnp.zeros((rows, width), f32)
        c0 = 0.7978845608028654
        c1 = 0.044715
        for t in range(tiles):
            cols = slice(t * tile, (t + 1) * tile)
            act = dot(mid[u], wu[:, cols]) + bu[:, cols]
            square = act * act
            th = jnp.tanh(act * (c0 + (c0 * c1) * square))
            part = 0.5 + 0.5 * th
            smooth = act * part
            low = smooth.astype(bf16)
            hid[u, :, cols] = low
            slope[:rows, cols] = part + smooth * (1.0 - part) * (2.0 * c0 + (6.0 * c0 * c1) * square)
            total = total + dot(low, wd[cols, :])
        total = total + bd[...]
        unit2, inv2 = normed(x_mid + total)
        post = jnp.where(keep, unit2 * g2[...] + b2[...], 0.0).astype(bf16)
        added = jnp.where(keep, attention + total, 0.0).astype(bf16)
        post_v[2 * u : 2 * u + 2] = post.reshape(2, half, width)
        added_v[2 * u : 2 * u + 2] = added.reshape(2, half, width)
        for k in chunks:
            out_start(k)
        store(added_v.at[2 * u : 2 * u + 2], added_o.at[2 * u : 2 * u + 2])
        post_c = jnp.where(keep, pcs[2 * u : 2 * u + 2].reshape(rows, width).astype(f32), 0.0)
        accum_c = jnp.where(keep, acs[2 * u : 2 * u + 2].reshape(rows, width).astype(f32), 0.0)
        mid_grad2 = norm_back(post_c * g2[...], unit2, inv2)
        small[2:3, :width] += jnp.sum(post_c * unit2, axis=0, keepdims=True)
        small[3:4, :width] += jnp.sum(post_c, axis=0, keepdims=True)
        feed_grad = (mid_grad2 + accum_c).astype(bf16)
        fgrad[u] = feed_grad
        small[4:5, :width] += jnp.sum(feed_grad.astype(f32), axis=0, keepdims=True)
        back[...] = mid_grad2
        for t in range(tiles):
            cols = slice(t * tile, (t + 1) * tile)
            hidden_grad = dot_nt(fgrad[u], wd[cols, :]).astype(bf16)
            pre_grad = (hidden_grad.astype(f32) * slope[:rows, cols]).astype(bf16)
            pre[u, :, cols] = pre_grad
            small[5:6, cols] += jnp.sum(pre_grad.astype(f32), axis=0, keepdims=True)
            back[...] += dot_nt(pre_grad, wu[:, cols])
        mid_grad = back[...]
        small[0:1, :width] += jnp.sum(mid_grad * unit1, axis=0, keepdims=True)
        small[1:2, :width] += jnp.sum(mid_grad, axis=0, keepdims=True)
        first = norm_back(mid_grad * g1[...], unit1, inv1)
        first_v[2 * u : 2 * u + 2] = first.reshape(2, half, width)
        store(first_v.at[2 * u : 2 * u + 2], first_o.at[2 * u : 2 * u + 2])
        attn_grad = (first + accum_c).astype(bf16)
        agrad[u] = attn_grad
        mgrad[2 * u : 2 * u + 2] = dot_nt(attn_grad, wo[...]).astype(bf16).reshape(2, half, width)
        for p in (0, 1):
            g_copy(p, u).start()
            own = mgrad.at[2 * u : 2 * u + 2, :, pl.ds(aligned((2 * core + p) * 128, 128), 128)]
            store(own, go_o.at[p, 2 * u : 2 * u + 2, here])

    wo_in.wait()
    wu_in.wait()
    wd_in.wait()
    for a in (1, 2):
        for k in range(parts):
            in_wait(a, k)
    for p in (0, 1):
        m_copy(p).wait_recv()
    for u in (0, 1):
        feed(u)

    n, up_rows, vector_rows, total_rows = grad_rows(width, hidden, shards)
    halves = (0, 1)

    def spot_of(shard):
        return lax.rem(core + shard % 2, 2), shard // 2

    edges = (0, up_rows, 2 * up_rows, total_rows)

    def c_copy(i):
        at = slice(edges[i], edges[i + 1])
        return across(grads.at[1, :, at], core_in.at[:, at], (csem.at[0, i], csem.at[1, i]))

    for t in range(tiles):
        cols = slice(t * tile, (t + 1) * tile)
        slope[:width, cols] = sum(dot_tn(mid[u], pre[u, :, cols]) for u in halves)
    for shard in range(shards):
        own = slice(shard * n, (shard + 1) * n)
        block = jnp.concatenate([slope[own, t * tile : (t + 1) * tile] for t in range(tiles)], 0)
        side, spot = spot_of(shard)
        grads[side, spot, :up_rows] = block.astype(bf16)
    c_copy(0).start()
    per = tile // up_rows
    for t in range(tiles):
        cols = slice(t * tile, (t + 1) * tile)
        block = sum(dot_tn(hid[u, :, cols], fgrad[u]) for u in halves).astype(bf16)
        for i in range(per):
            side, spot = spot_of(t * per + i)
            grads[side, spot, up_rows : 2 * up_rows] = block[i * up_rows : (i + 1) * up_rows]
    c_copy(1).start()
    out_all = sum(dot_tn(mix[2 * u : 2 * u + 2].reshape(rows, width), agrad[u]) for u in halves)
    line = lax.broadcasted_iota(jnp.int32, (8, width), 0)
    short = small[:, :width]
    long = small[...]
    for shard in range(shards):
        a = pltpu.roll(short, (width - shard * n) % width, 1)
        b = pltpu.roll(long, (hidden - shard * up_rows) % hidden, 1)[:, :width]
        extra = jnp.where(line == 5, b, a)
        rest = total_rows - 2 * up_rows - n - 8
        block = jnp.concatenate(
            [out_all[shard * n : (shard + 1) * n], extra, jnp.zeros((rest, width), f32)], 0
        )
        side, spot = spot_of(shard)
        grads[side, spot, 2 * up_rows :] = block.astype(bf16)
    c_copy(2).start()
    for i in range(3):
        c_copy(i).wait_recv()

        def add_cores(spot, carry, i=i):
            at = slice(edges[i], edges[i + 1])
            grads[0, spot, at] = (grads[0, spot, at].astype(f32) + core_in[spot, at].astype(f32)).astype(bf16)
            return carry

        lax.fori_loop(0, shards // 2, add_cores, None)
    store(grads.at[0], grads_o)
    for i in range(3):
        c_copy(i).wait_send()

    pl.when(from_core == core)(functools.partial(in_sent, 0, 0))
    in_sent(0, 1)
    for a in (1, 2):
        for twist in (0, 1):
            in_sent(a, twist)
    for k in range(parts):
        pass_on(k).wait_send()
    size_copy.wait_send()
    for p in (0, 1):
        m_copy(p).wait_send()
        for u in (0, 1):
            g_copy(p, u).wait()
    out_wait()
    for copy in stores:
        copy.wait()


def first_call(parts, shards, lengths, streams, weights):
    groups, rows, width = streams[0].shape
    hidden = weights[4].shape[1]
    full = rows * parts
    half = rows // 2
    total_rows = grad_rows(width, hidden, shards)[3]
    held = jax.ShapeDtypeStruct((groups, rows, width), bf16)
    return pl.pallas_call(
        functools.partial(first_kernel, parts, shards),
        in_specs=[SMEM] + [ANY] * 5 + [VMEM, VMEM, ANY, VMEM, ANY, VMEM, VMEM, VMEM],
        out_specs=[ANY] * 9 + [VMEM],
        out_shape=[
            held,
            jax.ShapeDtypeStruct((parts, half, width), bf16),
            jax.ShapeDtypeStruct((parts, half, width), f32),
            jax.ShapeDtypeStruct((2, 3, full, 128), bf16),
            jax.ShapeDtypeStruct((2, full, 128), bf16),
            jax.ShapeDtypeStruct((2, parts, rows, 128), bf16),
            jax.ShapeDtypeStruct((2, parts, rows, 128), bf16),
            jax.ShapeDtypeStruct((parts, rows, width), bf16),
            jax.ShapeDtypeStruct((shards // 2, total_rows, width), bf16),
            jax.ShapeDtypeStruct((8, 128), f32),
        ],
        scratch_shapes=[
            pltpu.VMEM((parts, rows, width), bf16),
            pltpu.VMEM((parts, half, width), bf16),
            pltpu.VMEM((parts, half, width), bf16),
            pltpu.VMEM((width, 768), bf16),
            pltpu.VMEM((2, 3, full, 128), bf16),
            pltpu.VMEM((4, full, 128), bf16),
            pltpu.VMEM((4, full, 128), bf16),
            pltpu.VMEM((4, 72, full), bf16),
            pltpu.VMEM((2, parts, rows, 128), bf16),
            pltpu.VMEM((2, full, 128), bf16),
            pltpu.VMEM((4, 8, full), f32),
            pltpu.VMEM((4, 72, full), f32),
            pltpu.VMEM((width, width), bf16),
            pltpu.VMEM((width, hidden), bf16),
            pltpu.VMEM((hidden, width), bf16),
            pltpu.VMEM((parts, half, width), bf16),
            pltpu.VMEM((2, rows, hidden), bf16),
            pltpu.VMEM((2, rows, hidden), bf16),
            pltpu.VMEM((max(rows, width), hidden), f32),
            pltpu.VMEM((rows, width), f32),
            pltpu.VMEM((2, rows, width), bf16),
            pltpu.VMEM((2, rows, width), bf16),
            pltpu.VMEM((2, rows, width), bf16),
            pltpu.VMEM((parts, half, width), bf16),
            pltpu.VMEM((parts, half, width), bf16),
            pltpu.VMEM((parts, half, width), bf16),
            pltpu.VMEM((parts, half, width), f32),
            pltpu.VMEM((8, hidden), f32),
            pltpu.VMEM((2, shards // 2, total_rows, width), bf16),
            pltpu.VMEM((shards // 2, total_rows, width), bf16),
            pltpu.VMEM((2, 8, 128), f32),
            DMA((8,)),
            DMA((16,)),
            DMA((5,)),
            DMA((2, 3, 4)),
            DMA((2, parts)),
            DMA((2, 2)),
            DMA((2, 2, 2)),
            DMA((2, 4)),
            DMA((2,)),
            DMA((2, 3)),
        ],
        compiler_params=pltpu.CompilerParams(
            vmem_limit_bytes=VMEM_LIMIT, collective_id=0, has_side_effects=True
        ),
        name="forward_and_feed",
    )(lengths, *streams, *weights)


def second_kernel(
    parts,
    shards,
    grad_norm,
    length_v,
    qkv_h,
    lse_h,
    mixed_h,
    go_h,
    xs_h,
    grads_h,
    first_h,
    added_h,
    wqkv_h,
    dx_o,
    added_o,
    wqkv_o,
    up_o,
    down_o,
    out_o,
    vec_o,
    xs,
    qkv,
    lse,
    mixed,
    go,
    wqkv,
    first,
    grads,
    a1_in,
    b1_in,
    a2_in,
    b2_in,
    z_in,
    all_out,
    all_in,
    final,
    ka,
    va,
    qa,
    da,
    kt,
    qt,
    gt,
    dqt,
    dsend,
    dfull,
    dx_v,
    late,
    late_out,
    late_sum,
    late_step,
    late_got,
    late_all,
    load_sem,
    store_sem,
    self_sem,
    dsem,
    rsem,
    lsem,
    osem,
):
    parts, rows, width = xs.shape
    half_rows = rows // 2
    full = rows * parts
    hidden = up_o.shape[1]
    me = lax.axis_index("head")
    place = lax.axis_index("seq")
    core = lax.rem(place, 2)
    other = place + 1 - 2 * core
    from_core = lax.div(me, 2)
    from_group = lax.rem(me, 2)
    here = pl.ds(aligned(core * half_rows, half_rows), half_rows)
    there = pl.ds(aligned((1 - core) * half_rows, half_rows), half_rows)
    length = length_v[0:1, 0:1]
    lane, mine, base = lane_sets()
    one = jnp.ones((), bf16)
    zero = jnp.zeros((), bf16)
    n, up_rows, vector_rows, total_rows = grad_rows(width, hidden, shards)
    seq_bits = bits_of(shards)
    load_count = itertools.count()

    def load(src, dst):
        copy = pltpu.make_async_copy(src, dst, load_sem.at[next(load_count)])
        copy.start()
        return copy

    def pair_load(p):
        return [
            load(qkv_h.at[p], qkv.at[p]),
            load(go_h.at[p], go.at[p]),
            load(mixed_h.at[p], mixed.at[p]),
            load(lse_h.at[p], lse.at[p]),
        ]

    pair_in = [pair_load(0)]
    grads_in = load(grads_h, grads)
    xs_in = load(xs_h, xs)
    pair_in.append(pair_load(1))
    wqkv_in = load(wqkv_h, wqkv)
    first_in = load(first_h, first)

    enter(plane(me, place, parts) + [(me, flip(place, bit, shards)) for bit in seq_bits[1:]])

    sends = []

    def launch(make, *which):
        make(*which).start()
        sends.append(functools.partial(make, *which))

    spots = shards // 2
    half, quarter = total_rows // 2, total_rows // 4
    eighth = total_rows // 8
    x_bit = lax.rem(me, 2)
    y_bit = lax.div(me, 2)

    def to_head(src, dst, i, k):
        return send(src, dst, (rsem.at[0, i], rsem.at[1, i]), (flip(me, k, parts), place))

    def to_seq(src, dst, i, bit):
        return send(src, dst, (rsem.at[0, i], rsem.at[1, i]), (me, flip(place, bit, shards)))

    a_keep = x_bit * quarter
    a_give = (1 - x_bit) * quarter
    b_keep = half + y_bit * quarter
    b_give = half + (1 - y_bit) * quarter
    a1_copy = lambda: to_head(grads_h.at[:, pl.ds(aligned(a_give, 16), quarter)], a1_in, 1, 1)
    b1_copy = lambda: to_head(grads_h.at[:, pl.ds(aligned(b_give, 16), quarter)], b1_in, 2, 2)
    a_own = a_keep + y_bit * eighth
    a_pass = a_keep + (1 - y_bit) * eighth
    b_own = b_keep + x_bit * eighth
    b_pass = b_keep + (1 - x_bit) * eighth
    a2_copy = lambda: to_head(grads.at[:, pl.ds(aligned(a_pass, 16), eighth)], a2_in, 3, 2)
    b2_copy = lambda: to_head(grads.at[:, pl.ds(aligned(b_pass, 16), eighth)], b2_in, 4, 1)

    def add_rows(into, spot, start, count, other):
        at = pl.ds(aligned(start, 16), count)
        into[spot, at] = (into[spot, at].astype(f32) + other.astype(f32)).astype(bf16)

    def early_first():
        grads_in.wait()
        a1_copy().wait_recv()
        b1_copy().wait_recv()

        def body(i, carry):
            add_rows(grads, i, a_keep, quarter, a1_in[i])
            add_rows(grads, i, b_keep, quarter, b1_in[i])
            return carry

        lax.fori_loop(0, spots, body, None)
        launch(a2_copy)
        launch(b2_copy)

    def early_second_and_on():
        a2_copy().wait_recv()
        b2_copy().wait_recv()

        def body(i, carry):
            add_rows(grads, i, a_own, eighth, a2_in[i])
            add_rows(grads, i, b_own, eighth, b2_in[i])
            return carry

        lax.fori_loop(0, spots, body, None)

        def gather(i, carry):
            all_out[i, :eighth] = grads[i, pl.ds(aligned(a_own, 16), eighth)]
            all_out[i, eighth:] = grads[i, pl.ds(aligned(b_own, 16), eighth)]
            return carry

        lax.fori_loop(0, spots, gather, None)
        if steps:
            z_send(0)

    offsets = []
    at = 0
    size = spots
    for bit in seq_bits[1:]:
        offsets.append((at, size))
        at += size
        size //= 2
    offsets.append((at, 1))
    steps = len(offsets) - 1
    z_offsets = []
    at = 0
    for _, size in offsets[:-1]:
        z_offsets.append(at)
        at += size // 2

    def z_copy(i):
        at, size = offsets[i]
        bit = seq_bits[1 + i]
        return to_seq(
            all_in.at[pl.ds(z_offsets[i], size // 2)], z_in.at[pl.ds(z_offsets[i], size // 2)], 5 + i, bit
        )

    def z_send(i):
        at, size = offsets[i]
        own = lax.rem(lax.div(place, seq_bits[1 + i]), 2)
        for j in range(size // 2):
            all_in[z_offsets[i] + j] = all_out[at + 2 * j + (1 - own)]
        launch(z_copy, i)

    def z_add(i):
        at, size = offsets[i]
        after = offsets[i + 1][0]
        own = lax.rem(lax.div(place, seq_bits[1 + i]), 2)
        z_copy(i).wait_recv()
        for j in range(size // 2):
            all_out[after + j] = (
                all_out[at + 2 * j + own].astype(f32) + z_in[z_offsets[i] + j].astype(f32)
            ).astype(bf16)

    ag_from = 5 + steps
    last = offsets[-1][0]
    ag = sum(size // 2 for _, size in offsets[:-1])

    def ag_copy(k):
        return to_head(all_out.at[last], all_in.at[ag + k], ag_from + k, k)

    def ag_send():
        for k in range(parts - 1, 0, -1):
            launch(ag_copy, k)

    def ag_out():
        moves = [
            (final.at[t * n : (t + 1) * n], up_o.at[:, t * width : (t + 1) * width])
            for t in range(hidden // width)
        ]
        moves.append((final.at[up_rows : 2 * up_rows], down_o))
        moves.append((final.at[2 * up_rows : 2 * up_rows + n], out_o))
        return [pltpu.make_async_copy(src, dst, store_sem.at[i]) for i, (src, dst) in enumerate(moves)]

    def ag_finish():
        for k in range(parts):
            if k:
                ag_copy(k).wait_recv()
                block = all_in[ag + k]
            else:
                block = all_out[last]
            block = block.astype(f32) * grad_norm
            who = flip(me, k, parts)
            x_of, y_of = lax.rem(who, 2), lax.div(who, 2)
            a_at = x_of * quarter + y_of * eighth
            b_at = half + y_of * quarter + x_of * eighth
            final[pl.ds(aligned(a_at, 16), eighth)] = block[:eighth]
            final[pl.ds(aligned(b_at, 16), eighth)] = block[eighth:]
        for copy in ag_out():
            copy.start()
        vec_o[...] = final[2 * up_rows + n : 2 * up_rows + n + 8]

    def d_copy(p, part):
        return send(
            dsend.at[p, part, :, there],
            dfull.at[:, :, pl.ds(aligned(part * width + (2 * core + p) * 128, 128), 128)],
            (dsem.at[0, p, part], dsem.at[1, p, part]),
            (me, other),
        )

    def prepare(p):
        for copy in pair_in[p]:
            copy.wait()
        low_half = lane < 64
        row_of = lax.broadcasted_iota(jnp.int32, (128, 128), 0)
        lane_of = lax.broadcasted_iota(jnp.int32, (128, 128), 1)
        picks = ((row_of < 64) & (lane_of >= 64) & (lane_of < 67)) | ((row_of >= 64) & (lane_of < 3))
        picks = jnp.where(picks, -1.0, 0.0).astype(bf16)
        step = lax.rem(lane, 64)
        kt[...] = qkv[p, 1].T
        qt[...] = qkv[p, 0].T
        gt[...] = go[p].reshape(full, 128).T
        for k in range(parts):
            at = slice(k * rows, (k + 1) * rows)
            query, keys, values = qkv[p, 0, at], qkv[p, 1, at], qkv[p, 2, at]
            pos = lax.broadcasted_iota(jnp.int32, (rows, 1), 0) + flip(me, k, parts) * rows
            bias = jnp.where(pos.astype(f32) < length, 0.0, NEG)
            key_more = jnp.where(step == 0, bias, 1.0).astype(bf16)
            grad = go[p, k]
            prod = grad.astype(f32) * mixed[p, k].astype(f32)
            high = prod.astype(bf16)
            sums = dot(high, picks) + dot((prod - high.astype(f32)).astype(bf16), picks)
            second = sums - sums.astype(bf16).astype(f32)
            third = second - second.astype(bf16).astype(f32)
            grad_more = jnp.where(step == 0, sums, jnp.where(step == 1, second, third)).astype(bf16)
            query_more = lse[p, at]
            ka[0, at] = jnp.where(low_half, keys, key_more)
            ka[1, at] = jnp.where(low_half, key_more, keys)
            va[0, at] = jnp.where(low_half, values, one)
            va[1, at] = jnp.where(low_half, one, values)
            qa[0, at] = jnp.where(low_half, query, query_more)
            qa[1, at] = jnp.where(low_half, query_more, query)
            da[0, at] = jnp.where(low_half, grad, grad_more)
            da[1, at] = jnp.where(low_half, grad_more, grad)
        dqt[...] = jnp.zeros_like(dqt)

    steps_each = 2 * parts
    cols_each = full // 2

    def attend_back(p, events):
        def body(j, carry):
            at = pl.ds(aligned(j * rows, rows), rows)
            totals = [None, None]
            for i in range(2):
                for when, event in events.items():
                    if when % 2 == i:
                        pl.when(j == when // 2)(event)
                cols = slice(i * cols_each, (i + 1) * cols_each)
                for h in range(2):
                    part = slice(h * 64, h * 64 + 64)
                    probs = jnp.exp2(dot_nt(qa[h, cols], ka[h, at, :]))
                    inner = dot_nt(da[h, cols], va[h, at, :])
                    low = probs.astype(bf16)
                    grad = (probs * inner).astype(bf16)
                    dv = dot(gt[part, cols], low)
                    dk = dot(qt[part, cols], grad)
                    dqt[part, cols] += dot_nt(kt[part, at], grad)
                    totals[h] = (dv, dk) if i == 0 else (totals[h][0] + dv, totals[h][1] + dk)
            dv = jnp.concatenate([totals[0][0], totals[1][0]], 0).T
            dk = jnp.concatenate([totals[0][1], totals[1][1]], 0).T
            dsend[p, 1, j] = (dk * (1.0 / LOG2E)).astype(bf16)
            dsend[p, 2, j] = dv.astype(bf16)
            return carry

        lax.fori_loop(0, parts, body, None)
        dsend[p, 0] = (dqt[...] * 64 ** (-0.5)).T.astype(bf16).reshape(parts, rows, 128)
        for part in range(3):
            d_copy(p, part).start()
            dfull[:, :, pl.ds(aligned(part * width + (2 * core + p) * 128, 128), 128)] = dsend[p, part, :, here]

    def late_term(p):
        late[p] = sum(
            dot_tn(xs[k], jnp.concatenate([dsend[p, part, k] for part in range(3)], 1)) for k in range(parts)
        )

    l_steps = len(seq_bits)
    l_sizes = [0] + [spots >> i for i in range(l_steps - 1)]
    l_offsets = [0] + [sum(size // 2 for size in l_sizes[1:i]) for i in range(1, l_steps)]

    def l_copy(p, i):
        at = pl.ds(l_offsets[i], l_sizes[i] // 2)
        return send(
            late_step.at[p, at],
            late_got.at[p, at],
            (lsem.at[0, p, i], lsem.at[1, p, i]),
            (me, flip(place, seq_bits[i], shards)),
        )

    def lg_copy(p, k, o):
        slot = 2 * k + o
        return send(
            late_out.at[p, core if o == 0 else 1 - core],
            late_all.at[p, slot],
            (lsem.at[0, p, l_steps + slot], lsem.at[1, p, l_steps + slot]),
            (flip(me, k, parts), place if o == 0 else other),
        )

    def late_spot(p, i, spot):
        if i == 1:
            return late[p, pl.ds(aligned(spot * (2 * n), 16), 2 * n)]
        return late_sum[p, spot]

    def late_split(p, i):
        own = lax.rem(lax.div(place, seq_bits[i]), 2)
        for j in range(l_sizes[i] // 2):
            late_step[p, l_offsets[i] + j] = late_spot(p, i, 2 * j + 1 - own).astype(bf16)
        launch(l_copy, p, i)

    def late_merge(p, i):
        own = lax.rem(lax.div(place, seq_bits[i]), 2)
        l_copy(p, i).wait_recv()
        for j in range(l_sizes[i] // 2):
            late_sum[p, j] = late_spot(p, i, 2 * j + own) + late_got[p, l_offsets[i] + j].astype(f32)

    def late_share(p):
        total = late_sum[p, 0] if l_steps > 1 else late[p]
        late_out[p, 0] = total[:n].astype(bf16)
        late_out[p, 1] = total[n:].astype(bf16)
        for k in range(parts - 1, -1, -1):
            for o in range(2):
                if k or o:
                    launch(lg_copy, p, k, o)

    def late_finish(p):
        for o in range(2):
            total = late_out[p, core].astype(f32) if o == 0 else None
            for k in range(parts):
                if k or o:
                    lg_copy(p, k, o).wait_recv()
                    piece = late_all[p, 2 * k + o].astype(f32)
                    total = piece if total is None else total + piece
            total = total * grad_norm
            owner = core if o == 0 else 1 - core
            for part in range(3):
                to = aligned(part * width + (2 * owner + p) * 128, 128)
                wqkv_o[:, pl.ds(to, 128)] = total[:, part * 128 : part * 128 + 128]

    def late_start(p):
        if l_steps > 1:
            late_split(p, 1)
        else:
            late_share(p)

    def late_events(p):
        steps_of = []
        for i in range(1, l_steps):

            def step(i=i):
                late_merge(p, i)
                if i + 1 < l_steps:
                    late_split(p, i + 1)
                else:
                    late_share(p)

            steps_of.append(step)
        return steps_of

    def both_events(one_event, two_event):
        def run():
            one_event()
            two_event()

        return run

    def out_copies(a, k):
        src = (added_h, dx_v)[a].at[k]
        dst = (added_o, dx_o)[a].at[from_group, here]
        to = (flip(me, k, parts), place - core + from_core)
        remote = send(src, dst, (osem.at[0, a, k], osem.at[1, a, 2 * from_group + core]), to)
        return remote, pltpu.make_async_copy(src, dst, self_sem.at[a])

    def out_start(a, k):
        remote, local = out_copies(a, k)
        if k:
            remote.start()
        else:
            pl.when(from_core == core)(local.start)
            pl.when(from_core != core)(remote.start)

    def out_wait(a):
        for k in range(parts):
            remote, local = out_copies(a, k)
            if k:
                remote.wait_send()
            else:
                pl.when(from_core == core)(local.wait)
                pl.when(from_core != core)(remote.wait_send)
        for s in (0, 1):
            for r in (0, 1):
                chip = 2 * core + s
                dst = (added_o, dx_o)[a].at[s, r * half_rows : (r + 1) * half_rows]
                remote = send(
                    (added_h, dx_v)[a].at[0],
                    dst,
                    (osem.at[0, a, 0], osem.at[1, a, 2 * s + r]),
                    (chip, place - core + r),
                )
                pl.when(jnp.logical_not((chip == me) & (core == r)))(remote.wait_recv)

    def early_second_and_added():
        early_second_and_on()
        for k in range(parts - 1, -1, -1):
            out_start(0, k)

    launch(a1_copy)
    launch(b1_copy)
    prepare(0)
    attend_back(0, {6: early_first})
    xs_in.wait()
    late_term(0)
    late_start(0)
    prepare(1)
    early_steps = [early_second_and_added]
    for i in range(1, steps):

        def early_step(i=i):
            z_add(i - 1)
            z_send(i)

        early_steps.append(early_step)

    def early_last():
        if steps:
            z_add(steps - 1)
        ag_send()

    early_steps.append(early_last)
    events = {}
    later = []

    def schedule(steps_list, slots):
        for index, event in enumerate(steps_list):
            slot = slots[index] if index < len(slots) else steps_each
            if slot >= steps_each:
                later.append(event)
            elif slot in events:
                events[slot] = both_events(events[slot], event)
            else:
                events[slot] = event

    schedule(early_steps, (0, 4, 7))
    schedule(late_events(0), (2, 5))
    attend_back(1, events)
    for event in later:
        event()
    late_term(1)
    late_start(1)
    tail = late_events(1)
    wqkv_in.wait()
    first_in.wait()
    for p in range(2):
        for part in range(3):
            d_copy(p, part).wait_recv()
    for k in range(parts - 1, -1, -1):
        dx_v[k] = (first[k] + dot_nt(dfull[k], wqkv[...])).astype(bf16)
        out_start(1, k)
    if tail:
        tail.pop(0)()
    ag_finish()
    late_finish(0)
    for event in tail:
        event()
    late_finish(1)
    for make in sends:
        make().wait_send()
    for p in range(2):
        for part in range(3):
            d_copy(p, part).wait_send()
    out_wait(0)
    out_wait(1)
    for copy in ag_out():
        copy.wait()


def second_call(parts, shards, grad_norm, length, saved, grads, first, added, wqkv, hidden):
    xs_shape = saved[4].shape
    _, rows, width = xs_shape
    full = rows * parts
    half_rows = rows // 2
    n, up_rows, vector_rows, total_rows = grad_rows(width, hidden, shards)
    spots = shards // 2
    quarter, eighth = total_rows // 4, total_rows // 8
    heads = (2, full, 128)
    return pl.pallas_call(
        functools.partial(second_kernel, parts, shards, grad_norm),
        in_specs=[VMEM] + [ANY] * 9,
        out_specs=[ANY, ANY, VMEM, ANY, ANY, ANY, VMEM],
        out_shape=[
            jax.ShapeDtypeStruct((2, rows, width), bf16),
            jax.ShapeDtypeStruct((2, rows, width), bf16),
            jax.ShapeDtypeStruct((n, 3 * width), f32),
            jax.ShapeDtypeStruct((n, hidden), f32),
            jax.ShapeDtypeStruct((up_rows, width), f32),
            jax.ShapeDtypeStruct((n, width), f32),
            jax.ShapeDtypeStruct((8, width), f32),
        ],
        scratch_shapes=[
            pltpu.VMEM(xs_shape, bf16),
            pltpu.VMEM((2, 3, full, 128), bf16),
            pltpu.VMEM((2, full, 128), bf16),
            pltpu.VMEM((2, parts, rows, 128), bf16),
            pltpu.VMEM((2, parts, rows, 128), bf16),
            pltpu.VMEM((width, 3 * width), bf16),
            pltpu.VMEM((parts, half_rows, width), f32),
            pltpu.VMEM((spots, total_rows, width), bf16),
            pltpu.VMEM((spots, quarter, width), bf16),
            pltpu.VMEM((spots, quarter, width), bf16),
            pltpu.VMEM((spots, eighth, width), bf16),
            pltpu.VMEM((spots, eighth, width), bf16),
            pltpu.VMEM((spots, quarter, width), bf16),
            pltpu.VMEM((2 * spots, quarter, width), bf16),
            pltpu.VMEM((spots + parts, quarter, width), bf16),
            pltpu.VMEM((total_rows, width), f32),
            pltpu.VMEM(heads, bf16),
            pltpu.VMEM(heads, bf16),
            pltpu.VMEM(heads, bf16),
            pltpu.VMEM(heads, bf16),
            pltpu.VMEM((128, full), bf16),
            pltpu.VMEM((128, full), bf16),
            pltpu.VMEM((128, full), bf16),
            pltpu.VMEM((128, full), f32),
            pltpu.VMEM((2, 3, parts, rows, 128), bf16),
            pltpu.VMEM((parts, half_rows, 3 * width), bf16),
            pltpu.VMEM((parts, half_rows, width), bf16),
            pltpu.VMEM((2, width, 384), f32),
            pltpu.VMEM((2, 2, n, 384), bf16),
            pltpu.VMEM((2, spots, 2 * n, 384), f32),
            pltpu.VMEM((2, spots, 2 * n, 384), bf16),
            pltpu.VMEM((2, spots, 2 * n, 384), bf16),
            pltpu.VMEM((2, 2 * parts, n, 384), bf16),
            DMA((16,)),
            DMA((16,)),
            DMA((2,)),
            DMA((2, 2, 3)),
            DMA((2, 24)),
            DMA((2, 2, 16)),
            DMA((2, 2, 4)),
        ],
        compiler_params=pltpu.CompilerParams(
            vmem_limit_bytes=VMEM_LIMIT, collective_id=1, has_side_effects=True
        ),
        name="backward_and_sums",
    )(length, *saved, grads, first, added, wqkv)


def last_kernel(rows_here, lengths, post_h, added_h, dx_h, y, ac, vec, *rest):
    ins, (post_o, accum_o, dx_o, accg_o), outs, vectors = rest[:4], rest[4:8], rest[8:12], rest[12:]
    step = pl.program_id(0)
    for src, dst in zip(ins, outs):
        dst[...] = src[...]

    @pl.when(step == 0)
    def _():
        for i, out in enumerate(vectors):
            out[...] = vec[i : i + 1, : out.shape[1]]

    _, rows, _ = y.shape
    steps = pl.num_programs(0)
    length = lengths[lax.div(step * 2, steps)]
    start = lax.axis_index("head") * rows_here + lax.rem(step, lax.div(steps, 2)) * rows
    keep = lax.broadcasted_iota(jnp.int32, (1, rows, 1), 1) + start < length
    post_o[...] = post_h[...].astype(f32)
    accum_o[...] = jnp.where(keep, y[...].astype(f32) + added_h[...].astype(f32), 0.0)
    dx_o[...] = dx_h[...].astype(f32)
    accg_o[...] = jnp.where(keep, ac[...].astype(f32), 0.0)


def last_call(lengths, tokens, streams, vectors, grads, shards):
    groups, rows, width = tokens[0].shape
    cut = 2
    steps = groups * cut
    block = pl.BlockSpec((1, rows // cut, width), lambda i: (i // cut, i % cut, 0))
    whole = jax.ShapeDtypeStruct((groups, rows, width), f32)
    n = width // shards
    hidden = grads[1].shape[1]
    short = [jax.ShapeDtypeStruct((1, n), f32)] * 5 + [jax.ShapeDtypeStruct((1, hidden // shards), f32)]
    moved = [pl.BlockSpec((g.shape[0], g.shape[1] // steps), lambda i: (0, i)) for g in grads]
    return pl.pallas_call(
        functools.partial(last_kernel, rows),
        grid=(steps,),
        in_specs=[SMEM] + [block] * 5 + [pl.BlockSpec(vectors.shape, lambda i: (0, 0))] + moved,
        out_specs=[block] * 4 + moved + [pl.BlockSpec(o.shape, lambda i: (0, 0)) for o in short],
        out_shape=[whole] * 4 + [jax.ShapeDtypeStruct(g.shape, f32) for g in grads] + short,
        compiler_params=pltpu.CompilerParams(vmem_limit_bytes=VMEM_LIMIT),
        name="outputs",
    )(lengths, *tokens, *streams, vectors, *grads)


def local(
    post_stream,
    accum_stream,
    seq_lengths,
    qkv_weight,
    out_weight,
    norm1_gain,
    norm1_bias,
    up_weight,
    up_bias,
    down_weight,
    down_bias,
    norm2_gain,
    norm2_bias,
    post_cotan,
    accum_cotan,
):
    groups, rows, width = post_stream.shape
    parts = lax.axis_size("head")
    shards = lax.axis_size("seq")
    hidden = up_weight.shape[1]
    grad_norm = float(groups * shards * rows * parts) ** (-0.5)

    def row(vector):
        return vector.reshape(1, -1)

    weights = (
        qkv_weight,
        out_weight,
        row(norm1_gain),
        row(norm1_bias),
        up_weight,
        row(up_bias),
        down_weight,
        row(down_bias),
        row(norm2_gain),
        row(norm2_bias),
    )
    post, added, first, qkv, lse, mixed, go, xs, grads, length = first_call(
        parts, shards, seq_lengths, (post_stream, post_cotan, accum_cotan), weights
    )
    dx, added, qkv_grad, up_grad, down_grad, out_grad, vectors = second_call(
        parts, shards, grad_norm, length, (qkv, lse, mixed, go, xs), grads, first, added, qkv_weight, hidden
    )
    post, accum, post_grad, accum_grad, qkv_grad, up_grad, down_grad, out_grad, *short = last_call(
        seq_lengths,
        (post, added, dx),
        (accum_stream, accum_cotan),
        vectors,
        (qkv_grad, up_grad, down_grad, out_grad),
        shards,
    )
    gain1, bias1, gain2, bias2, down_bias_grad, up_bias_grad = [v.reshape(-1) for v in short]
    return (
        post,
        accum,
        post_grad,
        accum_grad,
        qkv_grad,
        out_grad,
        gain1,
        bias1,
        up_grad,
        up_bias_grad,
        down_grad,
        down_bias_grad,
        gain2,
        bias2,
    )


def solution(mesh):
    tokens = P("seq", "head", None)
    in_specs = (tokens, tokens, P("seq")) + (P(),) * 10 + (tokens, tokens)
    rows = P("seq", None)
    vector = P("seq")
    out_specs = (tokens,) * 4 + (rows, rows, vector, vector, rows, vector, rows, vector, vector, vector)
    return jax.shard_map(local, mesh=mesh, in_specs=in_specs, out_specs=out_specs, check_vma=False)
```

```python
import functools
import itertools

import jax
import jax.numpy as jnp
from jax import lax
from jax.experimental import pallas as pl
from jax.experimental.pallas import tpu as pltpu
from jax.sharding import PartitionSpec as P

H = 8
EPS = 1e-05
NEG = -1e30
LOG2E = 1.4426950408889634
VMEM_LIMIT = 62 * 2**20
bf16 = jnp.bfloat16
f32 = jnp.float32
SMEM = pl.BlockSpec(memory_space=pltpu.SMEM)
VMEM = pl.BlockSpec(memory_space=pltpu.VMEM)
ANY = pl.BlockSpec(memory_space=pl.ANY)
DMA = pltpu.SemaphoreType.DMA


def dot(a, b):
    return jnp.dot(a, b, preferred_element_type=f32)


def dot_nt(a, b):
    return lax.dot_general(a, b, (((1,), (1,)), ((), ())), preferred_element_type=f32)


def dot_tn(a, b):
    return lax.dot_general(a, b, (((0,), (0,)), ((), ())), preferred_element_type=f32)


def split3(value):
    first = value.astype(bf16)
    rest = value - first.astype(f32)
    second = rest.astype(bf16)
    third = (rest - second.astype(f32)).astype(bf16)
    return first, second, third


def lane_sets():
    lane = lax.broadcasted_iota(jnp.int32, (1, 128), 1)
    return lane, (lane < 64, lane >= 64), (64, 0)


def bits_of(count):
    return [1 << b for b in range(count.bit_length() - 1)]


def flip(index, k, count):
    out = 0
    for bit in bits_of(count):
        out = out + (lax.rem(lax.div(index, bit) + (k // bit), 2)) * bit
    return out


def aligned(start, step):
    if isinstance(start, int):
        return start
    return pl.multiple_of(start, step)


def send(src, dst, pair, to):
    return pltpu.make_async_remote_copy(
        src_ref=src,
        dst_ref=dst,
        send_sem=pair[0],
        recv_sem=pair[1],
        device_id=to,
        device_id_type=pl.DeviceIdType.MESH,
    )


def enter(partners):
    barrier = pltpu.get_barrier_semaphore()
    for to in partners:
        pl.semaphore_signal(barrier, inc=1, device_id=to, device_id_type=pl.DeviceIdType.MESH)
    pl.semaphore_wait(barrier, len(partners))


def plane(me, place, parts):
    core = lax.rem(place, 2)
    others = []
    for k in range(parts):
        for other in range(2):
            if k or other:
                seat = place if not other else place + 1 - 2 * core
                others.append((flip(me, k, parts), seat))
    return others


def grad_rows(width, hidden, shards):
    n = width // shards
    up = n * (hidden // width)
    vectors = 16 - n % 16
    total = 2 * up + n + vectors
    return n, up, vectors, -(-total // 128) * 128


def normed(value):
    centre = value - jnp.mean(value, axis=-1, keepdims=True)
    spread = jnp.mean(centre * centre, axis=-1, keepdims=True)
    inv = lax.rsqrt(spread + EPS)
    return centre * inv, inv


def norm_back(cot, unit, inv):
    return (
        cot - jnp.mean(cot, axis=-1, keepdims=True) - unit * jnp.mean(cot * unit, axis=-1, keepdims=True)
    ) * inv


def first_kernel(
    parts,
    shards,
    lengths,
    x,
    pc,
    ac,
    wqkv,
    wo_h,
    g1,
    b1,
    wu_h,
    bu,
    wd_h,
    bd,
    g2,
    b2,
    post_o,
    added_o,
    first_o,
    qkv_o,
    lse_o,
    mixed_o,
    go_o,
    xs_o,
    grads_o,
    length_o,
    xs,
    pcs,
    acs,
    w,
    qkv,
    ka,
    qa,
    vt,
    mixed,
    lse,
    tops,
    accs,
    wo,
    wu,
    wd,
    mix,
    hid,
    pre,
    slope,
    back,
    fgrad,
    mid,
    agrad,
    mgrad,
    post_v,
    added_v,
    first_v,
    small,
    grads,
    core_in,
    sizes,
    load_sem,
    store_sem,
    self_sem,
    insem,
    fsem,
    msem,
    gsem,
    osem,
    nsem,
    csem,
):
    groups, rows, width = x.shape
    hidden = wu.shape[1]
    full = rows * parts
    half = rows // 2
    me = lax.axis_index("head")
    place = lax.axis_index("seq")
    core = lax.rem(place, 2)
    other = place + 1 - 2 * core
    from_core = lax.div(me, 2)
    from_group = lax.rem(me, 2)
    lane, mine, base = lane_sets()
    one = jnp.ones((), bf16)
    zero = jnp.zeros((), bf16)
    here = pl.ds(aligned(core * half, half), half)
    there = pl.ds(aligned((1 - core) * half, half), half)

    load_count = itertools.count()

    def load(src, dst):
        copy = pltpu.make_async_copy(src, dst, load_sem.at[next(load_count)])
        copy.start()
        return copy

    stores = []
    store_count = itertools.count()

    def store(src, dst):
        copy = pltpu.make_async_copy(src, dst, store_sem.at[next(store_count)])
        copy.start()
        stores.append(copy)

    w_in = [
        load(
            wqkv.at[:, pl.ds(aligned(part * width + core * 256, 128), 256)],
            w.at[:, part * 256 : part * 256 + 256],
        )
        for part in range(3)
    ]
    wo_in = load(wo_h, wo)
    wu_in = load(wu_h, wu)
    wd_in = load(wd_h, wd)

    enter(plane(me, place, parts))

    def in_copies(a, twist, r):
        group = from_group if not twist else 1 - from_group
        src = (x, pc, ac)[a].at[group, r * half : (r + 1) * half]
        slot = twist + 2 * lax.rem(from_core + core, 2)
        dst = xs.at[slot, r * half : (r + 1) * half] if a == 0 else (pcs, acs)[a - 1].at[slot]
        sems = (insem.at[0, a, 2 * twist + r], insem.at[1, a, slot])
        remote = send(src, dst, sems, (2 * core + group, place - core + r))
        if twist:
            return remote, None, None
        return remote, pltpu.make_async_copy(src, dst, self_sem.at[a]), (from_core == core) & (core == r)

    def in_start(a, twist):
        for r in (0, 1):
            remote, local, own = in_copies(a, twist, r)
            if twist:
                remote.start()
            else:
                pl.when(own)(local.start)
                pl.when(jnp.logical_not(own))(remote.start)

    def in_sent(a, twist):
        for r in (0, 1):
            remote, local, own = in_copies(a, twist, r)
            if twist:
                remote.wait_send()
            else:
                pl.when(jnp.logical_not(own))(remote.wait_send)

    def in_wait(a, k):
        dst = xs.at[k, here] if a == 0 else (pcs, acs)[a - 1].at[k]
        src = (x, pc, ac)[a].at[0, :half]
        remote = send(src, dst, (insem.at[0, a, 0], insem.at[1, a, k]), (flip(me, k, parts), place))
        if k:
            remote.wait_recv()
        else:
            local = pltpu.make_async_copy(src, dst, self_sem.at[a])
            pl.when(from_core == core)(local.wait)
            pl.when(from_core != core)(remote.wait_recv)

    def across(src, dst, pair):
        return send(src, dst, pair, (me, other))

    def pass_on(k):
        part = xs.at[k, here]
        return across(part, part, (fsem.at[0, k], fsem.at[1, k]))

    size_copy = across(sizes.at[0], sizes.at[1], (nsem.at[0], nsem.at[1]))

    def m_copy(p):
        return across(
            mixed.at[p, :, there],
            mix.at[:, :, pl.ds(aligned((2 * core + p) * 128, 128), 128)],
            (msem.at[0, p], msem.at[1, p]),
        )

    def g_copy(p, u):
        chunks = slice(2 * u, 2 * u + 2)
        return across(
            mgrad.at[chunks, :, pl.ds(aligned((2 * (1 - core) + p) * 128, 128), 128)],
            go_o.at[p, chunks, here],
            (gsem.at[0, p, u], gsem.at[1, p, u]),
        )

    def out_copies(k):
        dst = post_o.at[from_group, here]
        to = (flip(me, k, parts), place - core + from_core)
        remote = send(post_v.at[k], dst, (osem.at[0, k], osem.at[1, 2 * from_group + core]), to)
        return remote, pltpu.make_async_copy(post_v.at[k], dst, self_sem.at[3])

    def out_start(k):
        remote, local = out_copies(k)
        if k:
            remote.start()
        else:
            pl.when(from_core == core)(local.start)
            pl.when(from_core != core)(remote.start)

    def out_wait():
        for k in range(parts):
            remote, local = out_copies(k)
            if k:
                remote.wait_send()
            else:
                pl.when(from_core == core)(local.wait)
                pl.when(from_core != core)(remote.wait_send)
        for s in (0, 1):
            for r in (0, 1):
                chip = 2 * core + s
                dst = post_o.at[s, r * half : (r + 1) * half]
                remote = send(
                    post_v.at[0], dst, (osem.at[0, 0], osem.at[1, 2 * s + r]), (chip, place - core + r)
                )
                pl.when(jnp.logical_not((chip == me) & (core == r)))(remote.wait_recv)

    in_start(0, 0)
    pl.when(from_core == core)(functools.partial(in_start, 0, 1))
    which = lax.broadcasted_iota(jnp.int32, (8, 128), 0)
    sizes[0] = jnp.where(which == 0, lengths[0], lengths[1]).astype(f32)
    size_copy.start()
    for copy in w_in:
        copy.wait()
    size_copy.wait_recv()
    held = jnp.where(from_core == core, sizes[0], sizes[1])
    length = jnp.sum(jnp.where(which == from_group, held, 0.0), axis=0, keepdims=True)
    length_o[...] = jnp.broadcast_to(length, (8, 128))
    length = length[:, :1]

    def below(count, start):
        pos = lax.broadcasted_iota(jnp.int32, (count, 1), 0) + start
        return pos.astype(f32) < length

    @pl.when(from_core != core)
    def _():
        in_sent(0, 0)
        in_start(0, 1)

    def project(k):
        pass_on(k).wait_recv()
        at = slice(k * rows, (k + 1) * rows)
        three = dot(xs[k], w[...])
        bias = jnp.where(below(rows, flip(me, k, parts) * rows), 0.0, NEG)
        step = lax.rem(lane, 64)
        key_more = jnp.where(step == 0, bias, 0.0).astype(bf16)
        query_more = jnp.where(step == 0, one, zero)
        for p in (0, 1):
            cut = slice(p * 128, p * 128 + 128)
            query = (three[:, :256][:, cut] * (LOG2E * 64 ** (-0.5))).astype(bf16)
            keys = three[:, 256:512][:, cut].astype(bf16)
            values = three[:, 512:][:, cut].astype(bf16)
            qkv[p, 0, at] = query
            qkv[p, 1, at] = keys
            qkv[p, 2, at] = values
            turned = values.T
            for h in range(2):
                ka[2 * p + h, at] = jnp.where(mine[h], keys, key_more)
                qa[2 * p + h, at] = jnp.where(mine[h], query, query_more)
                vt[2 * p + h, :64, at] = turned[h * 64 : h * 64 + 64]
                vt[2 * p + h, 64:, at] = jnp.ones((8, rows), bf16)

    def rectangle(p, keys, queries):
        for h in range(2):
            g = 2 * p + h
            scores = dot_nt(ka[g, keys, :], qa[g, queries, :])
            top = tops[g, 0:1, queries]
            new_top = jnp.maximum(top, jnp.max(scores, axis=0, keepdims=True))
            probs = jnp.exp2(scores - new_top)
            tops[g, 0:1, queries] = new_top
            accs[g, :, queries] = accs[g, :, queries] * jnp.exp2(top - new_top) + dot(
                vt[g, :, keys], probs.astype(bf16)
            )

    early = full - rows

    def attend_early(p):
        def body(j, carry):
            rectangle(p, pl.ds(aligned(j * rows, rows), rows), slice(0, early))
            return carry

        lax.fori_loop(0, parts - 1, body, None)

    tops[...] = jnp.full(tops.shape, NEG, f32)
    accs[...] = jnp.zeros_like(accs)
    for k in range(parts - 1):
        in_wait(0, k)
        pass_on(k).start()
    for k in range(parts - 1):
        project(k)
    for a in (1, 2):
        for twist in (0, 1):
            in_start(a, twist)
    attend_early(0)
    in_wait(0, parts - 1)
    pass_on(parts - 1).start()
    attend_early(1)
    project(parts - 1)
    store(qkv, qkv_o)
    store(xs, xs_o)

    def attend(p):
        rectangle(p, slice(early, full), slice(0, full))
        rectangle(p, slice(0, early), slice(early, full))
        pieces = []
        terms = []
        for h in range(2):
            top, acc = tops[2 * p + h, 0:1], accs[2 * p + h]
            total = acc[64:65]
            pieces.append(acc[:64] / total)
            a, b, c = split3(-(top + jnp.log2(total)))
            flat = [jnp.ones((1, full), f32)] + [v.astype(f32) for v in (a, b, c)]
            terms.append(jnp.concatenate(flat + [jnp.zeros((60, full), f32)], 0))
        lse[p] = jnp.concatenate([terms[1], terms[0]], 0).T.astype(bf16)
        mixed[p] = jnp.concatenate(pieces, 0).T.astype(bf16).reshape(parts, rows, 128)
        m_copy(p).start()
        mix[:, :, pl.ds(aligned((2 * core + p) * 128, 128), 128)] = mixed[p, :, here]

    attend(0)
    attend(1)
    store(mixed, mixed_o)
    store(lse, lse_o)

    tile = 512
    tiles = hidden // tile
    small[...] = jnp.zeros_like(small)

    def feed(u):
        chunks = (2 * u, 2 * u + 1)
        keep = jnp.concatenate([below(half, flip(me, k, parts) * rows + core * half) for k in chunks], 0)
        mix_u = mix[2 * u : 2 * u + 2].reshape(rows, width)
        x_u = jnp.concatenate([xs[k, here] for k in chunks], 0)
        attention = dot(mix_u, wo[...])
        unit1, inv1 = normed(x_u.astype(f32) + attention)
        x_mid = unit1 * g1[...] + b1[...]
        mid[u] = x_mid.astype(bf16)
        total = jnp.zeros((rows, width), f32)
        c0 = 0.7978845608028654
        c1 = 0.044715
        for t in range(tiles):
            cols = slice(t * tile, (t + 1) * tile)
            act = dot(mid[u], wu[:, cols]) + bu[:, cols]
            square = act * act
            th = jnp.tanh(act * (c0 + (c0 * c1) * square))
            part = 0.5 + 0.5 * th
            smooth = act * part
            low = smooth.astype(bf16)
            hid[u, :, cols] = low
            slope[:rows, cols] = part + smooth * (1.0 - part) * (2.0 * c0 + (6.0 * c0 * c1) * square)
            total = total + dot(low, wd[cols, :])
        total = total + bd[...]
        unit2, inv2 = normed(x_mid + total)
        post = jnp.where(keep, unit2 * g2[...] + b2[...], 0.0).astype(bf16)
        added = jnp.where(keep, attention + total, 0.0).astype(bf16)
        post_v[2 * u : 2 * u + 2] = post.reshape(2, half, width)
        added_v[2 * u : 2 * u + 2] = added.reshape(2, half, width)
        for k in chunks:
            out_start(k)
        store(added_v.at[2 * u : 2 * u + 2], added_o.at[2 * u : 2 * u + 2])
        post_c = jnp.where(keep, pcs[2 * u : 2 * u + 2].reshape(rows, width).astype(f32), 0.0)
        accum_c = jnp.where(keep, acs[2 * u : 2 * u + 2].reshape(rows, width).astype(f32), 0.0)
        mid_grad2 = norm_back(post_c * g2[...], unit2, inv2)
        small[2:3, :width] += jnp.sum(post_c * unit2, axis=0, keepdims=True)
        small[3:4, :width] += jnp.sum(post_c, axis=0, keepdims=True)
        feed_grad = (mid_grad2 + accum_c).astype(bf16)
        fgrad[u] = feed_grad
        small[4:5, :width] += jnp.sum(feed_grad.astype(f32), axis=0, keepdims=True)
        back[...] = mid_grad2
        for t in range(tiles):
            cols = slice(t * tile, (t + 1) * tile)
            hidden_grad = dot_nt(fgrad[u], wd[cols, :]).astype(bf16)
            pre_grad = (hidden_grad.astype(f32) * slope[:rows, cols]).astype(bf16)
            pre[u, :, cols] = pre_grad
            small[5:6, cols] += jnp.sum(pre_grad.astype(f32), axis=0, keepdims=True)
            back[...] += dot_nt(pre_grad, wu[:, cols])
        mid_grad = back[...]
        small[0:1, :width] += jnp.sum(mid_grad * unit1, axis=0, keepdims=True)
        small[1:2, :width] += jnp.sum(mid_grad, axis=0, keepdims=True)
        first = norm_back(mid_grad * g1[...], unit1, inv1)
        first_v[2 * u : 2 * u + 2] = first.reshape(2, half, width)
        store(first_v.at[2 * u : 2 * u + 2], first_o.at[2 * u : 2 * u + 2])
        attn_grad = (first + accum_c).astype(bf16)
        agrad[u] = attn_grad
        mgrad[2 * u : 2 * u + 2] = dot_nt(attn_grad, wo[...]).astype(bf16).reshape(2, half, width)
        for p in (0, 1):
            g_copy(p, u).start()
            own = mgrad.at[2 * u : 2 * u + 2, :, pl.ds(aligned((2 * core + p) * 128, 128), 128)]
            store(own, go_o.at[p, 2 * u : 2 * u + 2, here])

    wo_in.wait()
    wu_in.wait()
    wd_in.wait()
    for a in (1, 2):
        for k in range(parts):
            in_wait(a, k)
    for p in (0, 1):
        m_copy(p).wait_recv()
    for u in (0, 1):
        feed(u)

    n, up_rows, vector_rows, total_rows = grad_rows(width, hidden, shards)
    halves = (0, 1)

    def spot_of(shard):
        return lax.rem(core + shard % 2, 2), shard // 2

    edges = (0, up_rows, 2 * up_rows, total_rows)

    def c_copy(i):
        at = slice(edges[i], edges[i + 1])
        return across(grads.at[1, :, at], core_in.at[:, at], (csem.at[0, i], csem.at[1, i]))

    for t in range(tiles):
        cols = slice(t * tile, (t + 1) * tile)
        slope[:width, cols] = sum(dot_tn(mid[u], pre[u, :, cols]) for u in halves)
    for shard in range(shards):
        own = slice(shard * n, (shard + 1) * n)
        block = jnp.concatenate([slope[own, t * tile : (t + 1) * tile] for t in range(tiles)], 0)
        side, spot = spot_of(shard)
        grads[side, spot, :up_rows] = block.astype(bf16)
    c_copy(0).start()
    per = tile // up_rows
    for t in range(tiles):
        cols = slice(t * tile, (t + 1) * tile)
        block = sum(dot_tn(hid[u, :, cols], fgrad[u]) for u in halves).astype(bf16)
        for i in range(per):
            side, spot = spot_of(t * per + i)
            grads[side, spot, up_rows : 2 * up_rows] = block[i * up_rows : (i + 1) * up_rows]
    c_copy(1).start()
    out_all = sum(dot_tn(mix[2 * u : 2 * u + 2].reshape(rows, width), agrad[u]) for u in halves)
    line = lax.broadcasted_iota(jnp.int32, (8, width), 0)
    short = small[:, :width]
    long = small[...]
    for shard in range(shards):
        a = pltpu.roll(short, (width - shard * n) % width, 1)
        b = pltpu.roll(long, (hidden - shard * up_rows) % hidden, 1)[:, :width]
        extra = jnp.where(line == 5, b, a)
        rest = total_rows - 2 * up_rows - n - 8
        block = jnp.concatenate(
            [out_all[shard * n : (shard + 1) * n], extra, jnp.zeros((rest, width), f32)], 0
        )
        side, spot = spot_of(shard)
        grads[side, spot, 2 * up_rows :] = block.astype(bf16)
    c_copy(2).start()
    for i in range(3):
        c_copy(i).wait_recv()

        def add_cores(spot, carry, i=i):
            at = slice(edges[i], edges[i + 1])
            grads[0, spot, at] = (grads[0, spot, at].astype(f32) + core_in[spot, at].astype(f32)).astype(bf16)
            return carry

        lax.fori_loop(0, shards // 2, add_cores, None)
    store(grads.at[0], grads_o)
    for i in range(3):
        c_copy(i).wait_send()

    pl.when(from_core == core)(functools.partial(in_sent, 0, 0))
    in_sent(0, 1)
    for a in (1, 2):
        for twist in (0, 1):
            in_sent(a, twist)
    for k in range(parts):
        pass_on(k).wait_send()
    size_copy.wait_send()
    for p in (0, 1):
        m_copy(p).wait_send()
        for u in (0, 1):
            g_copy(p, u).wait()
    out_wait()
    for copy in stores:
        copy.wait()


def first_call(parts, shards, lengths, streams, weights):
    groups, rows, width = streams[0].shape
    hidden = weights[4].shape[1]
    full = rows * parts
    half = rows // 2
    total_rows = grad_rows(width, hidden, shards)[3]
    held = jax.ShapeDtypeStruct((groups, rows, width), bf16)
    return pl.pallas_call(
        functools.partial(first_kernel, parts, shards),
        in_specs=[SMEM] + [ANY] * 5 + [VMEM, VMEM, ANY, VMEM, ANY, VMEM, VMEM, VMEM],
        out_specs=[ANY] * 9 + [VMEM],
        out_shape=[
            held,
            jax.ShapeDtypeStruct((parts, half, width), bf16),
            jax.ShapeDtypeStruct((parts, half, width), f32),
            jax.ShapeDtypeStruct((2, 3, full, 128), bf16),
            jax.ShapeDtypeStruct((2, full, 128), bf16),
            jax.ShapeDtypeStruct((2, parts, rows, 128), bf16),
            jax.ShapeDtypeStruct((2, parts, rows, 128), bf16),
            jax.ShapeDtypeStruct((parts, rows, width), bf16),
            jax.ShapeDtypeStruct((shards // 2, total_rows, width), bf16),
            jax.ShapeDtypeStruct((8, 128), f32),
        ],
        scratch_shapes=[
            pltpu.VMEM((parts, rows, width), bf16),
            pltpu.VMEM((parts, half, width), bf16),
            pltpu.VMEM((parts, half, width), bf16),
            pltpu.VMEM((width, 768), bf16),
            pltpu.VMEM((2, 3, full, 128), bf16),
            pltpu.VMEM((4, full, 128), bf16),
            pltpu.VMEM((4, full, 128), bf16),
            pltpu.VMEM((4, 72, full), bf16),
            pltpu.VMEM((2, parts, rows, 128), bf16),
            pltpu.VMEM((2, full, 128), bf16),
            pltpu.VMEM((4, 8, full), f32),
            pltpu.VMEM((4, 72, full), f32),
            pltpu.VMEM((width, width), bf16),
            pltpu.VMEM((width, hidden), bf16),
            pltpu.VMEM((hidden, width), bf16),
            pltpu.VMEM((parts, half, width), bf16),
            pltpu.VMEM((2, rows, hidden), bf16),
            pltpu.VMEM((2, rows, hidden), bf16),
            pltpu.VMEM((max(rows, width), hidden), f32),
            pltpu.VMEM((rows, width), f32),
            pltpu.VMEM((2, rows, width), bf16),
            pltpu.VMEM((2, rows, width), bf16),
            pltpu.VMEM((2, rows, width), bf16),
            pltpu.VMEM((parts, half, width), bf16),
            pltpu.VMEM((parts, half, width), bf16),
            pltpu.VMEM((parts, half, width), bf16),
            pltpu.VMEM((parts, half, width), f32),
            pltpu.VMEM((8, hidden), f32),
            pltpu.VMEM((2, shards // 2, total_rows, width), bf16),
            pltpu.VMEM((shards // 2, total_rows, width), bf16),
            pltpu.VMEM((2, 8, 128), f32),
            DMA((8,)),
            DMA((16,)),
            DMA((5,)),
            DMA((2, 3, 4)),
            DMA((2, parts)),
            DMA((2, 2)),
            DMA((2, 2, 2)),
            DMA((2, 4)),
            DMA((2,)),
            DMA((2, 3)),
        ],
        compiler_params=pltpu.CompilerParams(
            vmem_limit_bytes=VMEM_LIMIT, collective_id=0, has_side_effects=True
        ),
        name="forward_and_feed",
    )(lengths, *streams, *weights)


def second_kernel(
    parts,
    shards,
    grad_norm,
    length_v,
    qkv_h,
    lse_h,
    mixed_h,
    go_h,
    xs_h,
    grads_h,
    first_h,
    added_h,
    wqkv_h,
    dx_o,
    added_o,
    wqkv_o,
    up_o,
    down_o,
    out_o,
    vec_o,
    xs,
    qkv,
    lse,
    mixed,
    go,
    wqkv,
    first,
    grads,
    a1_in,
    b1_in,
    a2_in,
    b2_in,
    z_in,
    all_out,
    all_in,
    final,
    ka,
    va,
    qa,
    da,
    kt,
    qt,
    gt,
    dqt,
    dkt,
    dvt,
    dsend,
    dfull,
    dx_v,
    late,
    late_out,
    late_sum,
    late_step,
    late_got,
    late_all,
    load_sem,
    store_sem,
    self_sem,
    dsem,
    rsem,
    lsem,
    osem,
    esem,
):
    parts, rows, width = xs.shape
    half_rows = rows // 2
    full = rows * parts
    hidden = up_o.shape[1]
    me = lax.axis_index("head")
    place = lax.axis_index("seq")
    core = lax.rem(place, 2)
    other = place + 1 - 2 * core
    from_core = lax.div(me, 2)
    from_group = lax.rem(me, 2)
    here = pl.ds(aligned(core * half_rows, half_rows), half_rows)
    there = pl.ds(aligned((1 - core) * half_rows, half_rows), half_rows)
    length = length_v[0:1, 0:1]
    lane, mine, base = lane_sets()
    one = jnp.ones((), bf16)
    zero = jnp.zeros((), bf16)
    n, up_rows, vector_rows, total_rows = grad_rows(width, hidden, shards)
    seq_bits = bits_of(shards)
    load_count = itertools.count()

    def load(src, dst):
        copy = pltpu.make_async_copy(src, dst, load_sem.at[next(load_count)])
        copy.start()
        return copy

    def pair_load(p):
        return [
            load(qkv_h.at[p], qkv.at[p]),
            load(go_h.at[p], go.at[p]),
            load(mixed_h.at[p], mixed.at[p]),
            load(lse_h.at[p], lse.at[p]),
        ]

    pair_in = [pair_load(0)]
    grads_in = load(grads_h, grads)
    xs_in = load(xs_h, xs)
    pair_in.append(pair_load(1))
    wqkv_in = load(wqkv_h, wqkv)
    first_in = load(first_h, first)

    enter(plane(me, place, parts) + [(me, flip(place, bit, shards)) for bit in seq_bits[1:]])

    sends = []

    def launch(make, *which):
        make(*which).start()
        sends.append(functools.partial(make, *which))

    spots = shards // 2
    half, quarter = total_rows // 2, total_rows // 4
    eighth = total_rows // 8
    x_bit = lax.rem(me, 2)
    y_bit = lax.div(me, 2)

    def to_head(src, dst, i, k):
        return send(src, dst, (rsem.at[0, i], rsem.at[1, i]), (flip(me, k, parts), place))

    def to_seq(src, dst, i, bit):
        return send(src, dst, (rsem.at[0, i], rsem.at[1, i]), (me, flip(place, bit, shards)))

    a_keep = x_bit * quarter
    a_give = (1 - x_bit) * quarter
    b_keep = half + y_bit * quarter
    b_give = half + (1 - y_bit) * quarter
    a1_copy = lambda: to_head(grads_h.at[:, pl.ds(aligned(a_give, 16), quarter)], a1_in, 1, 1)
    b1_copy = lambda: to_head(grads_h.at[:, pl.ds(aligned(b_give, 16), quarter)], b1_in, 2, 2)
    a_own = a_keep + y_bit * eighth
    a_pass = a_keep + (1 - y_bit) * eighth
    b_own = b_keep + x_bit * eighth
    b_pass = b_keep + (1 - x_bit) * eighth
    a2_copy = lambda: to_head(grads.at[:, pl.ds(aligned(a_pass, 16), eighth)], a2_in, 3, 2)
    b2_copy = lambda: to_head(grads.at[:, pl.ds(aligned(b_pass, 16), eighth)], b2_in, 4, 1)

    def add_rows(into, spot, start, count, other):
        at = pl.ds(aligned(start, 16), count)
        into[spot, at] = (into[spot, at].astype(f32) + other.astype(f32)).astype(bf16)

    def early_first():
        grads_in.wait()
        a1_copy().wait_recv()
        b1_copy().wait_recv()

        def body(i, carry):
            add_rows(grads, i, a_keep, quarter, a1_in[i])
            add_rows(grads, i, b_keep, quarter, b1_in[i])
            return carry

        lax.fori_loop(0, spots, body, None)
        launch(a2_copy)
        launch(b2_copy)

    def early_second_and_on():
        a2_copy().wait_recv()
        b2_copy().wait_recv()

        def body(i, carry):
            add_rows(grads, i, a_own, eighth, a2_in[i])
            add_rows(grads, i, b_own, eighth, b2_in[i])
            return carry

        lax.fori_loop(0, spots, body, None)

        def gather(i, carry):
            all_out[i, :eighth] = grads[i, pl.ds(aligned(a_own, 16), eighth)]
            all_out[i, eighth:] = grads[i, pl.ds(aligned(b_own, 16), eighth)]
            return carry

        lax.fori_loop(0, spots, gather, None)
        if steps:
            z_send(0)

    offsets = []
    at = 0
    size = spots
    for bit in seq_bits[1:]:
        offsets.append((at, size))
        at += size
        size //= 2
    offsets.append((at, 1))
    steps = len(offsets) - 1
    z_offsets = []
    at = 0
    for _, size in offsets[:-1]:
        z_offsets.append(at)
        at += size // 2

    def z_copy(i):
        at, size = offsets[i]
        bit = seq_bits[1 + i]
        return to_seq(
            all_in.at[pl.ds(z_offsets[i], size // 2)], z_in.at[pl.ds(z_offsets[i], size // 2)], 5 + i, bit
        )

    def z_send(i):
        at, size = offsets[i]
        own = lax.rem(lax.div(place, seq_bits[1 + i]), 2)
        for j in range(size // 2):
            all_in[z_offsets[i] + j] = all_out[at + 2 * j + (1 - own)]
        launch(z_copy, i)

    def z_add(i):
        at, size = offsets[i]
        after = offsets[i + 1][0]
        own = lax.rem(lax.div(place, seq_bits[1 + i]), 2)
        z_copy(i).wait_recv()
        for j in range(size // 2):
            all_out[after + j] = (
                all_out[at + 2 * j + own].astype(f32) + z_in[z_offsets[i] + j].astype(f32)
            ).astype(bf16)

    ag_from = 5 + steps
    last = offsets[-1][0]
    ag = sum(size // 2 for _, size in offsets[:-1])

    def ag_copy(k):
        return to_head(all_out.at[last], all_in.at[ag + k], ag_from + k, k)

    def ag_send():
        for k in range(parts - 1, 0, -1):
            launch(ag_copy, k)

    def ag_out():
        moves = [
            (final.at[t * n : (t + 1) * n], up_o.at[:, t * width : (t + 1) * width])
            for t in range(hidden // width)
        ]
        moves.append((final.at[up_rows : 2 * up_rows], down_o))
        moves.append((final.at[2 * up_rows : 2 * up_rows + n], out_o))
        return [pltpu.make_async_copy(src, dst, store_sem.at[i]) for i, (src, dst) in enumerate(moves)]

    def ag_finish():
        for k in range(parts):
            if k:
                ag_copy(k).wait_recv()
                block = all_in[ag + k]
            else:
                block = all_out[last]
            block = block.astype(f32) * grad_norm
            who = flip(me, k, parts)
            x_of, y_of = lax.rem(who, 2), lax.div(who, 2)
            a_at = x_of * quarter + y_of * eighth
            b_at = half + y_of * quarter + x_of * eighth
            final[pl.ds(aligned(a_at, 16), eighth)] = block[:eighth]
            final[pl.ds(aligned(b_at, 16), eighth)] = block[eighth:]
        for copy in ag_out():
            copy.start()
        vec_o[...] = final[2 * up_rows + n : 2 * up_rows + n + 8]

    def d_copy(part):
        return send(
            dsend.at[0, part, :, there],
            dfull.at[:, :, pl.ds(aligned(part * width + 2 * core * 128, 128), 128)],
            (dsem.at[0, part], dsem.at[1, part]),
            (me, other),
        )

    def e_copy(part, k):
        return send(
            dsend.at[1, part, k, there],
            dfull.at[k, :, pl.ds(aligned(part * width + (2 * core + 1) * 128, 128), 128)],
            (esem.at[0, part, k], esem.at[1, part, k]),
            (me, other),
        )

    def prepare(p):
        for copy in pair_in[p]:
            copy.wait()
        low_half = lane < 64
        row_of = lax.broadcasted_iota(jnp.int32, (128, 128), 0)
        lane_of = lax.broadcasted_iota(jnp.int32, (128, 128), 1)
        picks = ((row_of < 64) & (lane_of >= 64) & (lane_of < 67)) | ((row_of >= 64) & (lane_of < 3))
        picks = jnp.where(picks, -1.0, 0.0).astype(bf16)
        step = lax.rem(lane, 64)
        kt[...] = qkv[p, 1].T
        qt[...] = qkv[p, 0].T
        gt[...] = go[p].reshape(full, 128).T
        for k in range(parts):
            at = slice(k * rows, (k + 1) * rows)
            query, keys, values = qkv[p, 0, at], qkv[p, 1, at], qkv[p, 2, at]
            pos = lax.broadcasted_iota(jnp.int32, (rows, 1), 0) + flip(me, k, parts) * rows
            bias = jnp.where(pos.astype(f32) < length, 0.0, NEG)
            key_more = jnp.where(step == 0, bias, 1.0).astype(bf16)
            grad = go[p, k]
            prod = grad.astype(f32) * mixed[p, k].astype(f32)
            high = prod.astype(bf16)
            sums = dot(high, picks) + dot((prod - high.astype(f32)).astype(bf16), picks)
            second = sums - sums.astype(bf16).astype(f32)
            third = second - second.astype(bf16).astype(f32)
            grad_more = jnp.where(step == 0, sums, jnp.where(step == 1, second, third)).astype(bf16)
            query_more = lse[p, at]
            ka[0, at] = jnp.where(low_half, keys, key_more)
            ka[1, at] = jnp.where(low_half, key_more, keys)
            va[0, at] = jnp.where(low_half, values, one)
            va[1, at] = jnp.where(low_half, one, values)
            qa[0, at] = jnp.where(low_half, query, query_more)
            qa[1, at] = jnp.where(low_half, query_more, query)
            da[0, at] = jnp.where(low_half, grad, grad_more)
            da[1, at] = jnp.where(low_half, grad_more, grad)
        dqt[...] = jnp.zeros_like(dqt)

    steps_each = 2 * parts
    cols_each = full // 2

    def attend_back(p, events):
        def body(j, carry):
            at = pl.ds(aligned(j * rows, rows), rows)
            totals = [None, None]
            for i in range(2):
                for when, event in events.items():
                    if when % 2 == i:
                        pl.when(j == when // 2)(event)
                cols = slice(i * cols_each, (i + 1) * cols_each)
                for h in range(2):
                    part = slice(h * 64, h * 64 + 64)
                    probs = jnp.exp2(dot_nt(qa[h, cols], ka[h, at, :]))
                    inner = dot_nt(da[h, cols], va[h, at, :])
                    low = probs.astype(bf16)
                    grad = (probs * inner).astype(bf16)
                    dv = dot(gt[part, cols], low)
                    dk = dot(qt[part, cols], grad)
                    dqt[part, cols] += dot_nt(kt[part, at], grad)
                    totals[h] = (dv, dk) if i == 0 else (totals[h][0] + dv, totals[h][1] + dk)
            dv = jnp.concatenate([totals[0][0], totals[1][0]], 0).T
            dk = jnp.concatenate([totals[0][1], totals[1][1]], 0).T
            dsend[p, 1, j] = (dk * (1.0 / LOG2E)).astype(bf16)
            dsend[p, 2, j] = dv.astype(bf16)
            return carry

        lax.fori_loop(0, parts, body, None)
        dsend[p, 0] = (dqt[...] * 64 ** (-0.5)).T.astype(bf16).reshape(parts, rows, 128)
        for part in range(3):
            d_copy(part).start()
            dfull[:, :, pl.ds(aligned(part * width + (2 * core + p) * 128, 128), 128)] = dsend[p, part, :, here]

    def cross(queries, keys):
        for q0 in range(queries[0], queries[1], 2 * rows):
            q = slice(q0, min(q0 + 2 * rows, queries[1]))
            for k0 in range(keys[0], keys[1], rows):
                k = slice(k0, k0 + rows)
                for h in range(2):
                    part = slice(h * 64, h * 64 + 64)
                    probs = jnp.exp2(dot_nt(qa[h, q], ka[h, k]))
                    inner = dot_nt(da[h, q], va[h, k])
                    low = probs.astype(bf16)
                    grad = (probs * inner).astype(bf16)
                    dvt[part, k] += dot(gt[part, q], low)
                    dkt[part, k] += dot(qt[part, q], grad)
                    dqt[part, q] += dot_nt(kt[part, k], grad)

    def cross_end(k):
        at = slice(k * rows, (k + 1) * rows)
        parts_of = (dqt[:, at] * 64 ** (-0.5), dkt[:, at] * (1.0 / LOG2E), dvt[:, at])
        for part, value in enumerate(parts_of):
            dsend[1, part, k] = value.T.astype(bf16)
            e_copy(part, k).start()
            to = pl.ds(aligned(part * width + (2 * core + 1) * 128, 128), 128)
            dfull[k, :, to] = dsend[1, part, k, here]

    def post_slot(k):
        for part in range(3):
            e_copy(part, k).wait_recv()
        dx_v[k] = (first[k] + dot_nt(dfull[k], wqkv[...])).astype(bf16)
        out_start(1, k)

    def late_term(p):
        late[p] = sum(
            dot_tn(xs[k], jnp.concatenate([dsend[p, part, k] for part in range(3)], 1)) for k in range(parts)
        )

    l_steps = len(seq_bits)
    l_sizes = [0] + [spots >> i for i in range(l_steps - 1)]
    l_offsets = [0] + [sum(size // 2 for size in l_sizes[1:i]) for i in range(1, l_steps)]

    def l_copy(p, i):
        at = pl.ds(l_offsets[i], l_sizes[i] // 2)
        return send(
            late_step.at[p, at],
            late_got.at[p, at],
            (lsem.at[0, p, i], lsem.at[1, p, i]),
            (me, flip(place, seq_bits[i], shards)),
        )

    def lg_copy(p, k, o):
        slot = 2 * k + o
        return send(
            late_out.at[p, core if o == 0 else 1 - core],
            late_all.at[p, slot],
            (lsem.at[0, p, l_steps + slot], lsem.at[1, p, l_steps + slot]),
            (flip(me, k, parts), place if o == 0 else other),
        )

    def late_spot(p, i, spot):
        if i == 1:
            return late[p, pl.ds(aligned(spot * (2 * n), 16), 2 * n)]
        return late_sum[p, spot]

    def late_split(p, i):
        own = lax.rem(lax.div(place, seq_bits[i]), 2)
        for j in range(l_sizes[i] // 2):
            late_step[p, l_offsets[i] + j] = late_spot(p, i, 2 * j + 1 - own).astype(bf16)
        launch(l_copy, p, i)

    def late_merge(p, i):
        own = lax.rem(lax.div(place, seq_bits[i]), 2)
        l_copy(p, i).wait_recv()
        for j in range(l_sizes[i] // 2):
            late_sum[p, j] = late_spot(p, i, 2 * j + own) + late_got[p, l_offsets[i] + j].astype(f32)

    def late_share(p):
        total = late_sum[p, 0] if l_steps > 1 else late[p]
        late_out[p, 0] = total[:n].astype(bf16)
        late_out[p, 1] = total[n:].astype(bf16)
        for k in range(parts - 1, -1, -1):
            for o in range(2):
                if k or o:
                    launch(lg_copy, p, k, o)

    def late_finish(p):
        for o in range(2):
            total = late_out[p, core].astype(f32) if o == 0 else None
            for k in range(parts):
                if k or o:
                    lg_copy(p, k, o).wait_recv()
                    piece = late_all[p, 2 * k + o].astype(f32)
                    total = piece if total is None else total + piece
            total = total * grad_norm
            owner = core if o == 0 else 1 - core
            for part in range(3):
                to = aligned(part * width + (2 * owner + p) * 128, 128)
                wqkv_o[:, pl.ds(to, 128)] = total[:, part * 128 : part * 128 + 128]

    def late_start(p):
        if l_steps > 1:
            late_split(p, 1)
        else:
            late_share(p)

    def late_events(p):
        steps_of = []
        for i in range(1, l_steps):

            def step(i=i):
                late_merge(p, i)
                if i + 1 < l_steps:
                    late_split(p, i + 1)
                else:
                    late_share(p)

            steps_of.append(step)
        return steps_of

    def out_copies(a, k):
        src = (added_h, dx_v)[a].at[k]
        dst = (added_o, dx_o)[a].at[from_group, here]
        to = (flip(me, k, parts), place - core + from_core)
        remote = send(src, dst, (osem.at[0, a, k], osem.at[1, a, 2 * from_group + core]), to)
        return remote, pltpu.make_async_copy(src, dst, self_sem.at[a])

    def out_start(a, k):
        remote, local = out_copies(a, k)
        if k:
            remote.start()
        else:
            pl.when(from_core == core)(local.start)
            pl.when(from_core != core)(remote.start)

    def out_wait(a):
        for k in range(parts):
            remote, local = out_copies(a, k)
            if k:
                remote.wait_send()
            else:
                pl.when(from_core == core)(local.wait)
                pl.when(from_core != core)(remote.wait_send)
        for s in (0, 1):
            for r in (0, 1):
                chip = 2 * core + s
                dst = (added_o, dx_o)[a].at[s, r * half_rows : (r + 1) * half_rows]
                remote = send(
                    (added_h, dx_v)[a].at[0],
                    dst,
                    (osem.at[0, a, 0], osem.at[1, a, 2 * s + r]),
                    (chip, place - core + r),
                )
                pl.when(jnp.logical_not((chip == me) & (core == r)))(remote.wait_recv)

    def early_second_and_added():
        early_second_and_on()
        for k in range(parts - 1, -1, -1):
            out_start(0, k)

    launch(a1_copy)
    launch(b1_copy)
    prepare(0)
    attend_back(0, {6: early_first})
    xs_in.wait()
    late_term(0)
    late_start(0)
    prepare(1)
    early_steps = [early_second_and_added]
    for i in range(1, steps):

        def early_step(i=i):
            z_add(i - 1)
            z_send(i)

        early_steps.append(early_step)

    def early_last():
        if steps:
            z_add(steps - 1)
        ag_send()

    early_steps.append(early_last)
    dkt[...] = jnp.zeros_like(dkt)
    dvt[...] = jnp.zeros_like(dvt)
    late_steps = late_events(0)

    def next_of(queue):
        if queue:
            queue.pop(0)()

    next_of(early_steps)
    for k in range(parts - 1, -1, -1):
        low, high = k * rows, (k + 1) * rows
        cross((0, high), (low, high))
        if k == parts - 1:
            wqkv_in.wait()
            first_in.wait()
            for part in range(3):
                d_copy(part).wait_recv()
            next_of(late_steps)
        else:
            post_slot(k + 1)
        if k == parts - 2:
            next_of(late_steps)
        if k:
            cross((low, high), (0, low))
        cross_end(k)
        if k in (parts - 1, 1):
            next_of(early_steps)
    late_term(1)
    late_start(1)
    post_slot(0)
    while early_steps:
        next_of(early_steps)
    while late_steps:
        next_of(late_steps)
    tail = late_events(1)
    next_of(tail)
    ag_finish()
    late_finish(0)
    while tail:
        next_of(tail)
    late_finish(1)
    for make in sends:
        make().wait_send()
    for part in range(3):
        d_copy(part).wait_send()
        for k in range(parts):
            e_copy(part, k).wait_send()
    out_wait(0)
    out_wait(1)
    for copy in ag_out():
        copy.wait()


def second_call(parts, shards, grad_norm, length, saved, grads, first, added, wqkv, hidden):
    xs_shape = saved[4].shape
    _, rows, width = xs_shape
    full = rows * parts
    half_rows = rows // 2
    n, up_rows, vector_rows, total_rows = grad_rows(width, hidden, shards)
    spots = shards // 2
    quarter, eighth = total_rows // 4, total_rows // 8
    heads = (2, full, 128)
    return pl.pallas_call(
        functools.partial(second_kernel, parts, shards, grad_norm),
        in_specs=[VMEM] + [ANY] * 9,
        out_specs=[ANY, ANY, VMEM, ANY, ANY, ANY, VMEM],
        out_shape=[
            jax.ShapeDtypeStruct((2, rows, width), bf16),
            jax.ShapeDtypeStruct((2, rows, width), bf16),
            jax.ShapeDtypeStruct((n, 3 * width), f32),
            jax.ShapeDtypeStruct((n, hidden), f32),
            jax.ShapeDtypeStruct((up_rows, width), f32),
            jax.ShapeDtypeStruct((n, width), f32),
            jax.ShapeDtypeStruct((8, width), f32),
        ],
        scratch_shapes=[
            pltpu.VMEM(xs_shape, bf16),
            pltpu.VMEM((2, 3, full, 128), bf16),
            pltpu.VMEM((2, full, 128), bf16),
            pltpu.VMEM((2, parts, rows, 128), bf16),
            pltpu.VMEM((2, parts, rows, 128), bf16),
            pltpu.VMEM((width, 3 * width), bf16),
            pltpu.VMEM((parts, half_rows, width), f32),
            pltpu.VMEM((spots, total_rows, width), bf16),
            pltpu.VMEM((spots, quarter, width), bf16),
            pltpu.VMEM((spots, quarter, width), bf16),
            pltpu.VMEM((spots, eighth, width), bf16),
            pltpu.VMEM((spots, eighth, width), bf16),
            pltpu.VMEM((spots, quarter, width), bf16),
            pltpu.VMEM((2 * spots, quarter, width), bf16),
            pltpu.VMEM((spots + parts, quarter, width), bf16),
            pltpu.VMEM((total_rows, width), f32),
            pltpu.VMEM(heads, bf16),
            pltpu.VMEM(heads, bf16),
            pltpu.VMEM(heads, bf16),
            pltpu.VMEM(heads, bf16),
            pltpu.VMEM((128, full), bf16),
            pltpu.VMEM((128, full), bf16),
            pltpu.VMEM((128, full), bf16),
            pltpu.VMEM((128, full), f32),
            pltpu.VMEM((128, full), f32),
            pltpu.VMEM((128, full), f32),
            pltpu.VMEM((2, 3, parts, rows, 128), bf16),
            pltpu.VMEM((parts, half_rows, 3 * width), bf16),
            pltpu.VMEM((parts, half_rows, width), bf16),
            pltpu.VMEM((2, width, 384), f32),
            pltpu.VMEM((2, 2, n, 384), bf16),
            pltpu.VMEM((2, spots, 2 * n, 384), f32),
            pltpu.VMEM((2, spots, 2 * n, 384), bf16),
            pltpu.VMEM((2, spots, 2 * n, 384), bf16),
            pltpu.VMEM((2, 2 * parts, n, 384), bf16),
            DMA((16,)),
            DMA((16,)),
            DMA((2,)),
            DMA((2, 3)),
            DMA((2, 24)),
            DMA((2, 2, 16)),
            DMA((2, 2, 4)),
            DMA((2, 3, 4)),
        ],
        compiler_params=pltpu.CompilerParams(
            vmem_limit_bytes=VMEM_LIMIT, collective_id=1, has_side_effects=True
        ),
        name="backward_and_sums",
    )(length, *saved, grads, first, added, wqkv)


def last_kernel(rows_here, lengths, post_h, added_h, dx_h, y, ac, vec, *rest):
    ins, (post_o, accum_o, dx_o, accg_o), outs, vectors = rest[:4], rest[4:8], rest[8:12], rest[12:]
    step = pl.program_id(0)
    for src, dst in zip(ins, outs):
        dst[...] = src[...]

    @pl.when(step == 0)
    def _():
        for i, out in enumerate(vectors):
            out[...] = vec[i : i + 1, : out.shape[1]]

    _, rows, _ = y.shape
    steps = pl.num_programs(0)
    length = lengths[lax.div(step * 2, steps)]
    start = lax.axis_index("head") * rows_here + lax.rem(step, lax.div(steps, 2)) * rows
    keep = lax.broadcasted_iota(jnp.int32, (1, rows, 1), 1) + start < length
    post_o[...] = post_h[...].astype(f32)
    accum_o[...] = jnp.where(keep, y[...].astype(f32) + added_h[...].astype(f32), 0.0)
    dx_o[...] = dx_h[...].astype(f32)
    accg_o[...] = jnp.where(keep, ac[...].astype(f32), 0.0)


def last_call(lengths, tokens, streams, vectors, grads, shards):
    groups, rows, width = tokens[0].shape
    cut = 2
    steps = groups * cut
    block = pl.BlockSpec((1, rows // cut, width), lambda i: (i // cut, i % cut, 0))
    whole = jax.ShapeDtypeStruct((groups, rows, width), f32)
    n = width // shards
    hidden = grads[1].shape[1]
    short = [jax.ShapeDtypeStruct((1, n), f32)] * 5 + [jax.ShapeDtypeStruct((1, hidden // shards), f32)]
    moved = [pl.BlockSpec((g.shape[0], g.shape[1] // steps), lambda i: (0, i)) for g in grads]
    return pl.pallas_call(
        functools.partial(last_kernel, rows),
        grid=(steps,),
        in_specs=[SMEM] + [block] * 5 + [pl.BlockSpec(vectors.shape, lambda i: (0, 0))] + moved,
        out_specs=[block] * 4 + moved + [pl.BlockSpec(o.shape, lambda i: (0, 0)) for o in short],
        out_shape=[whole] * 4 + [jax.ShapeDtypeStruct(g.shape, f32) for g in grads] + short,
        compiler_params=pltpu.CompilerParams(vmem_limit_bytes=VMEM_LIMIT),
        name="outputs",
    )(lengths, *tokens, *streams, vectors, *grads)


def local(
    post_stream,
    accum_stream,
    seq_lengths,
    qkv_weight,
    out_weight,
    norm1_gain,
    norm1_bias,
    up_weight,
    up_bias,
    down_weight,
    down_bias,
    norm2_gain,
    norm2_bias,
    post_cotan,
    accum_cotan,
):
    groups, rows, width = post_stream.shape
    parts = lax.axis_size("head")
    shards = lax.axis_size("seq")
    hidden = up_weight.shape[1]
    grad_norm = float(groups * shards * rows * parts) ** (-0.5)

    def row(vector):
        return vector.reshape(1, -1)

    weights = (
        qkv_weight,
        out_weight,
        row(norm1_gain),
        row(norm1_bias),
        up_weight,
        row(up_bias),
        down_weight,
        row(down_bias),
        row(norm2_gain),
        row(norm2_bias),
    )
    post, added, first, qkv, lse, mixed, go, xs, grads, length = first_call(
        parts, shards, seq_lengths, (post_stream, post_cotan, accum_cotan), weights
    )
    dx, added, qkv_grad, up_grad, down_grad, out_grad, vectors = second_call(
        parts, shards, grad_norm, length, (qkv, lse, mixed, go, xs), grads, first, added, qkv_weight, hidden
    )
    post, accum, post_grad, accum_grad, qkv_grad, up_grad, down_grad, out_grad, *short = last_call(
        seq_lengths,
        (post, added, dx),
        (accum_stream, accum_cotan),
        vectors,
        (qkv_grad, up_grad, down_grad, out_grad),
        shards,
    )
    gain1, bias1, gain2, bias2, down_bias_grad, up_bias_grad = [v.reshape(-1) for v in short]
    return (
        post,
        accum,
        post_grad,
        accum_grad,
        qkv_grad,
        out_grad,
        gain1,
        bias1,
        up_grad,
        up_bias_grad,
        down_grad,
        down_bias_grad,
        gain2,
        bias2,
    )


def solution(mesh):
    tokens = P("seq", "head", None)
    in_specs = (tokens, tokens, P("seq")) + (P(),) * 10 + (tokens, tokens)
    rows = P("seq", None)
    vector = P("seq")
    out_specs = (tokens,) * 4 + (rows, rows, vector, vector, rows, vector, rows, vector, vector, vector)
    return jax.shard_map(local, mesh=mesh, in_specs=in_specs, out_specs=out_specs, check_vma=False)
```

```python
import functools
import itertools

import jax
import jax.numpy as jnp
from jax import lax
from jax.experimental import pallas as pl
from jax.experimental.pallas import tpu as pltpu
from jax.sharding import PartitionSpec as P

H = 8
EPS = 1e-05
NEG = -1e30
LOG2E = 1.4426950408889634
VMEM_LIMIT = 62 * 2**20
bf16 = jnp.bfloat16
f32 = jnp.float32
SMEM = pl.BlockSpec(memory_space=pltpu.SMEM)
VMEM = pl.BlockSpec(memory_space=pltpu.VMEM)
ANY = pl.BlockSpec(memory_space=pl.ANY)
DMA = pltpu.SemaphoreType.DMA


def dot(a, b):
    return jnp.dot(a, b, preferred_element_type=f32)


def dot_nt(a, b):
    return lax.dot_general(a, b, (((1,), (1,)), ((), ())), preferred_element_type=f32)


def dot_tn(a, b):
    return lax.dot_general(a, b, (((0,), (0,)), ((), ())), preferred_element_type=f32)


def split3(value):
    first = value.astype(bf16)
    rest = value - first.astype(f32)
    second = rest.astype(bf16)
    third = (rest - second.astype(f32)).astype(bf16)
    return first, second, third


def lane_sets():
    lane = lax.broadcasted_iota(jnp.int32, (1, 128), 1)
    return lane, (lane < 64, lane >= 64), (64, 0)


def bits_of(count):
    return [1 << b for b in range(count.bit_length() - 1)]


def flip(index, k, count):
    out = 0
    for bit in bits_of(count):
        out = out + (lax.rem(lax.div(index, bit) + (k // bit), 2)) * bit
    return out


def aligned(start, step):
    if isinstance(start, int):
        return start
    return pl.multiple_of(start, step)


def send(src, dst, pair, to):
    return pltpu.make_async_remote_copy(
        src_ref=src,
        dst_ref=dst,
        send_sem=pair[0],
        recv_sem=pair[1],
        device_id=to,
        device_id_type=pl.DeviceIdType.MESH,
    )


def enter(partners):
    barrier = pltpu.get_barrier_semaphore()
    for to in partners:
        pl.semaphore_signal(barrier, inc=1, device_id=to, device_id_type=pl.DeviceIdType.MESH)
    pl.semaphore_wait(barrier, len(partners))


def plane(me, place, parts):
    core = lax.rem(place, 2)
    others = []
    for k in range(parts):
        for other in range(2):
            if k or other:
                seat = place if not other else place + 1 - 2 * core
                others.append((flip(me, k, parts), seat))
    return others


def grad_rows(width, hidden, shards):
    n = width // shards
    up = n * (hidden // width)
    vectors = 16 - n % 16
    total = 2 * up + n + vectors
    return n, up, vectors, -(-total // 128) * 128


def normed(value):
    centre = value - jnp.mean(value, axis=-1, keepdims=True)
    spread = jnp.mean(centre * centre, axis=-1, keepdims=True)
    inv = lax.rsqrt(spread + EPS)
    return centre * inv, inv


def norm_back(cot, unit, inv):
    return (
        cot - jnp.mean(cot, axis=-1, keepdims=True) - unit * jnp.mean(cot * unit, axis=-1, keepdims=True)
    ) * inv


def first_kernel(
    parts,
    shards,
    lengths,
    x,
    pc,
    ac,
    wqkv,
    wo_h,
    g1,
    b1,
    wu_h,
    bu,
    wd_h,
    bd,
    g2,
    b2,
    post_o,
    added_o,
    first_o,
    qkv_o,
    lse_o,
    mixed_o,
    go_o,
    xs_o,
    grads_o,
    length_o,
    xs,
    pcs,
    acs,
    w,
    qkv,
    ka,
    qa,
    vt,
    mixed,
    lse,
    tops,
    accs,
    wo,
    wu,
    wd,
    mix,
    hid,
    pre,
    slope,
    back,
    fgrad,
    mid,
    agrad,
    mgrad,
    post_v,
    added_v,
    first_v,
    small,
    grads,
    core_in,
    sizes,
    load_sem,
    store_sem,
    self_sem,
    insem,
    fsem,
    msem,
    gsem,
    osem,
    nsem,
    csem,
):
    groups, rows, width = x.shape
    hidden = wu.shape[1]
    full = rows * parts
    half = rows // 2
    me = lax.axis_index("head")
    place = lax.axis_index("seq")
    core = lax.rem(place, 2)
    other = place + 1 - 2 * core
    from_core = lax.div(me, 2)
    from_group = lax.rem(me, 2)
    lane, mine, base = lane_sets()
    one = jnp.ones((), bf16)
    zero = jnp.zeros((), bf16)
    here = pl.ds(aligned(core * half, half), half)
    there = pl.ds(aligned((1 - core) * half, half), half)

    load_count = itertools.count()

    def load(src, dst):
        copy = pltpu.make_async_copy(src, dst, load_sem.at[next(load_count)])
        copy.start()
        return copy

    stores = []
    store_count = itertools.count()

    def store(src, dst):
        copy = pltpu.make_async_copy(src, dst, store_sem.at[next(store_count)])
        copy.start()
        stores.append(copy)

    w_in = [
        load(
            wqkv.at[:, pl.ds(aligned(part * width + core * 256, 128), 256)],
            w.at[:, part * 256 : part * 256 + 256],
        )
        for part in range(3)
    ]
    wo_in = load(wo_h, wo)
    wu_in = load(wu_h, wu)
    wd_in = load(wd_h, wd)

    enter(plane(me, place, parts))

    def in_copies(a, twist, r):
        group = from_group if not twist else 1 - from_group
        src = (x, pc, ac)[a].at[group, r * half : (r + 1) * half]
        slot = twist + 2 * lax.rem(from_core + core, 2)
        dst = xs.at[slot, r * half : (r + 1) * half] if a == 0 else (pcs, acs)[a - 1].at[slot]
        sems = (insem.at[0, a, 2 * twist + r], insem.at[1, a, slot])
        remote = send(src, dst, sems, (2 * core + group, place - core + r))
        if twist:
            return remote, None, None
        return remote, pltpu.make_async_copy(src, dst, self_sem.at[a]), (from_core == core) & (core == r)

    def in_start(a, twist):
        for r in (0, 1):
            remote, local, own = in_copies(a, twist, r)
            if twist:
                remote.start()
            else:
                pl.when(own)(local.start)
                pl.when(jnp.logical_not(own))(remote.start)

    def in_sent(a, twist):
        for r in (0, 1):
            remote, local, own = in_copies(a, twist, r)
            if twist:
                remote.wait_send()
            else:
                pl.when(jnp.logical_not(own))(remote.wait_send)

    def in_wait(a, k):
        dst = xs.at[k, here] if a == 0 else (pcs, acs)[a - 1].at[k]
        src = (x, pc, ac)[a].at[0, :half]
        remote = send(src, dst, (insem.at[0, a, 0], insem.at[1, a, k]), (flip(me, k, parts), place))
        if k:
            remote.wait_recv()
        else:
            local = pltpu.make_async_copy(src, dst, self_sem.at[a])
            pl.when(from_core == core)(local.wait)
            pl.when(from_core != core)(remote.wait_recv)

    def across(src, dst, pair):
        return send(src, dst, pair, (me, other))

    def pass_on(k):
        part = xs.at[k, here]
        return across(part, part, (fsem.at[0, k], fsem.at[1, k]))

    size_copy = across(sizes.at[0], sizes.at[1], (nsem.at[0], nsem.at[1]))

    def m_copy(p):
        return across(
            mixed.at[p, :, there],
            mix.at[:, :, pl.ds(aligned((2 * core + p) * 128, 128), 128)],
            (msem.at[0, p], msem.at[1, p]),
        )

    def g_copy(p, u):
        chunks = slice(2 * u, 2 * u + 2)
        return across(
            mgrad.at[chunks, :, pl.ds(aligned((2 * (1 - core) + p) * 128, 128), 128)],
            go_o.at[p, chunks, here],
            (gsem.at[0, p, u], gsem.at[1, p, u]),
        )

    def out_copies(k):
        dst = post_o.at[from_group, here]
        to = (flip(me, k, parts), place - core + from_core)
        remote = send(post_v.at[k], dst, (osem.at[0, k], osem.at[1, 2 * from_group + core]), to)
        return remote, pltpu.make_async_copy(post_v.at[k], dst, self_sem.at[3])

    def out_start(k):
        remote, local = out_copies(k)
        if k:
            remote.start()
        else:
            pl.when(from_core == core)(local.start)
            pl.when(from_core != core)(remote.start)

    def out_wait():
        for k in range(parts):
            remote, local = out_copies(k)
            if k:
                remote.wait_send()
            else:
                pl.when(from_core == core)(local.wait)
                pl.when(from_core != core)(remote.wait_send)
        for s in (0, 1):
            for r in (0, 1):
                chip = 2 * core + s
                dst = post_o.at[s, r * half : (r + 1) * half]
                remote = send(
                    post_v.at[0], dst, (osem.at[0, 0], osem.at[1, 2 * s + r]), (chip, place - core + r)
                )
                pl.when(jnp.logical_not((chip == me) & (core == r)))(remote.wait_recv)

    in_start(0, 0)
    pl.when(from_core == core)(functools.partial(in_start, 0, 1))
    which = lax.broadcasted_iota(jnp.int32, (8, 128), 0)
    sizes[0] = jnp.where(which == 0, lengths[0], lengths[1]).astype(f32)
    size_copy.start()
    for copy in w_in:
        copy.wait()
    size_copy.wait_recv()
    held = jnp.where(from_core == core, sizes[0], sizes[1])
    length = jnp.sum(jnp.where(which == from_group, held, 0.0), axis=0, keepdims=True)
    length_o[...] = jnp.broadcast_to(length, (8, 128))
    length = length[:, :1]

    def below(count, start):
        pos = lax.broadcasted_iota(jnp.int32, (count, 1), 0) + start
        return pos.astype(f32) < length

    @pl.when(from_core != core)
    def _():
        in_sent(0, 0)
        in_start(0, 1)

    def project(k):
        pass_on(k).wait_recv()
        at = slice(k * rows, (k + 1) * rows)
        three = dot(xs[k], w[...])
        bias = jnp.where(below(rows, flip(me, k, parts) * rows), 0.0, NEG)
        step = lax.rem(lane, 64)
        key_more = jnp.where(step == 0, bias, 0.0).astype(bf16)
        query_more = jnp.where(step == 0, one, zero)
        for p in (0, 1):
            cut = slice(p * 128, p * 128 + 128)
            query = (three[:, :256][:, cut] * (LOG2E * 64 ** (-0.5))).astype(bf16)
            keys = three[:, 256:512][:, cut].astype(bf16)
            values = three[:, 512:][:, cut].astype(bf16)
            qkv[p, 0, at] = query
            qkv[p, 1, at] = keys
            qkv[p, 2, at] = values
            turned = values.T
            for h in range(2):
                ka[2 * p + h, at] = jnp.where(mine[h], keys, key_more)
                qa[2 * p + h, at] = jnp.where(mine[h], query, query_more)
                vt[2 * p + h, :64, at] = turned[h * 64 : h * 64 + 64]
                vt[2 * p + h, 64:, at] = jnp.ones((8, rows), bf16)

    def rectangle(p, keys, queries):
        for h in range(2):
            g = 2 * p + h
            scores = dot_nt(ka[g, keys, :], qa[g, queries, :])
            top = tops[g, 0:1, queries]
            new_top = jnp.maximum(top, jnp.max(scores, axis=0, keepdims=True))
            probs = jnp.exp2(scores - new_top)
            tops[g, 0:1, queries] = new_top
            accs[g, :, queries] = accs[g, :, queries] * jnp.exp2(top - new_top) + dot(
                vt[g, :, keys], probs.astype(bf16)
            )

    early = full - rows

    def attend_early(p):
        def body(j, carry):
            rectangle(p, pl.ds(aligned(j * rows, rows), rows), slice(0, early))
            return carry

        lax.fori_loop(0, parts - 1, body, None)

    tops[...] = jnp.full(tops.shape, NEG, f32)
    accs[...] = jnp.zeros_like(accs)
    for k in range(parts - 1):
        in_wait(0, k)
        pass_on(k).start()
    for k in range(parts - 1):
        project(k)
    for a in (1, 2):
        for twist in (0, 1):
            in_start(a, twist)
    attend_early(0)
    in_wait(0, parts - 1)
    pass_on(parts - 1).start()
    attend_early(1)
    project(parts - 1)
    store(qkv, qkv_o)
    store(xs, xs_o)

    def attend(p):
        rectangle(p, slice(early, full), slice(0, full))
        rectangle(p, slice(0, early), slice(early, full))
        pieces = []
        terms = []
        for h in range(2):
            top, acc = tops[2 * p + h, 0:1], accs[2 * p + h]
            total = acc[64:65]
            pieces.append(acc[:64] / total)
            a, b, c = split3(-(top + jnp.log2(total)))
            flat = [jnp.ones((1, full), f32)] + [v.astype(f32) for v in (a, b, c)]
            terms.append(jnp.concatenate(flat + [jnp.zeros((60, full), f32)], 0))
        lse[p] = jnp.concatenate([terms[1], terms[0]], 0).T.astype(bf16)
        mixed[p] = jnp.concatenate(pieces, 0).T.astype(bf16).reshape(parts, rows, 128)
        m_copy(p).start()
        mix[:, :, pl.ds(aligned((2 * core + p) * 128, 128), 128)] = mixed[p, :, here]

    attend(0)
    attend(1)
    store(mixed, mixed_o)
    store(lse, lse_o)

    tile = 512
    tiles = hidden // tile
    small[...] = jnp.zeros_like(small)

    def feed(u):
        chunks = (2 * u, 2 * u + 1)
        keep = jnp.concatenate([below(half, flip(me, k, parts) * rows + core * half) for k in chunks], 0)
        mix_u = mix[2 * u : 2 * u + 2].reshape(rows, width)
        x_u = jnp.concatenate([xs[k, here] for k in chunks], 0)
        attention = dot(mix_u, wo[...])
        unit1, inv1 = normed(x_u.astype(f32) + attention)
        x_mid = unit1 * g1[...] + b1[...]
        mid[u] = x_mid.astype(bf16)
        total = jnp.zeros((rows, width), f32)
        c0 = 0.7978845608028654
        c1 = 0.044715
        for t in range(tiles):
            cols = slice(t * tile, (t + 1) * tile)
            act = dot(mid[u], wu[:, cols]) + bu[:, cols]
            square = act * act
            th = jnp.tanh(act * (c0 + (c0 * c1) * square))
            part = 0.5 + 0.5 * th
            smooth = act * part
            low = smooth.astype(bf16)
            hid[u, :, cols] = low
            slope[:rows, cols] = part + smooth * (1.0 - part) * (2.0 * c0 + (6.0 * c0 * c1) * square)
            total = total + dot(low, wd[cols, :])
        total = total + bd[...]
        unit2, inv2 = normed(x_mid + total)
        post = jnp.where(keep, unit2 * g2[...] + b2[...], 0.0).astype(bf16)
        added = jnp.where(keep, attention + total, 0.0).astype(bf16)
        post_v[2 * u : 2 * u + 2] = post.reshape(2, half, width)
        added_v[2 * u : 2 * u + 2] = added.reshape(2, half, width)
        for k in chunks:
            out_start(k)
        store(added_v.at[2 * u : 2 * u + 2], added_o.at[2 * u : 2 * u + 2])
        post_c = jnp.where(keep, pcs[2 * u : 2 * u + 2].reshape(rows, width).astype(f32), 0.0)
        accum_c = jnp.where(keep, acs[2 * u : 2 * u + 2].reshape(rows, width).astype(f32), 0.0)
        mid_grad2 = norm_back(post_c * g2[...], unit2, inv2)
        small[2:3, :width] += jnp.sum(post_c * unit2, axis=0, keepdims=True)
        small[3:4, :width] += jnp.sum(post_c, axis=0, keepdims=True)
        feed_grad = (mid_grad2 + accum_c).astype(bf16)
        fgrad[u] = feed_grad
        small[4:5, :width] += jnp.sum(feed_grad.astype(f32), axis=0, keepdims=True)
        back[...] = mid_grad2
        for t in range(tiles):
            cols = slice(t * tile, (t + 1) * tile)
            hidden_grad = dot_nt(fgrad[u], wd[cols, :]).astype(bf16)
            pre_grad = (hidden_grad.astype(f32) * slope[:rows, cols]).astype(bf16)
            pre[u, :, cols] = pre_grad
            small[5:6, cols] += jnp.sum(pre_grad.astype(f32), axis=0, keepdims=True)
            back[...] += dot_nt(pre_grad, wu[:, cols])
        mid_grad = back[...]
        small[0:1, :width] += jnp.sum(mid_grad * unit1, axis=0, keepdims=True)
        small[1:2, :width] += jnp.sum(mid_grad, axis=0, keepdims=True)
        first = norm_back(mid_grad * g1[...], unit1, inv1)
        first_v[2 * u : 2 * u + 2] = first.reshape(2, half, width)
        store(first_v.at[2 * u : 2 * u + 2], first_o.at[2 * u : 2 * u + 2])
        attn_grad = (first + accum_c).astype(bf16)
        agrad[u] = attn_grad
        mgrad[2 * u : 2 * u + 2] = dot_nt(attn_grad, wo[...]).astype(bf16).reshape(2, half, width)
        for p in (0, 1):
            g_copy(p, u).start()
            own = mgrad.at[2 * u : 2 * u + 2, :, pl.ds(aligned((2 * core + p) * 128, 128), 128)]
            store(own, go_o.at[p, 2 * u : 2 * u + 2, here])

    wo_in.wait()
    wu_in.wait()
    wd_in.wait()
    for a in (1, 2):
        for k in range(parts):
            in_wait(a, k)
    for p in (0, 1):
        m_copy(p).wait_recv()
    for u in (0, 1):
        feed(u)

    n, up_rows, vector_rows, total_rows = grad_rows(width, hidden, shards)
    halves = (0, 1)

    def spot_of(shard):
        return lax.rem(core + shard % 2, 2), shard // 2

    edges = (0, up_rows, 2 * up_rows, total_rows)

    def c_copy(i):
        at = slice(edges[i], edges[i + 1])
        return across(grads.at[1, :, at], core_in.at[:, at], (csem.at[0, i], csem.at[1, i]))

    for t in range(tiles):
        cols = slice(t * tile, (t + 1) * tile)
        slope[:width, cols] = sum(dot_tn(mid[u], pre[u, :, cols]) for u in halves)
    for shard in range(shards):
        own = slice(shard * n, (shard + 1) * n)
        block = jnp.concatenate([slope[own, t * tile : (t + 1) * tile] for t in range(tiles)], 0)
        side, spot = spot_of(shard)
        grads[side, spot, :up_rows] = block.astype(bf16)
    c_copy(0).start()
    per = tile // up_rows
    for t in range(tiles):
        cols = slice(t * tile, (t + 1) * tile)
        block = sum(dot_tn(hid[u, :, cols], fgrad[u]) for u in halves).astype(bf16)
        for i in range(per):
            side, spot = spot_of(t * per + i)
            grads[side, spot, up_rows : 2 * up_rows] = block[i * up_rows : (i + 1) * up_rows]
    c_copy(1).start()
    out_all = sum(dot_tn(mix[2 * u : 2 * u + 2].reshape(rows, width), agrad[u]) for u in halves)
    line = lax.broadcasted_iota(jnp.int32, (8, width), 0)
    short = small[:, :width]
    long = small[...]
    for shard in range(shards):
        a = pltpu.roll(short, (width - shard * n) % width, 1)
        b = pltpu.roll(long, (hidden - shard * up_rows) % hidden, 1)[:, :width]
        extra = jnp.where(line == 5, b, a)
        rest = total_rows - 2 * up_rows - n - 8
        block = jnp.concatenate(
            [out_all[shard * n : (shard + 1) * n], extra, jnp.zeros((rest, width), f32)], 0
        )
        side, spot = spot_of(shard)
        grads[side, spot, 2 * up_rows :] = block.astype(bf16)
    c_copy(2).start()
    for i in range(3):
        c_copy(i).wait_recv()

        def add_cores(spot, carry, i=i):
            at = slice(edges[i], edges[i + 1])
            grads[0, spot, at] = (grads[0, spot, at].astype(f32) + core_in[spot, at].astype(f32)).astype(bf16)
            return carry

        lax.fori_loop(0, shards // 2, add_cores, None)
    store(grads.at[0], grads_o)
    for i in range(3):
        c_copy(i).wait_send()

    pl.when(from_core == core)(functools.partial(in_sent, 0, 0))
    in_sent(0, 1)
    for a in (1, 2):
        for twist in (0, 1):
            in_sent(a, twist)
    for k in range(parts):
        pass_on(k).wait_send()
    size_copy.wait_send()
    for p in (0, 1):
        m_copy(p).wait_send()
        for u in (0, 1):
            g_copy(p, u).wait()
    out_wait()
    for copy in stores:
        copy.wait()


def first_call(parts, shards, lengths, streams, weights):
    groups, rows, width = streams[0].shape
    hidden = weights[4].shape[1]
    full = rows * parts
    half = rows // 2
    total_rows = grad_rows(width, hidden, shards)[3]
    held = jax.ShapeDtypeStruct((groups, rows, width), bf16)
    return pl.pallas_call(
        functools.partial(first_kernel, parts, shards),
        in_specs=[SMEM] + [ANY] * 5 + [VMEM, VMEM, ANY, VMEM, ANY, VMEM, VMEM, VMEM],
        out_specs=[ANY] * 9 + [VMEM],
        out_shape=[
            held,
            jax.ShapeDtypeStruct((parts, half, width), bf16),
            jax.ShapeDtypeStruct((parts, half, width), f32),
            jax.ShapeDtypeStruct((2, 3, full, 128), bf16),
            jax.ShapeDtypeStruct((2, full, 128), bf16),
            jax.ShapeDtypeStruct((2, parts, rows, 128), bf16),
            jax.ShapeDtypeStruct((2, parts, rows, 128), bf16),
            jax.ShapeDtypeStruct((parts, rows, width), bf16),
            jax.ShapeDtypeStruct((shards // 2, total_rows, width), bf16),
            jax.ShapeDtypeStruct((8, 128), f32),
        ],
        scratch_shapes=[
            pltpu.VMEM((parts, rows, width), bf16),
            pltpu.VMEM((parts, half, width), bf16),
            pltpu.VMEM((parts, half, width), bf16),
            pltpu.VMEM((width, 768), bf16),
            pltpu.VMEM((2, 3, full, 128), bf16),
            pltpu.VMEM((4, full, 128), bf16),
            pltpu.VMEM((4, full, 128), bf16),
            pltpu.VMEM((4, 72, full), bf16),
            pltpu.VMEM((2, parts, rows, 128), bf16),
            pltpu.VMEM((2, full, 128), bf16),
            pltpu.VMEM((4, 8, full), f32),
            pltpu.VMEM((4, 72, full), f32),
            pltpu.VMEM((width, width), bf16),
            pltpu.VMEM((width, hidden), bf16),
            pltpu.VMEM((hidden, width), bf16),
            pltpu.VMEM((parts, half, width), bf16),
            pltpu.VMEM((2, rows, hidden), bf16),
            pltpu.VMEM((2, rows, hidden), bf16),
            pltpu.VMEM((max(rows, width), hidden), f32),
            pltpu.VMEM((rows, width), f32),
            pltpu.VMEM((2, rows, width), bf16),
            pltpu.VMEM((2, rows, width), bf16),
            pltpu.VMEM((2, rows, width), bf16),
            pltpu.VMEM((parts, half, width), bf16),
            pltpu.VMEM((parts, half, width), bf16),
            pltpu.VMEM((parts, half, width), bf16),
            pltpu.VMEM((parts, half, width), f32),
            pltpu.VMEM((8, hidden), f32),
            pltpu.VMEM((2, shards // 2, total_rows, width), bf16),
            pltpu.VMEM((shards // 2, total_rows, width), bf16),
            pltpu.VMEM((2, 8, 128), f32),
            DMA((8,)),
            DMA((16,)),
            DMA((5,)),
            DMA((2, 3, 4)),
            DMA((2, parts)),
            DMA((2, 2)),
            DMA((2, 2, 2)),
            DMA((2, 4)),
            DMA((2,)),
            DMA((2, 3)),
        ],
        compiler_params=pltpu.CompilerParams(
            vmem_limit_bytes=VMEM_LIMIT, collective_id=0, has_side_effects=True
        ),
        name="forward_and_feed",
    )(lengths, *streams, *weights)


def second_kernel(
    parts,
    shards,
    grad_norm,
    length_v,
    qkv_h,
    lse_h,
    mixed_h,
    go_h,
    xs_h,
    grads_h,
    first_h,
    added_h,
    wqkv_h,
    dx_o,
    added_o,
    wqkv_o,
    up_o,
    down_o,
    out_o,
    vec_o,
    xs,
    qkv,
    lse,
    mixed,
    go,
    wqkv,
    first,
    grads,
    a1_in,
    b1_in,
    a2_in,
    b2_in,
    z_in,
    all_out,
    all_in,
    final,
    ka,
    va,
    qa,
    da,
    kt,
    qt,
    gt,
    dqt,
    dkt,
    dvt,
    dsend,
    dfull,
    dx_v,
    late,
    late_out,
    late_sum,
    late_step,
    late_got,
    late_all,
    load_sem,
    store_sem,
    self_sem,
    dsem,
    rsem,
    lsem,
    osem,
    esem,
):
    parts, rows, width = xs.shape
    half_rows = rows // 2
    full = rows * parts
    hidden = up_o.shape[1]
    me = lax.axis_index("head")
    place = lax.axis_index("seq")
    core = lax.rem(place, 2)
    other = place + 1 - 2 * core
    from_core = lax.div(me, 2)
    from_group = lax.rem(me, 2)
    here = pl.ds(aligned(core * half_rows, half_rows), half_rows)
    there = pl.ds(aligned((1 - core) * half_rows, half_rows), half_rows)
    length = length_v[0:1, 0:1]
    lane, mine, base = lane_sets()
    one = jnp.ones((), bf16)
    zero = jnp.zeros((), bf16)
    n, up_rows, vector_rows, total_rows = grad_rows(width, hidden, shards)
    seq_bits = bits_of(shards)
    load_count = itertools.count()

    def load(src, dst):
        copy = pltpu.make_async_copy(src, dst, load_sem.at[next(load_count)])
        copy.start()
        return copy

    def pair_load(p):
        return [
            load(qkv_h.at[p], qkv.at[p]),
            load(go_h.at[p], go.at[p]),
            load(mixed_h.at[p], mixed.at[p]),
            load(lse_h.at[p], lse.at[p]),
        ]

    pair_in = [pair_load(0)]
    grads_in = load(grads_h, grads)
    xs_in = load(xs_h, xs)
    pair_in.append(pair_load(1))
    wqkv_in = load(wqkv_h, wqkv)
    first_in = load(first_h, first)

    enter(plane(me, place, parts) + [(me, flip(place, bit, shards)) for bit in seq_bits[1:]])

    sends = []

    def launch(make, *which):
        make(*which).start()
        sends.append(functools.partial(make, *which))

    spots = shards // 2
    half, quarter = total_rows // 2, total_rows // 4
    eighth = total_rows // 8
    x_bit = lax.rem(me, 2)
    y_bit = lax.div(me, 2)

    def to_head(src, dst, i, k):
        return send(src, dst, (rsem.at[0, i], rsem.at[1, i]), (flip(me, k, parts), place))

    def to_seq(src, dst, i, bit):
        return send(src, dst, (rsem.at[0, i], rsem.at[1, i]), (me, flip(place, bit, shards)))

    a_keep = x_bit * quarter
    a_give = (1 - x_bit) * quarter
    b_keep = half + y_bit * quarter
    b_give = half + (1 - y_bit) * quarter
    a1_copy = lambda: to_head(grads_h.at[:, pl.ds(aligned(a_give, 16), quarter)], a1_in, 1, 1)
    b1_copy = lambda: to_head(grads_h.at[:, pl.ds(aligned(b_give, 16), quarter)], b1_in, 2, 2)
    a_own = a_keep + y_bit * eighth
    a_pass = a_keep + (1 - y_bit) * eighth
    b_own = b_keep + x_bit * eighth
    b_pass = b_keep + (1 - x_bit) * eighth
    a2_copy = lambda: to_head(grads.at[:, pl.ds(aligned(a_pass, 16), eighth)], a2_in, 3, 2)
    b2_copy = lambda: to_head(grads.at[:, pl.ds(aligned(b_pass, 16), eighth)], b2_in, 4, 1)

    def add_rows(into, spot, start, count, other):
        at = pl.ds(aligned(start, 16), count)
        into[spot, at] = (into[spot, at].astype(f32) + other.astype(f32)).astype(bf16)

    def early_first():
        grads_in.wait()
        a1_copy().wait_recv()
        b1_copy().wait_recv()

        def body(i, carry):
            add_rows(grads, i, a_keep, quarter, a1_in[i])
            add_rows(grads, i, b_keep, quarter, b1_in[i])
            return carry

        lax.fori_loop(0, spots, body, None)
        launch(a2_copy)
        launch(b2_copy)

    def early_second_and_on():
        a2_copy().wait_recv()
        b2_copy().wait_recv()

        def body(i, carry):
            add_rows(grads, i, a_own, eighth, a2_in[i])
            add_rows(grads, i, b_own, eighth, b2_in[i])
            return carry

        lax.fori_loop(0, spots, body, None)

        def gather(i, carry):
            all_out[i, :eighth] = grads[i, pl.ds(aligned(a_own, 16), eighth)]
            all_out[i, eighth:] = grads[i, pl.ds(aligned(b_own, 16), eighth)]
            return carry

        lax.fori_loop(0, spots, gather, None)
        if steps:
            z_send(0)

    offsets = []
    at = 0
    size = spots
    for bit in seq_bits[1:]:
        offsets.append((at, size))
        at += size
        size //= 2
    offsets.append((at, 1))
    steps = len(offsets) - 1
    z_offsets = []
    at = 0
    for _, size in offsets[:-1]:
        z_offsets.append(at)
        at += size // 2

    def z_copy(i):
        at, size = offsets[i]
        bit = seq_bits[1 + i]
        return to_seq(
            all_in.at[pl.ds(z_offsets[i], size // 2)], z_in.at[pl.ds(z_offsets[i], size // 2)], 5 + i, bit
        )

    def z_send(i):
        at, size = offsets[i]
        own = lax.rem(lax.div(place, seq_bits[1 + i]), 2)
        for j in range(size // 2):
            all_in[z_offsets[i] + j] = all_out[at + 2 * j + (1 - own)]
        launch(z_copy, i)

    def z_add(i):
        at, size = offsets[i]
        after = offsets[i + 1][0]
        own = lax.rem(lax.div(place, seq_bits[1 + i]), 2)
        z_copy(i).wait_recv()
        for j in range(size // 2):
            all_out[after + j] = (
                all_out[at + 2 * j + own].astype(f32) + z_in[z_offsets[i] + j].astype(f32)
            ).astype(bf16)

    ag_from = 5 + steps
    last = offsets[-1][0]
    ag = sum(size // 2 for _, size in offsets[:-1])

    def ag_copy(k):
        return to_head(all_out.at[last], all_in.at[ag + k], ag_from + k, k)

    def ag_send():
        for k in range(parts - 1, 0, -1):
            launch(ag_copy, k)

    def ag_out():
        moves = [
            (final.at[t * n : (t + 1) * n], up_o.at[:, t * width : (t + 1) * width])
            for t in range(hidden // width)
        ]
        moves.append((final.at[up_rows : 2 * up_rows], down_o))
        moves.append((final.at[2 * up_rows : 2 * up_rows + n], out_o))
        return [pltpu.make_async_copy(src, dst, store_sem.at[i]) for i, (src, dst) in enumerate(moves)]

    def ag_finish():
        for k in range(parts):
            if k:
                ag_copy(k).wait_recv()
                block = all_in[ag + k]
            else:
                block = all_out[last]
            block = block.astype(f32) * grad_norm
            who = flip(me, k, parts)
            x_of, y_of = lax.rem(who, 2), lax.div(who, 2)
            a_at = x_of * quarter + y_of * eighth
            b_at = half + y_of * quarter + x_of * eighth
            final[pl.ds(aligned(a_at, 16), eighth)] = block[:eighth]
            final[pl.ds(aligned(b_at, 16), eighth)] = block[eighth:]
        for copy in ag_out():
            copy.start()
        vec_o[...] = final[2 * up_rows + n : 2 * up_rows + n + 8]

    def d_copy(part):
        return send(
            dsend.at[0, part, :, there],
            dfull.at[:, :, pl.ds(aligned(part * width + 2 * core * 128, 128), 128)],
            (dsem.at[0, part], dsem.at[1, part]),
            (me, other),
        )

    def e_copy(part, k):
        return send(
            dsend.at[1, part, k, there],
            dfull.at[k, :, pl.ds(aligned(part * width + (2 * core + 1) * 128, 128), 128)],
            (esem.at[0, part, k], esem.at[1, part, k]),
            (me, other),
        )

    def prepare(p):
        for copy in pair_in[p]:
            copy.wait()
        low_half = lane < 64
        row_of = lax.broadcasted_iota(jnp.int32, (128, 128), 0)
        lane_of = lax.broadcasted_iota(jnp.int32, (128, 128), 1)
        picks = ((row_of < 64) & (lane_of >= 64) & (lane_of < 67)) | ((row_of >= 64) & (lane_of < 3))
        picks = jnp.where(picks, -1.0, 0.0).astype(bf16)
        step = lax.rem(lane, 64)
        kt[...] = qkv[p, 1].T
        qt[...] = qkv[p, 0].T
        gt[...] = go[p].reshape(full, 128).T
        for k in range(parts):
            at = slice(k * rows, (k + 1) * rows)
            query, keys, values = qkv[p, 0, at], qkv[p, 1, at], qkv[p, 2, at]
            pos = lax.broadcasted_iota(jnp.int32, (rows, 1), 0) + flip(me, k, parts) * rows
            bias = jnp.where(pos.astype(f32) < length, 0.0, NEG)
            key_more = jnp.where(step == 0, bias, 1.0).astype(bf16)
            grad = go[p, k]
            prod = grad.astype(f32) * mixed[p, k].astype(f32)
            high = prod.astype(bf16)
            sums = dot(high, picks) + dot((prod - high.astype(f32)).astype(bf16), picks)
            second = sums - sums.astype(bf16).astype(f32)
            third = second - second.astype(bf16).astype(f32)
            grad_more = jnp.where(step == 0, sums, jnp.where(step == 1, second, third)).astype(bf16)
            query_more = lse[p, at]
            ka[0, at] = jnp.where(low_half, keys, key_more)
            ka[1, at] = jnp.where(low_half, key_more, keys)
            va[0, at] = jnp.where(low_half, values, one)
            va[1, at] = jnp.where(low_half, one, values)
            qa[0, at] = jnp.where(low_half, query, query_more)
            qa[1, at] = jnp.where(low_half, query_more, query)
            da[0, at] = jnp.where(low_half, grad, grad_more)
            da[1, at] = jnp.where(low_half, grad_more, grad)
        dqt[...] = jnp.zeros_like(dqt)

    steps_each = 2 * parts
    cols_each = full // 2

    def attend_back(p, events):
        def body(j, carry):
            at = pl.ds(aligned(j * rows, rows), rows)
            totals = [None, None]
            for i in range(2):
                for when, event in events.items():
                    if when % 2 == i:
                        pl.when(j == when // 2)(event)
                cols = slice(i * cols_each, (i + 1) * cols_each)
                for h in range(2):
                    part = slice(h * 64, h * 64 + 64)
                    probs = jnp.exp2(dot_nt(qa[h, cols], ka[h, at, :]))
                    inner = dot_nt(da[h, cols], va[h, at, :])
                    low = probs.astype(bf16)
                    grad = (probs * inner).astype(bf16)
                    dv = dot(gt[part, cols], low)
                    dk = dot(qt[part, cols], grad)
                    dqt[part, cols] += dot_nt(kt[part, at], grad)
                    totals[h] = (dv, dk) if i == 0 else (totals[h][0] + dv, totals[h][1] + dk)
            dv = jnp.concatenate([totals[0][0], totals[1][0]], 0).T
            dk = jnp.concatenate([totals[0][1], totals[1][1]], 0).T
            dsend[p, 1, j] = (dk * (1.0 / LOG2E)).astype(bf16)
            dsend[p, 2, j] = dv.astype(bf16)
            return carry

        lax.fori_loop(0, parts, body, None)
        dsend[p, 0] = (dqt[...] * 64 ** (-0.5)).T.astype(bf16).reshape(parts, rows, 128)
        for part in range(3):
            d_copy(part).start()
            dfull[:, :, pl.ds(aligned(part * width + (2 * core + p) * 128, 128), 128)] = dsend[p, part, :, here]

    def cross(queries, keys):
        for q0 in range(queries[0], queries[1], 2 * rows):
            q = slice(q0, min(q0 + 2 * rows, queries[1]))
            wide = rows if queries[1] - queries[0] > rows else 2 * rows
            for k0 in range(keys[0], keys[1], wide):
                k = slice(k0, min(k0 + wide, keys[1]))
                for h in range(2):
                    part = slice(h * 64, h * 64 + 64)
                    probs = jnp.exp2(dot_nt(qa[h, q], ka[h, k]))
                    inner = dot_nt(da[h, q], va[h, k])
                    low = probs.astype(bf16)
                    grad = (probs * inner).astype(bf16)
                    dvt[part, k] += dot(gt[part, q], low)
                    dkt[part, k] += dot(qt[part, q], grad)
                    dqt[part, q] += dot_nt(kt[part, k], grad)

    def cross_end(k):
        at = slice(k * rows, (k + 1) * rows)
        parts_of = (dqt[:, at] * 64 ** (-0.5), dkt[:, at] * (1.0 / LOG2E), dvt[:, at])
        for part, value in enumerate(parts_of):
            dsend[1, part, k] = value.T.astype(bf16)
            e_copy(part, k).start()
            to = pl.ds(aligned(part * width + (2 * core + 1) * 128, 128), 128)
            dfull[k, :, to] = dsend[1, part, k, here]

    def post_slot(k):
        for part in range(3):
            e_copy(part, k).wait_recv()
        dx_v[k] = (first[k] + dot_nt(dfull[k], wqkv[...])).astype(bf16)
        out_start(1, k)

    def late_term(p):
        total = sum(
            dot_tn(xs[k], jnp.concatenate([dsend[p, part, k] for part in range(3)], 1)) for k in range(parts)
        )
        for part in range(3):
            late[3 * p + part] = total[:, part * 128 : part * 128 + 128]

    l_steps = len(seq_bits)
    l_sizes = [0] + [spots >> i for i in range(l_steps - 1)]
    l_offsets = [0] + [sum(size // 2 for size in l_sizes[1:i]) for i in range(1, l_steps)]

    def l_copy(u, i):
        at = pl.ds(l_offsets[i], l_sizes[i] // 2)
        return send(
            late_step.at[u, at],
            late_got.at[u, at],
            (lsem.at[0, u, i], lsem.at[1, u, i]),
            (me, flip(place, seq_bits[i], shards)),
        )

    def lg_copy(u, k, o):
        slot = 2 * k + o
        return send(
            late_out.at[u, core if o == 0 else 1 - core],
            late_all.at[u, slot],
            (lsem.at[0, u, l_steps + slot], lsem.at[1, u, l_steps + slot]),
            (flip(me, k, parts), place if o == 0 else other),
        )

    def late_spot(u, i, spot):
        if i == 1:
            return late[u, pl.ds(aligned(spot * (2 * n), 16), 2 * n)]
        return late_sum[u, spot]

    def late_split(u, i):
        own = lax.rem(lax.div(place, seq_bits[i]), 2)
        for j in range(l_sizes[i] // 2):
            late_step[u, l_offsets[i] + j] = late_spot(u, i, 2 * j + 1 - own).astype(bf16)
        launch(l_copy, u, i)

    def late_merge(u, i):
        own = lax.rem(lax.div(place, seq_bits[i]), 2)
        l_copy(u, i).wait_recv()
        for j in range(l_sizes[i] // 2):
            late_sum[u, j] = late_spot(u, i, 2 * j + own) + late_got[u, l_offsets[i] + j].astype(f32)

    def late_share(u):
        total = late_sum[u, 0] if l_steps > 1 else late[u, :]
        late_out[u, 0] = total[:n].astype(bf16)
        late_out[u, 1] = total[n:].astype(bf16)
        for k in range(parts - 1, -1, -1):
            for o in range(2):
                if k or o:
                    launch(lg_copy, u, k, o)

    def late_finish(u):
        for o in range(2):
            total = late_out[u, core].astype(f32) if o == 0 else None
            for k in range(parts):
                if k or o:
                    lg_copy(u, k, o).wait_recv()
                    piece = late_all[u, 2 * k + o].astype(f32)
                    total = piece if total is None else total + piece
            total = total * grad_norm
            owner = core if o == 0 else 1 - core
            to = aligned((u % 3) * width + (2 * owner + u // 3) * 128, 128)
            wqkv_o[:, pl.ds(to, 128)] = total

    def late_start(u):
        if l_steps > 1:
            late_split(u, 1)
        else:
            late_share(u)

    def late_events(u):
        steps_of = []
        for i in range(1, l_steps):

            def step(i=i):
                late_merge(u, i)
                if i + 1 < l_steps:
                    late_split(u, i + 1)
                else:
                    late_share(u)

            steps_of.append(step)
        return steps_of

    def out_copies(a, k):
        src = (added_h, dx_v)[a].at[k]
        dst = (added_o, dx_o)[a].at[from_group, here]
        to = (flip(me, k, parts), place - core + from_core)
        remote = send(src, dst, (osem.at[0, a, k], osem.at[1, a, 2 * from_group + core]), to)
        return remote, pltpu.make_async_copy(src, dst, self_sem.at[a])

    def out_start(a, k):
        remote, local = out_copies(a, k)
        if k:
            remote.start()
        else:
            pl.when(from_core == core)(local.start)
            pl.when(from_core != core)(remote.start)

    def out_wait(a):
        for k in range(parts):
            remote, local = out_copies(a, k)
            if k:
                remote.wait_send()
            else:
                pl.when(from_core == core)(local.wait)
                pl.when(from_core != core)(remote.wait_send)
        for s in (0, 1):
            for r in (0, 1):
                chip = 2 * core + s
                dst = (added_o, dx_o)[a].at[s, r * half_rows : (r + 1) * half_rows]
                remote = send(
                    (added_h, dx_v)[a].at[0],
                    dst,
                    (osem.at[0, a, 0], osem.at[1, a, 2 * s + r]),
                    (chip, place - core + r),
                )
                pl.when(jnp.logical_not((chip == me) & (core == r)))(remote.wait_recv)

    def early_second_and_added():
        early_second_and_on()
        for k in range(parts - 1, -1, -1):
            out_start(0, k)

    launch(a1_copy)
    launch(b1_copy)
    prepare(0)
    attend_back(0, {6: early_first})
    xs_in.wait()
    late_term(0)
    for u in range(3):
        late_start(u)
    prepare(1)
    early_steps = [early_second_and_added]
    for i in range(1, steps):

        def early_step(i=i):
            z_add(i - 1)
            z_send(i)

        early_steps.append(early_step)

    def early_last():
        if steps:
            z_add(steps - 1)
        ag_send()

    early_steps.append(early_last)
    dkt[...] = jnp.zeros_like(dkt)
    dvt[...] = jnp.zeros_like(dvt)

    def all_three(first_unit):
        lists = [late_events(first_unit + i) for i in range(3)]

        def at_step(i):
            def run():
                for one_list in lists:
                    one_list[i]()

            return run

        return [at_step(i) for i in range(len(lists[0]))]

    late_steps = all_three(0)

    def next_of(queue):
        if queue:
            queue.pop(0)()

    next_of(early_steps)
    for k in range(parts - 1, -1, -1):
        low, high = k * rows, (k + 1) * rows
        cross((0, high), (low, high))
        if k == parts - 1:
            wqkv_in.wait()
            first_in.wait()
            for part in range(3):
                d_copy(part).wait_recv()
            next_of(late_steps)
        else:
            post_slot(k + 1)
        if k == parts - 2:
            next_of(late_steps)
        if k:
            cross((low, high), (0, low))
        cross_end(k)
        if k in (parts - 1, 1):
            next_of(early_steps)
    late_term(1)
    for u in range(3, 6):
        late_start(u)
    post_slot(0)
    while early_steps:
        next_of(early_steps)
    while late_steps:
        next_of(late_steps)
    tail = all_three(3)
    next_of(tail)
    ag_finish()
    for u in range(3):
        late_finish(u)
    while tail:
        next_of(tail)
    for u in range(3, 6):
        late_finish(u)
    for make in sends:
        make().wait_send()
    for part in range(3):
        d_copy(part).wait_send()
        for k in range(parts):
            e_copy(part, k).wait_send()
    out_wait(0)
    out_wait(1)
    for copy in ag_out():
        copy.wait()


def second_call(parts, shards, grad_norm, length, saved, grads, first, added, wqkv, hidden):
    xs_shape = saved[4].shape
    _, rows, width = xs_shape
    full = rows * parts
    half_rows = rows // 2
    n, up_rows, vector_rows, total_rows = grad_rows(width, hidden, shards)
    spots = shards // 2
    quarter, eighth = total_rows // 4, total_rows // 8
    heads = (2, full, 128)
    return pl.pallas_call(
        functools.partial(second_kernel, parts, shards, grad_norm),
        in_specs=[VMEM] + [ANY] * 9,
        out_specs=[ANY, ANY, VMEM, ANY, ANY, ANY, VMEM],
        out_shape=[
            jax.ShapeDtypeStruct((2, rows, width), bf16),
            jax.ShapeDtypeStruct((2, rows, width), bf16),
            jax.ShapeDtypeStruct((n, 3 * width), f32),
            jax.ShapeDtypeStruct((n, hidden), f32),
            jax.ShapeDtypeStruct((up_rows, width), f32),
            jax.ShapeDtypeStruct((n, width), f32),
            jax.ShapeDtypeStruct((8, width), f32),
        ],
        scratch_shapes=[
            pltpu.VMEM(xs_shape, bf16),
            pltpu.VMEM((2, 3, full, 128), bf16),
            pltpu.VMEM((2, full, 128), bf16),
            pltpu.VMEM((2, parts, rows, 128), bf16),
            pltpu.VMEM((2, parts, rows, 128), bf16),
            pltpu.VMEM((width, 3 * width), bf16),
            pltpu.VMEM((parts, half_rows, width), f32),
            pltpu.VMEM((spots, total_rows, width), bf16),
            pltpu.VMEM((spots, quarter, width), bf16),
            pltpu.VMEM((spots, quarter, width), bf16),
            pltpu.VMEM((spots, eighth, width), bf16),
            pltpu.VMEM((spots, eighth, width), bf16),
            pltpu.VMEM((spots, quarter, width), bf16),
            pltpu.VMEM((2 * spots, quarter, width), bf16),
            pltpu.VMEM((spots + parts, quarter, width), bf16),
            pltpu.VMEM((total_rows, width), f32),
            pltpu.VMEM(heads, bf16),
            pltpu.VMEM(heads, bf16),
            pltpu.VMEM(heads, bf16),
            pltpu.VMEM(heads, bf16),
            pltpu.VMEM((128, full), bf16),
            pltpu.VMEM((128, full), bf16),
            pltpu.VMEM((128, full), bf16),
            pltpu.VMEM((128, full), f32),
            pltpu.VMEM((128, full), f32),
            pltpu.VMEM((128, full), f32),
            pltpu.VMEM((2, 3, parts, rows, 128), bf16),
            pltpu.VMEM((parts, half_rows, 3 * width), bf16),
            pltpu.VMEM((parts, half_rows, width), bf16),
            pltpu.VMEM((6, width, 128), f32),
            pltpu.VMEM((6, 2, n, 128), bf16),
            pltpu.VMEM((6, spots, 2 * n, 128), f32),
            pltpu.VMEM((6, spots, 2 * n, 128), bf16),
            pltpu.VMEM((6, spots, 2 * n, 128), bf16),
            pltpu.VMEM((6, 2 * parts, n, 128), bf16),
            DMA((16,)),
            DMA((16,)),
            DMA((2,)),
            DMA((2, 3)),
            DMA((2, 24)),
            DMA((2, 6, 16)),
            DMA((2, 2, 4)),
            DMA((2, 3, 4)),
        ],
        compiler_params=pltpu.CompilerParams(
            vmem_limit_bytes=VMEM_LIMIT, collective_id=1, has_side_effects=True
        ),
        name="backward_and_sums",
    )(length, *saved, grads, first, added, wqkv)


def last_kernel(rows_here, lengths, post_h, added_h, dx_h, y, ac, vec, *rest):
    ins, (post_o, accum_o, dx_o, accg_o), outs, vectors = rest[:4], rest[4:8], rest[8:12], rest[12:]
    step = pl.program_id(0)
    for src, dst in zip(ins, outs):
        dst[...] = src[...]

    @pl.when(step == 0)
    def _():
        for i, out in enumerate(vectors):
            out[...] = vec[i : i + 1, : out.shape[1]]

    _, rows, _ = y.shape
    steps = pl.num_programs(0)
    length = lengths[lax.div(step * 2, steps)]
    start = lax.axis_index("head") * rows_here + lax.rem(step, lax.div(steps, 2)) * rows
    keep = lax.broadcasted_iota(jnp.int32, (1, rows, 1), 1) + start < length
    post_o[...] = post_h[...].astype(f32)
    accum_o[...] = jnp.where(keep, y[...].astype(f32) + added_h[...].astype(f32), 0.0)
    dx_o[...] = dx_h[...].astype(f32)
    accg_o[...] = jnp.where(keep, ac[...].astype(f32), 0.0)


def last_call(lengths, tokens, streams, vectors, grads, shards):
    groups, rows, width = tokens[0].shape
    cut = 2
    steps = groups * cut
    block = pl.BlockSpec((1, rows // cut, width), lambda i: (i // cut, i % cut, 0))
    whole = jax.ShapeDtypeStruct((groups, rows, width), f32)
    n = width // shards
    hidden = grads[1].shape[1]
    short = [jax.ShapeDtypeStruct((1, n), f32)] * 5 + [jax.ShapeDtypeStruct((1, hidden // shards), f32)]
    moved = [pl.BlockSpec((g.shape[0], g.shape[1] // steps), lambda i: (0, i)) for g in grads]
    return pl.pallas_call(
        functools.partial(last_kernel, rows),
        grid=(steps,),
        in_specs=[SMEM] + [block] * 5 + [pl.BlockSpec(vectors.shape, lambda i: (0, 0))] + moved,
        out_specs=[block] * 4 + moved + [pl.BlockSpec(o.shape, lambda i: (0, 0)) for o in short],
        out_shape=[whole] * 4 + [jax.ShapeDtypeStruct(g.shape, f32) for g in grads] + short,
        compiler_params=pltpu.CompilerParams(vmem_limit_bytes=VMEM_LIMIT),
        name="outputs",
    )(lengths, *tokens, *streams, vectors, *grads)


def local(
    post_stream,
    accum_stream,
    seq_lengths,
    qkv_weight,
    out_weight,
    norm1_gain,
    norm1_bias,
    up_weight,
    up_bias,
    down_weight,
    down_bias,
    norm2_gain,
    norm2_bias,
    post_cotan,
    accum_cotan,
):
    groups, rows, width = post_stream.shape
    parts = lax.axis_size("head")
    shards = lax.axis_size("seq")
    hidden = up_weight.shape[1]
    grad_norm = float(groups * shards * rows * parts) ** (-0.5)

    def row(vector):
        return vector.reshape(1, -1)

    weights = (
        qkv_weight,
        out_weight,
        row(norm1_gain),
        row(norm1_bias),
        up_weight,
        row(up_bias),
        down_weight,
        row(down_bias),
        row(norm2_gain),
        row(norm2_bias),
    )
    post, added, first, qkv, lse, mixed, go, xs, grads, length = first_call(
        parts, shards, seq_lengths, (post_stream, post_cotan, accum_cotan), weights
    )
    dx, added, qkv_grad, up_grad, down_grad, out_grad, vectors = second_call(
        parts, shards, grad_norm, length, (qkv, lse, mixed, go, xs), grads, first, added, qkv_weight, hidden
    )
    post, accum, post_grad, accum_grad, qkv_grad, up_grad, down_grad, out_grad, *short = last_call(
        seq_lengths,
        (post, added, dx),
        (accum_stream, accum_cotan),
        vectors,
        (qkv_grad, up_grad, down_grad, out_grad),
        shards,
    )
    gain1, bias1, gain2, bias2, down_bias_grad, up_bias_grad = [v.reshape(-1) for v in short]
    return (
        post,
        accum,
        post_grad,
        accum_grad,
        qkv_grad,
        out_grad,
        gain1,
        bias1,
        up_grad,
        up_bias_grad,
        down_grad,
        down_bias_grad,
        gain2,
        bias2,
    )


def solution(mesh):
    tokens = P("seq", "head", None)
    in_specs = (tokens, tokens, P("seq")) + (P(),) * 10 + (tokens, tokens)
    rows = P("seq", None)
    vector = P("seq")
    out_specs = (tokens,) * 4 + (rows, rows, vector, vector, rows, vector, rows, vector, vector, vector)
    return jax.shard_map(local, mesh=mesh, in_specs=in_specs, out_specs=out_specs, check_vma=False)
```

```python
import functools
import itertools

import jax
import jax.numpy as jnp
from jax import lax
from jax.experimental import pallas as pl
from jax.experimental.pallas import tpu as pltpu
from jax.sharding import PartitionSpec as P

H = 8
EPS = 1e-05
NEG = -1e30
LOG2E = 1.4426950408889634
VMEM_LIMIT = 62 * 2**20
bf16 = jnp.bfloat16
f32 = jnp.float32
SMEM = pl.BlockSpec(memory_space=pltpu.SMEM)
VMEM = pl.BlockSpec(memory_space=pltpu.VMEM)
ANY = pl.BlockSpec(memory_space=pl.ANY)
DMA = pltpu.SemaphoreType.DMA


def dot(a, b):
    return jnp.dot(a, b, preferred_element_type=f32)


def dot_nt(a, b):
    return lax.dot_general(a, b, (((1,), (1,)), ((), ())), preferred_element_type=f32)


def dot_tn(a, b):
    return lax.dot_general(a, b, (((0,), (0,)), ((), ())), preferred_element_type=f32)


def split3(value):
    first = value.astype(bf16)
    rest = value - first.astype(f32)
    second = rest.astype(bf16)
    third = (rest - second.astype(f32)).astype(bf16)
    return first, second, third


def lane_sets():
    lane = lax.broadcasted_iota(jnp.int32, (1, 128), 1)
    return lane, (lane < 64, lane >= 64), (64, 0)


def bits_of(count):
    return [1 << b for b in range(count.bit_length() - 1)]


def flip(index, k, count):
    out = 0
    for bit in bits_of(count):
        out = out + (lax.rem(lax.div(index, bit) + (k // bit), 2)) * bit
    return out


def aligned(start, step):
    if isinstance(start, int):
        return start
    return pl.multiple_of(start, step)


def send(src, dst, pair, to):
    return pltpu.make_async_remote_copy(
        src_ref=src,
        dst_ref=dst,
        send_sem=pair[0],
        recv_sem=pair[1],
        device_id=to,
        device_id_type=pl.DeviceIdType.MESH,
    )


def enter(partners):
    barrier = pltpu.get_barrier_semaphore()
    for to in partners:
        pl.semaphore_signal(barrier, inc=1, device_id=to, device_id_type=pl.DeviceIdType.MESH)
    pl.semaphore_wait(barrier, len(partners))


def plane(me, place, parts):
    core = lax.rem(place, 2)
    others = []
    for k in range(parts):
        for other in range(2):
            if k or other:
                seat = place if not other else place + 1 - 2 * core
                others.append((flip(me, k, parts), seat))
    return others


def grad_rows(width, hidden, shards):
    n = width // shards
    up = n * (hidden // width)
    vectors = 16 - n % 16
    total = 2 * up + n + vectors
    return n, up, vectors, -(-total // 128) * 128


def normed(value):
    centre = value - jnp.mean(value, axis=-1, keepdims=True)
    spread = jnp.mean(centre * centre, axis=-1, keepdims=True)
    inv = lax.rsqrt(spread + EPS)
    return centre * inv, inv


def norm_back(cot, unit, inv):
    return (
        cot - jnp.mean(cot, axis=-1, keepdims=True) - unit * jnp.mean(cot * unit, axis=-1, keepdims=True)
    ) * inv


def first_kernel(
    parts,
    shards,
    lengths,
    x,
    pc,
    ac,
    wqkv,
    wo_h,
    g1,
    b1,
    wu_h,
    bu,
    wd_h,
    bd,
    g2,
    b2,
    post_o,
    added_o,
    first_o,
    qkv_o,
    lse_o,
    mixed_o,
    go_o,
    xs_o,
    grads_o,
    length_o,
    xs,
    pcs,
    acs,
    w,
    qkv,
    ka,
    qa,
    vt,
    mixed,
    lse,
    tops,
    accs,
    wo,
    wu,
    wd,
    mix,
    hid,
    pre,
    slope,
    back,
    fgrad,
    mid,
    agrad,
    mgrad,
    post_v,
    added_v,
    first_v,
    small,
    grads,
    core_in,
    sizes,
    load_sem,
    store_sem,
    self_sem,
    insem,
    fsem,
    msem,
    gsem,
    osem,
    nsem,
    csem,
):
    groups, rows, width = x.shape
    hidden = wu.shape[1]
    full = rows * parts
    half = rows // 2
    me = lax.axis_index("head")
    place = lax.axis_index("seq")
    core = lax.rem(place, 2)
    other = place + 1 - 2 * core
    from_core = lax.div(me, 2)
    from_group = lax.rem(me, 2)
    lane, mine, base = lane_sets()
    one = jnp.ones((), bf16)
    zero = jnp.zeros((), bf16)
    here = pl.ds(aligned(core * half, half), half)
    there = pl.ds(aligned((1 - core) * half, half), half)

    load_count = itertools.count()

    def load(src, dst):
        copy = pltpu.make_async_copy(src, dst, load_sem.at[next(load_count)])
        copy.start()
        return copy

    stores = []
    store_count = itertools.count()

    def store(src, dst):
        copy = pltpu.make_async_copy(src, dst, store_sem.at[next(store_count)])
        copy.start()
        stores.append(copy)

    w_in = [
        load(
            wqkv.at[:, pl.ds(aligned(part * width + core * 256, 128), 256)],
            w.at[:, part * 256 : part * 256 + 256],
        )
        for part in range(3)
    ]
    wo_in = load(wo_h, wo)
    wu_in = load(wu_h, wu)
    wd_in = load(wd_h, wd)

    enter(plane(me, place, parts))

    def in_copies(a, twist, r):
        group = from_group if not twist else 1 - from_group
        src = (x, pc, ac)[a].at[group, r * half : (r + 1) * half]
        slot = twist + 2 * lax.rem(from_core + core, 2)
        dst = xs.at[slot, r * half : (r + 1) * half] if a == 0 else (pcs, acs)[a - 1].at[slot]
        sems = (insem.at[0, a, 2 * twist + r], insem.at[1, a, slot])
        remote = send(src, dst, sems, (2 * core + group, place - core + r))
        if twist:
            return remote, None, None
        return remote, pltpu.make_async_copy(src, dst, self_sem.at[a]), (from_core == core) & (core == r)

    def in_start(a, twist):
        for r in (0, 1):
            remote, local, own = in_copies(a, twist, r)
            if twist:
                remote.start()
            else:
                pl.when(own)(local.start)
                pl.when(jnp.logical_not(own))(remote.start)

    def in_sent(a, twist):
        for r in (0, 1):
            remote, local, own = in_copies(a, twist, r)
            if twist:
                remote.wait_send()
            else:
                pl.when(jnp.logical_not(own))(remote.wait_send)

    def in_wait(a, k):
        dst = xs.at[k, here] if a == 0 else (pcs, acs)[a - 1].at[k]
        src = (x, pc, ac)[a].at[0, :half]
        remote = send(src, dst, (insem.at[0, a, 0], insem.at[1, a, k]), (flip(me, k, parts), place))
        if k:
            remote.wait_recv()
        else:
            local = pltpu.make_async_copy(src, dst, self_sem.at[a])
            pl.when(from_core == core)(local.wait)
            pl.when(from_core != core)(remote.wait_recv)

    def across(src, dst, pair):
        return send(src, dst, pair, (me, other))

    def pass_on(k):
        part = xs.at[k, here]
        return across(part, part, (fsem.at[0, k], fsem.at[1, k]))

    size_copy = across(sizes.at[0], sizes.at[1], (nsem.at[0], nsem.at[1]))

    def m_copy(p):
        return across(
            mixed.at[p, :, there],
            mix.at[:, :, pl.ds(aligned((2 * core + p) * 128, 128), 128)],
            (msem.at[0, p], msem.at[1, p]),
        )

    def g_copy(p, u):
        chunks = slice(2 * u, 2 * u + 2)
        return across(
            mgrad.at[chunks, :, pl.ds(aligned((2 * (1 - core) + p) * 128, 128), 128)],
            go_o.at[p, chunks, here],
            (gsem.at[0, p, u], gsem.at[1, p, u]),
        )

    def out_copies(k):
        dst = post_o.at[from_group, here]
        to = (flip(me, k, parts), place - core + from_core)
        remote = send(post_v.at[k], dst, (osem.at[0, k], osem.at[1, 2 * from_group + core]), to)
        return remote, pltpu.make_async_copy(post_v.at[k], dst, self_sem.at[3])

    def out_start(k):
        remote, local = out_copies(k)
        if k:
            remote.start()
        else:
            pl.when(from_core == core)(local.start)
            pl.when(from_core != core)(remote.start)

    def out_wait():
        for k in range(parts):
            remote, local = out_copies(k)
            if k:
                remote.wait_send()
            else:
                pl.when(from_core == core)(local.wait)
                pl.when(from_core != core)(remote.wait_send)
        for s in (0, 1):
            for r in (0, 1):
                chip = 2 * core + s
                dst = post_o.at[s, r * half : (r + 1) * half]
                remote = send(
                    post_v.at[0], dst, (osem.at[0, 0], osem.at[1, 2 * s + r]), (chip, place - core + r)
                )
                pl.when(jnp.logical_not((chip == me) & (core == r)))(remote.wait_recv)

    in_start(0, 0)
    pl.when(from_core == core)(functools.partial(in_start, 0, 1))
    which = lax.broadcasted_iota(jnp.int32, (8, 128), 0)
    sizes[0] = jnp.where(which == 0, lengths[0], lengths[1]).astype(f32)
    size_copy.start()
    for copy in w_in:
        copy.wait()
    size_copy.wait_recv()
    held = jnp.where(from_core == core, sizes[0], sizes[1])
    length = jnp.sum(jnp.where(which == from_group, held, 0.0), axis=0, keepdims=True)
    length_o[...] = jnp.broadcast_to(length, (8, 128))
    length = length[:, :1]

    def below(count, start):
        pos = lax.broadcasted_iota(jnp.int32, (count, 1), 0) + start
        return pos.astype(f32) < length

    @pl.when(from_core != core)
    def _():
        in_sent(0, 0)
        in_start(0, 1)

    def project(k):
        pass_on(k).wait_recv()
        at = slice(k * rows, (k + 1) * rows)
        three = dot(xs[k], w[...])
        bias = jnp.where(below(rows, flip(me, k, parts) * rows), 0.0, NEG)
        step = lax.rem(lane, 64)
        key_more = jnp.where(step == 0, bias, 0.0).astype(bf16)
        query_more = jnp.where(step == 0, one, zero)
        for p in (0, 1):
            cut = slice(p * 128, p * 128 + 128)
            query = (three[:, :256][:, cut] * (LOG2E * 64 ** (-0.5))).astype(bf16)
            keys = three[:, 256:512][:, cut].astype(bf16)
            values = three[:, 512:][:, cut].astype(bf16)
            qkv[p, 0, at] = query
            qkv[p, 1, at] = keys
            qkv[p, 2, at] = values
            turned = values.T
            for h in range(2):
                ka[2 * p + h, at] = jnp.where(mine[h], keys, key_more)
                qa[2 * p + h, at] = jnp.where(mine[h], query, query_more)
                vt[2 * p + h, :64, at] = turned[h * 64 : h * 64 + 64]
                vt[2 * p + h, 64:, at] = jnp.ones((8, rows), bf16)

    def rectangle(p, keys, queries):
        for h in range(2):
            g = 2 * p + h
            scores = dot_nt(ka[g, keys, :], qa[g, queries, :])
            top = tops[g, 0:1, queries]
            new_top = jnp.maximum(top, jnp.max(scores, axis=0, keepdims=True))
            probs = jnp.exp2(scores - new_top)
            tops[g, 0:1, queries] = new_top
            accs[g, :, queries] = accs[g, :, queries] * jnp.exp2(top - new_top) + dot(
                vt[g, :, keys], probs.astype(bf16)
            )

    early = full - rows

    def attend_early(p):
        def body(j, carry):
            rectangle(p, pl.ds(aligned(j * rows, rows), rows), slice(0, early))
            return carry

        lax.fori_loop(0, parts - 1, body, None)

    tops[...] = jnp.full(tops.shape, NEG, f32)
    accs[...] = jnp.zeros_like(accs)
    for k in range(parts - 1):
        in_wait(0, k)
        pass_on(k).start()
    for k in range(parts - 1):
        project(k)
    for a in (1, 2):
        for twist in (0, 1):
            in_start(a, twist)
    attend_early(0)
    in_wait(0, parts - 1)
    pass_on(parts - 1).start()
    attend_early(1)
    project(parts - 1)
    store(qkv, qkv_o)
    store(xs, xs_o)

    def attend(p):
        rectangle(p, slice(early, full), slice(0, full))
        rectangle(p, slice(0, early), slice(early, full))
        pieces = []
        terms = []
        for h in range(2):
            top, acc = tops[2 * p + h, 0:1], accs[2 * p + h]
            total = acc[64:65]
            pieces.append(acc[:64] / total)
            a, b, c = split3(-(top + jnp.log2(total)))
            flat = [jnp.ones((1, full), f32)] + [v.astype(f32) for v in (a, b, c)]
            terms.append(jnp.concatenate(flat + [jnp.zeros((60, full), f32)], 0))
        lse[p] = jnp.concatenate([terms[1], terms[0]], 0).T.astype(bf16)
        mixed[p] = jnp.concatenate(pieces, 0).T.astype(bf16).reshape(parts, rows, 128)
        m_copy(p).start()
        mix[:, :, pl.ds(aligned((2 * core + p) * 128, 128), 128)] = mixed[p, :, here]

    attend(0)
    attend(1)
    store(mixed, mixed_o)
    store(lse, lse_o)

    tile = 512
    tiles = hidden // tile
    small[...] = jnp.zeros_like(small)

    def feed(u):
        chunks = (2 * u, 2 * u + 1)
        keep = jnp.concatenate([below(half, flip(me, k, parts) * rows + core * half) for k in chunks], 0)
        mix_u = mix[2 * u : 2 * u + 2].reshape(rows, width)
        x_u = jnp.concatenate([xs[k, here] for k in chunks], 0)
        attention = dot(mix_u, wo[...])
        unit1, inv1 = normed(x_u.astype(f32) + attention)
        x_mid = unit1 * g1[...] + b1[...]
        mid[u] = x_mid.astype(bf16)
        total = jnp.zeros((rows, width), f32)
        c0 = 0.7978845608028654
        c1 = 0.044715
        for t in range(tiles):
            cols = slice(t * tile, (t + 1) * tile)
            act = dot(mid[u], wu[:, cols]) + bu[:, cols]
            square = act * act
            th = jnp.tanh(act * (c0 + (c0 * c1) * square))
            part = 0.5 + 0.5 * th
            smooth = act * part
            low = smooth.astype(bf16)
            hid[u, :, cols] = low
            slope[:rows, cols] = part + smooth * (1.0 - part) * (2.0 * c0 + (6.0 * c0 * c1) * square)
            total = total + dot(low, wd[cols, :])
        total = total + bd[...]
        unit2, inv2 = normed(x_mid + total)
        post = jnp.where(keep, unit2 * g2[...] + b2[...], 0.0).astype(bf16)
        added = jnp.where(keep, attention + total, 0.0).astype(bf16)
        post_v[2 * u : 2 * u + 2] = post.reshape(2, half, width)
        added_v[2 * u : 2 * u + 2] = added.reshape(2, half, width)
        for k in chunks:
            out_start(k)
        store(added_v.at[2 * u : 2 * u + 2], added_o.at[2 * u : 2 * u + 2])
        post_c = jnp.where(keep, pcs[2 * u : 2 * u + 2].reshape(rows, width).astype(f32), 0.0)
        accum_c = jnp.where(keep, acs[2 * u : 2 * u + 2].reshape(rows, width).astype(f32), 0.0)
        mid_grad2 = norm_back(post_c * g2[...], unit2, inv2)
        small[2:3, :width] += jnp.sum(post_c * unit2, axis=0, keepdims=True)
        small[3:4, :width] += jnp.sum(post_c, axis=0, keepdims=True)
        feed_grad = (mid_grad2 + accum_c).astype(bf16)
        fgrad[u] = feed_grad
        small[4:5, :width] += jnp.sum(feed_grad.astype(f32), axis=0, keepdims=True)
        back[...] = mid_grad2
        for t in range(tiles):
            cols = slice(t * tile, (t + 1) * tile)
            hidden_grad = dot_nt(fgrad[u], wd[cols, :]).astype(bf16)
            pre_grad = (hidden_grad.astype(f32) * slope[:rows, cols]).astype(bf16)
            pre[u, :, cols] = pre_grad
            small[5:6, cols] += jnp.sum(pre_grad.astype(f32), axis=0, keepdims=True)
            back[...] += dot_nt(pre_grad, wu[:, cols])
        mid_grad = back[...]
        small[0:1, :width] += jnp.sum(mid_grad * unit1, axis=0, keepdims=True)
        small[1:2, :width] += jnp.sum(mid_grad, axis=0, keepdims=True)
        first = norm_back(mid_grad * g1[...], unit1, inv1)
        first_v[2 * u : 2 * u + 2] = first.reshape(2, half, width)
        store(first_v.at[2 * u : 2 * u + 2], first_o.at[2 * u : 2 * u + 2])
        attn_grad = (first + accum_c).astype(bf16)
        agrad[u] = attn_grad
        mgrad[2 * u : 2 * u + 2] = dot_nt(attn_grad, wo[...]).astype(bf16).reshape(2, half, width)
        for p in (0, 1):
            g_copy(p, u).start()
            own = mgrad.at[2 * u : 2 * u + 2, :, pl.ds(aligned((2 * core + p) * 128, 128), 128)]
            store(own, go_o.at[p, 2 * u : 2 * u + 2, here])

    wo_in.wait()
    wu_in.wait()
    wd_in.wait()
    for a in (1, 2):
        for k in range(parts):
            in_wait(a, k)
    for p in (0, 1):
        m_copy(p).wait_recv()
    for u in (0, 1):
        feed(u)

    n, up_rows, vector_rows, total_rows = grad_rows(width, hidden, shards)
    halves = (0, 1)

    def spot_of(shard):
        return lax.rem(core + shard % 2, 2), shard // 2

    edges = (0, up_rows, 2 * up_rows, total_rows)

    def c_copy(i):
        at = slice(edges[i], edges[i + 1])
        return across(grads.at[1, :, at], core_in.at[:, at], (csem.at[0, i], csem.at[1, i]))

    for t in range(tiles):
        cols = slice(t * tile, (t + 1) * tile)
        slope[:width, cols] = sum(dot_tn(mid[u], pre[u, :, cols]) for u in halves)
    for shard in range(shards):
        own = slice(shard * n, (shard + 1) * n)
        block = jnp.concatenate([slope[own, t * tile : (t + 1) * tile] for t in range(tiles)], 0)
        side, spot = spot_of(shard)
        grads[side, spot, :up_rows] = block.astype(bf16)
    c_copy(0).start()
    per = tile // up_rows
    for t in range(tiles):
        cols = slice(t * tile, (t + 1) * tile)
        block = sum(dot_tn(hid[u, :, cols], fgrad[u]) for u in halves).astype(bf16)
        for i in range(per):
            side, spot = spot_of(t * per + i)
            grads[side, spot, up_rows : 2 * up_rows] = block[i * up_rows : (i + 1) * up_rows]
    c_copy(1).start()
    out_all = sum(dot_tn(mix[2 * u : 2 * u + 2].reshape(rows, width), agrad[u]) for u in halves)
    line = lax.broadcasted_iota(jnp.int32, (8, width), 0)
    short = small[:, :width]
    long = small[...]
    for shard in range(shards):
        a = pltpu.roll(short, (width - shard * n) % width, 1)
        b = pltpu.roll(long, (hidden - shard * up_rows) % hidden, 1)[:, :width]
        extra = jnp.where(line == 5, b, a)
        rest = total_rows - 2 * up_rows - n - 8
        block = jnp.concatenate(
            [out_all[shard * n : (shard + 1) * n], extra, jnp.zeros((rest, width), f32)], 0
        )
        side, spot = spot_of(shard)
        grads[side, spot, 2 * up_rows :] = block.astype(bf16)
    c_copy(2).start()
    for i in range(3):
        c_copy(i).wait_recv()

        def add_cores(spot, carry, i=i):
            at = slice(edges[i], edges[i + 1])
            grads[0, spot, at] = (grads[0, spot, at].astype(f32) + core_in[spot, at].astype(f32)).astype(bf16)
            return carry

        lax.fori_loop(0, shards // 2, add_cores, None)
    store(grads.at[0], grads_o)
    for i in range(3):
        c_copy(i).wait_send()

    pl.when(from_core == core)(functools.partial(in_sent, 0, 0))
    in_sent(0, 1)
    for a in (1, 2):
        for twist in (0, 1):
            in_sent(a, twist)
    for k in range(parts):
        pass_on(k).wait_send()
    size_copy.wait_send()
    for p in (0, 1):
        m_copy(p).wait_send()
        for u in (0, 1):
            g_copy(p, u).wait()
    out_wait()
    for copy in stores:
        copy.wait()


def first_call(parts, shards, lengths, streams, weights):
    groups, rows, width = streams[0].shape
    hidden = weights[4].shape[1]
    full = rows * parts
    half = rows // 2
    total_rows = grad_rows(width, hidden, shards)[3]
    held = jax.ShapeDtypeStruct((groups, rows, width), bf16)
    return pl.pallas_call(
        functools.partial(first_kernel, parts, shards),
        in_specs=[SMEM] + [ANY] * 5 + [VMEM, VMEM, ANY, VMEM, ANY, VMEM, VMEM, VMEM],
        out_specs=[ANY] * 9 + [VMEM],
        out_shape=[
            held,
            jax.ShapeDtypeStruct((parts, half, width), bf16),
            jax.ShapeDtypeStruct((parts, half, width), f32),
            jax.ShapeDtypeStruct((2, 3, full, 128), bf16),
            jax.ShapeDtypeStruct((2, full, 128), bf16),
            jax.ShapeDtypeStruct((2, parts, rows, 128), bf16),
            jax.ShapeDtypeStruct((2, parts, rows, 128), bf16),
            jax.ShapeDtypeStruct((parts, rows, width), bf16),
            jax.ShapeDtypeStruct((shards // 2, total_rows, width), bf16),
            jax.ShapeDtypeStruct((8, 128), f32),
        ],
        scratch_shapes=[
            pltpu.VMEM((parts, rows, width), bf16),
            pltpu.VMEM((parts, half, width), bf16),
            pltpu.VMEM((parts, half, width), bf16),
            pltpu.VMEM((width, 768), bf16),
            pltpu.VMEM((2, 3, full, 128), bf16),
            pltpu.VMEM((4, full, 128), bf16),
            pltpu.VMEM((4, full, 128), bf16),
            pltpu.VMEM((4, 72, full), bf16),
            pltpu.VMEM((2, parts, rows, 128), bf16),
            pltpu.VMEM((2, full, 128), bf16),
            pltpu.VMEM((4, 8, full), f32),
            pltpu.VMEM((4, 72, full), f32),
            pltpu.VMEM((width, width), bf16),
            pltpu.VMEM((width, hidden), bf16),
            pltpu.VMEM((hidden, width), bf16),
            pltpu.VMEM((parts, half, width), bf16),
            pltpu.VMEM((2, rows, hidden), bf16),
            pltpu.VMEM((2, rows, hidden), bf16),
            pltpu.VMEM((max(rows, width), hidden), f32),
            pltpu.VMEM((rows, width), f32),
            pltpu.VMEM((2, rows, width), bf16),
            pltpu.VMEM((2, rows, width), bf16),
            pltpu.VMEM((2, rows, width), bf16),
            pltpu.VMEM((parts, half, width), bf16),
            pltpu.VMEM((parts, half, width), bf16),
            pltpu.VMEM((parts, half, width), bf16),
            pltpu.VMEM((parts, half, width), f32),
            pltpu.VMEM((8, hidden), f32),
            pltpu.VMEM((2, shards // 2, total_rows, width), bf16),
            pltpu.VMEM((shards // 2, total_rows, width), bf16),
            pltpu.VMEM((2, 8, 128), f32),
            DMA((8,)),
            DMA((16,)),
            DMA((5,)),
            DMA((2, 3, 4)),
            DMA((2, parts)),
            DMA((2, 2)),
            DMA((2, 2, 2)),
            DMA((2, 4)),
            DMA((2,)),
            DMA((2, 3)),
        ],
        compiler_params=pltpu.CompilerParams(
            vmem_limit_bytes=VMEM_LIMIT, collective_id=0, has_side_effects=True
        ),
        name="forward_and_feed",
    )(lengths, *streams, *weights)


def second_kernel(
    parts,
    shards,
    grad_norm,
    length_v,
    qkv_h,
    lse_h,
    mixed_h,
    go_h,
    xs_h,
    grads_h,
    first_h,
    added_h,
    wqkv_h,
    dx_o,
    added_o,
    wqkv_o,
    up_o,
    down_o,
    out_o,
    vec_o,
    xs,
    qkv,
    lse,
    mixed,
    go,
    wqkv,
    first,
    grads,
    a1_in,
    b1_in,
    a2_in,
    b2_in,
    z_in,
    all_out,
    all_in,
    final,
    ka,
    va,
    qa,
    da,
    kt,
    qt,
    gt,
    dqt,
    dsend,
    dfull,
    dx_v,
    late,
    late_out,
    late_sum,
    late_step,
    late_got,
    late_all,
    load_sem,
    store_sem,
    self_sem,
    dsem,
    rsem,
    lsem,
    osem,
):
    parts, rows, width = xs.shape
    half_rows = rows // 2
    full = rows * parts
    hidden = up_o.shape[1]
    me = lax.axis_index("head")
    place = lax.axis_index("seq")
    core = lax.rem(place, 2)
    other = place + 1 - 2 * core
    from_core = lax.div(me, 2)
    from_group = lax.rem(me, 2)
    here = pl.ds(aligned(core * half_rows, half_rows), half_rows)
    there = pl.ds(aligned((1 - core) * half_rows, half_rows), half_rows)
    length = length_v[0:1, 0:1]
    lane, mine, base = lane_sets()
    one = jnp.ones((), bf16)
    zero = jnp.zeros((), bf16)
    n, up_rows, vector_rows, total_rows = grad_rows(width, hidden, shards)
    seq_bits = bits_of(shards)
    load_count = itertools.count()

    def load(src, dst):
        copy = pltpu.make_async_copy(src, dst, load_sem.at[next(load_count)])
        copy.start()
        return copy

    def pair_load(p):
        return [
            load(qkv_h.at[p], qkv.at[p]),
            load(go_h.at[p], go.at[p]),
            load(mixed_h.at[p], mixed.at[p]),
            load(lse_h.at[p], lse.at[p]),
        ]

    pair_in = [pair_load(0)]
    grads_in = load(grads_h, grads)
    xs_in = load(xs_h, xs)
    pair_in.append(pair_load(1))
    wqkv_in = load(wqkv_h, wqkv)
    first_in = load(first_h, first)

    enter(plane(me, place, parts) + [(me, flip(place, bit, shards)) for bit in seq_bits[1:]])

    sends = []

    def launch(make, *which):
        make(*which).start()
        sends.append(functools.partial(make, *which))

    spots = shards // 2
    half, quarter = total_rows // 2, total_rows // 4
    eighth = total_rows // 8
    x_bit = lax.rem(me, 2)
    y_bit = lax.div(me, 2)

    def to_head(src, dst, i, k):
        return send(src, dst, (rsem.at[0, i], rsem.at[1, i]), (flip(me, k, parts), place))

    def to_seq(src, dst, i, bit):
        return send(src, dst, (rsem.at[0, i], rsem.at[1, i]), (me, flip(place, bit, shards)))

    a_keep = x_bit * quarter
    a_give = (1 - x_bit) * quarter
    b_keep = half + y_bit * quarter
    b_give = half + (1 - y_bit) * quarter
    a1_copy = lambda: to_head(grads_h.at[:, pl.ds(aligned(a_give, 16), quarter)], a1_in, 1, 1)
    b1_copy = lambda: to_head(grads_h.at[:, pl.ds(aligned(b_give, 16), quarter)], b1_in, 2, 2)
    a_own = a_keep + y_bit * eighth
    a_pass = a_keep + (1 - y_bit) * eighth
    b_own = b_keep + x_bit * eighth
    b_pass = b_keep + (1 - x_bit) * eighth
    a2_copy = lambda: to_head(grads.at[:, pl.ds(aligned(a_pass, 16), eighth)], a2_in, 3, 2)
    b2_copy = lambda: to_head(grads.at[:, pl.ds(aligned(b_pass, 16), eighth)], b2_in, 4, 1)

    def add_rows(into, spot, start, count, other):
        at = pl.ds(aligned(start, 16), count)
        into[spot, at] = (into[spot, at].astype(f32) + other.astype(f32)).astype(bf16)

    def early_first():
        grads_in.wait()
        a1_copy().wait_recv()
        b1_copy().wait_recv()

        def body(i, carry):
            add_rows(grads, i, a_keep, quarter, a1_in[i])
            add_rows(grads, i, b_keep, quarter, b1_in[i])
            return carry

        lax.fori_loop(0, spots, body, None)
        launch(a2_copy)
        launch(b2_copy)

    def early_second_and_on():
        a2_copy().wait_recv()
        b2_copy().wait_recv()

        def body(i, carry):
            add_rows(grads, i, a_own, eighth, a2_in[i])
            add_rows(grads, i, b_own, eighth, b2_in[i])
            return carry

        lax.fori_loop(0, spots, body, None)

        def gather(i, carry):
            all_out[i, :eighth] = grads[i, pl.ds(aligned(a_own, 16), eighth)]
            all_out[i, eighth:] = grads[i, pl.ds(aligned(b_own, 16), eighth)]
            return carry

        lax.fori_loop(0, spots, gather, None)
        if steps:
            z_send(0)

    offsets = []
    at = 0
    size = spots
    for bit in seq_bits[1:]:
        offsets.append((at, size))
        at += size
        size //= 2
    offsets.append((at, 1))
    steps = len(offsets) - 1
    z_offsets = []
    at = 0
    for _, size in offsets[:-1]:
        z_offsets.append(at)
        at += size // 2

    def z_copy(i):
        at, size = offsets[i]
        bit = seq_bits[1 + i]
        return to_seq(
            all_in.at[pl.ds(z_offsets[i], size // 2)], z_in.at[pl.ds(z_offsets[i], size // 2)], 5 + i, bit
        )

    def z_send(i):
        at, size = offsets[i]
        own = lax.rem(lax.div(place, seq_bits[1 + i]), 2)
        for j in range(size // 2):
            all_in[z_offsets[i] + j] = all_out[at + 2 * j + (1 - own)]
        launch(z_copy, i)

    def z_add(i):
        at, size = offsets[i]
        after = offsets[i + 1][0]
        own = lax.rem(lax.div(place, seq_bits[1 + i]), 2)
        z_copy(i).wait_recv()
        for j in range(size // 2):
            all_out[after + j] = (
                all_out[at + 2 * j + own].astype(f32) + z_in[z_offsets[i] + j].astype(f32)
            ).astype(bf16)

    ag_from = 5 + steps
    last = offsets[-1][0]
    ag = sum(size // 2 for _, size in offsets[:-1])

    def ag_copy(k):
        return to_head(all_out.at[last], all_in.at[ag + k], ag_from + k, k)

    def ag_send():
        for k in range(parts - 1, 0, -1):
            launch(ag_copy, k)

    def ag_out():
        moves = [
            (final.at[t * n : (t + 1) * n], up_o.at[:, t * width : (t + 1) * width])
            for t in range(hidden // width)
        ]
        moves.append((final.at[up_rows : 2 * up_rows], down_o))
        moves.append((final.at[2 * up_rows : 2 * up_rows + n], out_o))
        return [pltpu.make_async_copy(src, dst, store_sem.at[i]) for i, (src, dst) in enumerate(moves)]

    def ag_finish():
        for k in range(parts):
            if k:
                ag_copy(k).wait_recv()
                block = all_in[ag + k]
            else:
                block = all_out[last]
            block = block.astype(f32) * grad_norm
            who = flip(me, k, parts)
            x_of, y_of = lax.rem(who, 2), lax.div(who, 2)
            a_at = x_of * quarter + y_of * eighth
            b_at = half + y_of * quarter + x_of * eighth
            final[pl.ds(aligned(a_at, 16), eighth)] = block[:eighth]
            final[pl.ds(aligned(b_at, 16), eighth)] = block[eighth:]
        for copy in ag_out():
            copy.start()
        vec_o[...] = final[2 * up_rows + n : 2 * up_rows + n + 8]

    def d_copy(p, part):
        return send(
            dsend.at[p, part, :, there],
            dfull.at[:, :, pl.ds(aligned(part * width + (2 * core + p) * 128, 128), 128)],
            (dsem.at[0, p, part], dsem.at[1, p, part]),
            (me, other),
        )

    def prepare(p):
        for copy in pair_in[p]:
            copy.wait()
        low_half = lane < 64
        row_of = lax.broadcasted_iota(jnp.int32, (128, 128), 0)
        lane_of = lax.broadcasted_iota(jnp.int32, (128, 128), 1)
        picks = ((row_of < 64) & (lane_of >= 64) & (lane_of < 67)) | ((row_of >= 64) & (lane_of < 3))
        picks = jnp.where(picks, -1.0, 0.0).astype(bf16)
        step = lax.rem(lane, 64)
        kt[...] = qkv[p, 1].T
        qt[...] = qkv[p, 0].T
        gt[...] = go[p].reshape(full, 128).T
        for k in range(parts):
            at = slice(k * rows, (k + 1) * rows)
            query, keys, values = qkv[p, 0, at], qkv[p, 1, at], qkv[p, 2, at]
            pos = lax.broadcasted_iota(jnp.int32, (rows, 1), 0) + flip(me, k, parts) * rows
            bias = jnp.where(pos.astype(f32) < length, 0.0, NEG)
            key_more = jnp.where(step == 0, bias, 1.0).astype(bf16)
            grad = go[p, k]
            prod = grad.astype(f32) * mixed[p, k].astype(f32)
            high = prod.astype(bf16)
            sums = dot(high, picks) + dot((prod - high.astype(f32)).astype(bf16), picks)
            second = sums - sums.astype(bf16).astype(f32)
            third = second - second.astype(bf16).astype(f32)
            grad_more = jnp.where(step == 0, sums, jnp.where(step == 1, second, third)).astype(bf16)
            query_more = lse[p, at]
            ka[0, at] = jnp.where(low_half, keys, key_more)
            ka[1, at] = jnp.where(low_half, key_more, keys)
            va[0, at] = jnp.where(low_half, values, one)
            va[1, at] = jnp.where(low_half, one, values)
            qa[0, at] = jnp.where(low_half, query, query_more)
            qa[1, at] = jnp.where(low_half, query_more, query)
            da[0, at] = jnp.where(low_half, grad, grad_more)
            da[1, at] = jnp.where(low_half, grad_more, grad)
        dqt[...] = jnp.zeros_like(dqt)

    steps_each = 2 * parts
    cols_each = full // 2

    def attend_back(p, events):
        def body(j, carry):
            at = pl.ds(aligned(j * rows, rows), rows)
            totals = [None, None]
            for i in range(2):
                for when, event in events.items():
                    if when % 2 == i:
                        pl.when(j == when // 2)(event)
                cols = slice(i * cols_each, (i + 1) * cols_each)
                for h in range(2):
                    part = slice(h * 64, h * 64 + 64)
                    probs = jnp.exp2(dot_nt(qa[h, cols], ka[h, at, :]))
                    inner = dot_nt(da[h, cols], va[h, at, :])
                    low = probs.astype(bf16)
                    grad = (probs * inner).astype(bf16)
                    dv = dot(gt[part, cols], low)
                    dk = dot(qt[part, cols], grad)
                    dqt[part, cols] += dot_nt(kt[part, at], grad)
                    totals[h] = (dv, dk) if i == 0 else (totals[h][0] + dv, totals[h][1] + dk)
            dv = jnp.concatenate([totals[0][0], totals[1][0]], 0).T
            dk = jnp.concatenate([totals[0][1], totals[1][1]], 0).T
            dsend[p, 1, j] = (dk * (1.0 / LOG2E)).astype(bf16)
            dsend[p, 2, j] = dv.astype(bf16)
            return carry

        lax.fori_loop(0, parts, body, None)
        dsend[p, 0] = (dqt[...] * 64 ** (-0.5)).T.astype(bf16).reshape(parts, rows, 128)
        for part in range(3):
            d_copy(p, part).start()
            dfull[:, :, pl.ds(aligned(part * width + (2 * core + p) * 128, 128), 128)] = dsend[p, part, :, here]

    def late_term(p):
        late[p] = sum(
            dot_tn(xs[k], jnp.concatenate([dsend[p, part, k] for part in range(3)], 1)) for k in range(parts)
        )

    l_steps = len(seq_bits)
    l_sizes = [0] + [spots >> i for i in range(l_steps - 1)]
    l_offsets = [0] + [sum(size // 2 for size in l_sizes[1:i]) for i in range(1, l_steps)]

    def l_copy(p, i):
        at = pl.ds(l_offsets[i], l_sizes[i] // 2)
        return send(
            late_step.at[p, at],
            late_got.at[p, at],
            (lsem.at[0, p, i], lsem.at[1, p, i]),
            (me, flip(place, seq_bits[i], shards)),
        )

    def lg_copy(p, k, o):
        slot = 2 * k + o
        return send(
            late_out.at[p, core if o == 0 else 1 - core],
            late_all.at[p, slot],
            (lsem.at[0, p, l_steps + slot], lsem.at[1, p, l_steps + slot]),
            (flip(me, k, parts), place if o == 0 else other),
        )

    def late_spot(p, i, spot):
        if i == 1:
            return late[p, pl.ds(aligned(spot * (2 * n), 16), 2 * n)]
        return late_sum[p, spot]

    def late_split(p, i):
        own = lax.rem(lax.div(place, seq_bits[i]), 2)
        for j in range(l_sizes[i] // 2):
            late_step[p, l_offsets[i] + j] = late_spot(p, i, 2 * j + 1 - own).astype(bf16)
        launch(l_copy, p, i)

    def late_merge(p, i):
        own = lax.rem(lax.div(place, seq_bits[i]), 2)
        l_copy(p, i).wait_recv()
        for j in range(l_sizes[i] // 2):
            late_sum[p, j] = late_spot(p, i, 2 * j + own) + late_got[p, l_offsets[i] + j].astype(f32)

    def late_share(p):
        total = late_sum[p, 0] if l_steps > 1 else late[p]
        late_out[p, 0] = total[:n].astype(bf16)
        late_out[p, 1] = total[n:].astype(bf16)
        for k in range(parts - 1, -1, -1):
            for o in range(2):
                if k or o:
                    launch(lg_copy, p, k, o)

    def late_finish(p):
        for o in range(2):
            total = late_out[p, core].astype(f32) if o == 0 else None
            for k in range(parts):
                if k or o:
                    lg_copy(p, k, o).wait_recv()
                    piece = late_all[p, 2 * k + o].astype(f32)
                    total = piece if total is None else total + piece
            total = total * grad_norm
            owner = core if o == 0 else 1 - core
            for part in range(3):
                to = aligned(part * width + (2 * owner + p) * 128, 128)
                wqkv_o[:, pl.ds(to, 128)] = total[:, part * 128 : part * 128 + 128]

    def late_start(p):
        if l_steps > 1:
            late_split(p, 1)
        else:
            late_share(p)

    def late_events(p):
        steps_of = []
        for i in range(1, l_steps):

            def step(i=i):
                late_merge(p, i)
                if i + 1 < l_steps:
                    late_split(p, i + 1)
                else:
                    late_share(p)

            steps_of.append(step)
        return steps_of

    def both_events(one_event, two_event):
        def run():
            one_event()
            two_event()

        return run

    def out_copies(a, k):
        src = (added_h, dx_v)[a].at[k]
        dst = (added_o, dx_o)[a].at[from_group, here]
        to = (flip(me, k, parts), place - core + from_core)
        remote = send(src, dst, (osem.at[0, a, k], osem.at[1, a, 2 * from_group + core]), to)
        return remote, pltpu.make_async_copy(src, dst, self_sem.at[a])

    def out_start(a, k):
        remote, local = out_copies(a, k)
        if k:
            remote.start()
        else:
            pl.when(from_core == core)(local.start)
            pl.when(from_core != core)(remote.start)

    def out_wait(a):
        for k in range(parts):
            remote, local = out_copies(a, k)
            if k:
                remote.wait_send()
            else:
                pl.when(from_core == core)(local.wait)
                pl.when(from_core != core)(remote.wait_send)
        for s in (0, 1):
            for r in (0, 1):
                chip = 2 * core + s
                dst = (added_o, dx_o)[a].at[s, r * half_rows : (r + 1) * half_rows]
                remote = send(
                    (added_h, dx_v)[a].at[0],
                    dst,
                    (osem.at[0, a, 0], osem.at[1, a, 2 * s + r]),
                    (chip, place - core + r),
                )
                pl.when(jnp.logical_not((chip == me) & (core == r)))(remote.wait_recv)

    def early_second_and_added():
        early_second_and_on()
        for k in range(parts - 1, -1, -1):
            out_start(0, k)

    launch(a1_copy)
    launch(b1_copy)
    prepare(0)
    attend_back(0, {6: early_first})
    xs_in.wait()
    late_term(0)
    late_start(0)
    prepare(1)
    early_steps = [early_second_and_added]
    for i in range(1, steps):

        def early_step(i=i):
            z_add(i - 1)
            z_send(i)

        early_steps.append(early_step)

    def early_last():
        if steps:
            z_add(steps - 1)
        ag_send()

    early_steps.append(early_last)
    events = {}
    later = []

    def schedule(steps_list, slots):
        for index, event in enumerate(steps_list):
            slot = slots[index] if index < len(slots) else steps_each
            if slot >= steps_each:
                later.append(event)
            elif slot in events:
                events[slot] = both_events(events[slot], event)
            else:
                events[slot] = event

    schedule(early_steps, (0, 4, 7))
    schedule(late_events(0), (2, 5))
    attend_back(1, events)
    for event in later:
        event()
    late_term(1)
    late_start(1)
    tail = late_events(1)
    wqkv_in.wait()
    first_in.wait()
    for p in range(2):
        for part in range(3):
            d_copy(p, part).wait_recv()
    for k in range(parts - 1, -1, -1):
        dx_v[k] = (first[k] + dot_nt(dfull[k], wqkv[...])).astype(bf16)
        out_start(1, k)
    if tail:
        tail.pop(0)()
    ag_finish()
    late_finish(0)
    for event in tail:
        event()
    late_finish(1)
    for make in sends:
        make().wait_send()
    for p in range(2):
        for part in range(3):
            d_copy(p, part).wait_send()
    out_wait(0)
    out_wait(1)
    for copy in ag_out():
        copy.wait()


def second_call(parts, shards, grad_norm, length, saved, grads, first, added, wqkv, hidden):
    xs_shape = saved[4].shape
    _, rows, width = xs_shape
    full = rows * parts
    half_rows = rows // 2
    n, up_rows, vector_rows, total_rows = grad_rows(width, hidden, shards)
    spots = shards // 2
    quarter, eighth = total_rows // 4, total_rows // 8
    heads = (2, full, 128)
    return pl.pallas_call(
        functools.partial(second_kernel, parts, shards, grad_norm),
        in_specs=[VMEM] + [ANY] * 9,
        out_specs=[ANY, ANY, VMEM, ANY, ANY, ANY, VMEM],
        out_shape=[
            jax.ShapeDtypeStruct((2, rows, width), bf16),
            jax.ShapeDtypeStruct((2, rows, width), bf16),
            jax.ShapeDtypeStruct((n, 3 * width), f32),
            jax.ShapeDtypeStruct((n, hidden), f32),
            jax.ShapeDtypeStruct((up_rows, width), f32),
            jax.ShapeDtypeStruct((n, width), f32),
            jax.ShapeDtypeStruct((8, width), f32),
        ],
        scratch_shapes=[
            pltpu.VMEM(xs_shape, bf16),
            pltpu.VMEM((2, 3, full, 128), bf16),
            pltpu.VMEM((2, full, 128), bf16),
            pltpu.VMEM((2, parts, rows, 128), bf16),
            pltpu.VMEM((2, parts, rows, 128), bf16),
            pltpu.VMEM((width, 3 * width), bf16),
            pltpu.VMEM((parts, half_rows, width), f32),
            pltpu.VMEM((spots, total_rows, width), bf16),
            pltpu.VMEM((spots, quarter, width), bf16),
            pltpu.VMEM((spots, quarter, width), bf16),
            pltpu.VMEM((spots, eighth, width), bf16),
            pltpu.VMEM((spots, eighth, width), bf16),
            pltpu.VMEM((spots, quarter, width), bf16),
            pltpu.VMEM((2 * spots, quarter, width), bf16),
            pltpu.VMEM((spots + parts, quarter, width), bf16),
            pltpu.VMEM((total_rows, width), f32),
            pltpu.VMEM(heads, bf16),
            pltpu.VMEM(heads, bf16),
            pltpu.VMEM(heads, bf16),
            pltpu.VMEM(heads, bf16),
            pltpu.VMEM((128, full), bf16),
            pltpu.VMEM((128, full), bf16),
            pltpu.VMEM((128, full), bf16),
            pltpu.VMEM((128, full), f32),
            pltpu.VMEM((2, 3, parts, rows, 128), bf16),
            pltpu.VMEM((parts, half_rows, 3 * width), bf16),
            pltpu.VMEM((parts, half_rows, width), bf16),
            pltpu.VMEM((2, width, 384), f32),
            pltpu.VMEM((2, 2, n, 384), bf16),
            pltpu.VMEM((2, spots, 2 * n, 384), f32),
            pltpu.VMEM((2, spots, 2 * n, 384), bf16),
            pltpu.VMEM((2, spots, 2 * n, 384), bf16),
            pltpu.VMEM((2, 2 * parts, n, 384), bf16),
            DMA((16,)),
            DMA((16,)),
            DMA((2,)),
            DMA((2, 2, 3)),
            DMA((2, 24)),
            DMA((2, 2, 16)),
            DMA((2, 2, 4)),
        ],
        compiler_params=pltpu.CompilerParams(
            vmem_limit_bytes=VMEM_LIMIT, collective_id=1, has_side_effects=True
        ),
        name="backward_and_sums",
    )(length, *saved, grads, first, added, wqkv)


def last_kernel(rows_here, lengths, post_h, added_h, dx_h, y, ac, vec, *rest):
    ins, (post_o, accum_o, dx_o, accg_o), outs, vectors = rest[:4], rest[4:8], rest[8:12], rest[12:]
    step = pl.program_id(0)
    for src, dst in zip(ins, outs):
        dst[...] = src[...]

    @pl.when(step == 0)
    def _():
        for i, out in enumerate(vectors):
            out[...] = vec[i : i + 1, : out.shape[1]]

    _, rows, _ = y.shape
    steps = pl.num_programs(0)
    length = lengths[lax.div(step * 2, steps)]
    start = lax.axis_index("head") * rows_here + lax.rem(step, lax.div(steps, 2)) * rows
    keep = lax.broadcasted_iota(jnp.int32, (1, rows, 1), 1) + start < length
    post_o[...] = post_h[...].astype(f32)
    accum_o[...] = jnp.where(keep, y[...].astype(f32) + added_h[...].astype(f32), 0.0)
    dx_o[...] = dx_h[...].astype(f32)
    accg_o[...] = jnp.where(keep, ac[...].astype(f32), 0.0)


def last_call(lengths, tokens, streams, vectors, grads, shards):
    groups, rows, width = tokens[0].shape
    cut = 2
    steps = groups * cut
    block = pl.BlockSpec((1, rows // cut, width), lambda i: (i // cut, i % cut, 0))
    whole = jax.ShapeDtypeStruct((groups, rows, width), f32)
    n = width // shards
    hidden = grads[1].shape[1]
    short = [jax.ShapeDtypeStruct((1, n), f32)] * 5 + [jax.ShapeDtypeStruct((1, hidden // shards), f32)]
    moved = [pl.BlockSpec((g.shape[0], g.shape[1] // steps), lambda i: (0, i)) for g in grads]
    return pl.pallas_call(
        functools.partial(last_kernel, rows),
        grid=(steps,),
        in_specs=[SMEM] + [block] * 5 + [pl.BlockSpec(vectors.shape, lambda i: (0, 0))] + moved,
        out_specs=[block] * 4 + moved + [pl.BlockSpec(o.shape, lambda i: (0, 0)) for o in short],
        out_shape=[whole] * 4 + [jax.ShapeDtypeStruct(g.shape, f32) for g in grads] + short,
        compiler_params=pltpu.CompilerParams(vmem_limit_bytes=VMEM_LIMIT),
        name="outputs",
    )(lengths, *tokens, *streams, vectors, *grads)


def local(
    post_stream,
    accum_stream,
    seq_lengths,
    qkv_weight,
    out_weight,
    norm1_gain,
    norm1_bias,
    up_weight,
    up_bias,
    down_weight,
    down_bias,
    norm2_gain,
    norm2_bias,
    post_cotan,
    accum_cotan,
):
    groups, rows, width = post_stream.shape
    parts = lax.axis_size("head")
    shards = lax.axis_size("seq")
    hidden = up_weight.shape[1]
    grad_norm = float(groups * shards * rows * parts) ** (-0.5)

    def row(vector):
        return vector.reshape(1, -1)

    weights = (
        qkv_weight,
        out_weight,
        row(norm1_gain),
        row(norm1_bias),
        up_weight,
        row(up_bias),
        down_weight,
        row(down_bias),
        row(norm2_gain),
        row(norm2_bias),
    )
    post, added, first, qkv, lse, mixed, go, xs, grads, length = first_call(
        parts, shards, seq_lengths, (post_stream, post_cotan, accum_cotan), weights
    )
    dx, added, qkv_grad, up_grad, down_grad, out_grad, vectors = second_call(
        parts, shards, grad_norm, length, (qkv, lse, mixed, go, xs), grads, first, added, qkv_weight, hidden
    )
    post, accum, post_grad, accum_grad, qkv_grad, up_grad, down_grad, out_grad, *short = last_call(
        seq_lengths,
        (post, added, dx),
        (accum_stream, accum_cotan),
        vectors,
        (qkv_grad, up_grad, down_grad, out_grad),
        shards,
    )
    gain1, bias1, gain2, bias2, down_bias_grad, up_bias_grad = [v.reshape(-1) for v in short]
    return (
        post,
        accum,
        post_grad,
        accum_grad,
        qkv_grad,
        out_grad,
        gain1,
        bias1,
        up_grad,
        up_bias_grad,
        down_grad,
        down_bias_grad,
        gain2,
        bias2,
    )


def solution(mesh):
    tokens = P("seq", "head", None)
    in_specs = (tokens, tokens, P("seq")) + (P(),) * 10 + (tokens, tokens)
    rows = P("seq", None)
    vector = P("seq")
    out_specs = (tokens,) * 4 + (rows, rows, vector, vector, rows, vector, rows, vector, vector, vector)
    return jax.shard_map(local, mesh=mesh, in_specs=in_specs, out_specs=out_specs, check_vma=False)
```
